32 devices in a mesh: groups: 2 (over x), depth: 16 (over z, y, core).
Axes of the slice: x: 2, y: 2, z: 4, core: 2. Of those that a mesh axis runs over, the one named last changes fastest.
Arguments:
- field: bfloat16 [512, 32, 8192], P('depth', 'groups'), parts along dimension 1, may hold values from 0.049 to 5.05
- jitter: float32 [32, 8192], P('groups'), parts along dimension 0, may hold values from 0 to 1
- transfer: float32 [4], replicated, may hold values from 0.3 to 16
- depth_order: int32 [16], replicated, may hold values from 0 to 15, each once
- ray_start: int32 [128], replicated, may hold values from 0 to 255
- ray_end: int32 [128], replicated, may hold values from 256 to 512
Outputs:
- image: float32 [4, 32, 8192], P(None, 'groups', 'depth'), parts along dimension 1
The draws below stay inside these ranges and needn't reach their ends.
There are 2 independent parts, one for each index of `groups`. The reference program is written for one: setup_inputs(seed, part) draws one part's arguments, and reference() takes and returns one part's arrays. A program takes and returns all parts, laid end to end along the dimension named above; an argument that names none is the same for every part. Nothing has to cross between parts.
Inputs may be any that keep to these rules, and one draw needn't show every extreme that they name: `depth_order`: a permutation of the slab indices.
All inputs are finite; a program needn't handle non-finite values.
Results may differ from the reference program's by a relative error of at most 0.0003.
Values may be sent and summed in bfloat16 or wider, within the bound.
No kernel may reach another device: no remote copies, remote signals or barrier semaphores. Data moves between devices by JAX's collectives and lax.ppermute only.
A program may use at most 128 MiB of HBM per device.

```python
import math
import jax
import jax.numpy as jnp
from jax import lax

ROWS = 16
COLS = 8192
TILE = 64
SL = 32
NTILE = 128
NZ = 512
N_DEPTH = 16


def draw_field(key, part):
    key = jax.random.fold_in(key, 11)
    uniform_draw = jax.random.uniform(key, (NZ, ROWS, COLS), jnp.float32)
    values = 0.05 * jnp.exp(uniform_draw * math.log(100.0))
    return values.astype(jnp.bfloat16)


def draw_transfer(key, part):
    key = jax.random.fold_in(key, 23)
    key_levels, key_order, key_gain = jax.random.split(key, 3)
    lowest = jnp.array([0.3, 0.7, 1.3], jnp.float32)
    spans = jnp.array([0.2, 0.2, 0.4], jnp.float32)
    level_draw = jax.random.uniform(key_levels, (3,), jnp.float32)
    gain_draw = jax.random.uniform(key_gain, (1,), jnp.float32)
    levels = lowest + spans * level_draw
    order = jax.random.permutation(key_order, 3)
    chosen = jnp.take(levels, order)
    gain = 8.0 + 8.0 * gain_draw
    return jnp.concatenate([chosen, gain]).astype(jnp.float32)


def place_ends(values, rng, low, high):
    dims = values.shape
    place = [jax.random.randint(jax.random.fold_in(rng, axis), (), 0, dims[axis]) for axis in range(len(dims))]
    values = values.at[tuple(place)].set(low)
    longest = dims.index(max(dims))
    place[longest] = (place[longest] + 1) % dims[longest]
    return values.at[tuple(place)].set(high)


def setup_inputs(seed: int = 0, part: int = 0) -> dict:
    splits = jax.random.split(jax.random.key(seed), 7)
    part_splits = jax.random.split(jax.random.fold_in(splits[6], part), 7)
    return {
        "field": draw_field(jax.random.fold_in(jax.random.fold_in(splits[6], part), 71), part),
        "jitter": jnp.clip(jax.random.uniform(part_splits[1], (ROWS, COLS), jnp.float32, 0.0, 1.0), 0.0, 1.0),
        "transfer": draw_transfer(jax.random.fold_in(splits[6], 71), part),
        "depth_order": jax.random.permutation(splits[3], N_DEPTH).astype(jnp.int32),
        "ray_start": place_ends(jax.random.randint(splits[4], (NTILE,), 0, NZ // 2), jax.random.fold_in(splits[4], 1), 0, (NZ // 2) - 1).astype(jnp.int32),
        "ray_end": place_ends(jax.random.randint(splits[5], (NTILE,), NZ // 2, NZ + 1), jax.random.fold_in(splits[5], 1), NZ // 2, NZ).astype(jnp.int32),
    }


def slab_partial(planes, following, jitter, transfer, start_cols, end_cols, base, total):
    lower = planes.astype(jnp.float32)
    upper = jnp.concatenate([lower[1:], following.astype(jnp.float32)[None]], axis=0)
    value = (1.0 - jitter)[None] * lower + jitter[None] * upper
    sample = base + jnp.arange(planes.shape[0], dtype=jnp.int32)[:, None, None]
    active = (sample >= start_cols) & (sample < end_cols)
    tau = jnp.where(active, transfer[3] * 0.2 / total * value, jnp.float32(0.0))
    before = jnp.cumsum(tau, axis=0) - tau
    weight = jnp.exp(-before) * (1.0 - jnp.exp(-tau))
    red = jnp.sum(weight * (value / (transfer[0] + value)), axis=0)
    green = jnp.sum(weight * (value / (transfer[1] + value)), axis=0)
    blue = jnp.sum(weight * (value / (transfer[2] + value)), axis=0)
    depth_sum = jnp.sum(tau, axis=0)
    return jnp.stack([red, green, blue, depth_sum], axis=0)


def reference(field, jitter, transfer, depth_order, ray_start, ray_end):
    rows = field.shape[1]
    cols = field.shape[2]
    slabs = field.reshape(N_DEPTH, SL, rows, cols)
    following = jnp.concatenate([field[SL::SL], jnp.zeros((1, rows, cols), field.dtype)], axis=0)
    start_cols = jnp.repeat(ray_start, TILE, total_repeat_length=cols)[None, None, :]
    end_cols = jnp.repeat(ray_end, TILE, total_repeat_length=cols)[None, None, :]
    bases = (jnp.arange(N_DEPTH, dtype=jnp.int32) * SL).astype(jnp.int32)

    def one_slab(carry, items):
        planes, nextplane, base = items
        return carry, slab_partial(planes, nextplane, jitter, transfer, start_cols, end_cols, base, NZ)

    unused, partials = lax.scan(one_slab, jnp.float32(0.0), (slabs, following, bases))
    ordered = jnp.take(partials, depth_order, axis=0)
    depths = ordered[:, 3]
    prefix = jnp.cumsum(depths, axis=0) - depths
    color = jnp.sum(jnp.exp(-prefix)[:, None] * ordered[:, :3], axis=0)
    alpha = 1.0 - jnp.exp(-jnp.sum(depths, axis=0))
    return jnp.concatenate([color, alpha[None]], axis=0)
```

```python
import functools
import math

import jax
import jax.numpy as jnp
from jax import lax
from jax.experimental import pallas as pl
from jax.experimental.pallas import tpu as pltpu
from jax.sharding import PartitionSpec as P

TOP = 5.2
LOG2E = math.log2(math.e)
LANES = 128


def spans(slab_len):
    deep = math.log2(slab_len)
    return 6.8 + deep, 13.2 + deep


def shifted(value, axis, steps):
    count = lax.axis_size(axis)
    initial, last = (max(0, -steps), min(count, count - steps))
    return lax.ppermute(value, axis, [(source, source + steps) for source in range(initial, last)])


def encode(value, span):
    code = jnp.log2(value) * (65535.0 / span) + 65535.5
    code = jnp.minimum(jnp.maximum(code, 0.0), 65535.0)
    return (code.astype(jnp.int32) - 32768).astype(jnp.int16)


def slab_kernel(total, tile_cols, chunk, chunks, base_ref, transfer_ref, start_ref, end_ref, field_ref, halo_ref,
                jitter_ref, out_ref, gain_ref):
    slab_len, rows, width = field_ref.shape
    base = base_ref[0]
    first_col = (pl.program_id(0) * chunks + chunk) * width
    depth_gain = jnp.full((rows, LANES), transfer_ref[3]) * (0.2 / total)
    levels = [jnp.full((rows, LANES), transfer_ref[i]) for i in range(3)]
    depth_unit = 1.0 / (depth_gain * (slab_len * TOP))
    color_unit = [depth_unit * ((levels[i] + TOP) * (1.0 / TOP)) for i in range(3)]
    depth_span, color_span = spans(slab_len)
    sample = lax.broadcasted_iota(jnp.int32, (8, LANES), 0) + base
    lane = lax.broadcasted_iota(jnp.int32, (8, LANES), 1)
    tile_gain = depth_gain[:8] * -LOG2E

    def block(n, carry):
        cols = pl.ds(pl.multiple_of(n * LANES, LANES), LANES)
        tile = (first_col + n * LANES) // tile_cols
        start = jnp.full((8, LANES), start_ref[tile])
        end = jnp.full((8, LANES), end_ref[tile])
        for t in range(1, LANES // tile_cols):
            start = jnp.where(lane >= t * tile_cols, start_ref[tile + t], start)
            end = jnp.where(lane >= t * tile_cols, end_ref[tile + t], end)
        for k in range(0, slab_len, 8):
            active = (sample + k >= start) & (sample + k < end)
            gain_ref[k:k + 8, :] = jnp.where(active, tile_gain, 0.0)
        jitter = jitter_ref[:, cols]
        stay = 1.0 - jitter
        lower = field_ref[0, :, cols].astype(jnp.float32)
        before = jnp.zeros((rows, LANES), jnp.float32)
        through = jnp.ones((rows, LANES), jnp.float32)
        sums = [jnp.zeros((rows, LANES), jnp.float32) for _ in range(3)]
        for k in range(slab_len):
            following = field_ref[k + 1, :, cols] if k + 1 < slab_len else halo_ref[:, cols]
            upper = following.astype(jnp.float32)
            value = stay * lower + jitter * upper
            before = before + gain_ref[k:k + 1, :] * value
            beyond = jnp.exp2(before)
            emitted = (through - beyond) * value
            for i in range(3):
                sums[i] = sums[i] + emitted * pl.reciprocal(levels[i] + value, approx=True)
            through = beyond
            lower = upper
        for i in range(3):
            out_ref[0, i, :, cols] = encode(sums[i] * color_unit[i], color_span)
        out_ref[0, 3, :, cols] = encode(before * (depth_unit * (-1.0 / LOG2E)), depth_span)
        return carry

    lax.fori_loop(0, width // LANES, block, 0)


def slab_codes(field, halo, jitter, transfer, ray_start, ray_end, base, total, pieces, chunk, chunks):
    slab_len, rows, cols = field.shape
    width = cols // (pieces * chunks)
    tile_cols = cols // ray_start.shape[0]
    smem = pl.BlockSpec(memory_space=pltpu.SMEM)
    return pl.pallas_call(
        functools.partial(slab_kernel, total, tile_cols, chunk, chunks),
        grid=(pieces,),
        in_specs=[
            smem, smem, smem, smem,
            pl.BlockSpec((slab_len, rows, width), lambda p: (0, 0, p * chunks + chunk)),
            pl.BlockSpec((rows, width), lambda p: (0, p * chunks + chunk)),
            pl.BlockSpec((rows, width), lambda p: (0, p * chunks + chunk)),
        ],
        out_specs=pl.BlockSpec((1, 4, rows, width), lambda p: (p, 0, 0, 0)),
        out_shape=jax.ShapeDtypeStruct((pieces, 4, rows, width), jnp.int16),
        scratch_shapes=[pltpu.VMEM((slab_len, LANES), jnp.float32)],
        compiler_params=pltpu.CompilerParams(vmem_limit_bytes=32 * 1024 * 1024),
        cost_estimate=pl.CostEstimate(
            flops=slab_len * rows * width * pieces * 20,
            bytes_accessed=slab_len * rows * width * pieces * 2,
            transcendentals=slab_len * rows * width * pieces * 4,
        ),
        name="slab_codes",
    )(base, transfer, ray_start, ray_end, field, halo, jitter)


def composite_kernel(total, slab_len, chunks, order_ref, transfer_ref, *refs):
    code_refs, out_ref = refs[:chunks], refs[chunks]
    count, _, rows, width = code_refs[0].shape
    lanes = min(width, LANES)
    depth_span, color_span = spans(slab_len)
    depth_gain = jnp.full((rows, lanes), transfer_ref[3]) * (0.2 / total)
    unit = depth_gain * (slab_len * TOP)
    depth_unit = unit * LOG2E

    def decode(codes, span, shift):
        code = codes.astype(jnp.int32).astype(jnp.float32)
        value = jnp.exp2(code * (span / 65535.0) + (span * (32768.0 / 65535.0) - span) - shift)
        return jnp.where(code > -32768.0, value, 0.0)

    for c in range(chunks):
        for n in range(width // lanes):
            cols = slice(n * lanes, (n + 1) * lanes)

            def step(j, carry):
                depth, red, green, blue = carry
                slab = order_ref[j]
                colors = [red, green, blue]
                for i in range(3):
                    colors[i] = colors[i] + decode(code_refs[c][slab, i, :, cols], color_span, depth)
                depth = depth + depth_unit * decode(code_refs[c][slab, 3, :, cols], depth_span, 0.0)
                return depth, *colors

            zero = jnp.zeros((rows, lanes), jnp.float32)
            depth, *colors = lax.fori_loop(0, count, step, (zero, zero, zero, zero))
            place = slice(c * width + n * lanes, c * width + (n + 1) * lanes)
            for i in range(3):
                level = jnp.full((rows, lanes), transfer_ref[i])
                out_ref[i, :, place] = colors[i] * (unit * (TOP / (level + TOP)))
            out_ref[3, :, place] = 1.0 - jnp.exp2(-depth)


def composite(codes, transfer, depth_order, total, slab_len):
    _, _, rows, width = codes[0].shape
    smem = pl.BlockSpec(memory_space=pltpu.SMEM)
    vmem = pl.BlockSpec(memory_space=pltpu.VMEM)
    return pl.pallas_call(
        functools.partial(composite_kernel, total, slab_len, len(codes)),
        in_specs=[smem, smem] + [vmem] * len(codes),
        out_specs=vmem,
        out_shape=jax.ShapeDtypeStruct((4, rows, width * len(codes)), jnp.float32),
        compiler_params=pltpu.CompilerParams(vmem_limit_bytes=32 * 1024 * 1024),
        name="composite",
    )(depth_order, transfer, *codes)


def on_device(field, jitter, transfer, depth_order, ray_start, ray_end):
    count = lax.axis_size("depth")
    here = lax.axis_index("depth")
    slab_len, rows, cols = field.shape
    total = slab_len * count
    width = cols // count
    halo = shifted(field[0], "depth", -1)
    base = jnp.reshape(here * slab_len, (1,)).astype(jnp.int32)
    args = (field, halo, jitter, transfer, ray_start, ray_end, base, total)
    received = []
    if width % (2 * LANES) == 0:
        chunks = 2
        for chunk in range(chunks):
            codes = slab_codes(*args, count, chunk, chunks)
            received.append(lax.all_to_all(codes, "depth", split_axis=0, concat_axis=0, tiled=True))
    else:
        blocks = cols // LANES
        codes = slab_codes(*args, blocks, 0, 1)
        codes = codes.transpose(1, 2, 0, 3).reshape(4, rows, count, width).transpose(2, 0, 1, 3)
        received.append(lax.all_to_all(codes, "depth", split_axis=0, concat_axis=0, tiled=True))
    return composite(received, transfer, depth_order, total, slab_len)


def solution(mesh):
    in_specs = (P("depth", "groups", None), P("groups", None), P(), P(), P(), P())
    out_specs = P(None, "groups", "depth")
    return jax.shard_map(
        on_device, mesh=mesh, in_specs=in_specs, out_specs=out_specs, check_vma=False
    )
```

```python
import functools
import math

import jax
import jax.numpy as jnp
from jax import lax
from jax.experimental import pallas as pl
from jax.experimental.pallas import tpu as pltpu
from jax.sharding import PartitionSpec as P

TOP = 5.2
LOG2E = math.log2(math.e)
LANES = 128
MARCH_BYTES = 54 * 1024 * 1024
SMALL_BYTES = 16 * 1024 * 1024


def spans(slab_len):
    deep = math.log2(slab_len)
    return 6.8 + deep, 13.2 + deep


def shifted(value, axis, steps):
    count = lax.axis_size(axis)
    initial, last = (max(0, -steps), min(count, count - steps))
    return lax.ppermute(value, axis, [(source, source + steps) for source in range(initial, last)])


def encode(value, span):
    code = jnp.log2(value) * (65535.0 / span) + 65535.5
    code = jnp.minimum(jnp.maximum(code, 0.0), 65535.0)
    return (code.astype(jnp.int32) - 32768).astype(jnp.int16)


def tile_gains(gain_ref, gain, base, first_col, tile_cols, start_ref, end_ref):
    sample = lax.broadcasted_iota(jnp.int32, (8, LANES), 0) + base
    lane = lax.broadcasted_iota(jnp.int32, (8, LANES), 1)
    tile = first_col // tile_cols
    start = jnp.full((8, LANES), start_ref[tile])
    end = jnp.full((8, LANES), end_ref[tile])
    for t in range(1, LANES // tile_cols):
        start = jnp.where(lane >= t * tile_cols, start_ref[tile + t], start)
        end = jnp.where(lane >= t * tile_cols, end_ref[tile + t], end)
    for k in range(0, gain_ref.shape[0], 8):
        active = (sample + k >= start) & (sample + k < end)
        gain_ref[k:k + 8, :] = jnp.where(active, gain, 0.0)


def march_kernel(total, tile_cols, base_ref, transfer_ref, start_ref, end_ref, field_ref, jitter_ref, state_ref, last_ref,
                 gain_ref):
    slab_len, rows, width = field_ref.shape
    base = base_ref[0]
    first_col = pl.program_id(0) * width
    levels = [jnp.full((rows, LANES), transfer_ref[i]) for i in range(3)]
    gain = jnp.full((8, LANES), transfer_ref[3]) * (-LOG2E * 0.2 / total)

    def block(n, carry):
        cols = pl.ds(pl.multiple_of(n * LANES, LANES), LANES)
        tile_gains(gain_ref, gain, base, first_col + n * LANES, tile_cols, start_ref, end_ref)
        jitter = jitter_ref[:, cols]
        stay = 1.0 - jitter
        lower = field_ref[0, :, cols].astype(jnp.float32)
        before = jnp.zeros((rows, LANES), jnp.float32)
        through = jnp.ones((rows, LANES), jnp.float32)
        sums = [jnp.zeros((rows, LANES), jnp.float32) for _ in range(3)]
        for k in range(slab_len - 1):
            upper = field_ref[k + 1, :, cols].astype(jnp.float32)
            value = stay * lower + jitter * upper
            before = before + gain_ref[k:k + 1, :] * value
            beyond = jnp.exp2(before)
            emitted = (through - beyond) * value
            for i in range(3):
                sums[i] = sums[i] + emitted * pl.reciprocal(levels[i] + value, approx=True)
            through = beyond
            lower = upper
        for i in range(3):
            state_ref[i, :, cols] = sums[i]
        state_ref[3, :, cols] = before
        last_ref[:, cols] = field_ref[slab_len - 1, :, cols]
        return carry

    lax.fori_loop(0, width // LANES, block, 0)


def finish_kernel(total, tile_cols, slab_len, base_ref, transfer_ref, start_ref, end_ref, last_ref, halo_ref, jitter_ref,
                  state_ref, out_ref, gain_ref):
    pieces, _, rows, width = out_ref.shape
    base = base_ref[0] + slab_len - 1
    first_col = pl.program_id(0) * (pieces * width)
    depth_gain = jnp.full((rows, LANES), transfer_ref[3]) * (0.2 / total)
    levels = [jnp.full((rows, LANES), transfer_ref[i]) for i in range(3)]
    depth_unit = 1.0 / (depth_gain * (slab_len * TOP))
    color_unit = [depth_unit * ((levels[i] + TOP) * (1.0 / TOP)) for i in range(3)]
    depth_span, color_span = spans(slab_len)
    gain = depth_gain[:8] * -LOG2E

    for p in range(pieces):
        for n in range(width // LANES):
            place = p * width + n * LANES
            cols = slice(place, place + LANES)
            tile_gains(gain_ref, gain, base, first_col + place, tile_cols, start_ref, end_ref)
            jitter = jitter_ref[:, cols]
            lower = last_ref[:, cols].astype(jnp.float32)
            upper = halo_ref[:, cols].astype(jnp.float32)
            value = (1.0 - jitter) * lower + jitter * upper
            before = state_ref[3, :, cols]
            beyond = before + gain_ref[0:1, :] * value
            emitted = (jnp.exp2(before) - jnp.exp2(beyond)) * value
            out = slice(n * LANES, (n + 1) * LANES)
            for i in range(3):
                color = state_ref[i, :, cols] + emitted * pl.reciprocal(levels[i] + value, approx=True)
                out_ref[p, i, :, out] = encode(color * color_unit[i], color_span)
            out_ref[p, 3, :, out] = encode(beyond * (depth_unit * (-1.0 / LOG2E)), depth_span)


def slab_codes(field, halo, jitter, transfer, ray_start, ray_end, base, total, pieces):
    slab_len, rows, cols = field.shape
    width = cols // pieces
    step = max(width, min(1024, cols))
    tile_cols = cols // ray_start.shape[0]
    smem = pl.BlockSpec(memory_space=pltpu.SMEM)
    state, last = pl.pallas_call(
        functools.partial(march_kernel, total, tile_cols),
        grid=(cols // step,),
        in_specs=[
            smem, smem, smem, smem,
            pl.BlockSpec((slab_len, rows, step), lambda p: (0, 0, p)),
            pl.BlockSpec((rows, step), lambda p: (0, p)),
        ],
        out_specs=[
            pl.BlockSpec((4, rows, step), lambda p: (0, 0, p)),
            pl.BlockSpec((rows, step), lambda p: (0, p)),
        ],
        out_shape=[
            jax.ShapeDtypeStruct((4, rows, cols), jnp.float32),
            jax.ShapeDtypeStruct((rows, cols), field.dtype),
        ],
        scratch_shapes=[pltpu.VMEM((slab_len, LANES), jnp.float32)],
        compiler_params=pltpu.CompilerParams(vmem_limit_bytes=MARCH_BYTES),
        cost_estimate=pl.CostEstimate(
            flops=slab_len * rows * cols * 20,
            bytes_accessed=slab_len * rows * cols * 2,
            transcendentals=slab_len * rows * cols * 4,
        ),
        name="march",
    )(base, transfer, ray_start, ray_end, field, jitter)
    per = step // width
    return pl.pallas_call(
        functools.partial(finish_kernel, total, tile_cols, slab_len),
        grid=(cols // step,),
        in_specs=[
            smem, smem, smem, smem,
            pl.BlockSpec((rows, step), lambda p: (0, p)),
            pl.BlockSpec((rows, step), lambda p: (0, p)),
            pl.BlockSpec((rows, step), lambda p: (0, p)),
            pl.BlockSpec((4, rows, step), lambda p: (0, 0, p)),
        ],
        out_specs=pl.BlockSpec((per, 4, rows, width), lambda p: (p, 0, 0, 0)),
        out_shape=jax.ShapeDtypeStruct((pieces, 4, rows, width), jnp.int16),
        scratch_shapes=[pltpu.VMEM((8, LANES), jnp.float32)],
        compiler_params=pltpu.CompilerParams(vmem_limit_bytes=SMALL_BYTES),
        name="finish",
    )(base, transfer, ray_start, ray_end, last, halo, jitter, state)


def composite_kernel(total, slab_len, order_ref, transfer_ref, code_ref, out_ref):
    count, _, rows, width = code_ref.shape
    lanes = min(width, LANES)
    depth_span, color_span = spans(slab_len)
    depth_gain = jnp.full((rows, lanes), transfer_ref[3]) * (0.2 / total)
    unit = depth_gain * (slab_len * TOP)
    depth_unit = unit * LOG2E

    def decode(codes, span, shift):
        code = codes.astype(jnp.int32).astype(jnp.float32)
        value = jnp.exp2(code * (span / 65535.0) + (span * (32768.0 / 65535.0) - span) - shift)
        return jnp.where(code > -32768.0, value, 0.0)

    for n in range(width // lanes):
        cols = slice(n * lanes, (n + 1) * lanes)

        def step(j, carry):
            depth, red, green, blue = carry
            slab = order_ref[j]
            colors = [red, green, blue]
            for i in range(3):
                colors[i] = colors[i] + decode(code_ref[slab, i, :, cols], color_span, depth)
            depth = depth + depth_unit * decode(code_ref[slab, 3, :, cols], depth_span, 0.0)
            return depth, *colors

        zero = jnp.zeros((rows, lanes), jnp.float32)
        depth, *colors = lax.fori_loop(0, count, step, (zero, zero, zero, zero), unroll=4)
        for i in range(3):
            level = jnp.full((rows, lanes), transfer_ref[i])
            out_ref[i, :, cols] = colors[i] * (unit * (TOP / (level + TOP)))
        out_ref[3, :, cols] = 1.0 - jnp.exp2(-depth)


def composite(codes, transfer, depth_order, total, slab_len):
    _, _, rows, width = codes.shape
    smem = pl.BlockSpec(memory_space=pltpu.SMEM)
    vmem = pl.BlockSpec(memory_space=pltpu.VMEM)
    return pl.pallas_call(
        functools.partial(composite_kernel, total, slab_len),
        in_specs=[smem, smem, vmem],
        out_specs=vmem,
        out_shape=jax.ShapeDtypeStruct((4, rows, width), jnp.float32),
        compiler_params=pltpu.CompilerParams(vmem_limit_bytes=SMALL_BYTES),
        name="composite",
    )(depth_order, transfer, codes)


def on_device(field, jitter, transfer, depth_order, ray_start, ray_end):
    count = lax.axis_size("depth")
    here = lax.axis_index("depth")
    slab_len, rows, cols = field.shape
    total = slab_len * count
    width = cols // count
    halo = shifted(field[0], "depth", -1)
    base = jnp.reshape(here * slab_len, (1,)).astype(jnp.int32)
    args = (field, halo, jitter, transfer, ray_start, ray_end, base, total)
    if width % LANES == 0:
        codes = slab_codes(*args, count)
    else:
        codes = slab_codes(*args, cols // LANES)
        codes = codes.transpose(1, 2, 0, 3).reshape(4, rows, count, width).transpose(2, 0, 1, 3)
    received = lax.all_to_all(codes, "depth", split_axis=0, concat_axis=0, tiled=True)
    return composite(received, transfer, depth_order, total, slab_len)


def solution(mesh):
    in_specs = (P("depth", "groups", None), P("groups", None), P(), P(), P(), P())
    out_specs = P(None, "groups", "depth")
    return jax.shard_map(
        on_device, mesh=mesh, in_specs=in_specs, out_specs=out_specs, check_vma=False
    )
```

```python
import functools
import math

import jax
import jax.numpy as jnp
from jax import lax
from jax.experimental import pallas as pl
from jax.experimental.pallas import tpu as pltpu
from jax.sharding import PartitionSpec as P

TOP = 5.2
LOG2E = math.log2(math.e)
LANES = 128
MARCH_BYTES = 54 * 1024 * 1024
SMALL_BYTES = 16 * 1024 * 1024


def spans(slab_len):
    deep = math.log2(slab_len)
    return 6.8 + deep, 13.2 + deep


def shifted(value, axis, steps):
    count = lax.axis_size(axis)
    initial, last = (max(0, -steps), min(count, count - steps))
    return lax.ppermute(value, axis, [(source, source + steps) for source in range(initial, last)])


def encode(value, span):
    code = jnp.log2(value) * (65535.0 / span) + 65535.5
    code = jnp.minimum(jnp.maximum(code, 0.0), 65535.0)
    return (code.astype(jnp.int32) - 32768).astype(jnp.int16)


def tile_gains(gain_ref, gain, base, first_col, tile_cols, start_ref, end_ref):
    sample = lax.broadcasted_iota(jnp.int32, (8, LANES), 0) + base
    lane = lax.broadcasted_iota(jnp.int32, (8, LANES), 1)
    tile = first_col // tile_cols
    start = jnp.full((8, LANES), start_ref[tile])
    end = jnp.full((8, LANES), end_ref[tile])
    for t in range(1, LANES // tile_cols):
        start = jnp.where(lane >= t * tile_cols, start_ref[tile + t], start)
        end = jnp.where(lane >= t * tile_cols, end_ref[tile + t], end)
    for k in range(0, gain_ref.shape[0], 8):
        active = (sample + k >= start) & (sample + k < end)
        gain_ref[k:k + 8, :] = jnp.where(active, gain, 0.0)


def march(gain_ref, field_ref, cols, jitter, levels, halo=None):
    slab_len = field_ref.shape[0]
    rows = jitter.shape[0]
    stay = 1.0 - jitter
    lower = field_ref[0, :, cols].astype(jnp.float32)
    before = jnp.zeros((rows, LANES), jnp.float32)
    through = jnp.ones((rows, LANES), jnp.float32)
    sums = [jnp.zeros((rows, LANES), jnp.float32) for _ in range(3)]
    for k in range(slab_len - (halo is None)):
        following = field_ref[k + 1, :, cols] if k + 1 < slab_len else halo
        upper = following.astype(jnp.float32)
        value = stay * lower + jitter * upper
        before = before + gain_ref[k:k + 1, :] * value
        beyond = jnp.exp2(before)
        emitted = (through - beyond) * value
        for i in range(3):
            sums[i] = sums[i] + emitted * pl.reciprocal(levels[i] + value, approx=True)
        through = beyond
        lower = upper
    return sums, before


def open_kernel(total, tile_cols, base_ref, transfer_ref, start_ref, end_ref, field_ref, jitter_ref, state_ref, last_ref,
                gain_ref):
    slab_len, rows, width = field_ref.shape
    first_col = pl.program_id(0) * width
    levels = [jnp.full((rows, LANES), transfer_ref[i]) for i in range(3)]
    gain = jnp.full((8, LANES), transfer_ref[3]) * (-LOG2E * 0.2 / total)

    def block(n, carry):
        cols = pl.ds(pl.multiple_of(n * LANES, LANES), LANES)
        tile_gains(gain_ref, gain, base_ref[0], first_col + n * LANES, tile_cols, start_ref, end_ref)
        sums, before = march(gain_ref, field_ref, cols, jitter_ref[:, cols], levels)
        for i in range(3):
            state_ref[i, :, cols] = sums[i]
        state_ref[3, :, cols] = before
        last_ref[:, cols] = field_ref[slab_len - 1, :, cols]
        return carry

    lax.fori_loop(0, width // LANES, block, 0)


def close_kernel(total, tile_cols, opened, base_ref, transfer_ref, start_ref, end_ref, field_ref, halo_ref, jitter_ref,
                 state_ref, last_ref, out_ref, gain_ref):
    slab_len, rows, step = field_ref.shape
    pieces, _, _, width = out_ref.shape
    first_col = pl.program_id(0) * step
    depth_gain = jnp.full((rows, LANES), transfer_ref[3]) * (0.2 / total)
    levels = [jnp.full((rows, LANES), transfer_ref[i]) for i in range(3)]
    depth_unit = 1.0 / (depth_gain * (slab_len * TOP))
    color_unit = [depth_unit * ((levels[i] + TOP) * (1.0 / TOP)) for i in range(3)]
    depth_span, color_span = spans(slab_len)
    gain = depth_gain[:8] * -LOG2E

    def each_block(body):
        for p in range(pieces):
            def block(n, carry):
                out = pl.ds(pl.multiple_of(n * LANES, LANES), LANES)
                place = p * width + n * LANES
                cols = pl.ds(pl.multiple_of(place, LANES), LANES)
                sums, before = body(place, cols)
                for i in range(3):
                    out_ref[p, i, :, out] = encode(sums[i] * color_unit[i], color_span)
                out_ref[p, 3, :, out] = encode(before * (depth_unit * (-1.0 / LOG2E)), depth_span)
                return carry

            lax.fori_loop(0, width // LANES, block, 0)

    def finish(place, cols):
        tile_gains(gain_ref.at[0:8, :], gain, base_ref[0] + slab_len - 1, first_col + place, tile_cols, start_ref, end_ref)
        jitter = jitter_ref[:, cols]
        lower = last_ref[:, cols].astype(jnp.float32)
        upper = halo_ref[:, cols].astype(jnp.float32)
        value = (1.0 - jitter) * lower + jitter * upper
        before = state_ref[3, :, cols]
        beyond = before + gain_ref[0:1, :] * value
        emitted = (jnp.exp2(before) - jnp.exp2(beyond)) * value
        sums = [state_ref[i, :, cols] + emitted * pl.reciprocal(levels[i] + value, approx=True) for i in range(3)]
        return sums, beyond

    def whole(place, cols):
        tile_gains(gain_ref, gain, base_ref[0], first_col + place, tile_cols, start_ref, end_ref)
        return march(gain_ref, field_ref, cols, jitter_ref[:, cols], levels, halo_ref[:, cols])

    @pl.when(pl.program_id(0) < opened)
    def _():
        each_block(finish)

    @pl.when(pl.program_id(0) >= opened)
    def _():
        each_block(whole)


def slab_codes(field, halo, jitter, transfer, ray_start, ray_end, base, total, pieces):
    slab_len, rows, cols = field.shape
    width = cols // pieces
    step = max(width, min(1024, cols))
    steps = cols // step
    opened = max(1, steps * 5 // 8)
    tile_cols = cols // ray_start.shape[0]
    smem = pl.BlockSpec(memory_space=pltpu.SMEM)
    params = pltpu.CompilerParams(vmem_limit_bytes=MARCH_BYTES)
    scalars = (base, transfer, ray_start, ray_end)

    def cost(share):
        work = slab_len * rows * cols * share // steps
        return pl.CostEstimate(flops=work * 20, bytes_accessed=work * 2, transcendentals=work * 4)

    state, last = pl.pallas_call(
        functools.partial(open_kernel, total, tile_cols),
        grid=(opened,),
        in_specs=[
            smem, smem, smem, smem,
            pl.BlockSpec((slab_len, rows, step), lambda p: (0, 0, p)),
            pl.BlockSpec((rows, step), lambda p: (0, p)),
        ],
        out_specs=[
            pl.BlockSpec((4, rows, step), lambda p: (0, 0, p)),
            pl.BlockSpec((rows, step), lambda p: (0, p)),
        ],
        out_shape=[
            jax.ShapeDtypeStruct((4, rows, opened * step), jnp.float32),
            jax.ShapeDtypeStruct((rows, opened * step), field.dtype),
        ],
        scratch_shapes=[pltpu.VMEM((slab_len, LANES), jnp.float32)],
        compiler_params=params,
        cost_estimate=cost(opened),
        name="open",
    )(*scalars, field, jitter)
    per = step // width
    return pl.pallas_call(
        functools.partial(close_kernel, total, tile_cols, opened),
        grid=(steps,),
        in_specs=[
            smem, smem, smem, smem,
            pl.BlockSpec((slab_len, rows, step), lambda p: (0, 0, jnp.maximum(p, min(opened, steps - 1)))),
            pl.BlockSpec((rows, step), lambda p: (0, p)),
            pl.BlockSpec((rows, step), lambda p: (0, p)),
            pl.BlockSpec((4, rows, step), lambda p: (0, 0, jnp.minimum(p, opened - 1))),
            pl.BlockSpec((rows, step), lambda p: (0, jnp.minimum(p, opened - 1))),
        ],
        out_specs=pl.BlockSpec((per, 4, rows, width), lambda p: (p, 0, 0, 0)),
        out_shape=jax.ShapeDtypeStruct((pieces, 4, rows, width), jnp.int16),
        scratch_shapes=[pltpu.VMEM((slab_len, LANES), jnp.float32)],
        compiler_params=params,
        cost_estimate=cost(steps - opened),
        name="close",
    )(*scalars, field, halo, jitter, state, last)


def composite_kernel(total, slab_len, order_ref, transfer_ref, code_ref, out_ref):
    count, _, rows, width = code_ref.shape
    lanes = min(width, LANES)
    depth_span, color_span = spans(slab_len)
    depth_gain = jnp.full((rows, lanes), transfer_ref[3]) * (0.2 / total)
    unit = depth_gain * (slab_len * TOP)
    depth_unit = unit * LOG2E

    def decode(codes, span, shift):
        code = codes.astype(jnp.int32).astype(jnp.float32)
        value = jnp.exp2(code * (span / 65535.0) + (span * (32768.0 / 65535.0) - span) - shift)
        return jnp.where(code > -32768.0, value, 0.0)

    for n in range(width // lanes):
        cols = slice(n * lanes, (n + 1) * lanes)

        def step(j, carry):
            depth, red, green, blue = carry
            slab = order_ref[j]
            colors = [red, green, blue]
            for i in range(3):
                colors[i] = colors[i] + decode(code_ref[slab, i, :, cols], color_span, depth)
            depth = depth + depth_unit * decode(code_ref[slab, 3, :, cols], depth_span, 0.0)
            return depth, *colors

        zero = jnp.zeros((rows, lanes), jnp.float32)
        depth, *colors = lax.fori_loop(0, count, step, (zero, zero, zero, zero), unroll=4)
        for i in range(3):
            level = jnp.full((rows, lanes), transfer_ref[i])
            out_ref[i, :, cols] = colors[i] * (unit * (TOP / (level + TOP)))
        out_ref[3, :, cols] = 1.0 - jnp.exp2(-depth)


def composite(codes, transfer, depth_order, total, slab_len):
    _, _, rows, width = codes.shape
    smem = pl.BlockSpec(memory_space=pltpu.SMEM)
    vmem = pl.BlockSpec(memory_space=pltpu.VMEM)
    return pl.pallas_call(
        functools.partial(composite_kernel, total, slab_len),
        in_specs=[smem, smem, vmem],
        out_specs=vmem,
        out_shape=jax.ShapeDtypeStruct((4, rows, width), jnp.float32),
        compiler_params=pltpu.CompilerParams(vmem_limit_bytes=SMALL_BYTES),
        name="composite",
    )(depth_order, transfer, codes)


def on_device(field, jitter, transfer, depth_order, ray_start, ray_end):
    count = lax.axis_size("depth")
    here = lax.axis_index("depth")
    slab_len, rows, cols = field.shape
    total = slab_len * count
    width = cols // count
    halo = shifted(field[0], "depth", -1)
    base = jnp.reshape(here * slab_len, (1,)).astype(jnp.int32)
    args = (field, halo, jitter, transfer, ray_start, ray_end, base, total)
    if width % LANES == 0:
        codes = slab_codes(*args, count)
    else:
        codes = slab_codes(*args, cols // LANES)
        codes = codes.transpose(1, 2, 0, 3).reshape(4, rows, count, width).transpose(2, 0, 1, 3)
    received = lax.all_to_all(codes, "depth", split_axis=0, concat_axis=0, tiled=True)
    return composite(received, transfer, depth_order, total, slab_len)


def solution(mesh):
    in_specs = (P("depth", "groups", None), P("groups", None), P(), P(), P(), P())
    out_specs = P(None, "groups", "depth")
    return jax.shard_map(
        on_device, mesh=mesh, in_specs=in_specs, out_specs=out_specs, check_vma=False
    )
```

```python
import functools
import math

import jax
import jax.numpy as jnp
from jax import lax
from jax.experimental import pallas as pl
from jax.experimental.pallas import tpu as pltpu
from jax.sharding import PartitionSpec as P

TOP = 5.2
LOG2E = math.log2(math.e)
LANES = 128
MARCH_BYTES = 54 * 1024 * 1024
SMALL_BYTES = 16 * 1024 * 1024


def spans(slab_len):
    deep = math.log2(slab_len)
    return 6.8 + deep, 13.2 + deep


def shifted(value, axis, steps):
    count = lax.axis_size(axis)
    initial, last = (max(0, -steps), min(count, count - steps))
    return lax.ppermute(value, axis, [(source, source + steps) for source in range(initial, last)])


def encode(value, span):
    code = jnp.log2(value) * (65535.0 / span) + 65535.5
    code = jnp.minimum(jnp.maximum(code, 0.0), 65535.0)
    return (code.astype(jnp.int32) - 32768).astype(jnp.int16)


def tile_gains(gain_ref, gain, base, first_col, tile_cols, start_ref, end_ref):
    sample = lax.broadcasted_iota(jnp.int32, (8, LANES), 0) + base
    lane = lax.broadcasted_iota(jnp.int32, (8, LANES), 1)

    def block(n, carry):
        col = n * LANES
        tile = (first_col + col) // tile_cols
        start = jnp.full((8, LANES), start_ref[tile])
        end = jnp.full((8, LANES), end_ref[tile])
        for t in range(1, LANES // tile_cols):
            start = jnp.where(lane >= t * tile_cols, start_ref[tile + t], start)
            end = jnp.where(lane >= t * tile_cols, end_ref[tile + t], end)
        cols = pl.ds(pl.multiple_of(col, LANES), LANES)
        for k in range(0, gain_ref.shape[0], 8):
            active = (sample + k >= start) & (sample + k < end)
            gain_ref[k:k + 8, cols] = jnp.where(active, gain, 0.0)
        return carry

    blocks = gain_ref.shape[1] // LANES
    lax.fori_loop(0, blocks, block, 0, unroll=math.gcd(blocks, 4))


def march(gain_ref, plane_ref, chunk, cols, place, jitter, levels, halo=None):
    slab_len = plane_ref.shape[1]
    shape = jitter.shape
    stay = 1.0 - jitter
    lower = plane_ref[chunk, 0, :, cols].astype(jnp.float32)
    before = jnp.zeros(shape, jnp.float32)
    through = jnp.ones(shape, jnp.float32)
    sums = [jnp.zeros(shape, jnp.float32) for _ in range(3)]
    for k in range(slab_len - (halo is None)):
        following = plane_ref[chunk, k + 1, :, cols] if k + 1 < slab_len else halo
        upper = following.astype(jnp.float32)
        value = stay * lower + jitter * upper
        before = before + gain_ref[k:k + 1, place] * value
        beyond = jnp.exp2(before)
        emitted = (through - beyond) * value
        for i in range(3):
            sums[i] = sums[i] + emitted * pl.reciprocal(levels[i] + value, approx=True)
        through = beyond
        lower = upper
    return sums, before


def chunk_copy(field_ref, plane_ref, sems, first, chunk):
    width = plane_ref.shape[3]
    cols = pl.ds(pl.multiple_of((first + chunk) * width, width), width)
    return pltpu.make_async_copy(field_ref.at[:, :, cols], plane_ref.at[chunk], sems.at[chunk])


def each_block(plane_ref, copy, block_cols, body):
    chunks, _, _, width = plane_ref.shape

    def chunk_step(chunk, carry):
        copy(chunk).wait()

        def block(n, carry):
            cols = pl.ds(pl.multiple_of(n * block_cols, block_cols), block_cols)
            place = pl.ds(pl.multiple_of(chunk * width + n * block_cols, block_cols), block_cols)
            body(chunk, cols, place)
            return carry

        return lax.fori_loop(0, width // block_cols, block, carry)

    lax.fori_loop(0, chunks, chunk_step, 0)


def open_kernel(total, tile_cols, block_cols, base_ref, transfer_ref, start_ref, end_ref, field_ref, jitter_ref, state_ref,
                plane_ref, gain_ref, sems):
    chunks, slab_len, rows, width = plane_ref.shape
    copy = functools.partial(chunk_copy, field_ref, plane_ref, sems, 0)
    for chunk in range(chunks):
        copy(chunk).start()
    levels = [jnp.full((rows, block_cols), transfer_ref[i]) for i in range(3)]
    gain = jnp.full((8, LANES), transfer_ref[3]) * (-LOG2E * 0.2 / total)
    tile_gains(gain_ref, gain, base_ref[0], 0, tile_cols, start_ref, end_ref)

    def body(chunk, cols, place):
        sums, before = march(gain_ref, plane_ref, chunk, cols, place, jitter_ref[:, place], levels)
        for i in range(3):
            state_ref[i, :, place] = sums[i]
        state_ref[3, :, place] = before

    each_block(plane_ref, copy, block_cols, body)


def close_kernel(total, tile_cols, block_cols, base_ref, transfer_ref, start_ref, end_ref, field_ref, halo_ref, jitter_ref,
                 state_ref, out_ref, plane_ref, gain_ref, last_ref, last_gain_ref, sems, last_sem):
    chunks, slab_len, rows, width = plane_ref.shape
    opened = state_ref.shape[2]
    copy = functools.partial(chunk_copy, field_ref, plane_ref, sems, opened // width)
    last_copy = pltpu.make_async_copy(field_ref.at[slab_len - 1, :, pl.ds(0, opened)], last_ref, last_sem)
    last_copy.start()
    for chunk in range(chunks):
        copy(chunk).start()
    shape = (rows, block_cols)
    depth_gain = jnp.full(shape, transfer_ref[3]) * (0.2 / total)
    levels = [jnp.full(shape, transfer_ref[i]) for i in range(3)]
    depth_unit = 1.0 / (depth_gain * (slab_len * TOP))
    color_unit = [depth_unit * ((levels[i] + TOP) * (1.0 / TOP)) for i in range(3)]
    depth_span, color_span = spans(slab_len)
    gain = depth_gain[:8, :LANES] * -LOG2E
    piece_width = out_ref.shape[3]
    tile_gains(last_gain_ref, gain, base_ref[0] + slab_len - 1, 0, tile_cols, start_ref, end_ref)
    tile_gains(gain_ref, gain, base_ref[0], opened, tile_cols, start_ref, end_ref)

    def store(col, sums, before):
        piece = col // piece_width
        out = pl.ds(pl.multiple_of(col % piece_width, block_cols), block_cols)
        for i in range(3):
            out_ref[piece, i, :, out] = encode(sums[i] * color_unit[i], color_span)
        out_ref[piece, 3, :, out] = encode(before * (depth_unit * (-1.0 / LOG2E)), depth_span)

    last_copy.wait()

    def finish(n, carry):
        cols = pl.ds(pl.multiple_of(n * block_cols, block_cols), block_cols)
        jitter = jitter_ref[:, cols]
        lower = last_ref[:, cols].astype(jnp.float32)
        upper = halo_ref[:, cols].astype(jnp.float32)
        value = (1.0 - jitter) * lower + jitter * upper
        before = state_ref[3, :, cols]
        beyond = before + last_gain_ref[0:1, cols] * value
        emitted = (jnp.exp2(before) - jnp.exp2(beyond)) * value
        sums = [state_ref[i, :, cols] + emitted * pl.reciprocal(levels[i] + value, approx=True) for i in range(3)]
        store(n * block_cols, sums, beyond)
        return carry

    lax.fori_loop(0, opened // block_cols, finish, 0)

    def body(chunk, cols, place):
        col = pl.multiple_of(opened + place.start, block_cols)
        whole = pl.ds(col, block_cols)
        sums, before = march(gain_ref, plane_ref, chunk, cols, place, jitter_ref[:, whole], levels, halo_ref[:, whole])
        store(col, sums, before)

    each_block(plane_ref, copy, block_cols, body)


def slab_codes(field, halo, jitter, transfer, ray_start, ray_end, base, total, pieces):
    slab_len, rows, cols = field.shape
    width = cols // pieces
    chunk = max(width, min(1024, cols // 2))
    chunks = cols // chunk
    opened = max(1, chunks * 5 // 8)
    closed = chunks - opened
    block_cols = min(2 * LANES, width)
    tile_cols = cols // ray_start.shape[0]
    smem = pl.BlockSpec(memory_space=pltpu.SMEM)
    vmem = pl.BlockSpec(memory_space=pltpu.VMEM)
    hbm = pl.BlockSpec(memory_space=pl.ANY)
    params = pltpu.CompilerParams(vmem_limit_bytes=MARCH_BYTES)
    scalars = (base, transfer, ray_start, ray_end)

    def cost(share):
        work = slab_len * rows * cols * share // chunks
        return pl.CostEstimate(flops=work * 20, bytes_accessed=work * 2, transcendentals=work * 4)

    state = pl.pallas_call(
        functools.partial(open_kernel, total, tile_cols, block_cols),
        in_specs=[smem, smem, smem, smem, hbm, vmem],
        out_specs=vmem,
        out_shape=jax.ShapeDtypeStruct((4, rows, opened * chunk), jnp.float32),
        scratch_shapes=[
            pltpu.VMEM((opened, slab_len, rows, chunk), field.dtype),
            pltpu.VMEM((slab_len, opened * chunk), jnp.float32),
            pltpu.SemaphoreType.DMA((opened,)),
        ],
        compiler_params=params,
        cost_estimate=cost(opened),
        name="open",
    )(*scalars, field, jitter)
    return pl.pallas_call(
        functools.partial(close_kernel, total, tile_cols, block_cols),
        in_specs=[smem, smem, smem, smem, hbm, vmem, vmem, vmem],
        out_specs=vmem,
        out_shape=jax.ShapeDtypeStruct((pieces, 4, rows, width), jnp.int16),
        scratch_shapes=[
            pltpu.VMEM((closed, slab_len, rows, chunk), field.dtype),
            pltpu.VMEM((slab_len, closed * chunk), jnp.float32),
            pltpu.VMEM((rows, opened * chunk), field.dtype),
            pltpu.VMEM((8, opened * chunk), jnp.float32),
            pltpu.SemaphoreType.DMA((closed,)),
            pltpu.SemaphoreType.DMA,
        ],
        compiler_params=params,
        cost_estimate=cost(closed),
        name="close",
    )(*scalars, field, halo, jitter, state)


def composite_kernel(total, slab_len, order_ref, transfer_ref, code_ref, out_ref):
    count, _, rows, width = code_ref.shape
    lanes = min(width, LANES)
    depth_span, color_span = spans(slab_len)
    depth_gain = jnp.full((rows, lanes), transfer_ref[3]) * (0.2 / total)
    unit = depth_gain * (slab_len * TOP)
    depth_unit = unit * LOG2E

    def decode(codes, span, shift):
        code = codes.astype(jnp.int32).astype(jnp.float32)
        value = jnp.exp2(code * (span / 65535.0) + (span * (32768.0 / 65535.0) - span) - shift)
        return jnp.where(code > -32768.0, value, 0.0)

    for n in range(width // lanes):
        cols = slice(n * lanes, (n + 1) * lanes)

        def step(j, carry):
            depth, red, green, blue = carry
            slab = order_ref[j]
            colors = [red, green, blue]
            for i in range(3):
                colors[i] = colors[i] + decode(code_ref[slab, i, :, cols], color_span, depth)
            depth = depth + depth_unit * decode(code_ref[slab, 3, :, cols], depth_span, 0.0)
            return depth, *colors

        zero = jnp.zeros((rows, lanes), jnp.float32)
        depth, *colors = lax.fori_loop(0, count, step, (zero, zero, zero, zero), unroll=4)
        for i in range(3):
            level = jnp.full((rows, lanes), transfer_ref[i])
            out_ref[i, :, cols] = colors[i] * (unit * (TOP / (level + TOP)))
        out_ref[3, :, cols] = 1.0 - jnp.exp2(-depth)


def composite(codes, transfer, depth_order, total, slab_len):
    _, _, rows, width = codes.shape
    smem = pl.BlockSpec(memory_space=pltpu.SMEM)
    vmem = pl.BlockSpec(memory_space=pltpu.VMEM)
    return pl.pallas_call(
        functools.partial(composite_kernel, total, slab_len),
        in_specs=[smem, smem, vmem],
        out_specs=vmem,
        out_shape=jax.ShapeDtypeStruct((4, rows, width), jnp.float32),
        compiler_params=pltpu.CompilerParams(vmem_limit_bytes=SMALL_BYTES),
        name="composite",
    )(depth_order, transfer, codes)


def on_device(field, jitter, transfer, depth_order, ray_start, ray_end):
    count = lax.axis_size("depth")
    here = lax.axis_index("depth")
    slab_len, rows, cols = field.shape
    total = slab_len * count
    width = cols // count
    halo = shifted(field[0], "depth", -1)
    base = jnp.reshape(here * slab_len, (1,)).astype(jnp.int32)
    args = (field, halo, jitter, transfer, ray_start, ray_end, base, total)
    if width % LANES == 0:
        codes = slab_codes(*args, count)
    else:
        codes = slab_codes(*args, cols // LANES)
        codes = codes.transpose(1, 2, 0, 3).reshape(4, rows, count, width).transpose(2, 0, 1, 3)
    received = lax.all_to_all(codes, "depth", split_axis=0, concat_axis=0, tiled=True)
    return composite(received, transfer, depth_order, total, slab_len)


def solution(mesh):
    in_specs = (P("depth", "groups", None), P("groups", None), P(), P(), P(), P())
    out_specs = P(None, "groups", "depth")
    return jax.shard_map(
        on_device, mesh=mesh, in_specs=in_specs, out_specs=out_specs, check_vma=False
    )
```

```python
import functools
import math

import jax
import jax.numpy as jnp
from jax import lax
from jax.experimental import pallas as pl
from jax.experimental.pallas import tpu as pltpu
from jax.sharding import PartitionSpec as P

TOP = 5.2
LOG2E = math.log2(math.e)
LANES = 128
MARCH_BYTES = 54 * 1024 * 1024
SMALL_BYTES = 16 * 1024 * 1024


def spans(slab_len):
    deep = math.log2(slab_len)
    return 6.8 + deep, 13.2 + deep


def shifted(value, axis, steps):
    count = lax.axis_size(axis)
    initial, last = (max(0, -steps), min(count, count - steps))
    return lax.ppermute(value, axis, [(source, source + steps) for source in range(initial, last)])


def encode(value, span):
    code = jnp.log2(value) * (65535.0 / span) + 65535.5
    code = jnp.minimum(jnp.maximum(code, 0.0), 65535.0)
    return (code.astype(jnp.int32) - 32768).astype(jnp.int16)


def tile_gains(gain_ref, gain, base, first_col, tile_cols, start_ref, end_ref):
    sample = lax.broadcasted_iota(jnp.int32, (8, LANES), 0) + base
    lane = lax.broadcasted_iota(jnp.int32, (8, LANES), 1)

    def block(n, carry):
        col = n * LANES
        tile = (first_col + col) // tile_cols
        start = jnp.full((8, LANES), start_ref[tile])
        end = jnp.full((8, LANES), end_ref[tile])
        for t in range(1, LANES // tile_cols):
            start = jnp.where(lane >= t * tile_cols, start_ref[tile + t], start)
            end = jnp.where(lane >= t * tile_cols, end_ref[tile + t], end)
        cols = pl.ds(pl.multiple_of(col, LANES), LANES)
        for k in range(0, gain_ref.shape[0], 8):
            active = (sample + k >= start) & (sample + k < end)
            gain_ref[k:k + 8, cols] = jnp.where(active, gain, 0.0)
        return carry

    blocks = gain_ref.shape[1] // LANES
    lax.fori_loop(0, blocks, block, 0, unroll=math.gcd(blocks, 4))


def moment(sums, emitted, value, levels):
    share = emitted * pl.reciprocal((levels[0] + value) * (levels[1] + value) * (levels[2] + value), approx=True)
    for n in range(3):
        sums[n] = sums[n] + share
        share = share * value


def colors(sums, levels):
    others = [(levels[1], levels[2]), (levels[2], levels[0]), (levels[0], levels[1])]
    return [sums[2] + (p + q) * sums[1] + (p * q) * sums[0] for p, q in others]


def march(gain_ref, plane_ref, chunk, cols, place, jitter, levels, halo=None):
    slab_len = plane_ref.shape[1]
    shape = jitter.shape
    stay = 1.0 - jitter
    lower = plane_ref[chunk, 0, :, cols].astype(jnp.float32)
    before = jnp.zeros(shape, jnp.float32)
    through = jnp.ones(shape, jnp.float32)
    sums = [jnp.zeros(shape, jnp.float32) for _ in range(3)]
    for k in range(slab_len - (halo is None)):
        following = plane_ref[chunk, k + 1, :, cols] if k + 1 < slab_len else halo
        upper = following.astype(jnp.float32)
        value = stay * lower + jitter * upper
        before = before + gain_ref[k:k + 1, place] * value
        beyond = jnp.exp2(before)
        emitted = (through - beyond) * value
        moment(sums, emitted, value, levels)
        through = beyond
        lower = upper
    return sums, before


def chunk_copy(field_ref, plane_ref, sems, first, chunk):
    width = plane_ref.shape[3]
    cols = pl.ds(pl.multiple_of((first + chunk) * width, width), width)
    return pltpu.make_async_copy(field_ref.at[:, :, cols], plane_ref.at[chunk], sems.at[chunk])


def each_block(plane_ref, copy, block_cols, body):
    chunks, _, _, width = plane_ref.shape

    def chunk_step(chunk, carry):
        copy(chunk).wait()

        def block(n, carry):
            cols = pl.ds(pl.multiple_of(n * block_cols, block_cols), block_cols)
            place = pl.ds(pl.multiple_of(chunk * width + n * block_cols, block_cols), block_cols)
            body(chunk, cols, place)
            return carry

        return lax.fori_loop(0, width // block_cols, block, carry)

    lax.fori_loop(0, chunks, chunk_step, 0)


def open_kernel(total, tile_cols, block_cols, base_ref, transfer_ref, start_ref, end_ref, field_ref, jitter_ref, state_ref,
                plane_ref, gain_ref, sems):
    chunks, slab_len, rows, width = plane_ref.shape
    copy = functools.partial(chunk_copy, field_ref, plane_ref, sems, 0)
    for chunk in range(chunks):
        copy(chunk).start()
    levels = [jnp.full((rows, block_cols), transfer_ref[i]) for i in range(3)]
    gain = jnp.full((8, LANES), transfer_ref[3]) * (-LOG2E * 0.2 / total)
    tile_gains(gain_ref, gain, base_ref[0], 0, tile_cols, start_ref, end_ref)

    def body(chunk, cols, place):
        sums, before = march(gain_ref, plane_ref, chunk, cols, place, jitter_ref[:, place], levels)
        for i in range(3):
            state_ref[i, :, place] = sums[i]
        state_ref[3, :, place] = before

    each_block(plane_ref, copy, block_cols, body)


def close_kernel(total, tile_cols, block_cols, base_ref, transfer_ref, start_ref, end_ref, field_ref, halo_ref, jitter_ref,
                 state_ref, out_ref, plane_ref, gain_ref, last_ref, last_gain_ref, sems, last_sem):
    chunks, slab_len, rows, width = plane_ref.shape
    opened = state_ref.shape[2]
    copy = functools.partial(chunk_copy, field_ref, plane_ref, sems, opened // width)
    last_copy = pltpu.make_async_copy(field_ref.at[slab_len - 1, :, pl.ds(0, opened)], last_ref, last_sem)
    last_copy.start()
    for chunk in range(chunks):
        copy(chunk).start()
    shape = (rows, block_cols)
    depth_gain = jnp.full(shape, transfer_ref[3]) * (0.2 / total)
    levels = [jnp.full(shape, transfer_ref[i]) for i in range(3)]
    depth_unit = 1.0 / (depth_gain * (slab_len * TOP))
    color_unit = [depth_unit * ((levels[i] + TOP) * (1.0 / TOP)) for i in range(3)]
    depth_span, color_span = spans(slab_len)
    gain = depth_gain[:8, :LANES] * -LOG2E
    piece_width = out_ref.shape[3]
    tile_gains(last_gain_ref, gain, base_ref[0] + slab_len - 1, 0, tile_cols, start_ref, end_ref)
    tile_gains(gain_ref, gain, base_ref[0], opened, tile_cols, start_ref, end_ref)

    def store(col, sums, before):
        piece = col // piece_width
        out = pl.ds(pl.multiple_of(col % piece_width, block_cols), block_cols)
        for i, color in enumerate(colors(sums, levels)):
            out_ref[piece, i, :, out] = encode(color * color_unit[i], color_span)
        out_ref[piece, 3, :, out] = encode(before * (depth_unit * (-1.0 / LOG2E)), depth_span)

    last_copy.wait()

    def finish(n, carry):
        cols = pl.ds(pl.multiple_of(n * block_cols, block_cols), block_cols)
        jitter = jitter_ref[:, cols]
        lower = last_ref[:, cols].astype(jnp.float32)
        upper = halo_ref[:, cols].astype(jnp.float32)
        value = (1.0 - jitter) * lower + jitter * upper
        before = state_ref[3, :, cols]
        beyond = before + last_gain_ref[0:1, cols] * value
        emitted = (jnp.exp2(before) - jnp.exp2(beyond)) * value
        sums = [state_ref[i, :, cols] for i in range(3)]
        moment(sums, emitted, value, levels)
        store(n * block_cols, sums, beyond)
        return carry

    lax.fori_loop(0, opened // block_cols, finish, 0)

    def body(chunk, cols, place):
        col = pl.multiple_of(opened + place.start, block_cols)
        whole = pl.ds(col, block_cols)
        sums, before = march(gain_ref, plane_ref, chunk, cols, place, jitter_ref[:, whole], levels, halo_ref[:, whole])
        store(col, sums, before)

    each_block(plane_ref, copy, block_cols, body)


def slab_codes(field, halo, jitter, transfer, ray_start, ray_end, base, total, pieces):
    slab_len, rows, cols = field.shape
    width = cols // pieces
    chunk = max(width, min(1024, cols // 2))
    chunks = cols // chunk
    opened = max(1, chunks * 5 // 8)
    closed = chunks - opened
    block_cols = min(2 * LANES, width)
    tile_cols = cols // ray_start.shape[0]
    smem = pl.BlockSpec(memory_space=pltpu.SMEM)
    vmem = pl.BlockSpec(memory_space=pltpu.VMEM)
    hbm = pl.BlockSpec(memory_space=pl.ANY)
    params = pltpu.CompilerParams(vmem_limit_bytes=MARCH_BYTES)
    scalars = (base, transfer, ray_start, ray_end)

    def cost(share):
        work = slab_len * rows * cols * share // chunks
        return pl.CostEstimate(flops=work * 20, bytes_accessed=work * 2, transcendentals=work * 4)

    state = pl.pallas_call(
        functools.partial(open_kernel, total, tile_cols, block_cols),
        in_specs=[smem, smem, smem, smem, hbm, vmem],
        out_specs=vmem,
        out_shape=jax.ShapeDtypeStruct((4, rows, opened * chunk), jnp.float32),
        scratch_shapes=[
            pltpu.VMEM((opened, slab_len, rows, chunk), field.dtype),
            pltpu.VMEM((slab_len, opened * chunk), jnp.float32),
            pltpu.SemaphoreType.DMA((opened,)),
        ],
        compiler_params=params,
        cost_estimate=cost(opened),
        name="open",
    )(*scalars, field, jitter)
    return pl.pallas_call(
        functools.partial(close_kernel, total, tile_cols, block_cols),
        in_specs=[smem, smem, smem, smem, hbm, vmem, vmem, vmem],
        out_specs=vmem,
        out_shape=jax.ShapeDtypeStruct((pieces, 4, rows, width), jnp.int16),
        scratch_shapes=[
            pltpu.VMEM((closed, slab_len, rows, chunk), field.dtype),
            pltpu.VMEM((slab_len, closed * chunk), jnp.float32),
            pltpu.VMEM((rows, opened * chunk), field.dtype),
            pltpu.VMEM((8, opened * chunk), jnp.float32),
            pltpu.SemaphoreType.DMA((closed,)),
            pltpu.SemaphoreType.DMA,
        ],
        compiler_params=params,
        cost_estimate=cost(closed),
        name="close",
    )(*scalars, field, halo, jitter, state)


def composite_kernel(total, slab_len, order_ref, transfer_ref, code_ref, out_ref):
    count, _, rows, width = code_ref.shape
    lanes = min(width, LANES)
    depth_span, color_span = spans(slab_len)
    depth_gain = jnp.full((rows, lanes), transfer_ref[3]) * (0.2 / total)
    unit = depth_gain * (slab_len * TOP)
    depth_unit = unit * LOG2E

    def decode(codes, span, shift):
        code = codes.astype(jnp.int32).astype(jnp.float32)
        value = jnp.exp2(code * (span / 65535.0) + (span * (32768.0 / 65535.0) - span) - shift)
        return jnp.where(code > -32768.0, value, 0.0)

    for n in range(width // lanes):
        cols = slice(n * lanes, (n + 1) * lanes)

        def step(j, carry):
            depth, red, green, blue = carry
            slab = order_ref[j]
            colors = [red, green, blue]
            for i in range(3):
                colors[i] = colors[i] + decode(code_ref[slab, i, :, cols], color_span, depth)
            depth = depth + depth_unit * decode(code_ref[slab, 3, :, cols], depth_span, 0.0)
            return depth, *colors

        zero = jnp.zeros((rows, lanes), jnp.float32)
        depth, *colors = lax.fori_loop(0, count, step, (zero, zero, zero, zero), unroll=4)
        for i in range(3):
            level = jnp.full((rows, lanes), transfer_ref[i])
            out_ref[i, :, cols] = colors[i] * (unit * (TOP / (level + TOP)))
        out_ref[3, :, cols] = 1.0 - jnp.exp2(-depth)


def composite(codes, transfer, depth_order, total, slab_len):
    _, _, rows, width = codes.shape
    smem = pl.BlockSpec(memory_space=pltpu.SMEM)
    vmem = pl.BlockSpec(memory_space=pltpu.VMEM)
    return pl.pallas_call(
        functools.partial(composite_kernel, total, slab_len),
        in_specs=[smem, smem, vmem],
        out_specs=vmem,
        out_shape=jax.ShapeDtypeStruct((4, rows, width), jnp.float32),
        compiler_params=pltpu.CompilerParams(vmem_limit_bytes=SMALL_BYTES),
        name="composite",
    )(depth_order, transfer, codes)


def on_device(field, jitter, transfer, depth_order, ray_start, ray_end):
    count = lax.axis_size("depth")
    here = lax.axis_index("depth")
    slab_len, rows, cols = field.shape
    total = slab_len * count
    width = cols // count
    halo = shifted(field[0], "depth", -1)
    base = jnp.reshape(here * slab_len, (1,)).astype(jnp.int32)
    args = (field, halo, jitter, transfer, ray_start, ray_end, base, total)
    if width % LANES == 0:
        codes = slab_codes(*args, count)
    else:
        codes = slab_codes(*args, cols // LANES)
        codes = codes.transpose(1, 2, 0, 3).reshape(4, rows, count, width).transpose(2, 0, 1, 3)
    received = lax.all_to_all(codes, "depth", split_axis=0, concat_axis=0, tiled=True)
    return composite(received, transfer, depth_order, total, slab_len)


def solution(mesh):
    in_specs = (P("depth", "groups", None), P("groups", None), P(), P(), P(), P())
    out_specs = P(None, "groups", "depth")
    return jax.shard_map(
        on_device, mesh=mesh, in_specs=in_specs, out_specs=out_specs, check_vma=False
    )
```

```python
import functools
import math

import jax
import jax.numpy as jnp
from jax import lax
from jax.experimental import pallas as pl
from jax.experimental.pallas import tpu as pltpu
from jax.sharding import PartitionSpec as P

TOP = 5.2
LOG2E = math.log2(math.e)
SUBLANES = 8
LANES = 128
MARCH_BYTES = 54 * 1024 * 1024
SMALL_BYTES = 16 * 1024 * 1024


def spans(slab_len):
    deep = math.log2(slab_len)
    return 6.8 + deep, 13.2 + deep


def shifted(value, axis, steps):
    count = lax.axis_size(axis)
    initial, last = (max(0, -steps), min(count, count - steps))
    return lax.ppermute(value, axis, [(source, source + steps) for source in range(initial, last)])


def encode(value, span):
    code = jnp.log2(value) * (65535.0 / span) + 65535.5
    code = jnp.minimum(jnp.maximum(code, 0.0), 65535.0)
    return code.astype(jnp.int32) - 32768


def halves(plane):
    wide = plane.astype(jnp.float32)
    return wide[:SUBLANES], wide[SUBLANES:]


def gather(sums, weight, depth, levels):
    whole = (levels[0] + depth) * (levels[1] + depth) * (levels[2] + depth)
    share = weight * pl.reciprocal(whole, approx=True, full_range=False) * depth
    out = []
    for n in range(3):
        out.append(sums[n] + share)
        share = share * depth
    return out


def colors(sums, levels):
    others = [(levels[1], levels[2]), (levels[2], levels[0]), (levels[0], levels[1])]
    return [sums[2] + (p + q) * sums[1] + (p * q) * sums[0] for p, q in others]


def march(planes, jitter, gain, levels, active):
    sides = []
    for j in halves(jitter):
        lean = j * gain
        zero = jnp.zeros_like(j)
        sides.append((gain - lean, lean, zero, jnp.ones_like(j), [zero, zero, zero]))
    lower = halves(planes[0])
    for k in range(len(planes) - 1):
        upper = halves(planes[k + 1])
        mask = active(k)
        for h in range(2):
            stay, lean, before, through, sums = sides[h]
            depth = stay * lower[h] + lean * upper[h]
            before = before - (depth if mask is None else jnp.where(mask, depth, 0.0))
            beyond = jnp.exp2(before)
            sides[h] = (stay, lean, before, beyond, gather(sums, through - beyond, depth, levels))
        lower = upper
    return [(side[4], side[2]) for side in sides]


class Tiles:
    def __init__(self, start_ref, end_ref, col, tile_cols):
        tile = col // tile_cols
        self.cols = tile_cols
        self.starts = [start_ref[tile + t] for t in range(LANES // tile_cols)]
        self.ends = [end_ref[tile + t] for t in range(LANES // tile_cols)]

    def full(self, first, last):
        return (functools.reduce(jnp.maximum, self.starts) <= first) & (functools.reduce(jnp.minimum, self.ends) >= last)

    def idle(self, first, last):
        return (functools.reduce(jnp.maximum, self.ends) <= first) | (functools.reduce(jnp.minimum, self.starts) >= last)

    def mask(self, first):
        lane = lax.broadcasted_iota(jnp.int32, (SUBLANES, LANES), 1)
        start = jnp.full((SUBLANES, LANES), self.starts[0])
        end = jnp.full((SUBLANES, LANES), self.ends[0])
        for t in range(1, len(self.starts)):
            start = jnp.where(lane >= t * self.cols, self.starts[t], start)
            end = jnp.where(lane >= t * self.cols, self.ends[t], end)
        start, end = start - first, end - first
        return lambda k: (start <= k) & (end > k)


def chunk_copy(field_ref, plane_ref, sems, first, chunk):
    width = plane_ref.shape[3]
    cols = pl.ds(pl.multiple_of((first + chunk) * width, width), width)
    return pltpu.make_async_copy(field_ref.at[:, :, cols], plane_ref.at[chunk], sems.at[chunk])


def each_block(plane_ref, copy, body):
    chunks, _, _, width = plane_ref.shape

    def chunk_step(chunk, carry):
        copy(chunk).wait()

        def block(n, carry):
            body(chunk, pl.ds(pl.multiple_of(n * LANES, LANES), LANES), pl.multiple_of(chunk * width + n * LANES, LANES))
            return carry

        return lax.fori_loop(0, width // LANES, block, carry)

    lax.fori_loop(0, chunks, chunk_step, 0)


def gains(total, transfer_ref):
    shape = (SUBLANES, LANES)
    gain = jnp.full(shape, transfer_ref[3]) * (LOG2E * 0.2 / total)
    return gain, [jnp.full(shape, transfer_ref[i]) * gain for i in range(3)]


def branches(tiles, first, last, run, idle):
    full, none = tiles.full(first, last), tiles.idle(first, last)
    pl.when(full)(lambda: run(lambda k: None))
    pl.when(none)(idle)
    pl.when(jnp.logical_not(full | none))(lambda: run(tiles.mask(first)))


def open_kernel(total, tile_cols, base_ref, transfer_ref, start_ref, end_ref, field_ref, jitter_ref, state_ref, plane_ref,
                sems):
    chunks, slab_len, rows, width = plane_ref.shape
    copy = functools.partial(chunk_copy, field_ref, plane_ref, sems, 0)
    for chunk in range(chunks):
        copy(chunk).start()
    gain, levels = gains(total, transfer_ref)
    first = base_ref[0]

    def body(chunk, cols, col):
        place = pl.ds(col, LANES)

        def run(active):
            planes = [plane_ref[chunk, k, :, cols] for k in range(slab_len)]
            done = march(planes, jitter_ref[:, place], gain, levels, active)
            for h, (sums, before) in enumerate(done):
                for i, value in enumerate([*sums, before]):
                    state_ref[i, h * SUBLANES:(h + 1) * SUBLANES, place] = value

        def idle():
            state_ref[:, :, place] = jnp.zeros((4, rows, LANES), jnp.float32)

        branches(Tiles(start_ref, end_ref, col, tile_cols), first, first + slab_len - 1, run, idle)

    each_block(plane_ref, copy, body)


def close_kernel(total, tile_cols, base_ref, transfer_ref, start_ref, end_ref, field_ref, halo_ref, jitter_ref,
                 state_ref, out_ref, plane_ref, last_ref, sems, last_sem):
    chunks, slab_len, rows, width = plane_ref.shape
    opened = state_ref.shape[2]
    copy = functools.partial(chunk_copy, field_ref, plane_ref, sems, opened // width)
    last_copy = pltpu.make_async_copy(field_ref.at[slab_len - 1, :, pl.ds(0, opened)], last_ref, last_sem)
    last_copy.start()
    for chunk in range(chunks):
        copy(chunk).start()
    gain, levels = gains(total, transfer_ref)
    first = base_ref[0]
    depth_unit = 1.0 / (gain * (slab_len * TOP))
    color_unit = [LOG2E * depth_unit * ((transfer_ref[i] + TOP) * (1.0 / TOP)) for i in range(3)]
    depth_span, color_span = spans(slab_len)
    piece_width = out_ref.shape[3]

    def store(col, done):
        piece = col // piece_width
        out = pl.ds(pl.multiple_of(col % piece_width, LANES), LANES)
        parts = [[], [], [], []]
        for sums, before in done:
            for i, color in enumerate(colors(sums, levels)):
                parts[i].append(encode(color * color_unit[i], color_span))
            parts[3].append(encode(before * -depth_unit, depth_span))
        for i, part in enumerate(parts):
            out_ref[piece, i, :, out] = jnp.concatenate(part, axis=0).astype(jnp.int16)

    last_copy.wait()

    def finish(n, carry):
        col = pl.multiple_of(n * LANES, LANES)
        cols = pl.ds(col, LANES)
        lower, upper, jitter = halves(last_ref[:, cols]), halves(halo_ref[:, cols]), halves(jitter_ref[:, cols])
        active = Tiles(start_ref, end_ref, col, tile_cols).mask(first + slab_len - 1)(0)
        done = []
        for h in range(2):
            *sums, before = [state_ref[i, h * SUBLANES:(h + 1) * SUBLANES, cols] for i in range(4)]
            lean = jitter[h] * gain
            depth = (gain - lean) * lower[h] + lean * upper[h]
            beyond = before - jnp.where(active, depth, 0.0)
            done.append((gather(sums, jnp.exp2(before) - jnp.exp2(beyond), depth, levels), beyond))
        store(col, done)
        return carry

    blocks = opened // LANES
    lax.fori_loop(0, blocks, finish, 0, unroll=math.gcd(blocks, 4))

    def body(chunk, cols, place):
        col = pl.multiple_of(opened + place, LANES)
        whole = pl.ds(col, LANES)

        def run(active):
            planes = [plane_ref[chunk, k, :, cols] for k in range(slab_len)] + [halo_ref[:, whole]]
            store(col, march(planes, jitter_ref[:, whole], gain, levels, active))

        def idle():
            out = pl.ds(pl.multiple_of(col % piece_width, LANES), LANES)
            out_ref[col // piece_width, :, :, out] = jnp.full((4, rows, LANES), -32768, jnp.int16)

        branches(Tiles(start_ref, end_ref, col, tile_cols), first, first + slab_len, run, idle)

    each_block(plane_ref, copy, body)


def slab_codes(field, halo, jitter, transfer, ray_start, ray_end, base, total, pieces):
    slab_len, rows, cols = field.shape
    width = cols // pieces
    chunk = max(width, min(1024, cols // 2))
    chunks = cols // chunk
    opened = max(1, chunks * 5 // 8)
    closed = chunks - opened
    tile_cols = cols // ray_start.shape[0]
    smem = pl.BlockSpec(memory_space=pltpu.SMEM)
    vmem = pl.BlockSpec(memory_space=pltpu.VMEM)
    hbm = pl.BlockSpec(memory_space=pl.ANY)
    params = pltpu.CompilerParams(vmem_limit_bytes=MARCH_BYTES)
    scalars = (base, transfer, ray_start, ray_end)

    def cost(share):
        work = slab_len * rows * cols * share // chunks
        return pl.CostEstimate(flops=work * 20, bytes_accessed=work * 2, transcendentals=work * 4)

    state = pl.pallas_call(
        functools.partial(open_kernel, total, tile_cols),
        in_specs=[smem, smem, smem, smem, hbm, vmem],
        out_specs=vmem,
        out_shape=jax.ShapeDtypeStruct((4, rows, opened * chunk), jnp.float32),
        scratch_shapes=[
            pltpu.VMEM((opened, slab_len, rows, chunk), field.dtype),
            pltpu.SemaphoreType.DMA((opened,)),
        ],
        compiler_params=params,
        cost_estimate=cost(opened),
        name="open",
    )(*scalars, field, jitter)
    return pl.pallas_call(
        functools.partial(close_kernel, total, tile_cols),
        in_specs=[smem, smem, smem, smem, hbm, vmem, vmem, vmem],
        out_specs=vmem,
        out_shape=jax.ShapeDtypeStruct((pieces, 4, rows, width), jnp.int16),
        scratch_shapes=[
            pltpu.VMEM((closed, slab_len, rows, chunk), field.dtype),
            pltpu.VMEM((rows, opened * chunk), field.dtype),
            pltpu.SemaphoreType.DMA((closed,)),
            pltpu.SemaphoreType.DMA,
        ],
        compiler_params=params,
        cost_estimate=cost(closed),
        name="close",
    )(*scalars, field, halo, jitter, state)


def composite_kernel(total, slab_len, order_ref, transfer_ref, code_ref, out_ref):
    count, _, rows, width = code_ref.shape
    lanes = min(width, LANES)
    depth_span, color_span = spans(slab_len)
    depth_gain = jnp.full((rows, lanes), transfer_ref[3]) * (0.2 / total)
    unit = depth_gain * (slab_len * TOP)
    depth_unit = unit * LOG2E

    def decode(codes, span, shift):
        code = codes.astype(jnp.int32).astype(jnp.float32)
        value = jnp.exp2(code * (span / 65535.0) + (span * (32768.0 / 65535.0) - span) - shift)
        return jnp.where(code > -32768.0, value, 0.0)

    for n in range(width // lanes):
        cols = slice(n * lanes, (n + 1) * lanes)

        def step(j, carry):
            depth, red, green, blue = carry
            slab = order_ref[j]
            colors = [red, green, blue]
            for i in range(3):
                colors[i] = colors[i] + decode(code_ref[slab, i, :, cols], color_span, depth)
            depth = depth + depth_unit * decode(code_ref[slab, 3, :, cols], depth_span, 0.0)
            return depth, *colors

        zero = jnp.zeros((rows, lanes), jnp.float32)
        depth, *colors = lax.fori_loop(0, count, step, (zero, zero, zero, zero), unroll=4)
        for i in range(3):
            level = jnp.full((rows, lanes), transfer_ref[i])
            out_ref[i, :, cols] = colors[i] * (unit * (TOP / (level + TOP)))
        out_ref[3, :, cols] = 1.0 - jnp.exp2(-depth)


def composite(codes, transfer, depth_order, total, slab_len):
    _, _, rows, width = codes.shape
    smem = pl.BlockSpec(memory_space=pltpu.SMEM)
    vmem = pl.BlockSpec(memory_space=pltpu.VMEM)
    return pl.pallas_call(
        functools.partial(composite_kernel, total, slab_len),
        in_specs=[smem, smem, vmem],
        out_specs=vmem,
        out_shape=jax.ShapeDtypeStruct((4, rows, width), jnp.float32),
        compiler_params=pltpu.CompilerParams(vmem_limit_bytes=SMALL_BYTES),
        name="composite",
    )(depth_order, transfer, codes)


def on_device(field, jitter, transfer, depth_order, ray_start, ray_end):
    count = lax.axis_size("depth")
    here = lax.axis_index("depth")
    slab_len, rows, cols = field.shape
    total = slab_len * count
    width = cols // count
    halo = shifted(field[0], "depth", -1)
    base = jnp.reshape(here * slab_len, (1,)).astype(jnp.int32)
    args = (field, halo, jitter, transfer, ray_start, ray_end, base, total)
    if width % LANES == 0:
        codes = slab_codes(*args, count)
    else:
        codes = slab_codes(*args, cols // LANES)
        codes = codes.transpose(1, 2, 0, 3).reshape(4, rows, count, width).transpose(2, 0, 1, 3)
    received = lax.all_to_all(codes, "depth", split_axis=0, concat_axis=0, tiled=True)
    return composite(received, transfer, depth_order, total, slab_len)


def solution(mesh):
    in_specs = (P("depth", "groups", None), P("groups", None), P(), P(), P(), P())
    out_specs = P(None, "groups", "depth")
    return jax.shard_map(
        on_device, mesh=mesh, in_specs=in_specs, out_specs=out_specs, check_vma=False
    )
```

```python
import functools
import math

import jax
import jax.numpy as jnp
from jax import lax
from jax.experimental import pallas as pl
from jax.experimental.pallas import tpu as pltpu
from jax.sharding import PartitionSpec as P

TOP = 5.2
LOG2E = math.log2(math.e)
SUBLANES = 8
LANES = 128
BLOCK = 256
STEP = 512
OPEN_BYTES = 54 * 1024 * 1024
CLOSE_BYTES = 52 * 1024 * 1024
SMALL_BYTES = 16 * 1024 * 1024


def spans(slab_len):
    deep = math.log2(slab_len)
    return 6.8 + deep, 13.2 + deep


def shifted(value, axis, steps):
    count = lax.axis_size(axis)
    initial, last = (max(0, -steps), min(count, count - steps))
    return lax.ppermute(value, axis, [(source, source + steps) for source in range(initial, last)])


def encode(value, span):
    code = jnp.log2(value) * (65535.0 / span) + 65535.5
    code = jnp.minimum(jnp.maximum(code, 0.0), 65535.0)
    return (code.astype(jnp.int32) - 32768).astype(jnp.int16)


def tile_gains(gain_ref, gain, base, first_col, tile_cols, start_ref, end_ref):
    sample = lax.broadcasted_iota(jnp.int32, (8, LANES), 0) + base
    lane = lax.broadcasted_iota(jnp.int32, (8, LANES), 1)

    def block(n, carry):
        col = n * LANES
        tile = (first_col + col) // tile_cols
        start = jnp.full((8, LANES), start_ref[tile])
        end = jnp.full((8, LANES), end_ref[tile])
        for t in range(1, LANES // tile_cols):
            start = jnp.where(lane >= t * tile_cols, start_ref[tile + t], start)
            end = jnp.where(lane >= t * tile_cols, end_ref[tile + t], end)
        cols = pl.ds(pl.multiple_of(col, LANES), LANES)
        for k in range(0, gain_ref.shape[0], 8):
            active = (sample + k >= start) & (sample + k < end)
            gain_ref[k:k + 8, cols] = jnp.where(active, gain, 0.0)
        return carry

    blocks = gain_ref.shape[1] // LANES
    lax.fori_loop(0, blocks, block, 0, unroll=math.gcd(blocks, 4))


def moment(sums, emitted, value, levels):
    share = emitted * pl.reciprocal((levels[0] + value) * (levels[1] + value) * (levels[2] + value), approx=True)
    for n in range(3):
        sums[n] = sums[n] + share
        share = share * value


def colors(sums, levels):
    others = [(levels[1], levels[2]), (levels[2], levels[0]), (levels[0], levels[1])]
    return [sums[2] + (p + q) * sums[1] + (p * q) * sums[0] for p, q in others]


def march(gain_ref, plane_ref, chunk, cols, place, jitter, levels, halo=None):
    slab_len = plane_ref.shape[1]
    shape = jitter.shape
    stay = 1.0 - jitter
    lower = plane_ref[chunk, 0, :, cols].astype(jnp.float32)
    before = jnp.zeros(shape, jnp.float32)
    through = jnp.ones(shape, jnp.float32)
    sums = [jnp.zeros(shape, jnp.float32) for _ in range(3)]
    for k in range(slab_len - (halo is None)):
        following = plane_ref[chunk, k + 1, :, cols] if k + 1 < slab_len else halo
        upper = following.astype(jnp.float32)
        value = stay * lower + jitter * upper
        before = before + gain_ref[k:k + 1, place] * value
        beyond = jnp.exp2(before)
        emitted = (through - beyond) * value
        moment(sums, emitted, value, levels)
        through = beyond
        lower = upper
    return sums, before


class Arrivals:
    def __init__(self, pairs, sems):
        self.copies = [pltpu.make_async_copy(src, dst, sems.at[n]) for n, (src, dst) in enumerate(pairs)]

    def start(self):
        for copy in self.copies:
            copy.start()

    def wait(self, first, count=1):
        for copy in self.copies[first:first + count]:
            copy.wait()


def each_step(chunk_cols, body):
    def step(n, carry):
        for part in range(STEP // BLOCK):
            body(pl.multiple_of(n * STEP + part * BLOCK, BLOCK))
        return carry

    lax.fori_loop(0, chunk_cols // STEP, step, 0)


def open_kernel(total, tile_cols, transfer_any, start_any, end_any, field_ref, jitter_any, state_any, transfer_ref, start_ref,
                end_ref, plane_ref, jitter_ref, state_ref, gain_ref, sems, out_sems):
    chunks, slab_len, rows, width = plane_ref.shape
    scalars = [(transfer_any, transfer_ref), (start_any, start_ref), (end_any, end_ref)]
    chunk_pairs = []
    for chunk in range(chunks):
        cols = pl.ds(chunk * width, width)
        chunk_pairs.append((jitter_any.at[:, cols], jitter_ref.at[chunk]))
        chunk_pairs.append((field_ref.at[:, :, cols], plane_ref.at[chunk]))
    arrivals = Arrivals(scalars + chunk_pairs, sems)
    arrivals.start()
    base = lax.axis_index("depth") * slab_len
    arrivals.wait(0, len(scalars))
    levels = [jnp.full((rows, BLOCK), transfer_ref[i]) for i in range(3)]
    gain = jnp.full((SUBLANES, LANES), transfer_ref[3]) * (-LOG2E * 0.2 / total)
    tile_gains(gain_ref, gain, base, 0, tile_cols, start_ref, end_ref)
    leaving = []
    for chunk in range(chunks):
        arrivals.wait(len(scalars) + 2 * chunk, 2)

        def body(col):
            cols = pl.ds(col, BLOCK)
            place = pl.ds(pl.multiple_of(chunk * width + col, BLOCK), BLOCK)
            sums, before = march(gain_ref, plane_ref, chunk, cols, place, jitter_ref[chunk, :, cols], levels)
            for i in range(3):
                state_ref[chunk, i, :, cols] = sums[i]
            state_ref[chunk, 3, :, cols] = before

        each_step(width, body)
        leaving.append(pltpu.make_async_copy(state_ref.at[chunk], state_any.at[chunk], out_sems.at[chunk]))
        leaving[-1].start()
    for copy in leaving:
        copy.wait()


def close_kernel(total, tile_cols, opened, transfer_any, start_any, end_any, field_ref, halo_any, jitter_any, state_any, out_any,
                 transfer_ref, start_ref, end_ref, plane_ref, halo_ref, jitter_ref, state_ref, last_ref, out_ref, gain_ref,
                 last_gain_ref, sems, out_sems):
    chunks, slab_len, rows, width = plane_ref.shape
    first_col = opened * width
    pieces, _, _, piece_width = out_ref.shape
    per = width // piece_width
    scalars = [(transfer_any, transfer_ref), (start_any, start_ref), (end_any, end_ref), (halo_any, halo_ref)]
    pairs = list(scalars)
    for chunk in range(chunks):
        cols = pl.ds(first_col + chunk * width, width)
        pairs.append((jitter_any.at[:, cols], jitter_ref.at[opened + chunk]))
        pairs.append((field_ref.at[:, :, cols], plane_ref.at[chunk]))
    late = len(pairs)
    pairs.append((field_ref.at[slab_len - 1, :, pl.ds(0, first_col)], last_ref))
    pairs.append((state_any, state_ref))
    for chunk in range(opened):
        pairs.append((jitter_any.at[:, pl.ds(chunk * width, width)], jitter_ref.at[chunk]))
    arrivals = Arrivals(pairs, sems)
    arrivals.start()
    base = lax.axis_index("depth") * slab_len
    arrivals.wait(0, len(scalars))
    shape = (rows, BLOCK)
    depth_gain = jnp.full(shape, transfer_ref[3]) * (0.2 / total)
    levels = [jnp.full(shape, transfer_ref[i]) for i in range(3)]
    depth_unit = 1.0 / (depth_gain * (slab_len * TOP))
    color_unit = [depth_unit * ((levels[i] + TOP) * (1.0 / TOP)) for i in range(3)]
    depth_span, color_span = spans(slab_len)
    gain = depth_gain[:SUBLANES, :LANES] * -LOG2E
    tile_gains(gain_ref, gain, base, first_col, tile_cols, start_ref, end_ref)
    tile_gains(last_gain_ref, gain, base + slab_len - 1, 0, tile_cols, start_ref, end_ref)
    leaving = []

    def store(chunk, col, sums, before):
        piece = chunk * per + col // piece_width
        out = pl.ds(pl.multiple_of(col % piece_width, BLOCK), BLOCK)
        for i, color in enumerate(colors(sums, levels)):
            out_ref[piece, i, :, out] = encode(color * color_unit[i], color_span)
        out_ref[piece, 3, :, out] = encode(before * (depth_unit * (-1.0 / LOG2E)), depth_span)

    def leave(chunk):
        place = pl.ds(chunk * per, per)
        leaving.append(pltpu.make_async_copy(out_ref.at[place], out_any.at[place], out_sems.at[chunk]))
        leaving[-1].start()

    for chunk in range(chunks):
        arrivals.wait(len(scalars) + 2 * chunk, 2)

        def body(col):
            cols = pl.ds(col, BLOCK)
            place = pl.ds(pl.multiple_of(chunk * width + col, BLOCK), BLOCK)
            whole = pl.ds(pl.multiple_of(first_col + chunk * width + col, BLOCK), BLOCK)
            jitter = jitter_ref[opened + chunk, :, cols]
            sums, before = march(gain_ref, plane_ref, chunk, cols, place, jitter, levels, halo_ref[:, whole])
            store(opened + chunk, col, sums, before)

        each_step(width, body)
        leave(opened + chunk)
    arrivals.wait(late, len(pairs) - late)
    for chunk in range(opened):

        def finish(col):
            cols = pl.ds(col, BLOCK)
            whole = pl.ds(pl.multiple_of(chunk * width + col, BLOCK), BLOCK)
            jitter = jitter_ref[chunk, :, cols]
            lower = last_ref[:, whole].astype(jnp.float32)
            upper = halo_ref[:, whole].astype(jnp.float32)
            value = (1.0 - jitter) * lower + jitter * upper
            before = state_ref[chunk, 3, :, cols]
            beyond = before + last_gain_ref[0:1, whole] * value
            emitted = (jnp.exp2(before) - jnp.exp2(beyond)) * value
            sums = [state_ref[chunk, i, :, cols] for i in range(3)]
            moment(sums, emitted, value, levels)
            store(chunk, col, sums, beyond)

        each_step(width, finish)
        leave(chunk)
    for copy in leaving:
        copy.wait()


def slab_codes(field, halo, jitter, transfer, ray_start, ray_end, total, pieces):
    slab_len, rows, cols = field.shape
    width = cols // pieces
    chunk = max(width, min(1024, cols // 2))
    chunks = cols // chunk
    opened = max(1, chunks * 5 // 8)
    closed = chunks - opened
    ntiles = ray_start.shape[0]
    tile_cols = cols // ntiles
    own = pl.BlockSpec(memory_space=pl.ANY)
    scalars = [pltpu.SMEM(transfer.shape, transfer.dtype)] + [pltpu.SMEM((ntiles,), jnp.int32)] * 2

    def cost(share):
        work = slab_len * rows * cols * share // chunks
        return pl.CostEstimate(flops=work * 20, bytes_accessed=work * 2, transcendentals=work * 2)

    state = pl.pallas_call(
        functools.partial(open_kernel, total, tile_cols),
        in_specs=[own] * 5,
        out_specs=own,
        out_shape=jax.ShapeDtypeStruct((opened, 4, rows, chunk), jnp.float32),
        scratch_shapes=scalars + [
            pltpu.VMEM((opened, slab_len, rows, chunk), field.dtype),
            pltpu.VMEM((opened, rows, chunk), jnp.float32),
            pltpu.VMEM((opened, 4, rows, chunk), jnp.float32),
            pltpu.VMEM((slab_len, opened * chunk), jnp.float32),
            pltpu.SemaphoreType.DMA((3 + 2 * opened,)),
            pltpu.SemaphoreType.DMA((opened,)),
        ],
        compiler_params=pltpu.CompilerParams(vmem_limit_bytes=OPEN_BYTES),
        cost_estimate=cost(opened),
        name="open",
    )(transfer, ray_start, ray_end, field, jitter)
    return pl.pallas_call(
        functools.partial(close_kernel, total, tile_cols, opened),
        in_specs=[own] * 7,
        out_specs=own,
        out_shape=jax.ShapeDtypeStruct((pieces, 4, rows, width), jnp.int16),
        scratch_shapes=scalars + [
            pltpu.VMEM((closed, slab_len, rows, chunk), field.dtype),
            pltpu.VMEM((rows, cols), field.dtype),
            pltpu.VMEM((chunks, rows, chunk), jnp.float32),
            pltpu.VMEM((opened, 4, rows, chunk), jnp.float32),
            pltpu.VMEM((rows, opened * chunk), field.dtype),
            pltpu.VMEM((pieces, 4, rows, width), jnp.int16),
            pltpu.VMEM((slab_len, closed * chunk), jnp.float32),
            pltpu.VMEM((SUBLANES, opened * chunk), jnp.float32),
            pltpu.SemaphoreType.DMA((4 + 2 * closed + 2 + opened,)),
            pltpu.SemaphoreType.DMA((chunks,)),
        ],
        compiler_params=pltpu.CompilerParams(vmem_limit_bytes=CLOSE_BYTES),
        cost_estimate=cost(closed),
        name="close",
    )(transfer, ray_start, ray_end, field, halo, jitter, state)


def composite_kernel(total, slab_len, order_ref, transfer_ref, code_ref, out_ref):
    count, _, rows, width = code_ref.shape
    lanes = min(width, LANES)
    depth_span, color_span = spans(slab_len)
    depth_gain = jnp.full((rows, lanes), transfer_ref[3]) * (0.2 / total)
    unit = depth_gain * (slab_len * TOP)
    depth_unit = unit * LOG2E

    def decode(codes, span, shift):
        code = codes.astype(jnp.int32).astype(jnp.float32)
        value = jnp.exp2(code * (span / 65535.0) + (span * (32768.0 / 65535.0) - span) - shift)
        return jnp.where(code > -32768.0, value, 0.0)

    for n in range(width // lanes):
        cols = slice(n * lanes, (n + 1) * lanes)

        def step(j, carry):
            depth, red, green, blue = carry
            slab = order_ref[j]
            colors = [red, green, blue]
            for i in range(3):
                colors[i] = colors[i] + decode(code_ref[slab, i, :, cols], color_span, depth)
            depth = depth + depth_unit * decode(code_ref[slab, 3, :, cols], depth_span, 0.0)
            return depth, *colors

        zero = jnp.zeros((rows, lanes), jnp.float32)
        depth, *colors = lax.fori_loop(0, count, step, (zero, zero, zero, zero), unroll=4)
        for i in range(3):
            level = jnp.full((rows, lanes), transfer_ref[i])
            out_ref[i, :, cols] = colors[i] * (unit * (TOP / (level + TOP)))
        out_ref[3, :, cols] = 1.0 - jnp.exp2(-depth)


def composite(codes, transfer, depth_order, total, slab_len):
    _, _, rows, width = codes.shape
    smem = pl.BlockSpec(memory_space=pltpu.SMEM)
    vmem = pl.BlockSpec(memory_space=pltpu.VMEM)
    return pl.pallas_call(
        functools.partial(composite_kernel, total, slab_len),
        in_specs=[smem, smem, vmem],
        out_specs=vmem,
        out_shape=jax.ShapeDtypeStruct((4, rows, width), jnp.float32),
        compiler_params=pltpu.CompilerParams(vmem_limit_bytes=SMALL_BYTES),
        name="composite",
    )(depth_order, transfer, codes)


def on_device(field, jitter, transfer, depth_order, ray_start, ray_end):
    count = lax.axis_size("depth")
    slab_len, rows, cols = field.shape
    total = slab_len * count
    width = cols // count
    halo = shifted(field[0], "depth", -1)
    args = (field, halo, jitter, transfer, ray_start, ray_end, total)
    if width % BLOCK == 0:
        codes = slab_codes(*args, count)
    else:
        codes = slab_codes(*args, cols // BLOCK)
        codes = codes.transpose(1, 2, 0, 3).reshape(4, rows, count, width).transpose(2, 0, 1, 3)
    received = lax.all_to_all(codes, "depth", split_axis=0, concat_axis=0, tiled=True)
    return composite(received, transfer, depth_order, total, slab_len)


def solution(mesh):
    in_specs = (P("depth", "groups", None), P("groups", None), P(), P(), P(), P())
    out_specs = P(None, "groups", "depth")
    return jax.shard_map(
        on_device, mesh=mesh, in_specs=in_specs, out_specs=out_specs, check_vma=False
    )
```

```python
import functools
import math

import jax
import jax.numpy as jnp
from jax import lax
from jax.experimental import pallas as pl
from jax.experimental.pallas import tpu as pltpu
from jax.sharding import PartitionSpec as P

TOP = 5.2
LOG2E = math.log2(math.e)
SUBLANES = 8
LANES = 128
BLOCK = 256
STEP = 512
OPEN_BYTES = 54 * 1024 * 1024
CLOSE_BYTES = 52 * 1024 * 1024
SMALL_BYTES = 16 * 1024 * 1024


def spans(slab_len):
    deep = math.log2(slab_len)
    return 6.8 + deep, 13.2 + deep


def shifted(value, axis, steps):
    count = lax.axis_size(axis)
    initial, last = (max(0, -steps), min(count, count - steps))
    return lax.ppermute(value, axis, [(source, source + steps) for source in range(initial, last)])


def encode(value, span):
    code = jnp.log2(value) * (65535.0 / span) + 65535.5
    code = jnp.minimum(jnp.maximum(code, 0.0), 65535.0)
    return (code.astype(jnp.int32) - 32768).astype(jnp.int16)


def tile_gains(gain_ref, gain, base, first_col, tile_cols, start_ref, end_ref):
    sample = lax.broadcasted_iota(jnp.int32, (8, LANES), 0) + base
    lane = lax.broadcasted_iota(jnp.int32, (8, LANES), 1)

    def block(n, carry):
        col = n * LANES
        tile = (first_col + col) // tile_cols
        start = jnp.full((8, LANES), start_ref[tile])
        end = jnp.full((8, LANES), end_ref[tile])
        for t in range(1, LANES // tile_cols):
            start = jnp.where(lane >= t * tile_cols, start_ref[tile + t], start)
            end = jnp.where(lane >= t * tile_cols, end_ref[tile + t], end)
        cols = pl.ds(pl.multiple_of(col, LANES), LANES)
        for k in range(0, gain_ref.shape[0], 8):
            active = (sample + k >= start) & (sample + k < end)
            gain_ref[k:k + 8, cols] = jnp.where(active, gain, 0.0)
        return carry

    blocks = gain_ref.shape[1] // LANES
    lax.fori_loop(0, blocks, block, 0, unroll=math.gcd(blocks, 4))


def moment(sums, emitted, value, levels):
    share = emitted * pl.reciprocal((levels[0] + value) * (levels[1] + value) * (levels[2] + value), approx=True)
    for n in range(3):
        sums[n] = sums[n] + share
        share = share * value


def colors(sums, levels):
    others = [(levels[1], levels[2]), (levels[2], levels[0]), (levels[0], levels[1])]
    return [sums[2] + (p + q) * sums[1] + (p * q) * sums[0] for p, q in others]


def march(gain_ref, plane_ref, chunk, cols, place, jitter, levels, halo=None):
    slab_len = plane_ref.shape[1]
    shape = jitter.shape
    stay = 1.0 - jitter
    lower = plane_ref[chunk, 0, :, cols].astype(jnp.float32)
    before = jnp.zeros(shape, jnp.float32)
    through = jnp.ones(shape, jnp.float32)
    sums = [jnp.zeros(shape, jnp.float32) for _ in range(3)]
    for k in range(slab_len - (halo is None)):
        following = plane_ref[chunk, k + 1, :, cols] if k + 1 < slab_len else halo
        upper = following.astype(jnp.float32)
        value = stay * lower + jitter * upper
        before = before + gain_ref[k:k + 1, place] * value
        beyond = jnp.exp2(before)
        emitted = (through - beyond) * value
        moment(sums, emitted, value, levels)
        through = beyond
        lower = upper
    return sums, before


def each_step(chunk_cols, body):
    def step(n, carry):
        for part in range(STEP // BLOCK):
            body(pl.multiple_of(n * STEP + part * BLOCK, BLOCK))
        return carry

    lax.fori_loop(0, chunk_cols // STEP, step, 0)


def each_chunk(chunks, body):
    def step(chunk, carry):
        body(chunk)
        return carry

    lax.fori_loop(0, chunks, step, 0)


def start_all(pairs, sems):
    copies = [pltpu.make_async_copy(src, dst, sems.at[n]) for n, (src, dst) in enumerate(pairs)]
    for copy in copies:
        copy.start()
    return copies


def chunk_copies(field_ref, jitter_any, plane_ref, jitter_ref, sems, first, chunk):
    width = plane_ref.shape[3]
    cols = pl.ds(pl.multiple_of((first + chunk) * width, width), width)
    return [
        pltpu.make_async_copy(jitter_any.at[:, cols], jitter_ref.at[first + chunk], sems.at[0, chunk]),
        pltpu.make_async_copy(field_ref.at[:, :, cols], plane_ref.at[chunk], sems.at[1, chunk]),
    ]


def open_kernel(total, tile_cols, transfer_any, start_any, end_any, field_ref, jitter_any, state_any, transfer_ref, start_ref,
                end_ref, plane_ref, jitter_ref, state_ref, gain_ref, few_sems, sems, out_sems):
    chunks, slab_len, rows, width = plane_ref.shape
    early = start_all([(transfer_any, transfer_ref), (start_any, start_ref), (end_any, end_ref)], few_sems)
    arrivals = functools.partial(chunk_copies, field_ref, jitter_any, plane_ref, jitter_ref, sems, 0)
    for chunk in range(chunks):
        for copy in arrivals(chunk):
            copy.start()
    base = lax.axis_index("depth") * slab_len
    for copy in early:
        copy.wait()
    levels = [jnp.full((rows, BLOCK), transfer_ref[i]) for i in range(3)]
    gain = jnp.full((SUBLANES, LANES), transfer_ref[3]) * (-LOG2E * 0.2 / total)
    tile_gains(gain_ref, gain, base, 0, tile_cols, start_ref, end_ref)

    def leave(chunk):
        return pltpu.make_async_copy(state_ref.at[chunk], state_any.at[chunk], out_sems.at[chunk])

    def run(chunk):
        for copy in arrivals(chunk):
            copy.wait()

        def body(col):
            cols = pl.ds(col, BLOCK)
            place = pl.ds(pl.multiple_of(chunk * width + col, BLOCK), BLOCK)
            sums, before = march(gain_ref, plane_ref, chunk, cols, place, jitter_ref[chunk, :, cols], levels)
            for i in range(3):
                state_ref[chunk, i, :, cols] = sums[i]
            state_ref[chunk, 3, :, cols] = before

        each_step(width, body)
        leave(chunk).start()

    each_chunk(chunks, run)
    each_chunk(chunks, lambda chunk: leave(chunk).wait())


def close_kernel(total, tile_cols, opened, transfer_any, start_any, end_any, field_ref, halo_any, jitter_any, state_any, out_any,
                 transfer_ref, start_ref, end_ref, plane_ref, halo_ref, jitter_ref, state_ref, last_ref, out_ref, gain_ref,
                 last_gain_ref, few_sems, sems, out_sems):
    chunks, slab_len, rows, width = plane_ref.shape
    first_col = opened * width
    piece_width = out_ref.shape[3]
    per = width // piece_width
    few = [(transfer_any, transfer_ref), (start_any, start_ref), (end_any, end_ref), (halo_any, halo_ref)]
    early = start_all(few, few_sems)
    arrivals = functools.partial(chunk_copies, field_ref, jitter_any, plane_ref, jitter_ref, sems, opened)
    for chunk in range(chunks):
        for copy in arrivals(chunk):
            copy.start()
    pairs = [(field_ref.at[slab_len - 1, :, pl.ds(0, first_col)], last_ref), (state_any, state_ref)]
    for chunk in range(opened):
        pairs.append((jitter_any.at[:, pl.ds(chunk * width, width)], jitter_ref.at[chunk]))
    late = start_all(pairs, few_sems.at[pl.ds(len(few), len(pairs))])
    base = lax.axis_index("depth") * slab_len
    for copy in early:
        copy.wait()
    shape = (rows, BLOCK)
    depth_gain = jnp.full(shape, transfer_ref[3]) * (0.2 / total)
    levels = [jnp.full(shape, transfer_ref[i]) for i in range(3)]
    depth_unit = 1.0 / (depth_gain * (slab_len * TOP))
    color_unit = [depth_unit * ((levels[i] + TOP) * (1.0 / TOP)) for i in range(3)]
    depth_span, color_span = spans(slab_len)
    gain = depth_gain[:SUBLANES, :LANES] * -LOG2E
    tile_gains(gain_ref, gain, base, first_col, tile_cols, start_ref, end_ref)
    tile_gains(last_gain_ref, gain, base + slab_len - 1, 0, tile_cols, start_ref, end_ref)

    def store(chunk, col, sums, before):
        piece = chunk * per + col // piece_width
        out = pl.ds(pl.multiple_of(col % piece_width, BLOCK), BLOCK)
        for i, color in enumerate(colors(sums, levels)):
            out_ref[piece, i, :, out] = encode(color * color_unit[i], color_span)
        out_ref[piece, 3, :, out] = encode(before * (depth_unit * (-1.0 / LOG2E)), depth_span)

    def leave(chunk):
        place = pl.ds(chunk * per, per)
        return pltpu.make_async_copy(out_ref.at[place], out_any.at[place], out_sems.at[chunk])

    def run(chunk):
        for copy in arrivals(chunk):
            copy.wait()

        def body(col):
            cols = pl.ds(col, BLOCK)
            place = pl.ds(pl.multiple_of(chunk * width + col, BLOCK), BLOCK)
            whole = pl.ds(pl.multiple_of(first_col + chunk * width + col, BLOCK), BLOCK)
            jitter = jitter_ref[opened + chunk, :, cols]
            sums, before = march(gain_ref, plane_ref, chunk, cols, place, jitter, levels, halo_ref[:, whole])
            store(opened + chunk, col, sums, before)

        each_step(width, body)
        leave(opened + chunk).start()

    each_chunk(chunks, run)
    for copy in late:
        copy.wait()

    def finish(chunk):
        def body(col):
            cols = pl.ds(col, BLOCK)
            whole = pl.ds(pl.multiple_of(chunk * width + col, BLOCK), BLOCK)
            jitter = jitter_ref[chunk, :, cols]
            lower = last_ref[:, whole].astype(jnp.float32)
            upper = halo_ref[:, whole].astype(jnp.float32)
            value = (1.0 - jitter) * lower + jitter * upper
            before = state_ref[chunk, 3, :, cols]
            beyond = before + last_gain_ref[0:1, whole] * value
            emitted = (jnp.exp2(before) - jnp.exp2(beyond)) * value
            sums = [state_ref[chunk, i, :, cols] for i in range(3)]
            moment(sums, emitted, value, levels)
            store(chunk, col, sums, beyond)

        each_step(width, body)
        leave(chunk).start()

    each_chunk(opened, finish)
    each_chunk(opened + chunks, lambda chunk: leave(chunk).wait())


def slab_codes(field, halo, jitter, transfer, ray_start, ray_end, total, pieces):
    slab_len, rows, cols = field.shape
    width = cols // pieces
    chunk = max(width, min(1024, cols // 2))
    chunks = cols // chunk
    opened = max(1, chunks * 5 // 8)
    closed = chunks - opened
    ntiles = ray_start.shape[0]
    tile_cols = cols // ntiles
    own = pl.BlockSpec(memory_space=pl.ANY)
    scalars = [pltpu.SMEM(transfer.shape, transfer.dtype)] + [pltpu.SMEM((ntiles,), jnp.int32)] * 2

    def cost(share):
        work = slab_len * rows * cols * share // chunks
        return pl.CostEstimate(flops=work * 20, bytes_accessed=work * 2, transcendentals=work * 2)

    state = pl.pallas_call(
        functools.partial(open_kernel, total, tile_cols),
        in_specs=[own] * 5,
        out_specs=own,
        out_shape=jax.ShapeDtypeStruct((opened, 4, rows, chunk), jnp.float32),
        scratch_shapes=scalars + [
            pltpu.VMEM((opened, slab_len, rows, chunk), field.dtype),
            pltpu.VMEM((opened, rows, chunk), jnp.float32),
            pltpu.VMEM((opened, 4, rows, chunk), jnp.float32),
            pltpu.VMEM((slab_len, opened * chunk), jnp.float32),
            pltpu.SemaphoreType.DMA((3,)),
            pltpu.SemaphoreType.DMA((2, opened)),
            pltpu.SemaphoreType.DMA((opened,)),
        ],
        compiler_params=pltpu.CompilerParams(vmem_limit_bytes=OPEN_BYTES),
        cost_estimate=cost(opened),
        name="open",
    )(transfer, ray_start, ray_end, field, jitter)
    return pl.pallas_call(
        functools.partial(close_kernel, total, tile_cols, opened),
        in_specs=[own] * 7,
        out_specs=own,
        out_shape=jax.ShapeDtypeStruct((pieces, 4, rows, width), jnp.int16),
        scratch_shapes=scalars + [
            pltpu.VMEM((closed, slab_len, rows, chunk), field.dtype),
            pltpu.VMEM((rows, cols), field.dtype),
            pltpu.VMEM((chunks, rows, chunk), jnp.float32),
            pltpu.VMEM((opened, 4, rows, chunk), jnp.float32),
            pltpu.VMEM((rows, opened * chunk), field.dtype),
            pltpu.VMEM((pieces, 4, rows, width), jnp.int16),
            pltpu.VMEM((slab_len, closed * chunk), jnp.float32),
            pltpu.VMEM((SUBLANES, opened * chunk), jnp.float32),
            pltpu.SemaphoreType.DMA((6 + opened,)),
            pltpu.SemaphoreType.DMA((2, closed)),
            pltpu.SemaphoreType.DMA((chunks,)),
        ],
        compiler_params=pltpu.CompilerParams(vmem_limit_bytes=CLOSE_BYTES),
        cost_estimate=cost(closed),
        name="close",
    )(transfer, ray_start, ray_end, field, halo, jitter, state)


def composite_kernel(total, slab_len, order_ref, transfer_ref, code_ref, out_ref):
    count, _, rows, width = code_ref.shape
    lanes = min(width, LANES)
    depth_span, color_span = spans(slab_len)
    depth_gain = jnp.full((rows, lanes), transfer_ref[3]) * (0.2 / total)
    unit = depth_gain * (slab_len * TOP)
    depth_unit = unit * LOG2E

    def decode(codes, span, shift):
        code = codes.astype(jnp.int32).astype(jnp.float32)
        value = jnp.exp2(code * (span / 65535.0) + (span * (32768.0 / 65535.0) - span) - shift)
        return jnp.where(code > -32768.0, value, 0.0)

    for n in range(width // lanes):
        cols = slice(n * lanes, (n + 1) * lanes)

        def step(j, carry):
            depth, red, green, blue = carry
            slab = order_ref[j]
            colors = [red, green, blue]
            for i in range(3):
                colors[i] = colors[i] + decode(code_ref[slab, i, :, cols], color_span, depth)
            depth = depth + depth_unit * decode(code_ref[slab, 3, :, cols], depth_span, 0.0)
            return depth, *colors

        zero = jnp.zeros((rows, lanes), jnp.float32)
        depth, *colors = lax.fori_loop(0, count, step, (zero, zero, zero, zero), unroll=4)
        for i in range(3):
            level = jnp.full((rows, lanes), transfer_ref[i])
            out_ref[i, :, cols] = colors[i] * (unit * (TOP / (level + TOP)))
        out_ref[3, :, cols] = 1.0 - jnp.exp2(-depth)


def composite(codes, transfer, depth_order, total, slab_len):
    _, _, rows, width = codes.shape
    smem = pl.BlockSpec(memory_space=pltpu.SMEM)
    vmem = pl.BlockSpec(memory_space=pltpu.VMEM)
    return pl.pallas_call(
        functools.partial(composite_kernel, total, slab_len),
        in_specs=[smem, smem, vmem],
        out_specs=vmem,
        out_shape=jax.ShapeDtypeStruct((4, rows, width), jnp.float32),
        compiler_params=pltpu.CompilerParams(vmem_limit_bytes=SMALL_BYTES),
        name="composite",
    )(depth_order, transfer, codes)


def on_device(field, jitter, transfer, depth_order, ray_start, ray_end):
    count = lax.axis_size("depth")
    slab_len, rows, cols = field.shape
    total = slab_len * count
    width = cols // count
    halo = shifted(field[0], "depth", -1)
    args = (field, halo, jitter, transfer, ray_start, ray_end, total)
    if width % BLOCK == 0:
        codes = slab_codes(*args, count)
    else:
        codes = slab_codes(*args, cols // BLOCK)
        codes = codes.transpose(1, 2, 0, 3).reshape(4, rows, count, width).transpose(2, 0, 1, 3)
    received = lax.all_to_all(codes, "depth", split_axis=0, concat_axis=0, tiled=True)
    return composite(received, transfer, depth_order, total, slab_len)


def solution(mesh):
    in_specs = (P("depth", "groups", None), P("groups", None), P(), P(), P(), P())
    out_specs = P(None, "groups", "depth")
    return jax.shard_map(
        on_device, mesh=mesh, in_specs=in_specs, out_specs=out_specs, check_vma=False
    )
```

```python
import functools
import math

import jax
import jax.numpy as jnp
from jax import lax
from jax.experimental import pallas as pl
from jax.experimental.pallas import tpu as pltpu
from jax.sharding import PartitionSpec as P

TOP = 5.2
LOG2E = math.log2(math.e)
SUBLANES = 8
LANES = 128
STEP = 512
OPEN_BYTES = 54 * 1024 * 1024
CLOSE_BYTES = 52 * 1024 * 1024
SMALL_BYTES = 16 * 1024 * 1024


def spans(slab_len):
    deep = math.log2(slab_len)
    return 6.8 + deep, 13.2 + deep


def shifted(value, axis, steps):
    count = lax.axis_size(axis)
    initial, last = (max(0, -steps), min(count, count - steps))
    return lax.ppermute(value, axis, [(source, source + steps) for source in range(initial, last)])


def encode(value, span):
    code = jnp.log2(value) * (65535.0 / span) + 65535.5
    code = jnp.minimum(jnp.maximum(code, 0.0), 65535.0)
    return (code.astype(jnp.int32) - 32768).astype(jnp.int16)


def tile_gains(gain_ref, gain, base, first_col, tile_cols, start_ref, end_ref):
    sample = lax.broadcasted_iota(jnp.int32, (8, LANES), 0) + base
    lane = lax.broadcasted_iota(jnp.int32, (8, LANES), 1)

    def block(n, carry):
        col = n * LANES
        tile = (first_col + col) // tile_cols
        start = jnp.full((8, LANES), start_ref[tile])
        end = jnp.full((8, LANES), end_ref[tile])
        for t in range(1, LANES // tile_cols):
            start = jnp.where(lane >= t * tile_cols, start_ref[tile + t], start)
            end = jnp.where(lane >= t * tile_cols, end_ref[tile + t], end)
        cols = pl.ds(pl.multiple_of(col, LANES), LANES)
        for k in range(0, gain_ref.shape[0], 8):
            active = (sample + k >= start) & (sample + k < end)
            gain_ref[k:k + 8, cols] = jnp.where(active, gain, 0.0)
        return carry

    blocks = gain_ref.shape[1] // LANES
    lax.fori_loop(0, blocks, block, 0, unroll=math.gcd(blocks, 4))


def moment(sums, emitted, value, levels):
    whole = (levels[0] + value) * (levels[1] + value) * (levels[2] + value)
    share = emitted * pl.reciprocal(whole, approx=True, full_range=False)
    for n in range(3):
        sums[n] = sums[n] + share
        share = share * value


def colors(sums, levels):
    others = [(levels[1], levels[2]), (levels[2], levels[0]), (levels[0], levels[1])]
    return [sums[2] + (p + q) * sums[1] + (p * q) * sums[0] for p, q in others]


def march(gain_ref, plane_ref, chunk, cols, place, jitter, levels, halo=None):
    slab_len = plane_ref.shape[1]
    shape = jitter.shape
    before = jnp.zeros(shape, jnp.float32)
    through = jnp.ones(shape, jnp.float32)
    sums = [jnp.zeros(shape, jnp.float32) for _ in range(3)]
    lower = plane_ref[chunk, 0, :, cols].astype(jnp.float32)
    stay = lower - jitter * lower
    for k in range(slab_len - (halo is None)):
        following = plane_ref[chunk, k + 1, :, cols] if k + 1 < slab_len else halo
        upper = following.astype(jnp.float32)
        moved = jitter * upper
        value = stay + moved
        before = before + gain_ref[k:k + 1, place] * value
        beyond = jnp.exp2(before)
        moment(sums, (through - beyond) * value, value, levels)
        through = beyond
        stay = upper - moved
    return sums, before


def each_step(chunk_cols, compute, store):
    def step(n, carry):
        places = [pl.multiple_of(n * STEP + part * LANES, LANES) for part in range(STEP // LANES)]
        results = [compute(col) for col in places]
        for col, result in zip(places, results):
            store(col, *result)
        return carry

    lax.fori_loop(0, chunk_cols // STEP, step, 0)


def each_chunk(chunks, body):
    def step(chunk, carry):
        body(chunk)
        return carry

    lax.fori_loop(0, chunks, step, 0)


def start_all(pairs, sems):
    copies = [pltpu.make_async_copy(src, dst, sems.at[n]) for n, (src, dst) in enumerate(pairs)]
    for copy in copies:
        copy.start()
    return copies


def chunk_copies(field_ref, jitter_any, plane_ref, jitter_ref, sems, first, chunk):
    width = plane_ref.shape[3]
    cols = pl.ds(pl.multiple_of((first + chunk) * width, width), width)
    return [
        pltpu.make_async_copy(jitter_any.at[:, cols], jitter_ref.at[first + chunk], sems.at[0, chunk]),
        pltpu.make_async_copy(field_ref.at[:, :, cols], plane_ref.at[chunk], sems.at[1, chunk]),
    ]


def open_kernel(total, tile_cols, transfer_any, start_any, end_any, field_ref, jitter_any, state_any, transfer_ref, start_ref,
                end_ref, plane_ref, jitter_ref, state_ref, gain_ref, few_sems, sems, out_sems):
    chunks, slab_len, rows, width = plane_ref.shape
    early = start_all([(transfer_any, transfer_ref), (start_any, start_ref), (end_any, end_ref)], few_sems)
    arrivals = functools.partial(chunk_copies, field_ref, jitter_any, plane_ref, jitter_ref, sems, 0)
    for chunk in range(chunks):
        for copy in arrivals(chunk):
            copy.start()
    base = lax.axis_index("depth") * slab_len
    for copy in early:
        copy.wait()
    levels = [jnp.full((rows, LANES), transfer_ref[i]) for i in range(3)]
    gain = jnp.full((SUBLANES, LANES), transfer_ref[3]) * (-LOG2E * 0.2 / total)
    tile_gains(gain_ref, gain, base, 0, tile_cols, start_ref, end_ref)

    def leave(chunk):
        return pltpu.make_async_copy(state_ref.at[chunk], state_any.at[chunk], out_sems.at[chunk])

    def run(chunk):
        for copy in arrivals(chunk):
            copy.wait()

        def compute(col):
            cols = pl.ds(col, LANES)
            place = pl.ds(pl.multiple_of(chunk * width + col, LANES), LANES)
            return march(gain_ref, plane_ref, chunk, cols, place, jitter_ref[chunk, :, cols], levels)

        def store(col, sums, before):
            for i, value in enumerate([*sums, before]):
                state_ref[chunk, i, :, pl.ds(col, LANES)] = value

        each_step(width, compute, store)
        leave(chunk).start()

    each_chunk(chunks, run)
    each_chunk(chunks, lambda chunk: leave(chunk).wait())


def close_kernel(total, tile_cols, opened, transfer_any, start_any, end_any, field_ref, halo_any, jitter_any, state_any, out_any,
                 transfer_ref, start_ref, end_ref, plane_ref, halo_ref, jitter_ref, state_ref, last_ref, out_ref, gain_ref,
                 last_gain_ref, few_sems, sems, out_sems):
    chunks, slab_len, rows, width = plane_ref.shape
    first_col = opened * width
    piece_width = out_ref.shape[3]
    per = width // piece_width
    few = [(transfer_any, transfer_ref), (start_any, start_ref), (end_any, end_ref), (halo_any, halo_ref)]
    early = start_all(few, few_sems)
    arrivals = functools.partial(chunk_copies, field_ref, jitter_any, plane_ref, jitter_ref, sems, opened)
    for chunk in range(chunks):
        for copy in arrivals(chunk):
            copy.start()
    pairs = [(field_ref.at[slab_len - 1, :, pl.ds(0, first_col)], last_ref), (state_any, state_ref)]
    for chunk in range(opened):
        pairs.append((jitter_any.at[:, pl.ds(chunk * width, width)], jitter_ref.at[chunk]))
    late = start_all(pairs, few_sems.at[pl.ds(len(few), len(pairs))])
    base = lax.axis_index("depth") * slab_len
    for copy in early:
        copy.wait()
    shape = (rows, LANES)
    depth_gain = jnp.full(shape, transfer_ref[3]) * (0.2 / total)
    levels = [jnp.full(shape, transfer_ref[i]) for i in range(3)]
    depth_unit = 1.0 / (depth_gain * (slab_len * TOP))
    color_unit = [depth_unit * ((levels[i] + TOP) * (1.0 / TOP)) for i in range(3)]
    depth_span, color_span = spans(slab_len)
    gain = depth_gain[:SUBLANES, :LANES] * -LOG2E
    tile_gains(gain_ref, gain, base, first_col, tile_cols, start_ref, end_ref)
    tile_gains(last_gain_ref, gain, base + slab_len - 1, 0, tile_cols, start_ref, end_ref)

    def coded(sums, before):
        codes = [encode(color * color_unit[i], color_span) for i, color in enumerate(colors(sums, levels))]
        return codes + [encode(before * (depth_unit * (-1.0 / LOG2E)), depth_span)]

    def store(chunk, col, *codes):
        piece = chunk * per + col // piece_width
        out = pl.ds(pl.multiple_of(col % piece_width, LANES), LANES)
        for i, code in enumerate(codes):
            out_ref[piece, i, :, out] = code

    def leave(chunk):
        place = pl.ds(chunk * per, per)
        return pltpu.make_async_copy(out_ref.at[place], out_any.at[place], out_sems.at[chunk])

    def run(chunk):
        for copy in arrivals(chunk):
            copy.wait()

        def compute(col):
            cols = pl.ds(col, LANES)
            place = pl.ds(pl.multiple_of(chunk * width + col, LANES), LANES)
            whole = pl.ds(pl.multiple_of(first_col + chunk * width + col, LANES), LANES)
            jitter = jitter_ref[opened + chunk, :, cols]
            return coded(*march(gain_ref, plane_ref, chunk, cols, place, jitter, levels, halo_ref[:, whole]))

        each_step(width, compute, functools.partial(store, opened + chunk))
        leave(opened + chunk).start()

    each_chunk(chunks, run)
    for copy in late:
        copy.wait()

    def finish(chunk):
        def compute(col):
            cols = pl.ds(col, LANES)
            whole = pl.ds(pl.multiple_of(chunk * width + col, LANES), LANES)
            jitter = jitter_ref[chunk, :, cols]
            lower = last_ref[:, whole].astype(jnp.float32)
            upper = halo_ref[:, whole].astype(jnp.float32)
            value = (1.0 - jitter) * lower + jitter * upper
            before = state_ref[chunk, 3, :, cols]
            beyond = before + last_gain_ref[0:1, whole] * value
            emitted = (jnp.exp2(before) - jnp.exp2(beyond)) * value
            sums = [state_ref[chunk, i, :, cols] for i in range(3)]
            moment(sums, emitted, value, levels)
            return coded(sums, beyond)

        each_step(width, compute, functools.partial(store, chunk))
        leave(chunk).start()

    each_chunk(opened, finish)
    each_chunk(opened + chunks, lambda chunk: leave(chunk).wait())


def slab_codes(field, halo, jitter, transfer, ray_start, ray_end, total, pieces):
    slab_len, rows, cols = field.shape
    width = cols // pieces
    chunk = max(width, min(1024, cols // 2))
    chunks = cols // chunk
    opened = max(1, chunks * 5 // 8)
    closed = chunks - opened
    ntiles = ray_start.shape[0]
    tile_cols = cols // ntiles
    own = pl.BlockSpec(memory_space=pl.ANY)
    scalars = [pltpu.SMEM(transfer.shape, transfer.dtype)] + [pltpu.SMEM((ntiles,), jnp.int32)] * 2

    def cost(share):
        work = slab_len * rows * cols * share // chunks
        return pl.CostEstimate(flops=work * 20, bytes_accessed=work * 2, transcendentals=work * 2)

    state = pl.pallas_call(
        functools.partial(open_kernel, total, tile_cols),
        in_specs=[own] * 5,
        out_specs=own,
        out_shape=jax.ShapeDtypeStruct((opened, 4, rows, chunk), jnp.float32),
        scratch_shapes=scalars + [
            pltpu.VMEM((opened, slab_len, rows, chunk), field.dtype),
            pltpu.VMEM((opened, rows, chunk), jnp.float32),
            pltpu.VMEM((opened, 4, rows, chunk), jnp.float32),
            pltpu.VMEM((slab_len, opened * chunk), jnp.float32),
            pltpu.SemaphoreType.DMA((3,)),
            pltpu.SemaphoreType.DMA((2, opened)),
            pltpu.SemaphoreType.DMA((opened,)),
        ],
        compiler_params=pltpu.CompilerParams(vmem_limit_bytes=OPEN_BYTES),
        cost_estimate=cost(opened),
        name="open",
    )(transfer, ray_start, ray_end, field, jitter)
    return pl.pallas_call(
        functools.partial(close_kernel, total, tile_cols, opened),
        in_specs=[own] * 7,
        out_specs=own,
        out_shape=jax.ShapeDtypeStruct((pieces, 4, rows, width), jnp.int16),
        scratch_shapes=scalars + [
            pltpu.VMEM((closed, slab_len, rows, chunk), field.dtype),
            pltpu.VMEM((rows, cols), field.dtype),
            pltpu.VMEM((chunks, rows, chunk), jnp.float32),
            pltpu.VMEM((opened, 4, rows, chunk), jnp.float32),
            pltpu.VMEM((rows, opened * chunk), field.dtype),
            pltpu.VMEM((pieces, 4, rows, width), jnp.int16),
            pltpu.VMEM((slab_len, closed * chunk), jnp.float32),
            pltpu.VMEM((SUBLANES, opened * chunk), jnp.float32),
            pltpu.SemaphoreType.DMA((6 + opened,)),
            pltpu.SemaphoreType.DMA((2, closed)),
            pltpu.SemaphoreType.DMA((chunks,)),
        ],
        compiler_params=pltpu.CompilerParams(vmem_limit_bytes=CLOSE_BYTES),
        cost_estimate=cost(closed),
        name="close",
    )(transfer, ray_start, ray_end, field, halo, jitter, state)


def composite_kernel(total, slab_len, order_ref, transfer_ref, code_ref, out_ref):
    count, _, rows, width = code_ref.shape
    lanes = min(width, LANES)
    depth_span, color_span = spans(slab_len)
    depth_gain = jnp.full((rows, lanes), transfer_ref[3]) * (0.2 / total)
    unit = depth_gain * (slab_len * TOP)
    depth_unit = unit * LOG2E

    def decode(codes, span, shift):
        code = codes.astype(jnp.int32).astype(jnp.float32)
        value = jnp.exp2(code * (span / 65535.0) + (span * (32768.0 / 65535.0) - span) - shift)
        return jnp.where(code > -32768.0, value, 0.0)

    for n in range(width // lanes):
        cols = slice(n * lanes, (n + 1) * lanes)

        def step(j, carry):
            depth, red, green, blue = carry
            slab = order_ref[j]
            colors = [red, green, blue]
            for i in range(3):
                colors[i] = colors[i] + decode(code_ref[slab, i, :, cols], color_span, depth)
            depth = depth + depth_unit * decode(code_ref[slab, 3, :, cols], depth_span, 0.0)
            return depth, *colors

        zero = jnp.zeros((rows, lanes), jnp.float32)
        depth, *colors = lax.fori_loop(0, count, step, (zero, zero, zero, zero), unroll=4)
        for i in range(3):
            level = jnp.full((rows, lanes), transfer_ref[i])
            out_ref[i, :, cols] = colors[i] * (unit * (TOP / (level + TOP)))
        out_ref[3, :, cols] = 1.0 - jnp.exp2(-depth)


def composite(codes, transfer, depth_order, total, slab_len):
    _, _, rows, width = codes.shape
    smem = pl.BlockSpec(memory_space=pltpu.SMEM)
    vmem = pl.BlockSpec(memory_space=pltpu.VMEM)
    return pl.pallas_call(
        functools.partial(composite_kernel, total, slab_len),
        in_specs=[smem, smem, vmem],
        out_specs=vmem,
        out_shape=jax.ShapeDtypeStruct((4, rows, width), jnp.float32),
        compiler_params=pltpu.CompilerParams(vmem_limit_bytes=SMALL_BYTES),
        name="composite",
    )(depth_order, transfer, codes)


def on_device(field, jitter, transfer, depth_order, ray_start, ray_end):
    count = lax.axis_size("depth")
    slab_len, rows, cols = field.shape
    total = slab_len * count
    width = cols // count
    halo = shifted(field[0], "depth", -1)
    args = (field, halo, jitter, transfer, ray_start, ray_end, total)
    if width % STEP == 0:
        codes = slab_codes(*args, count)
    else:
        codes = slab_codes(*args, cols // STEP)
        codes = codes.transpose(1, 2, 0, 3).reshape(4, rows, count, width).transpose(2, 0, 1, 3)
    received = lax.all_to_all(codes, "depth", split_axis=0, concat_axis=0, tiled=True)
    return composite(received, transfer, depth_order, total, slab_len)


def solution(mesh):
    in_specs = (P("depth", "groups", None), P("groups", None), P(), P(), P(), P())
    out_specs = P(None, "groups", "depth")
    return jax.shard_map(
        on_device, mesh=mesh, in_specs=in_specs, out_specs=out_specs, check_vma=False
    )
```

```python
import functools
import math

import jax
import jax.numpy as jnp
from jax import lax
from jax.experimental import pallas as pl
from jax.experimental.pallas import tpu as pltpu
from jax.sharding import PartitionSpec as P

TOP = 5.2
LOG2E = math.log2(math.e)
SUBLANES = 8
LANES = 128
FAR = 1.0e4
STEP = 512
OPEN_BYTES = 54 * 1024 * 1024
CLOSE_BYTES = 52 * 1024 * 1024
SMALL_BYTES = 16 * 1024 * 1024


def spans(slab_len):
    deep = math.log2(slab_len)
    return 6.8 + deep, 13.2 + deep


def shifted(value, axis, steps):
    count = lax.axis_size(axis)
    initial, last = (max(0, -steps), min(count, count - steps))
    return lax.ppermute(value, axis, [(source, source + steps) for source in range(initial, last)])


def encode(value, span):
    code = jnp.log2(value) * (65535.0 / span) + 65535.5
    code = jnp.minimum(jnp.maximum(code, 0.0), 65535.0)
    return (code.astype(jnp.int32) - 32768).astype(jnp.int16)


def tile_gains(gain_ref, gain, base, first_col, tile_cols, start_ref, end_ref):
    sample = lax.broadcasted_iota(jnp.int32, (8, LANES), 0) + base
    lane = lax.broadcasted_iota(jnp.int32, (8, LANES), 1)

    def block(n, carry):
        col = n * LANES
        tile = (first_col + col) // tile_cols
        start = jnp.full((8, LANES), start_ref[tile])
        end = jnp.full((8, LANES), end_ref[tile])
        for t in range(1, LANES // tile_cols):
            start = jnp.where(lane >= t * tile_cols, start_ref[tile + t], start)
            end = jnp.where(lane >= t * tile_cols, end_ref[tile + t], end)
        cols = pl.ds(pl.multiple_of(col, LANES), LANES)
        for k in range(0, gain_ref.shape[0], 8):
            active = (sample + k >= start) & (sample + k < end)
            gain_ref[k:k + 8, cols] = jnp.where(active, gain, 0.0)
        return carry

    blocks = gain_ref.shape[1] // LANES
    lax.fori_loop(0, blocks, block, 0, unroll=math.gcd(blocks, 4))


def moment(sums, emitted, value, levels):
    whole = (levels[0] + value) * (levels[1] + value) * (levels[2] + value)
    share = emitted * pl.reciprocal(whole, approx=True, full_range=False)
    for n in range(3):
        sums[n] = sums[n] + share
        share = share * value


def colors(sums, levels):
    others = [(levels[1], levels[2]), (levels[2], levels[0]), (levels[0], levels[1])]
    return [sums[2] + (p + q) * sums[1] + (p * q) * sums[0] for p, q in others]


def march(gain_ref, plane_ref, chunk, cols, place, jitter, levels, halo=None):
    slab_len = plane_ref.shape[1]
    shape = jitter.shape
    before = jnp.zeros(shape, jnp.float32)
    through = jnp.ones(shape, jnp.float32)
    sums = [jnp.zeros(shape, jnp.float32) for _ in range(3)]
    lower = plane_ref[chunk, 0, :, cols].astype(jnp.float32)
    stay = lower - jitter * lower
    for k in range(slab_len - (halo is None)):
        following = plane_ref[chunk, k + 1, :, cols] if k + 1 < slab_len else halo
        upper = following.astype(jnp.float32)
        moved = jitter * upper
        value = stay + moved
        before = before + gain_ref[k:k + 1, place] * value
        beyond = jnp.exp2(before)
        moment(sums, (through - beyond) * value, value, levels)
        through = beyond
        stay = upper - moved
    return sums, before


def each_step(chunk_cols, compute, store):
    def step(n, carry):
        places = [pl.multiple_of(n * STEP + part * LANES, LANES) for part in range(STEP // LANES)]
        results = [compute(col) for col in places]
        for col, result in zip(places, results):
            store(col, *result)
        return carry

    lax.fori_loop(0, chunk_cols // STEP, step, 0)


def each_chunk(chunks, body):
    def step(chunk, carry):
        body(chunk)
        return carry

    lax.fori_loop(0, chunks, step, 0)


def start_all(pairs, sems):
    copies = [pltpu.make_async_copy(src, dst, sems.at[n]) for n, (src, dst) in enumerate(pairs)]
    for copy in copies:
        copy.start()
    return copies


def chunk_copies(field_ref, jitter_any, plane_ref, jitter_ref, sems, first, chunk):
    width = plane_ref.shape[3]
    cols = pl.ds(pl.multiple_of((first + chunk) * width, width), width)
    return [
        pltpu.make_async_copy(jitter_any.at[:, cols], jitter_ref.at[first + chunk], sems.at[0, chunk]),
        pltpu.make_async_copy(field_ref.at[:, :, cols], plane_ref.at[chunk], sems.at[1, chunk]),
    ]


def open_kernel(total, tile_cols, transfer_any, start_any, end_any, field_ref, jitter_any, state_any, transfer_ref, start_ref,
                end_ref, plane_ref, jitter_ref, state_ref, gain_ref, few_sems, sems, out_sems):
    chunks, slab_len, rows, width = plane_ref.shape
    early = start_all([(transfer_any, transfer_ref), (start_any, start_ref), (end_any, end_ref)], few_sems)
    arrivals = functools.partial(chunk_copies, field_ref, jitter_any, plane_ref, jitter_ref, sems, 0)
    for chunk in range(chunks):
        for copy in arrivals(chunk):
            copy.start()
    base = lax.axis_index("depth") * slab_len
    for copy in early:
        copy.wait()
    levels = [jnp.full((rows, LANES), transfer_ref[i]) for i in range(3)]
    gain = jnp.full((SUBLANES, LANES), transfer_ref[3]) * (-LOG2E * 0.2 / total)
    tile_gains(gain_ref, gain, base, 0, tile_cols, start_ref, end_ref)

    def leave(chunk):
        return pltpu.make_async_copy(state_ref.at[chunk], state_any.at[chunk], out_sems.at[chunk])

    def run(chunk):
        for copy in arrivals(chunk):
            copy.wait()

        def compute(col):
            cols = pl.ds(col, LANES)
            place = pl.ds(pl.multiple_of(chunk * width + col, LANES), LANES)
            return march(gain_ref, plane_ref, chunk, cols, place, jitter_ref[chunk, :, cols], levels)

        def store(col, sums, before):
            for i, value in enumerate([*sums, before]):
                state_ref[chunk, i, :, pl.ds(col, LANES)] = value

        each_step(width, compute, store)
        leave(chunk).start()

    each_chunk(chunks, run)
    each_chunk(chunks, lambda chunk: leave(chunk).wait())


def close_kernel(total, tile_cols, opened, transfer_any, start_any, end_any, field_ref, halo_any, jitter_any, state_any, out_any,
                 transfer_ref, start_ref, end_ref, plane_ref, halo_ref, jitter_ref, state_ref, last_ref, out_ref, gain_ref,
                 last_gain_ref, few_sems, sems, out_sems):
    chunks, slab_len, rows, width = plane_ref.shape
    first_col = opened * width
    piece_width = out_ref.shape[3]
    per = width // piece_width
    few = [(transfer_any, transfer_ref), (start_any, start_ref), (end_any, end_ref), (halo_any, halo_ref)]
    early = start_all(few, few_sems)
    arrivals = functools.partial(chunk_copies, field_ref, jitter_any, plane_ref, jitter_ref, sems, opened)
    for chunk in range(chunks):
        for copy in arrivals(chunk):
            copy.start()
    pairs = [(field_ref.at[slab_len - 1, :, pl.ds(0, first_col)], last_ref), (state_any, state_ref)]
    for chunk in range(opened):
        pairs.append((jitter_any.at[:, pl.ds(chunk * width, width)], jitter_ref.at[chunk]))
    late = start_all(pairs, few_sems.at[pl.ds(len(few), len(pairs))])
    base = lax.axis_index("depth") * slab_len
    for copy in early:
        copy.wait()
    shape = (rows, LANES)
    depth_gain = jnp.full(shape, transfer_ref[3]) * (0.2 / total)
    levels = [jnp.full(shape, transfer_ref[i]) for i in range(3)]
    depth_unit = 1.0 / (depth_gain * (slab_len * TOP))
    color_unit = [depth_unit * ((levels[i] + TOP) * (1.0 / TOP)) for i in range(3)]
    depth_span, color_span = spans(slab_len)
    gain = depth_gain[:SUBLANES, :LANES] * -LOG2E
    tile_gains(gain_ref, gain, base, first_col, tile_cols, start_ref, end_ref)
    tile_gains(last_gain_ref, gain, base + slab_len - 1, 0, tile_cols, start_ref, end_ref)

    def coded(sums, before):
        codes = [encode(color * color_unit[i], color_span) for i, color in enumerate(colors(sums, levels))]
        return codes + [encode(before * (depth_unit * (-1.0 / LOG2E)), depth_span)]

    def store(chunk, col, *codes):
        piece = chunk * per + col // piece_width
        out = pl.ds(pl.multiple_of(col % piece_width, LANES), LANES)
        for i, code in enumerate(codes):
            out_ref[piece, i, :, out] = code

    def leave(chunk):
        place = pl.ds(chunk * per, per)
        return pltpu.make_async_copy(out_ref.at[place], out_any.at[place], out_sems.at[chunk])

    def run(chunk):
        for copy in arrivals(chunk):
            copy.wait()

        def compute(col):
            cols = pl.ds(col, LANES)
            place = pl.ds(pl.multiple_of(chunk * width + col, LANES), LANES)
            whole = pl.ds(pl.multiple_of(first_col + chunk * width + col, LANES), LANES)
            jitter = jitter_ref[opened + chunk, :, cols]
            return coded(*march(gain_ref, plane_ref, chunk, cols, place, jitter, levels, halo_ref[:, whole]))

        each_step(width, compute, functools.partial(store, opened + chunk))
        leave(opened + chunk).start()

    each_chunk(chunks, run)
    for copy in late:
        copy.wait()

    def finish(chunk):
        def compute(col):
            cols = pl.ds(col, LANES)
            whole = pl.ds(pl.multiple_of(chunk * width + col, LANES), LANES)
            jitter = jitter_ref[chunk, :, cols]
            lower = last_ref[:, whole].astype(jnp.float32)
            upper = halo_ref[:, whole].astype(jnp.float32)
            value = (1.0 - jitter) * lower + jitter * upper
            before = state_ref[chunk, 3, :, cols]
            beyond = before + last_gain_ref[0:1, whole] * value
            emitted = (jnp.exp2(before) - jnp.exp2(beyond)) * value
            sums = [state_ref[chunk, i, :, cols] for i in range(3)]
            moment(sums, emitted, value, levels)
            return coded(sums, beyond)

        each_step(width, compute, functools.partial(store, chunk))
        leave(chunk).start()

    each_chunk(opened, finish)
    each_chunk(opened + chunks, lambda chunk: leave(chunk).wait())


def slab_codes(field, halo, jitter, transfer, ray_start, ray_end, total, pieces):
    slab_len, rows, cols = field.shape
    width = cols // pieces
    chunk = max(width, STEP)
    chunks = cols // chunk
    opened = max(1, chunks * 3 // 8)
    closed = chunks - opened
    ntiles = ray_start.shape[0]
    tile_cols = cols // ntiles
    own = pl.BlockSpec(memory_space=pl.ANY)
    scalars = [pltpu.SMEM(transfer.shape, transfer.dtype)] + [pltpu.SMEM((ntiles,), jnp.int32)] * 2

    def cost(share):
        work = slab_len * rows * cols * share // chunks
        return pl.CostEstimate(flops=work * 20, bytes_accessed=work * 2, transcendentals=work * 2)

    state = pl.pallas_call(
        functools.partial(open_kernel, total, tile_cols),
        in_specs=[own] * 5,
        out_specs=own,
        out_shape=jax.ShapeDtypeStruct((opened, 4, rows, chunk), jnp.float32),
        scratch_shapes=scalars + [
            pltpu.VMEM((opened, slab_len, rows, chunk), field.dtype),
            pltpu.VMEM((opened, rows, chunk), jnp.float32),
            pltpu.VMEM((opened, 4, rows, chunk), jnp.float32),
            pltpu.VMEM((slab_len, opened * chunk), jnp.float32),
            pltpu.SemaphoreType.DMA((3,)),
            pltpu.SemaphoreType.DMA((2, opened)),
            pltpu.SemaphoreType.DMA((opened,)),
        ],
        compiler_params=pltpu.CompilerParams(vmem_limit_bytes=OPEN_BYTES),
        cost_estimate=cost(opened),
        name="open",
    )(transfer, ray_start, ray_end, field, jitter)
    return pl.pallas_call(
        functools.partial(close_kernel, total, tile_cols, opened),
        in_specs=[own] * 7,
        out_specs=own,
        out_shape=jax.ShapeDtypeStruct((pieces, 4, rows, width), jnp.int16),
        scratch_shapes=scalars + [
            pltpu.VMEM((closed, slab_len, rows, chunk), field.dtype),
            pltpu.VMEM((rows, cols), field.dtype),
            pltpu.VMEM((chunks, rows, chunk), jnp.float32),
            pltpu.VMEM((opened, 4, rows, chunk), jnp.float32),
            pltpu.VMEM((rows, opened * chunk), field.dtype),
            pltpu.VMEM((pieces, 4, rows, width), jnp.int16),
            pltpu.VMEM((slab_len, closed * chunk), jnp.float32),
            pltpu.VMEM((SUBLANES, opened * chunk), jnp.float32),
            pltpu.SemaphoreType.DMA((6 + opened,)),
            pltpu.SemaphoreType.DMA((2, closed)),
            pltpu.SemaphoreType.DMA((chunks,)),
        ],
        compiler_params=pltpu.CompilerParams(vmem_limit_bytes=CLOSE_BYTES),
        cost_estimate=cost(closed),
        name="close",
    )(transfer, ray_start, ray_end, field, halo, jitter, state)


def composite_kernel(total, slab_len, order_any, transfer_any, code_any, out_ref, order_ref, transfer_ref, code_ref, sems):
    copies = start_all([(order_any, order_ref), (transfer_any, transfer_ref), (code_any, code_ref)], sems)
    count, _, rows, width = code_ref.shape
    block = math.gcd(width, 2 * LANES)
    shape = (rows, block)
    depth_span, color_span = spans(slab_len)
    for copy in copies:
        copy.wait()
    unit = jnp.full(shape, transfer_ref[3]) * (0.2 / total * slab_len * TOP)
    depth_unit = unit * LOG2E

    def power(codes, span):
        return codes * (span / 65535.0) + (span * (32768.0 / 65535.0) - span)

    def number(codes):
        return codes.astype(jnp.int32).astype(jnp.float32)

    for n in range(width // block):
        cols = slice(n * block, (n + 1) * block)

        def step(j, carry):
            depth, *colors = carry
            slab = order_ref[j]
            depth_code = number(code_ref[slab, 3, :, cols])
            idle = depth_code == -32768.0
            shift = jnp.where(idle, FAR, depth)
            for i in range(3):
                colors[i] = colors[i] + jnp.exp2(power(number(code_ref[slab, i, :, cols]), color_span) - shift)
            depth = depth + depth_unit * jnp.where(idle, 0.0, jnp.exp2(power(depth_code, depth_span)))
            return depth, *colors

        zero = jnp.zeros(shape, jnp.float32)
        depth, *colors = lax.fori_loop(0, count, step, (zero, zero, zero, zero), unroll=math.gcd(count, 4))
        for i in range(3):
            out_ref[i, :, cols] = colors[i] * (unit * (TOP / (transfer_ref[i] + jnp.full(shape, TOP))))
        out_ref[3, :, cols] = 1.0 - jnp.exp2(-depth)


def composite(codes, transfer, depth_order, total, slab_len):
    _, _, rows, width = codes.shape
    own = pl.BlockSpec(memory_space=pl.ANY)
    return pl.pallas_call(
        functools.partial(composite_kernel, total, slab_len),
        in_specs=[own] * 3,
        out_specs=pl.BlockSpec(memory_space=pltpu.VMEM),
        out_shape=jax.ShapeDtypeStruct((4, rows, width), jnp.float32),
        scratch_shapes=[
            pltpu.SMEM(depth_order.shape, depth_order.dtype),
            pltpu.SMEM(transfer.shape, transfer.dtype),
            pltpu.VMEM(codes.shape, codes.dtype),
            pltpu.SemaphoreType.DMA((3,)),
        ],
        compiler_params=pltpu.CompilerParams(vmem_limit_bytes=SMALL_BYTES),
        name="composite",
    )(depth_order, transfer, codes)


def on_device(field, jitter, transfer, depth_order, ray_start, ray_end):
    count = lax.axis_size("depth")
    slab_len, rows, cols = field.shape
    total = slab_len * count
    width = cols // count
    halo = shifted(field[0], "depth", -1)
    args = (field, halo, jitter, transfer, ray_start, ray_end, total)
    if width % STEP == 0:
        codes = slab_codes(*args, count)
    else:
        codes = slab_codes(*args, cols // STEP)
        codes = codes.transpose(1, 2, 0, 3).reshape(4, rows, count, width).transpose(2, 0, 1, 3)
    received = lax.all_to_all(codes, "depth", split_axis=0, concat_axis=0, tiled=True)
    return composite(received, transfer, depth_order, total, slab_len)


def solution(mesh):
    in_specs = (P("depth", "groups", None), P("groups", None), P(), P(), P(), P())
    out_specs = P(None, "groups", "depth")
    return jax.shard_map(
        on_device, mesh=mesh, in_specs=in_specs, out_specs=out_specs, check_vma=False
    )
```

```python
import functools
import math

import jax
import jax.numpy as jnp
from jax import lax
from jax.experimental import pallas as pl
from jax.experimental.pallas import tpu as pltpu
from jax.sharding import PartitionSpec as P

TOP = 5.2
LOG2E = math.log2(math.e)
SUBLANES = 8
LANES = 128
FAR = 1.0e4
UNIT = 256
OPEN_BYTES = 54 * 1024 * 1024
CLOSE_BYTES = 53 * 1024 * 1024
SMALL_BYTES = 16 * 1024 * 1024


def spans(slab_len):
    deep = math.log2(slab_len)
    return 6.8 + deep, 13.2 + deep


def shifted(value, axis, steps):
    count = lax.axis_size(axis)
    initial, last = (max(0, -steps), min(count, count - steps))
    return lax.ppermute(value, axis, [(source, source + steps) for source in range(initial, last)])


def encode(value, span):
    code = jnp.log2(value) * (65535.0 / span) + 65535.5
    code = jnp.minimum(jnp.maximum(code, 0.0), 65535.0)
    return (code.astype(jnp.int32) - 32768).astype(jnp.int16)


def tile_gains(gain_ref, gain, base, tile_cols, start_ref, end_ref, col_of):
    sample = lax.broadcasted_iota(jnp.int32, (SUBLANES, LANES), 0) + base
    lane = lax.broadcasted_iota(jnp.int32, (SUBLANES, LANES), 1)

    def block(n, carry):
        tile = col_of(n) // tile_cols
        start = jnp.full((SUBLANES, LANES), start_ref[tile])
        end = jnp.full((SUBLANES, LANES), end_ref[tile])
        for t in range(1, LANES // tile_cols):
            start = jnp.where(lane >= t * tile_cols, start_ref[tile + t], start)
            end = jnp.where(lane >= t * tile_cols, end_ref[tile + t], end)
        cols = pl.ds(pl.multiple_of(n * LANES, LANES), LANES)
        for k in range(0, gain_ref.shape[0], SUBLANES):
            active = (sample + k >= start) & (sample + k < end)
            gain_ref[k:k + SUBLANES, cols] = jnp.where(active, gain, 0.0)
        return carry

    blocks = gain_ref.shape[1] // LANES
    lax.fori_loop(0, blocks, block, 0, unroll=math.gcd(blocks, 4))


def moment(sums, emitted, value, levels):
    whole = (levels[0] + value) * (levels[1] + value) * (levels[2] + value)
    share = emitted * pl.reciprocal(whole, approx=True, full_range=False)
    for n in range(3):
        sums[n] = sums[n] + share
        share = share * value


def colors(sums, levels):
    others = [(levels[1], levels[2]), (levels[2], levels[0]), (levels[0], levels[1])]
    return [sums[2] + (p + q) * sums[1] + (p * q) * sums[0] for p, q in others]


def march(gain_ref, plane_ref, unit, cols, place, jitter, levels, halo=None):
    slab_len = plane_ref.shape[1]
    shape = jitter.shape
    before = jnp.zeros(shape, jnp.float32)
    through = jnp.ones(shape, jnp.float32)
    sums = [jnp.zeros(shape, jnp.float32) for _ in range(3)]
    lower = plane_ref[unit, 0, :, cols].astype(jnp.float32)
    stay = lower - jitter * lower
    for k in range(slab_len - (halo is None)):
        following = plane_ref[unit, k + 1, :, cols] if k + 1 < slab_len else halo
        upper = following.astype(jnp.float32)
        moved = jitter * upper
        value = stay + moved
        before = before + gain_ref[k:k + 1, place] * value
        beyond = jnp.exp2(before)
        moment(sums, (through - beyond) * value, value, levels)
        through = beyond
        stay = upper - moved
    return sums, before


def loop(count, body):
    def step(n, carry):
        body(n)
        return carry

    lax.fori_loop(0, count, step, 0)


def each_block(units, arrive, compute, store, leave):
    def pair(n):
        places = [(2 * n + u, c) for u in range(2) for c in range(0, UNIT, LANES)]
        for u in range(2):
            arrive(2 * n + u)
        results = [compute(unit, pl.ds(c, LANES), pl.ds(pl.multiple_of(unit * UNIT + c, LANES), LANES)) for unit, c in places]
        for (unit, c), result in zip(places, results):
            store(unit, pl.ds(c, LANES), result)
        for u in range(2):
            leave(2 * n + u)

    loop(units // 2, pair)


class Units:
    def __init__(self, first, half, pieces_width):
        self.first, self.half, self.width = first, half, pieces_width

    def column(self, unit):
        return (self.first + unit) * self.width + self.half * UNIT

    def columns(self, unit):
        return pl.ds(pl.multiple_of(self.column(unit), LANES), UNIT)

    def block_column(self, n):
        return self.column(n // (UNIT // LANES)) + n % (UNIT // LANES) * LANES


def start_all(pairs, sems):
    copies = [pltpu.make_async_copy(src, dst, sems.at[n]) for n, (src, dst) in enumerate(pairs)]
    for copy in copies:
        copy.start()
    return copies


def unit_copies(place, field_any, jitter_any, plane_ref, jitter_ref, sems, unit):
    cols = place.columns(unit)
    return [
        pltpu.make_async_copy(jitter_any.at[:, cols], jitter_ref.at[unit], sems.at[0, unit]),
        pltpu.make_async_copy(field_any.at[:, :, cols], plane_ref.at[unit], sems.at[1, unit]),
    ]


def open_kernel(total, tile_cols, place, transfer_any, start_any, end_any, field_any, jitter_any, state_any, transfer_ref,
                start_ref, end_ref, plane_ref, jitter_ref, state_ref, gain_ref, few_sems, sems, out_sems):
    units, slab_len, rows, _ = plane_ref.shape
    early = start_all([(transfer_any, transfer_ref), (start_any, start_ref), (end_any, end_ref)], few_sems)
    arrivals = functools.partial(unit_copies, place, field_any, jitter_any, plane_ref, jitter_ref, sems)
    for unit in range(units):
        for copy in arrivals(unit):
            copy.start()
    base = lax.axis_index("depth") * slab_len
    for copy in early:
        copy.wait()
    levels = [jnp.full((rows, LANES), transfer_ref[i]) for i in range(3)]
    gain = jnp.full((SUBLANES, LANES), transfer_ref[3]) * (-LOG2E * 0.2 / total)
    tile_gains(gain_ref, gain, base, tile_cols, start_ref, end_ref, place.block_column)

    def arrive(unit):
        for copy in arrivals(unit):
            copy.wait()

    def compute(unit, cols, table):
        return march(gain_ref, plane_ref, unit, cols, table, jitter_ref[unit, :, cols], levels)

    def store(unit, cols, result):
        sums, before = result
        for i, value in enumerate([*sums, before]):
            state_ref[unit, i, :, cols] = value

    def leave(unit):
        return pltpu.make_async_copy(state_ref.at[unit], state_any.at[unit], out_sems.at[unit])

    each_block(units, arrive, compute, store, lambda unit: leave(unit).start())
    loop(units, lambda unit: leave(unit).wait())


def close_kernel(total, tile_cols, opened, place, *refs):
    before_units = Units(0, place.half, place.width)
    ins = 7 if opened else 6
    transfer_any, start_any, end_any, field_any, halo_any, jitter_any = refs[:6]
    out_any = refs[ins]
    transfer_ref, start_ref, end_ref, plane_ref, halo_ref, jitter_ref, out_ref, gain_ref, few_sems, sems, out_sems = refs[
        ins + 1:ins + 12]
    units, slab_len, rows, _ = plane_ref.shape
    few = [(transfer_any, transfer_ref), (start_any, start_ref), (end_any, end_ref), (halo_any, halo_ref)]
    early = start_all(few, few_sems)
    arrivals = functools.partial(unit_copies, place, field_any, jitter_any, plane_ref, jitter_ref, sems)
    for unit in range(units):
        for copy in arrivals(unit):
            copy.start()
    if opened:
        state_any = refs[6]
        state_ref, last_ref, last_jitter_ref, last_gain_ref, state_sems = refs[ins + 12:]

        def opened_copies(unit):
            cols = before_units.columns(unit)
            pairs = [
                (field_any.at[slab_len - 1, :, cols], last_ref.at[unit]),
                (jitter_any.at[:, cols], last_jitter_ref.at[unit]),
                (state_any.at[unit], state_ref.at[unit]),
            ]
            return [pltpu.make_async_copy(src, dst, state_sems.at[n, unit]) for n, (src, dst) in enumerate(pairs)]

        for unit in range(opened):
            for copy in opened_copies(unit):
                copy.start()
    base = lax.axis_index("depth") * slab_len
    for copy in early:
        copy.wait()
    shape = (rows, LANES)
    depth_gain = jnp.full(shape, transfer_ref[3]) * (0.2 / total)
    levels = [jnp.full(shape, transfer_ref[i]) for i in range(3)]
    depth_unit = 1.0 / (depth_gain * (slab_len * TOP))
    color_unit = [depth_unit * ((levels[i] + TOP) * (1.0 / TOP)) for i in range(3)]
    depth_span, color_span = spans(slab_len)
    gain = depth_gain[:SUBLANES] * -LOG2E
    tile_gains(gain_ref, gain, base, tile_cols, start_ref, end_ref, place.block_column)

    def coded(sums, before):
        codes = [encode(color * color_unit[i], color_span) for i, color in enumerate(colors(sums, levels))]
        return codes + [encode(before * (depth_unit * (-1.0 / LOG2E)), depth_span)]

    def arrive(unit):
        for copy in arrivals(unit):
            copy.wait()

    def compute(unit, cols, table):
        whole = pl.ds(pl.multiple_of(place.column(unit) + cols.start, LANES), LANES)
        jitter = jitter_ref[unit, :, cols]
        return coded(*march(gain_ref, plane_ref, unit, cols, table, jitter, levels, halo_ref[:, whole]))

    def store(first, unit, cols, codes):
        for i, code in enumerate(codes):
            out_ref[first + unit, i, :, cols] = code

    def leave(piece):
        return pltpu.make_async_copy(out_ref.at[piece], out_any.at[piece], out_sems.at[piece])

    each_block(units, arrive, compute, functools.partial(store, place.first), lambda unit: leave(place.first + unit).start())
    if opened:
        tile_gains(last_gain_ref, gain, base + slab_len - 1, tile_cols, start_ref, end_ref, before_units.block_column)

        def arrive_opened(unit):
            for copy in opened_copies(unit):
                copy.wait()

        def finish(unit, cols, table):
            whole = pl.ds(pl.multiple_of(before_units.column(unit) + cols.start, LANES), LANES)
            jitter = last_jitter_ref[unit, :, cols]
            lower = last_ref[unit, :, cols].astype(jnp.float32)
            upper = halo_ref[:, whole].astype(jnp.float32)
            value = (1.0 - jitter) * lower + jitter * upper
            before = state_ref[unit, 3, :, cols]
            beyond = before + last_gain_ref[0:1, table] * value
            emitted = (jnp.exp2(before) - jnp.exp2(beyond)) * value
            sums = [state_ref[unit, i, :, cols] for i in range(3)]
            moment(sums, emitted, value, levels)
            return coded(sums, beyond)

        each_block(opened, arrive_opened, finish, functools.partial(store, 0), lambda unit: leave(unit).start())
    loop(out_ref.shape[0], lambda piece: leave(piece).wait())


def slab_codes(field, halo, jitter, transfer, ray_start, ray_end, total, pieces):
    slab_len, rows, cols = field.shape
    width = cols // pieces
    opened = pieces * 3 // 8 * 2
    ntiles = ray_start.shape[0]
    tile_cols = cols // ntiles
    own = pl.BlockSpec(memory_space=pl.ANY)
    scalars = [pltpu.SMEM(transfer.shape, transfer.dtype)] + [pltpu.SMEM((ntiles,), jnp.int32)] * 2

    def cost(units):
        work = slab_len * rows * units * UNIT
        return pl.CostEstimate(flops=work * 20, bytes_accessed=work * 2, transcendentals=work * 2)

    state = pl.pallas_call(
        functools.partial(open_kernel, total, tile_cols, Units(0, 0, width)),
        in_specs=[own] * 5,
        out_specs=own,
        out_shape=jax.ShapeDtypeStruct((opened, 4, rows, UNIT), jnp.float32),
        scratch_shapes=scalars + [
            pltpu.VMEM((opened, slab_len, rows, UNIT), field.dtype),
            pltpu.VMEM((opened, rows, UNIT), jnp.float32),
            pltpu.VMEM((opened, 4, rows, UNIT), jnp.float32),
            pltpu.VMEM((slab_len, opened * UNIT), jnp.float32),
            pltpu.SemaphoreType.DMA((3,)),
            pltpu.SemaphoreType.DMA((2, opened)),
            pltpu.SemaphoreType.DMA((opened,)),
        ],
        compiler_params=pltpu.CompilerParams(vmem_limit_bytes=OPEN_BYTES),
        cost_estimate=cost(opened),
        name="open",
    )(transfer, ray_start, ray_end, field, jitter)

    halves = []
    for half in range(2):
        first = opened if half == 0 else 0
        units = pieces - first
        scratch = scalars + [
            pltpu.VMEM((units, slab_len, rows, UNIT), field.dtype),
            pltpu.VMEM((rows, cols), field.dtype),
            pltpu.VMEM((units, rows, UNIT), jnp.float32),
            pltpu.VMEM((pieces, 4, rows, UNIT), jnp.int16),
            pltpu.VMEM((slab_len, units * UNIT), jnp.float32),
            pltpu.SemaphoreType.DMA((4,)),
            pltpu.SemaphoreType.DMA((2, units)),
            pltpu.SemaphoreType.DMA((pieces,)),
        ]
        operands = [transfer, ray_start, ray_end, field, halo, jitter]
        if first:
            operands.append(state)
            scratch += [
                pltpu.VMEM((first, 4, rows, UNIT), jnp.float32),
                pltpu.VMEM((first, rows, UNIT), field.dtype),
                pltpu.VMEM((first, rows, UNIT), jnp.float32),
                pltpu.VMEM((SUBLANES, first * UNIT), jnp.float32),
                pltpu.SemaphoreType.DMA((3, first)),
            ]
        halves.append(pl.pallas_call(
            functools.partial(close_kernel, total, tile_cols, first, Units(first, half, width)),
            in_specs=[own] * len(operands),
            out_specs=own,
            out_shape=jax.ShapeDtypeStruct((pieces, 4, rows, UNIT), jnp.int16),
            scratch_shapes=scratch,
            compiler_params=pltpu.CompilerParams(vmem_limit_bytes=CLOSE_BYTES),
            cost_estimate=cost(units),
            name="close",
        )(*operands))
    return halves


def composite_kernel(total, slab_len, first, order_any, transfer_any, code_any, *refs):
    image_any, order_ref, transfer_ref, code_ref, out_ref, sems, out_sem = refs[-7:]
    copies = start_all([(order_any, order_ref), (transfer_any, transfer_ref), (code_any, code_ref)], sems)
    count, _, rows, width = code_ref.shape
    shape = (rows, width)
    depth_span, color_span = spans(slab_len)
    for copy in copies:
        copy.wait()
    unit = jnp.full(shape, transfer_ref[3]) * (0.2 / total * slab_len * TOP)
    depth_unit = unit * LOG2E

    def power(codes, span):
        return codes * (span / 65535.0) + (span * (32768.0 / 65535.0) - span)

    def number(codes):
        return codes.astype(jnp.int32).astype(jnp.float32)

    def step(j, carry):
        depth, *colors = carry
        slab = order_ref[j]
        depth_code = number(code_ref[slab, 3])
        idle = depth_code == -32768.0
        shift = jnp.where(idle, FAR, depth)
        for i in range(3):
            colors[i] = colors[i] + jnp.exp2(power(number(code_ref[slab, i]), color_span) - shift)
        depth = depth + depth_unit * jnp.where(idle, 0.0, jnp.exp2(power(depth_code, depth_span)))
        return depth, *colors

    zero = jnp.zeros(shape, jnp.float32)
    depth, *colors = lax.fori_loop(0, count, step, (zero, zero, zero, zero), unroll=math.gcd(count, 4))
    for i in range(3):
        out_ref[i] = colors[i] * (unit * (TOP / (transfer_ref[i] + jnp.full(shape, TOP))))
    out_ref[3] = 1.0 - jnp.exp2(-depth)
    copy = pltpu.make_async_copy(out_ref, image_any.at[:, :, pl.ds(first, width)], out_sem)
    copy.start()
    copy.wait()


def composite(codes, transfer, depth_order, total, slab_len, first, columns, image):
    _, _, rows, width = codes.shape
    own = pl.BlockSpec(memory_space=pl.ANY)
    operands = [depth_order, transfer, codes] + ([] if image is None else [image])
    return pl.pallas_call(
        functools.partial(composite_kernel, total, slab_len, first),
        in_specs=[own] * len(operands),
        out_specs=own,
        out_shape=jax.ShapeDtypeStruct((4, rows, columns), jnp.float32),
        scratch_shapes=[
            pltpu.SMEM(depth_order.shape, depth_order.dtype),
            pltpu.SMEM(transfer.shape, transfer.dtype),
            pltpu.VMEM(codes.shape, codes.dtype),
            pltpu.VMEM((4, rows, width), jnp.float32),
            pltpu.SemaphoreType.DMA((3,)),
            pltpu.SemaphoreType.DMA,
        ],
        input_output_aliases={} if image is None else {3: 0},
        compiler_params=pltpu.CompilerParams(vmem_limit_bytes=SMALL_BYTES),
        name="composite",
    )(*operands)


def exchange(codes):
    return lax.all_to_all(codes, "depth", split_axis=0, concat_axis=0, tiled=True)


def on_device(field, jitter, transfer, depth_order, ray_start, ray_end):
    count = lax.axis_size("depth")
    slab_len, rows, cols = field.shape
    total = slab_len * count
    width = cols // count
    halo = shifted(field[0], "depth", -1)
    direct = width == 2 * UNIT
    pieces = count if direct else cols // (2 * UNIT)
    halves = slab_codes(field, halo, jitter, transfer, ray_start, ray_end, total, pieces)
    if not direct:
        codes = jnp.concatenate(halves, axis=3)
        halves = [codes.transpose(1, 2, 0, 3).reshape(4, rows, count, width).transpose(2, 0, 1, 3)]
    image = None
    for half, codes in enumerate(halves):
        image = composite(exchange(codes), transfer, depth_order, total, slab_len, half * UNIT, width, image)
    return image


def solution(mesh):
    in_specs = (P("depth", "groups", None), P("groups", None), P(), P(), P(), P())
    out_specs = P(None, "groups", "depth")
    return jax.shard_map(
        on_device, mesh=mesh, in_specs=in_specs, out_specs=out_specs, check_vma=False
    )
```

```python
import functools
import math

import jax
import jax.numpy as jnp
from jax import lax
from jax.experimental import pallas as pl
from jax.experimental.pallas import tpu as pltpu
from jax.sharding import PartitionSpec as P

TOP = 5.2
LOG2E = math.log2(math.e)
SUBLANES = 8
LANES = 128
FAR = 1.0e4
UNIT = 512
OPEN_BYTES = 54 * 1024 * 1024
CLOSE_BYTES = 53 * 1024 * 1024
SMALL_BYTES = 16 * 1024 * 1024


def spans(slab_len):
    deep = math.log2(slab_len)
    return 6.8 + deep, 13.2 + deep


def lift(span):
    return span * (32768.0 / 65535.0) - span


def shifted(value, axis, steps):
    count = lax.axis_size(axis)
    initial, last = (max(0, -steps), min(count, count - steps))
    return lax.ppermute(value, axis, [(source, source + steps) for source in range(initial, last)])


def encode(value, span):
    code = jnp.log2(value) * (65535.0 / span) + 65535.5
    code = jnp.minimum(jnp.maximum(code, 0.0), 65535.0)
    return (code.astype(jnp.int32) - 32768).astype(jnp.int16)


def tile_gains(gain_ref, gain, base, tile_cols, start_ref, end_ref, col_of):
    sample = lax.broadcasted_iota(jnp.int32, (SUBLANES, LANES), 0) + base
    lane = lax.broadcasted_iota(jnp.int32, (SUBLANES, LANES), 1)

    def block(n, carry):
        tile = col_of(n) // tile_cols
        start = jnp.full((SUBLANES, LANES), start_ref[tile])
        end = jnp.full((SUBLANES, LANES), end_ref[tile])
        for t in range(1, LANES // tile_cols):
            start = jnp.where(lane >= t * tile_cols, start_ref[tile + t], start)
            end = jnp.where(lane >= t * tile_cols, end_ref[tile + t], end)
        cols = pl.ds(pl.multiple_of(n * LANES, LANES), LANES)
        for k in range(0, gain_ref.shape[0], SUBLANES):
            active = (sample + k >= start) & (sample + k < end)
            gain_ref[k:k + SUBLANES, cols] = jnp.where(active, gain, 0.0)
        return carry

    blocks = gain_ref.shape[1] // LANES
    lax.fori_loop(0, blocks, block, 0, unroll=math.gcd(blocks, 4))


def moment(sums, emitted, value, levels):
    whole = (levels[0] + value) * (levels[1] + value) * (levels[2] + value)
    share = emitted * pl.reciprocal(whole, approx=True, full_range=False)
    for n in range(3):
        sums[n] = sums[n] + share
        share = share * value


def colors(sums, levels):
    others = [(levels[1], levels[2]), (levels[2], levels[0]), (levels[0], levels[1])]
    return [sums[2] + (p + q) * sums[1] + (p * q) * sums[0] for p, q in others]


def march(gain_ref, plane_ref, unit, cols, place, jitter, levels, halo=None):
    slab_len = plane_ref.shape[1]
    shape = jitter.shape
    before = jnp.zeros(shape, jnp.float32)
    through = jnp.ones(shape, jnp.float32)
    sums = [jnp.zeros(shape, jnp.float32) for _ in range(3)]
    lower = plane_ref[unit, 0, :, cols].astype(jnp.float32)
    stay = lower - jitter * lower
    for k in range(slab_len - (halo is None)):
        following = plane_ref[unit, k + 1, :, cols] if k + 1 < slab_len else halo
        upper = following.astype(jnp.float32)
        moved = jitter * upper
        value = stay + moved
        before = before + gain_ref[k:k + 1, place] * value
        beyond = jnp.exp2(before)
        moment(sums, (through - beyond) * value, value, levels)
        through = beyond
        stay = upper - moved
    return sums, before


def loop(count, body):
    def step(n, carry):
        body(n)
        return carry

    lax.fori_loop(0, count, step, 0)


def each_block(units, arrive, compute, store, leave):
    def pair(n):
        places = [(2 * n + u, c) for u in range(2) for c in range(0, UNIT, LANES)]
        for u in range(2):
            arrive(2 * n + u)
        results = [compute(unit, pl.ds(c, LANES), pl.ds(pl.multiple_of(unit * UNIT + c, LANES), LANES)) for unit, c in places]
        for (unit, c), result in zip(places, results):
            store(unit, pl.ds(c, LANES), result)
        for u in range(2):
            leave(2 * n + u)

    loop(units // 2, pair)


class Units:
    def __init__(self, first):
        self.first = first

    def column(self, unit):
        return (self.first + unit) * UNIT

    def columns(self, unit):
        return pl.ds(pl.multiple_of(self.column(unit), LANES), UNIT)

    def block_column(self, n):
        return self.column(n // (UNIT // LANES)) + n % (UNIT // LANES) * LANES


def start_all(pairs, sems):
    copies = [pltpu.make_async_copy(src, dst, sems.at[n]) for n, (src, dst) in enumerate(pairs)]
    for copy in copies:
        copy.start()
    return copies


def unit_copies(place, field_any, jitter_any, plane_ref, jitter_ref, sems, unit):
    cols = place.columns(unit)
    return [
        pltpu.make_async_copy(jitter_any.at[:, cols], jitter_ref.at[unit], sems.at[0, unit]),
        pltpu.make_async_copy(field_any.at[:, :, cols], plane_ref.at[unit], sems.at[1, unit]),
    ]


def open_kernel(total, tile_cols, place, transfer_any, start_any, end_any, field_any, jitter_any, state_any, transfer_ref,
                start_ref, end_ref, plane_ref, jitter_ref, state_ref, gain_ref, few_sems, sems, out_sems):
    units, slab_len, rows, _ = plane_ref.shape
    early = start_all([(transfer_any, transfer_ref), (start_any, start_ref), (end_any, end_ref)], few_sems)
    arrivals = functools.partial(unit_copies, place, field_any, jitter_any, plane_ref, jitter_ref, sems)
    for unit in range(units):
        for copy in arrivals(unit):
            copy.start()
    base = lax.axis_index("depth") * slab_len
    for copy in early:
        copy.wait()
    levels = [jnp.full((rows, LANES), transfer_ref[i]) for i in range(3)]
    gain = jnp.full((SUBLANES, LANES), transfer_ref[3]) * (-LOG2E * 0.2 / total)
    tile_gains(gain_ref, gain, base, tile_cols, start_ref, end_ref, place.block_column)

    def arrive(unit):
        for copy in arrivals(unit):
            copy.wait()

    def compute(unit, cols, table):
        return march(gain_ref, plane_ref, unit, cols, table, jitter_ref[unit, :, cols], levels)

    def store(unit, cols, result):
        sums, before = result
        for i, value in enumerate([*sums, before]):
            state_ref[unit, i, :, cols] = value

    def leave(unit):
        return pltpu.make_async_copy(state_ref.at[unit], state_any.at[unit], out_sems.at[unit])

    each_block(units, arrive, compute, store, lambda unit: leave(unit).start())
    loop(units, lambda unit: leave(unit).wait())


def close_kernel(total, tile_cols, opened, place, transfer_any, start_any, end_any, field_any, halo_any, jitter_any, state_any,
                 out_any, transfer_ref, start_ref, end_ref, plane_ref, halo_ref, jitter_ref, out_ref, gain_ref, few_sems, sems,
                 out_sems, state_ref, last_ref, last_jitter_ref, last_gain_ref, state_sems):
    before_units = Units(0)
    units, slab_len, rows, _ = plane_ref.shape
    few = [(transfer_any, transfer_ref), (start_any, start_ref), (end_any, end_ref), (halo_any, halo_ref)]
    early = start_all(few, few_sems)
    arrivals = functools.partial(unit_copies, place, field_any, jitter_any, plane_ref, jitter_ref, sems)
    for unit in range(units):
        for copy in arrivals(unit):
            copy.start()

    def opened_copies(unit):
        cols = before_units.columns(unit)
        pairs = [
            (field_any.at[slab_len - 1, :, cols], last_ref.at[unit]),
            (jitter_any.at[:, cols], last_jitter_ref.at[unit]),
            (state_any.at[unit], state_ref.at[unit]),
        ]
        return [pltpu.make_async_copy(src, dst, state_sems.at[n, unit]) for n, (src, dst) in enumerate(pairs)]

    for unit in range(opened):
        for copy in opened_copies(unit):
            copy.start()
    base = lax.axis_index("depth") * slab_len
    for copy in early:
        copy.wait()
    shape = (rows, LANES)
    depth_gain = jnp.full(shape, transfer_ref[3]) * (0.2 / total)
    levels = [jnp.full(shape, transfer_ref[i]) for i in range(3)]
    depth_unit = 1.0 / (depth_gain * (slab_len * TOP))
    color_unit = [depth_unit * ((levels[i] + TOP) * (1.0 / TOP)) for i in range(3)]
    depth_span, color_span = spans(slab_len)
    gain = depth_gain[:SUBLANES] * -LOG2E
    tile_gains(gain_ref, gain, base, tile_cols, start_ref, end_ref, place.block_column)

    def coded(sums, before):
        codes = [encode(color * color_unit[i], color_span) for i, color in enumerate(colors(sums, levels))]
        return codes + [encode(before * (depth_unit * (-1.0 / LOG2E)), depth_span)]

    def arrive(unit):
        for copy in arrivals(unit):
            copy.wait()

    def compute(unit, cols, table):
        whole = pl.ds(pl.multiple_of(place.column(unit) + cols.start, LANES), LANES)
        jitter = jitter_ref[unit, :, cols]
        return coded(*march(gain_ref, plane_ref, unit, cols, table, jitter, levels, halo_ref[:, whole]))

    def store(first, unit, cols, codes):
        for i, code in enumerate(codes):
            out_ref[first + unit, i, :, cols] = code

    def leave(piece):
        return pltpu.make_async_copy(out_ref.at[piece], out_any.at[piece], out_sems.at[piece])

    each_block(units, arrive, compute, functools.partial(store, place.first), lambda unit: leave(place.first + unit).start())
    tile_gains(last_gain_ref, gain, base + slab_len - 1, tile_cols, start_ref, end_ref, before_units.block_column)

    def arrive_opened(unit):
        for copy in opened_copies(unit):
            copy.wait()

    def finish(unit, cols, table):
        whole = pl.ds(pl.multiple_of(before_units.column(unit) + cols.start, LANES), LANES)
        jitter = last_jitter_ref[unit, :, cols]
        lower = last_ref[unit, :, cols].astype(jnp.float32)
        upper = halo_ref[:, whole].astype(jnp.float32)
        value = (1.0 - jitter) * lower + jitter * upper
        before = state_ref[unit, 3, :, cols]
        beyond = before + last_gain_ref[0:1, table] * value
        emitted = (jnp.exp2(before) - jnp.exp2(beyond)) * value
        sums = [state_ref[unit, i, :, cols] for i in range(3)]
        moment(sums, emitted, value, levels)
        return coded(sums, beyond)

    each_block(opened, arrive_opened, finish, functools.partial(store, 0), lambda unit: leave(unit).start())
    loop(out_ref.shape[0], lambda piece: leave(piece).wait())


def slab_codes(field, halo, jitter, transfer, ray_start, ray_end, total):
    slab_len, rows, cols = field.shape
    pieces = cols // UNIT
    opened = pieces * 3 // 16 * 2
    closed = pieces - opened
    ntiles = ray_start.shape[0]
    tile_cols = cols // ntiles
    own = pl.BlockSpec(memory_space=pl.ANY)
    scalars = [pltpu.SMEM(transfer.shape, transfer.dtype)] + [pltpu.SMEM((ntiles,), jnp.int32)] * 2

    def cost(units):
        work = slab_len * rows * units * UNIT
        return pl.CostEstimate(flops=work * 20, bytes_accessed=work * 2, transcendentals=work * 2)

    state = pl.pallas_call(
        functools.partial(open_kernel, total, tile_cols, Units(0)),
        in_specs=[own] * 5,
        out_specs=own,
        out_shape=jax.ShapeDtypeStruct((opened, 4, rows, UNIT), jnp.float32),
        scratch_shapes=scalars + [
            pltpu.VMEM((opened, slab_len, rows, UNIT), field.dtype),
            pltpu.VMEM((opened, rows, UNIT), jnp.float32),
            pltpu.VMEM((opened, 4, rows, UNIT), jnp.float32),
            pltpu.VMEM((slab_len, opened * UNIT), jnp.float32),
            pltpu.SemaphoreType.DMA((3,)),
            pltpu.SemaphoreType.DMA((2, opened)),
            pltpu.SemaphoreType.DMA((opened,)),
        ],
        compiler_params=pltpu.CompilerParams(vmem_limit_bytes=OPEN_BYTES),
        cost_estimate=cost(opened),
        name="open",
    )(transfer, ray_start, ray_end, field, jitter)

    return pl.pallas_call(
        functools.partial(close_kernel, total, tile_cols, opened, Units(opened)),
        in_specs=[own] * 7,
        out_specs=own,
        out_shape=jax.ShapeDtypeStruct((pieces, 4, rows, UNIT), jnp.int16),
        scratch_shapes=scalars + [
            pltpu.VMEM((closed, slab_len, rows, UNIT), field.dtype),
            pltpu.VMEM((rows, cols), field.dtype),
            pltpu.VMEM((closed, rows, UNIT), jnp.float32),
            pltpu.VMEM((pieces, 4, rows, UNIT), jnp.int16),
            pltpu.VMEM((slab_len, closed * UNIT), jnp.float32),
            pltpu.SemaphoreType.DMA((4,)),
            pltpu.SemaphoreType.DMA((2, closed)),
            pltpu.SemaphoreType.DMA((pieces,)),
            pltpu.VMEM((opened, 4, rows, UNIT), jnp.float32),
            pltpu.VMEM((opened, rows, UNIT), field.dtype),
            pltpu.VMEM((opened, rows, UNIT), jnp.float32),
            pltpu.VMEM((SUBLANES, opened * UNIT), jnp.float32),
            pltpu.SemaphoreType.DMA((3, opened)),
        ],
        compiler_params=pltpu.CompilerParams(vmem_limit_bytes=CLOSE_BYTES),
        cost_estimate=cost(closed),
        name="close",
    )(transfer, ray_start, ray_end, field, halo, jitter, state)


def composite_kernel(total, slab_len, order_any, transfer_any, code_any, image_any, order_ref, transfer_ref, code_ref, out_ref,
                     sems, out_sems):
    copies = start_all([(order_any, order_ref), (transfer_any, transfer_ref)], sems)
    count, _, rows, width = code_ref.shape
    block = math.gcd(width, 2 * LANES)
    places = [pl.ds(col, block) for col in range(0, width, block)]
    codes = start_all([(code_any.at[:, :, :, cols], code_ref.at[:, :, :, cols]) for cols in places], sems.at[pl.ds(2, len(places))])
    shape = (rows, block)
    depth_span, color_span = spans(slab_len)
    for copy in copies:
        copy.wait()
    unit = jnp.full(shape, transfer_ref[3]) * (0.2 / total * slab_len * TOP)
    depth_unit = unit * LOG2E
    leaving = []
    for n, cols in enumerate(places):
        codes[n].wait()

        def number(slab, channel, span):
            return code_ref[slab, channel, :, cols].astype(jnp.int32).astype(jnp.float32) * (span / 65535.0)

        def step(j, carry):
            shift, *colors = carry
            slab = order_ref[j]
            code = number(slab, 3, depth_span)
            idle = code < depth_span * (-32767.5 / 65535.0)
            away = jnp.where(idle, FAR, shift)
            for i in range(3):
                colors[i] = colors[i] + jnp.exp2(number(slab, i, color_span) - away)
            own = jnp.where(idle, 0.0, jnp.exp2(code + lift(depth_span)))
            return shift + depth_unit * own, *colors

        zero = jnp.zeros(shape, jnp.float32)
        first = jnp.full(shape, -lift(color_span))
        shift, *colors = lax.fori_loop(0, count, step, (first, zero, zero, zero), unroll=math.gcd(count, 4))
        for i in range(3):
            out_ref[i, :, cols] = colors[i] * (unit * (TOP / (transfer_ref[i] + jnp.full(shape, TOP))))
        out_ref[3, :, cols] = 1.0 - jnp.exp2(first - shift)
        leaving.append(pltpu.make_async_copy(out_ref.at[:, :, cols], image_any.at[:, :, cols], out_sems.at[n]))
        leaving[-1].start()
    for copy in leaving:
        copy.wait()


def composite(codes, transfer, depth_order, total, slab_len):
    _, _, rows, width = codes.shape
    blocks = width // math.gcd(width, 2 * LANES)
    own = pl.BlockSpec(memory_space=pl.ANY)
    return pl.pallas_call(
        functools.partial(composite_kernel, total, slab_len),
        in_specs=[own] * 3,
        out_specs=own,
        out_shape=jax.ShapeDtypeStruct((4, rows, width), jnp.float32),
        scratch_shapes=[
            pltpu.SMEM(depth_order.shape, depth_order.dtype),
            pltpu.SMEM(transfer.shape, transfer.dtype),
            pltpu.VMEM(codes.shape, codes.dtype),
            pltpu.VMEM((4, rows, width), jnp.float32),
            pltpu.SemaphoreType.DMA((2 + blocks,)),
            pltpu.SemaphoreType.DMA((blocks,)),
        ],
        compiler_params=pltpu.CompilerParams(vmem_limit_bytes=SMALL_BYTES),
        name="composite",
    )(depth_order, transfer, codes)


def on_device(field, jitter, transfer, depth_order, ray_start, ray_end):
    count = lax.axis_size("depth")
    slab_len, rows, cols = field.shape
    total = slab_len * count
    width = cols // count
    halo = shifted(field[0], "depth", -1)
    codes = slab_codes(field, halo, jitter, transfer, ray_start, ray_end, total)
    if width != UNIT:
        codes = codes.transpose(1, 2, 0, 3).reshape(4, rows, count, width).transpose(2, 0, 1, 3)
    received = lax.all_to_all(codes, "depth", split_axis=0, concat_axis=0, tiled=True)
    return composite(received, transfer, depth_order, total, slab_len)


def solution(mesh):
    in_specs = (P("depth", "groups", None), P("groups", None), P(), P(), P(), P())
    out_specs = P(None, "groups", "depth")
    return jax.shard_map(
        on_device, mesh=mesh, in_specs=in_specs, out_specs=out_specs, check_vma=False
    )
```

```python
import functools
import math

import jax
import jax.numpy as jnp
from jax import lax
from jax.experimental import pallas as pl
from jax.experimental.pallas import tpu as pltpu
from jax.sharding import PartitionSpec as P

TOP = 5.2
LOG2E = math.log2(math.e)
SUBLANES = 8
LANES = 128
FAR = 1.0e4
UNIT = 512
OPEN_BYTES = 54 * 1024 * 1024
CLOSE_BYTES = 58 * 1024 * 1024
SMALL_BYTES = 16 * 1024 * 1024


def spans(slab_len):
    deep = math.log2(slab_len)
    return 6.8 + deep, 13.2 + deep


def lift(span):
    return span * (32768.0 / 65535.0) - span


def pair_planes(value, axis):
    count = lax.axis_size(axis)
    gathered = []
    for odd in range(2):
        groups = [[first, (first + 1) % count] for first in range(odd, count, 2)]
        gathered.append(lax.all_gather(value, axis, axis_index_groups=groups))
    return gathered


def encode(value, span):
    code = jnp.log2(value) * (65535.0 / span) + 65535.5
    code = jnp.minimum(jnp.maximum(code, 0.0), 65535.0)
    return (code.astype(jnp.int32) - 32768).astype(jnp.int16)


def tile_gains(gain_ref, gain, base, tile_cols, start_ref, end_ref, col_of):
    sample = lax.broadcasted_iota(jnp.int32, (SUBLANES, LANES), 0) + base
    lane = lax.broadcasted_iota(jnp.int32, (SUBLANES, LANES), 1)

    def block(n, carry):
        tile = col_of(n) // tile_cols
        start = jnp.full((SUBLANES, LANES), start_ref[tile])
        end = jnp.full((SUBLANES, LANES), end_ref[tile])
        for t in range(1, LANES // tile_cols):
            start = jnp.where(lane >= t * tile_cols, start_ref[tile + t], start)
            end = jnp.where(lane >= t * tile_cols, end_ref[tile + t], end)
        cols = pl.ds(pl.multiple_of(n * LANES, LANES), LANES)
        for k in range(0, gain_ref.shape[0], SUBLANES):
            active = (sample + k >= start) & (sample + k < end)
            gain_ref[k:k + SUBLANES, cols] = jnp.where(active, gain, 0.0)
        return carry

    blocks = gain_ref.shape[1] // LANES
    lax.fori_loop(0, blocks, block, 0, unroll=math.gcd(blocks, 4))


def moment(sums, emitted, value, levels):
    whole = (levels[0] + value) * (levels[1] + value) * (levels[2] + value)
    share = emitted * pl.reciprocal(whole, approx=True, full_range=False)
    for n in range(3):
        sums[n] = sums[n] + share
        share = share * value


def colors(sums, levels):
    others = [(levels[1], levels[2]), (levels[2], levels[0]), (levels[0], levels[1])]
    return [sums[2] + (p + q) * sums[1] + (p * q) * sums[0] for p, q in others]


def march(gain_ref, plane_ref, unit, cols, place, jitter, levels, halo=None):
    slab_len = plane_ref.shape[1]
    shape = jitter.shape
    before = jnp.zeros(shape, jnp.float32)
    through = jnp.ones(shape, jnp.float32)
    sums = [jnp.zeros(shape, jnp.float32) for _ in range(3)]
    lower = plane_ref[unit, 0, :, cols].astype(jnp.float32)
    stay = lower - jitter * lower
    for k in range(slab_len - (halo is None)):
        following = plane_ref[unit, k + 1, :, cols] if k + 1 < slab_len else halo
        upper = following.astype(jnp.float32)
        moved = jitter * upper
        value = stay + moved
        before = before + gain_ref[k:k + 1, place] * value
        beyond = jnp.exp2(before)
        moment(sums, (through - beyond) * value, value, levels)
        through = beyond
        stay = upper - moved
    return sums, before


def loop(count, body):
    def step(n, carry):
        body(n)
        return carry

    lax.fori_loop(0, count, step, 0)


def each_block(units, group, arrive, compute, store, leave):
    def step(n):
        places = [(group * n + u, c) for u in range(group) for c in range(0, UNIT, LANES)]
        for u in range(group):
            arrive(group * n + u)
        results = [compute(unit, pl.ds(c, LANES), pl.ds(pl.multiple_of(unit * UNIT + c, LANES), LANES)) for unit, c in places]
        for (unit, c), result in zip(places, results):
            store(unit, pl.ds(c, LANES), result)
        for u in range(group):
            leave(group * n + u)

    loop(units // group, step)


class Units:
    def __init__(self, first):
        self.first = first

    def column(self, unit):
        return (self.first + unit) * UNIT

    def columns(self, unit):
        return pl.ds(pl.multiple_of(self.column(unit), LANES), UNIT)

    def block_column(self, n):
        return self.column(n // (UNIT // LANES)) + n % (UNIT // LANES) * LANES


def start_all(pairs, sems):
    copies = [pltpu.make_async_copy(src, dst, sems.at[n]) for n, (src, dst) in enumerate(pairs)]
    for copy in copies:
        copy.start()
    return copies


def unit_copies(place, field_any, jitter_any, plane_ref, jitter_ref, sems, unit):
    cols = place.columns(unit)
    return [
        pltpu.make_async_copy(jitter_any.at[:, cols], jitter_ref.at[unit], sems.at[0, unit]),
        pltpu.make_async_copy(field_any.at[:, :, cols], plane_ref.at[unit], sems.at[1, unit]),
    ]


def open_kernel(total, tile_cols, place, transfer_any, start_any, end_any, field_any, jitter_any, state_any, transfer_ref,
                start_ref, end_ref, plane_ref, jitter_ref, state_ref, gain_ref, few_sems, sems, out_sems):
    units, slab_len, rows, _ = plane_ref.shape
    early = start_all([(transfer_any, transfer_ref), (start_any, start_ref), (end_any, end_ref)], few_sems)
    arrivals = functools.partial(unit_copies, place, field_any, jitter_any, plane_ref, jitter_ref, sems)
    for unit in range(units):
        for copy in arrivals(unit):
            copy.start()
    base = lax.axis_index("depth") * slab_len
    for copy in early:
        copy.wait()
    levels = [jnp.full((rows, LANES), transfer_ref[i]) for i in range(3)]
    gain = jnp.full((SUBLANES, LANES), transfer_ref[3]) * (-LOG2E * 0.2 / total)
    tile_gains(gain_ref, gain, base, tile_cols, start_ref, end_ref, place.block_column)

    def arrive(unit):
        for copy in arrivals(unit):
            copy.wait()

    def compute(unit, cols, table):
        return march(gain_ref, plane_ref, unit, cols, table, jitter_ref[unit, :, cols], levels)

    def store(unit, cols, result):
        sums, before = result
        for i, value in enumerate([*sums, before]):
            state_ref[unit, i, :, cols] = value

    def leave(unit):
        return pltpu.make_async_copy(state_ref.at[unit], state_any.at[unit], out_sems.at[unit])

    each_block(units, 1, arrive, compute, store, lambda unit: leave(unit).start())
    loop(units, lambda unit: leave(unit).wait())


def close_kernel(total, tile_cols, opened, place, transfer_any, start_any, end_any, field_any, even_any, odd_any, jitter_any,
                 state_any, out_any, transfer_ref, start_ref, end_ref, plane_ref, halo_ref, jitter_ref, out_ref, gain_ref, few_sems, halo_sem, sems,
                 out_sems, state_ref, last_ref, last_jitter_ref, last_gain_ref, state_sems):
    before_units = Units(0)
    units, slab_len, rows, _ = plane_ref.shape
    here = lax.axis_index("depth")
    last = here == lax.axis_size("depth") - 1
    even = here % 2 == 0

    def halo_copy(planes_any):
        return pltpu.make_async_copy(planes_any.at[1], halo_ref, halo_sem)

    def opened_copies(unit):
        cols = before_units.columns(unit)
        pairs = [
            (field_any.at[slab_len - 1, :, cols], last_ref.at[unit]),
            (jitter_any.at[:, cols], last_jitter_ref.at[unit]),
            (state_any.at[unit], state_ref.at[unit]),
        ]
        return [pltpu.make_async_copy(src, dst, state_sems.at[n, unit]) for n, (src, dst) in enumerate(pairs)]

    early = start_all([(transfer_any, transfer_ref), (start_any, start_ref), (end_any, end_ref)], few_sems)
    pl.when(even)(lambda: halo_copy(even_any).start())
    pl.when(jnp.logical_not(even))(lambda: halo_copy(odd_any).start())
    for unit in range(opened):
        for copy in opened_copies(unit):
            copy.start()
    arrivals = functools.partial(unit_copies, place, field_any, jitter_any, plane_ref, jitter_ref, sems)
    for unit in range(units):
        for copy in arrivals(unit):
            copy.start()
    base = here * slab_len
    for copy in early:
        copy.wait()
    halo_copy(even_any).wait()

    @pl.when(last)
    def _():
        halo_ref[...] = jnp.zeros(halo_ref.shape, halo_ref.dtype)

    shape = (rows, LANES)
    depth_gain = jnp.full(shape, transfer_ref[3]) * (0.2 / total)
    levels = [jnp.full(shape, transfer_ref[i]) for i in range(3)]
    depth_unit = 1.0 / (depth_gain * (slab_len * TOP))
    color_unit = [depth_unit * ((levels[i] + TOP) * (1.0 / TOP)) for i in range(3)]
    depth_span, color_span = spans(slab_len)
    gain = depth_gain[:SUBLANES] * -LOG2E

    def coded(sums, before):
        codes = [encode(color * color_unit[i], color_span) for i, color in enumerate(colors(sums, levels))]
        return codes + [encode(before * (depth_unit * (-1.0 / LOG2E)), depth_span)]

    def arrive(unit):
        for copy in arrivals(unit):
            copy.wait()

    def compute(unit, cols, table):
        whole = pl.ds(pl.multiple_of(place.column(unit) + cols.start, LANES), LANES)
        jitter = jitter_ref[unit, :, cols]
        return coded(*march(gain_ref, plane_ref, unit, cols, table, jitter, levels, halo_ref[:, whole]))

    def store(first, unit, cols, codes):
        for i, code in enumerate(codes):
            out_ref[first + unit, i, :, cols] = code

    def leave(piece):
        return pltpu.make_async_copy(out_ref.at[piece], out_any.at[piece], out_sems.at[piece])

    tile_gains(last_gain_ref, gain, base + slab_len - 1, tile_cols, start_ref, end_ref, before_units.block_column)

    def arrive_opened(unit):
        for copy in opened_copies(unit):
            copy.wait()

    def finish(unit, cols, table):
        whole = pl.ds(pl.multiple_of(before_units.column(unit) + cols.start, LANES), LANES)
        jitter = last_jitter_ref[unit, :, cols]
        lower = last_ref[unit, :, cols].astype(jnp.float32)
        upper = halo_ref[:, whole].astype(jnp.float32)
        value = (1.0 - jitter) * lower + jitter * upper
        before = state_ref[unit, 3, :, cols]
        beyond = before + last_gain_ref[0:1, table] * value
        emitted = (jnp.exp2(before) - jnp.exp2(beyond)) * value
        sums = [state_ref[unit, i, :, cols] for i in range(3)]
        moment(sums, emitted, value, levels)
        return coded(sums, beyond)

    each_block(opened, 2, arrive_opened, finish, functools.partial(store, 0), lambda unit: leave(unit).start())
    tile_gains(gain_ref, gain, base, tile_cols, start_ref, end_ref, place.block_column)
    each_block(units, 1, arrive, compute, functools.partial(store, place.first), lambda unit: leave(place.first + unit).start())
    loop(out_ref.shape[0], lambda piece: leave(piece).wait())


def slab_codes(field, planes, jitter, transfer, ray_start, ray_end, total):
    slab_len, rows, cols = field.shape
    pieces = cols // UNIT
    opened = pieces * 3 // 16 * 2
    closed = pieces - opened
    ntiles = ray_start.shape[0]
    tile_cols = cols // ntiles
    own = pl.BlockSpec(memory_space=pl.ANY)
    scalars = [pltpu.SMEM(transfer.shape, transfer.dtype)] + [pltpu.SMEM((ntiles,), jnp.int32)] * 2

    def cost(units):
        work = slab_len * rows * units * UNIT
        return pl.CostEstimate(flops=work * 20, bytes_accessed=work * 2, transcendentals=work * 2)

    state = pl.pallas_call(
        functools.partial(open_kernel, total, tile_cols, Units(0)),
        in_specs=[own] * 5,
        out_specs=own,
        out_shape=jax.ShapeDtypeStruct((opened, 4, rows, UNIT), jnp.float32),
        scratch_shapes=scalars + [
            pltpu.VMEM((opened, slab_len, rows, UNIT), field.dtype),
            pltpu.VMEM((opened, rows, UNIT), jnp.float32),
            pltpu.VMEM((opened, 4, rows, UNIT), jnp.float32),
            pltpu.VMEM((slab_len, opened * UNIT), jnp.float32),
            pltpu.SemaphoreType.DMA((3,)),
            pltpu.SemaphoreType.DMA((2, opened)),
            pltpu.SemaphoreType.DMA((opened,)),
        ],
        compiler_params=pltpu.CompilerParams(vmem_limit_bytes=OPEN_BYTES),
        cost_estimate=cost(opened),
        name="open",
    )(transfer, ray_start, ray_end, field, jitter)

    return pl.pallas_call(
        functools.partial(close_kernel, total, tile_cols, opened, Units(opened)),
        in_specs=[own] * 8,
        out_specs=own,
        out_shape=jax.ShapeDtypeStruct((pieces, 4, rows, UNIT), jnp.int16),
        scratch_shapes=scalars + [
            pltpu.VMEM((closed, slab_len, rows, UNIT), field.dtype),
            pltpu.VMEM((rows, cols), field.dtype),
            pltpu.VMEM((closed, rows, UNIT), jnp.float32),
            pltpu.VMEM((pieces, 4, rows, UNIT), jnp.int16),
            pltpu.VMEM((slab_len, closed * UNIT), jnp.float32),
            pltpu.SemaphoreType.DMA((3,)),
            pltpu.SemaphoreType.DMA,
            pltpu.SemaphoreType.DMA((2, closed)),
            pltpu.SemaphoreType.DMA((pieces,)),
            pltpu.VMEM((opened, 4, rows, UNIT), jnp.float32),
            pltpu.VMEM((opened, rows, UNIT), field.dtype),
            pltpu.VMEM((opened, rows, UNIT), jnp.float32),
            pltpu.VMEM((SUBLANES, opened * UNIT), jnp.float32),
            pltpu.SemaphoreType.DMA((3, opened)),
        ],
        compiler_params=pltpu.CompilerParams(vmem_limit_bytes=CLOSE_BYTES),
        cost_estimate=cost(closed),
        name="close",
    )(transfer, ray_start, ray_end, field, *planes, jitter, state)


def composite_kernel(total, slab_len, order_any, transfer_any, code_any, image_any, order_ref, transfer_ref, code_ref, out_ref,
                     sems, out_sems):
    copies = start_all([(order_any, order_ref), (transfer_any, transfer_ref)], sems)
    count, _, rows, width = code_ref.shape
    block = math.gcd(width, 2 * LANES)
    places = [pl.ds(col, block) for col in range(0, width, block)]
    codes = start_all([(code_any.at[:, :, :, cols], code_ref.at[:, :, :, cols]) for cols in places], sems.at[pl.ds(2, len(places))])
    shape = (rows, block)
    depth_span, color_span = spans(slab_len)
    for copy in copies:
        copy.wait()
    unit = jnp.full(shape, transfer_ref[3]) * (0.2 / total * slab_len * TOP)
    depth_unit = unit * LOG2E
    leaving = []
    for n, cols in enumerate(places):
        codes[n].wait()

        def number(slab, channel, span):
            return code_ref[slab, channel, :, cols].astype(jnp.int32).astype(jnp.float32) * (span / 65535.0)

        def step(j, carry):
            shift, *colors = carry
            slab = order_ref[j]
            code = number(slab, 3, depth_span)
            idle = code < depth_span * (-32767.5 / 65535.0)
            away = jnp.where(idle, FAR, shift)
            for i in range(3):
                colors[i] = colors[i] + jnp.exp2(number(slab, i, color_span) - away)
            own = jnp.where(idle, 0.0, jnp.exp2(code + lift(depth_span)))
            return shift + depth_unit * own, *colors

        zero = jnp.zeros(shape, jnp.float32)
        first = jnp.full(shape, -lift(color_span))
        shift, *colors = lax.fori_loop(0, count, step, (first, zero, zero, zero), unroll=math.gcd(count, 4))
        for i in range(3):
            out_ref[i, :, cols] = colors[i] * (unit * (TOP / (transfer_ref[i] + jnp.full(shape, TOP))))
        out_ref[3, :, cols] = 1.0 - jnp.exp2(first - shift)
        leaving.append(pltpu.make_async_copy(out_ref.at[:, :, cols], image_any.at[:, :, cols], out_sems.at[n]))
        leaving[-1].start()
    for copy in leaving:
        copy.wait()


def composite(codes, transfer, depth_order, total, slab_len):
    _, _, rows, width = codes.shape
    blocks = width // math.gcd(width, 2 * LANES)
    own = pl.BlockSpec(memory_space=pl.ANY)
    return pl.pallas_call(
        functools.partial(composite_kernel, total, slab_len),
        in_specs=[own] * 3,
        out_specs=own,
        out_shape=jax.ShapeDtypeStruct((4, rows, width), jnp.float32),
        scratch_shapes=[
            pltpu.SMEM(depth_order.shape, depth_order.dtype),
            pltpu.SMEM(transfer.shape, transfer.dtype),
            pltpu.VMEM(codes.shape, codes.dtype),
            pltpu.VMEM((4, rows, width), jnp.float32),
            pltpu.SemaphoreType.DMA((2 + blocks,)),
            pltpu.SemaphoreType.DMA((blocks,)),
        ],
        compiler_params=pltpu.CompilerParams(vmem_limit_bytes=SMALL_BYTES),
        name="composite",
    )(depth_order, transfer, codes)


def on_device(field, jitter, transfer, depth_order, ray_start, ray_end):
    count = lax.axis_size("depth")
    slab_len, rows, cols = field.shape
    total = slab_len * count
    width = cols // count
    planes = pair_planes(field[0], "depth")
    codes = slab_codes(field, planes, jitter, transfer, ray_start, ray_end, total)
    if width != UNIT:
        codes = codes.transpose(1, 2, 0, 3).reshape(4, rows, count, width).transpose(2, 0, 1, 3)
    received = lax.all_to_all(codes, "depth", split_axis=0, concat_axis=0, tiled=True)
    return composite(received, transfer, depth_order, total, slab_len)


def solution(mesh):
    in_specs = (P("depth", "groups", None), P("groups", None), P(), P(), P(), P())
    out_specs = P(None, "groups", "depth")
    return jax.shard_map(
        on_device, mesh=mesh, in_specs=in_specs, out_specs=out_specs, check_vma=False
    )
```

```python
import functools
import math

import jax
import jax.numpy as jnp
from jax import lax
from jax.experimental import pallas as pl
from jax.experimental.pallas import tpu as pltpu
from jax.sharding import PartitionSpec as P

TOP = 5.2
LOG2E = math.log2(math.e)
SUBLANES = 8
LANES = 128
FAR = 1.0e4
UNIT = 512
OPEN_BYTES = 54 * 1024 * 1024
CLOSE_BYTES = 53 * 1024 * 1024
SMALL_BYTES = 16 * 1024 * 1024


def spans(slab_len):
    deep = math.log2(slab_len)
    return 6.8 + deep, 13.2 + deep


def lift(span):
    return span * (32768.0 / 65535.0) - span


def shifted(value, axis, steps):
    count = lax.axis_size(axis)
    initial, last = (max(0, -steps), min(count, count - steps))
    return lax.ppermute(value, axis, [(source, source + steps) for source in range(initial, last)])


def encode(value, span):
    code = jnp.log2(value) * (65535.0 / span) + 65535.5
    code = jnp.minimum(jnp.maximum(code, 0.0), 65535.0)
    return (code.astype(jnp.int32) - 32768).astype(jnp.int16)


def tile_gains(gain_ref, gain, base, tile_cols, start_ref, end_ref, col_of):
    sample = lax.broadcasted_iota(jnp.int32, (SUBLANES, LANES), 0) + base
    lane = lax.broadcasted_iota(jnp.int32, (SUBLANES, LANES), 1)

    def block(n, carry):
        tile = col_of(n) // tile_cols
        start = jnp.full((SUBLANES, LANES), start_ref[tile])
        end = jnp.full((SUBLANES, LANES), end_ref[tile])
        for t in range(1, LANES // tile_cols):
            start = jnp.where(lane >= t * tile_cols, start_ref[tile + t], start)
            end = jnp.where(lane >= t * tile_cols, end_ref[tile + t], end)
        cols = pl.ds(pl.multiple_of(n * LANES, LANES), LANES)
        for k in range(0, gain_ref.shape[0], SUBLANES):
            active = (sample + k >= start) & (sample + k < end)
            gain_ref[k:k + SUBLANES, cols] = jnp.where(active, gain, 0.0)
        return carry

    blocks = gain_ref.shape[1] // LANES
    lax.fori_loop(0, blocks, block, 0, unroll=math.gcd(blocks, 8))


def moment(sums, weight, value, levels):
    whole = (levels[0] + value) * (levels[1] + value) * (levels[2] + value)
    share = weight * pl.reciprocal(whole, approx=True, full_range=False)
    for n in range(3):
        sums[n] = sums[n] + share
        share = share * value


def colors(sums, before, levels):
    emitted = 1.0 - jnp.exp2(before)
    others = [(levels[1], levels[2]), (levels[2], levels[0]), (levels[0], levels[1])]
    return [emitted - t * (sums[2] + (p + q) * sums[1] + (p * q) * sums[0]) for t, (p, q) in zip(levels, others)]


def march(gain_ref, plane_ref, unit, cols, place, jitter, levels, halo=None):
    slab_len = plane_ref.shape[1]
    shape = jitter.shape
    before = jnp.zeros(shape, jnp.float32)
    through = jnp.ones(shape, jnp.float32)
    sums = [jnp.zeros(shape, jnp.float32) for _ in range(3)]
    lower = plane_ref[unit, 0, :, cols].astype(jnp.float32)
    stay = lower - jitter * lower
    for k in range(slab_len - (halo is None)):
        following = plane_ref[unit, k + 1, :, cols] if k + 1 < slab_len else halo
        upper = following.astype(jnp.float32)
        moved = jitter * upper
        value = stay + moved
        before = before + gain_ref[k:k + 1, place] * value
        beyond = jnp.exp2(before)
        moment(sums, through - beyond, value, levels)
        through = beyond
        stay = upper - moved
    return sums, before


def loop(count, body):
    def step(n, carry):
        body(n)
        return carry

    lax.fori_loop(0, count, step, 0)


def each_block(units, arrive, compute, store, leave):
    def pair(n):
        places = [(2 * n + u, c) for u in range(2) for c in range(0, UNIT, LANES)]
        for u in range(2):
            arrive(2 * n + u)
        results = [compute(unit, pl.ds(c, LANES), pl.ds(pl.multiple_of(unit * UNIT + c, LANES), LANES)) for unit, c in places]
        for (unit, c), result in zip(places, results):
            store(unit, pl.ds(c, LANES), result)
        for u in range(2):
            leave(2 * n + u)

    loop(units // 2, pair)


class Units:
    def __init__(self, first):
        self.first = first

    def column(self, unit):
        return (self.first + unit) * UNIT

    def columns(self, unit):
        return pl.ds(pl.multiple_of(self.column(unit), LANES), UNIT)

    def block_column(self, n):
        return self.column(n // (UNIT // LANES)) + n % (UNIT // LANES) * LANES


def start_all(pairs, sems):
    copies = [pltpu.make_async_copy(src, dst, sems.at[n]) for n, (src, dst) in enumerate(pairs)]
    for copy in copies:
        copy.start()
    return copies


def unit_copies(place, field_any, jitter_any, plane_ref, jitter_ref, sems, unit):
    cols = place.columns(unit)
    return [
        pltpu.make_async_copy(jitter_any.at[:, cols], jitter_ref.at[unit], sems.at[0, unit]),
        pltpu.make_async_copy(field_any.at[:, :, cols], plane_ref.at[unit], sems.at[1, unit]),
    ]


def open_kernel(total, tile_cols, place, transfer_any, start_any, end_any, field_any, jitter_any, state_any, transfer_ref,
                start_ref, end_ref, plane_ref, jitter_ref, state_ref, gain_ref, few_sems, sems, out_sems):
    units, slab_len, rows, _ = plane_ref.shape
    early = start_all([(transfer_any, transfer_ref), (start_any, start_ref), (end_any, end_ref)], few_sems)
    arrivals = functools.partial(unit_copies, place, field_any, jitter_any, plane_ref, jitter_ref, sems)
    for unit in range(units):
        for copy in arrivals(unit):
            copy.start()
    base = lax.axis_index("depth") * slab_len
    for copy in early:
        copy.wait()
    levels = [jnp.full((rows, LANES), transfer_ref[i]) for i in range(3)]
    gain = jnp.full((SUBLANES, LANES), transfer_ref[3]) * (-LOG2E * 0.2 / total)
    tile_gains(gain_ref, gain, base, tile_cols, start_ref, end_ref, place.block_column)

    def arrive(unit):
        for copy in arrivals(unit):
            copy.wait()

    def compute(unit, cols, table):
        return march(gain_ref, plane_ref, unit, cols, table, jitter_ref[unit, :, cols], levels)

    def store(unit, cols, result):
        sums, before = result
        for i, value in enumerate([*sums, before]):
            state_ref[unit, i, :, cols] = value

    def leave(unit):
        return pltpu.make_async_copy(state_ref.at[unit], state_any.at[unit], out_sems.at[unit])

    each_block(units, arrive, compute, store, lambda unit: leave(unit).start())
    loop(units, lambda unit: leave(unit).wait())


def close_kernel(total, tile_cols, opened, place, transfer_any, start_any, end_any, field_any, halo_any, jitter_any, state_any,
                 out_any, transfer_ref, start_ref, end_ref, plane_ref, halo_ref, jitter_ref, out_ref, gain_ref, few_sems, sems,
                 out_sems, state_ref, last_ref, last_jitter_ref, last_gain_ref, state_sems):
    before_units = Units(0)
    units, slab_len, rows, _ = plane_ref.shape
    few = [(transfer_any, transfer_ref), (start_any, start_ref), (end_any, end_ref), (halo_any, halo_ref)]
    early = start_all(few, few_sems)
    arrivals = functools.partial(unit_copies, place, field_any, jitter_any, plane_ref, jitter_ref, sems)
    for unit in range(units):
        for copy in arrivals(unit):
            copy.start()

    def opened_copies(unit):
        cols = before_units.columns(unit)
        pairs = [
            (field_any.at[slab_len - 1, :, cols], last_ref.at[unit]),
            (jitter_any.at[:, cols], last_jitter_ref.at[unit]),
            (state_any.at[unit], state_ref.at[unit]),
        ]
        return [pltpu.make_async_copy(src, dst, state_sems.at[n, unit]) for n, (src, dst) in enumerate(pairs)]

    for unit in range(opened):
        for copy in opened_copies(unit):
            copy.start()
    base = lax.axis_index("depth") * slab_len
    for copy in early:
        copy.wait()
    shape = (rows, LANES)
    depth_gain = jnp.full(shape, transfer_ref[3]) * (0.2 / total)
    levels = [jnp.full(shape, transfer_ref[i]) for i in range(3)]
    depth_unit = 1.0 / (depth_gain * (slab_len * TOP))
    color_unit = [depth_unit * ((levels[i] + TOP) * (1.0 / TOP)) for i in range(3)]
    depth_span, color_span = spans(slab_len)
    gain = depth_gain[:SUBLANES] * -LOG2E
    tile_gains(gain_ref, gain, base, tile_cols, start_ref, end_ref, place.block_column)

    def coded(sums, before):
        codes = [encode(color * color_unit[i], color_span) for i, color in enumerate(colors(sums, before, levels))]
        return codes + [encode(before * (depth_unit * (-1.0 / LOG2E)), depth_span)]

    def arrive(unit):
        for copy in arrivals(unit):
            copy.wait()

    def compute(unit, cols, table):
        whole = pl.ds(pl.multiple_of(place.column(unit) + cols.start, LANES), LANES)
        jitter = jitter_ref[unit, :, cols]
        return coded(*march(gain_ref, plane_ref, unit, cols, table, jitter, levels, halo_ref[:, whole]))

    def store(first, unit, cols, codes):
        for i, code in enumerate(codes):
            out_ref[first + unit, i, :, cols] = code

    def leave(piece):
        return pltpu.make_async_copy(out_ref.at[piece], out_any.at[piece], out_sems.at[piece])

    each_block(units, arrive, compute, functools.partial(store, place.first), lambda unit: leave(place.first + unit).start())
    tile_gains(last_gain_ref, gain, base + slab_len - 1, tile_cols, start_ref, end_ref, before_units.block_column)

    def arrive_opened(unit):
        for copy in opened_copies(unit):
            copy.wait()

    def finish(unit, cols, table):
        whole = pl.ds(pl.multiple_of(before_units.column(unit) + cols.start, LANES), LANES)
        jitter = last_jitter_ref[unit, :, cols]
        lower = last_ref[unit, :, cols].astype(jnp.float32)
        upper = halo_ref[:, whole].astype(jnp.float32)
        value = (1.0 - jitter) * lower + jitter * upper
        before = state_ref[unit, 3, :, cols]
        beyond = before + last_gain_ref[0:1, table] * value
        weight = jnp.exp2(before) - jnp.exp2(beyond)
        sums = [state_ref[unit, i, :, cols] for i in range(3)]
        moment(sums, weight, value, levels)
        return coded(sums, beyond)

    each_block(opened, arrive_opened, finish, functools.partial(store, 0), lambda unit: leave(unit).start())
    loop(out_ref.shape[0], lambda piece: leave(piece).wait())


def slab_codes(field, halo, jitter, transfer, ray_start, ray_end, total):
    slab_len, rows, cols = field.shape
    pieces = cols // UNIT
    opened = pieces * 3 // 16 * 2
    closed = pieces - opened
    ntiles = ray_start.shape[0]
    tile_cols = cols // ntiles
    own = pl.BlockSpec(memory_space=pl.ANY)
    scalars = [pltpu.SMEM(transfer.shape, transfer.dtype)] + [pltpu.SMEM((ntiles,), jnp.int32)] * 2

    def cost(units):
        work = slab_len * rows * units * UNIT
        return pl.CostEstimate(flops=work * 20, bytes_accessed=work * 2, transcendentals=work * 2)

    state = pl.pallas_call(
        functools.partial(open_kernel, total, tile_cols, Units(0)),
        in_specs=[own] * 5,
        out_specs=own,
        out_shape=jax.ShapeDtypeStruct((opened, 4, rows, UNIT), jnp.float32),
        scratch_shapes=scalars + [
            pltpu.VMEM((opened, slab_len, rows, UNIT), field.dtype),
            pltpu.VMEM((opened, rows, UNIT), jnp.float32),
            pltpu.VMEM((opened, 4, rows, UNIT), jnp.float32),
            pltpu.VMEM((slab_len, opened * UNIT), jnp.float32),
            pltpu.SemaphoreType.DMA((3,)),
            pltpu.SemaphoreType.DMA((2, opened)),
            pltpu.SemaphoreType.DMA((opened,)),
        ],
        compiler_params=pltpu.CompilerParams(vmem_limit_bytes=OPEN_BYTES),
        cost_estimate=cost(opened),
        name="open",
    )(transfer, ray_start, ray_end, field, jitter)

    return pl.pallas_call(
        functools.partial(close_kernel, total, tile_cols, opened, Units(opened)),
        in_specs=[own] * 7,
        out_specs=own,
        out_shape=jax.ShapeDtypeStruct((pieces, 4, rows, UNIT), jnp.int16),
        scratch_shapes=scalars + [
            pltpu.VMEM((closed, slab_len, rows, UNIT), field.dtype),
            pltpu.VMEM((rows, cols), field.dtype),
            pltpu.VMEM((closed, rows, UNIT), jnp.float32),
            pltpu.VMEM((pieces, 4, rows, UNIT), jnp.int16),
            pltpu.VMEM((slab_len, closed * UNIT), jnp.float32),
            pltpu.SemaphoreType.DMA((4,)),
            pltpu.SemaphoreType.DMA((2, closed)),
            pltpu.SemaphoreType.DMA((pieces,)),
            pltpu.VMEM((opened, 4, rows, UNIT), jnp.float32),
            pltpu.VMEM((opened, rows, UNIT), field.dtype),
            pltpu.VMEM((opened, rows, UNIT), jnp.float32),
            pltpu.VMEM((SUBLANES, opened * UNIT), jnp.float32),
            pltpu.SemaphoreType.DMA((3, opened)),
        ],
        compiler_params=pltpu.CompilerParams(vmem_limit_bytes=CLOSE_BYTES),
        cost_estimate=cost(closed),
        name="close",
    )(transfer, ray_start, ray_end, field, halo, jitter, state)


def composite_kernel(total, slab_len, order_any, transfer_any, code_any, image_any, order_ref, transfer_ref, code_ref, out_ref,
                     sems, out_sems):
    copies = start_all([(order_any, order_ref), (transfer_any, transfer_ref)], sems)
    count, _, rows, width = code_ref.shape
    block = math.gcd(width, 2 * LANES)
    places = [pl.ds(col, block) for col in range(0, width, block)]
    codes = start_all([(code_any.at[:, :, :, cols], code_ref.at[:, :, :, cols]) for cols in places], sems.at[pl.ds(2, len(places))])
    shape = (rows, block)
    depth_span, color_span = spans(slab_len)
    for copy in copies:
        copy.wait()
    unit = jnp.full(shape, transfer_ref[3]) * (0.2 / total * slab_len * TOP)
    depth_unit = unit * LOG2E
    leaving = []
    for n, cols in enumerate(places):
        codes[n].wait()

        def number(slab, channel, span):
            return code_ref[slab, channel, :, cols].astype(jnp.int32).astype(jnp.float32) * (span / 65535.0)

        def step(j, carry):
            shift, *colors = carry
            slab = order_ref[j]
            code = number(slab, 3, depth_span)
            idle = code < depth_span * (-32767.5 / 65535.0)
            away = jnp.where(idle, FAR, shift)
            for i in range(3):
                colors[i] = colors[i] + jnp.exp2(number(slab, i, color_span) - away)
            own = jnp.where(idle, 0.0, jnp.exp2(code + lift(depth_span)))
            return shift + depth_unit * own, *colors

        zero = jnp.zeros(shape, jnp.float32)
        first = jnp.full(shape, -lift(color_span))
        shift, *colors = lax.fori_loop(0, count, step, (first, zero, zero, zero), unroll=math.gcd(count, 4))
        for i in range(3):
            out_ref[i, :, cols] = colors[i] * (unit * (TOP / (transfer_ref[i] + jnp.full(shape, TOP))))
        out_ref[3, :, cols] = 1.0 - jnp.exp2(first - shift)
        leaving.append(pltpu.make_async_copy(out_ref.at[:, :, cols], image_any.at[:, :, cols], out_sems.at[n]))
        leaving[-1].start()
    for copy in leaving:
        copy.wait()


def composite(codes, transfer, depth_order, total, slab_len):
    _, _, rows, width = codes.shape
    blocks = width // math.gcd(width, 2 * LANES)
    own = pl.BlockSpec(memory_space=pl.ANY)
    return pl.pallas_call(
        functools.partial(composite_kernel, total, slab_len),
        in_specs=[own] * 3,
        out_specs=own,
        out_shape=jax.ShapeDtypeStruct((4, rows, width), jnp.float32),
        scratch_shapes=[
            pltpu.SMEM(depth_order.shape, depth_order.dtype),
            pltpu.SMEM(transfer.shape, transfer.dtype),
            pltpu.VMEM(codes.shape, codes.dtype),
            pltpu.VMEM((4, rows, width), jnp.float32),
            pltpu.SemaphoreType.DMA((2 + blocks,)),
            pltpu.SemaphoreType.DMA((blocks,)),
        ],
        compiler_params=pltpu.CompilerParams(vmem_limit_bytes=SMALL_BYTES),
        name="composite",
    )(depth_order, transfer, codes)


def on_device(field, jitter, transfer, depth_order, ray_start, ray_end):
    count = lax.axis_size("depth")
    slab_len, rows, cols = field.shape
    total = slab_len * count
    width = cols // count
    halo = shifted(field[0], "depth", -1)
    codes = slab_codes(field, halo, jitter, transfer, ray_start, ray_end, total)
    if width != UNIT:
        codes = codes.transpose(1, 2, 0, 3).reshape(4, rows, count, width).transpose(2, 0, 1, 3)
    received = lax.all_to_all(codes, "depth", split_axis=0, concat_axis=0, tiled=True)
    return composite(received, transfer, depth_order, total, slab_len)


def solution(mesh):
    in_specs = (P("depth", "groups", None), P("groups", None), P(), P(), P(), P())
    out_specs = P(None, "groups", "depth")
    return jax.shard_map(
        on_device, mesh=mesh, in_specs=in_specs, out_specs=out_specs, check_vma=False
    )
```

```python
import functools
import math

import jax
import jax.numpy as jnp
from jax import lax
from jax.experimental import pallas as pl
from jax.experimental.pallas import tpu as pltpu
from jax.sharding import PartitionSpec as P

TOP = 5.2
LOG2E = math.log2(math.e)
SUBLANES = 8
LANES = 128
FAR = 1.0e4
UNIT = 512
OPEN_BYTES = 54 * 1024 * 1024
CLOSE_BYTES = 53 * 1024 * 1024
SMALL_BYTES = 16 * 1024 * 1024


def spans(slab_len):
    deep = math.log2(slab_len)
    return 6.8 + deep, 13.2 + deep


def lift(span):
    return span * (32768.0 / 65535.0) - span


def shifted(value, axis, steps):
    count = lax.axis_size(axis)
    initial, last = (max(0, -steps), min(count, count - steps))
    return lax.ppermute(value, axis, [(source, source + steps) for source in range(initial, last)])


def encode(value, span):
    code = jnp.log2(value) * (65535.0 / span) + 65535.5
    code = jnp.minimum(jnp.maximum(code, 0.0), 65535.0)
    return (code.astype(jnp.int32) - 32768).astype(jnp.int16)


def tile_gains(gain_ref, gain, base, first_col, tile_cols, start_ref, end_ref):
    sample = lax.broadcasted_iota(jnp.int32, (SUBLANES, LANES), 0) + base
    lane = lax.broadcasted_iota(jnp.int32, (SUBLANES, LANES), 1)

    def block(n, carry):
        tile = (first_col + n * LANES) // tile_cols
        start = jnp.full((SUBLANES, LANES), start_ref[tile])
        end = jnp.full((SUBLANES, LANES), end_ref[tile])
        for t in range(1, LANES // tile_cols):
            start = jnp.where(lane >= t * tile_cols, start_ref[tile + t], start)
            end = jnp.where(lane >= t * tile_cols, end_ref[tile + t], end)
        cols = pl.ds(pl.multiple_of(n * LANES, LANES), LANES)
        for k in range(0, gain_ref.shape[0], SUBLANES):
            active = (sample + k >= start) & (sample + k < end)
            gain_ref[k:k + SUBLANES, cols] = jnp.where(active, gain, 0.0)
        return carry

    blocks = gain_ref.shape[1] // LANES
    lax.fori_loop(0, blocks, block, 0, unroll=math.gcd(blocks, 8))


def moment(sums, weight, value, levels):
    whole = (levels[0] + value) * (levels[1] + value) * (levels[2] + value)
    share = weight * pl.reciprocal(whole, approx=True, full_range=False)
    for n in range(3):
        sums[n] = sums[n] + share
        share = share * value


def colors(sums, before, levels):
    emitted = 1.0 - jnp.exp2(before)
    others = [(levels[1], levels[2]), (levels[2], levels[0]), (levels[0], levels[1])]
    return [emitted - t * (sums[2] + (p + q) * sums[1] + (p * q) * sums[0]) for t, (p, q) in zip(levels, others)]


def march(gain_ref, plane_ref, unit, cols, place, jitter, levels, halo=None):
    slab_len = plane_ref.shape[1]
    shape = jitter.shape
    before = jnp.zeros(shape, jnp.float32)
    through = jnp.ones(shape, jnp.float32)
    sums = [jnp.zeros(shape, jnp.float32) for _ in range(3)]
    lower = plane_ref[unit, 0, :, cols].astype(jnp.float32)
    stay = lower - jitter * lower
    for k in range(slab_len - (halo is None)):
        following = plane_ref[unit, k + 1, :, cols] if k + 1 < slab_len else halo
        upper = following.astype(jnp.float32)
        moved = jitter * upper
        value = stay + moved
        before = before + gain_ref[k:k + 1, place] * value
        beyond = jnp.exp2(before)
        moment(sums, through - beyond, value, levels)
        through = beyond
        stay = upper - moved
    return sums, before


def loop(count, body):
    def step(n, carry):
        body(n)
        return carry

    lax.fori_loop(0, count, step, 0)


def each_pair(units, arrive, compute, store, leave):
    def step(n):
        places = [(2 * n + u, c) for u in range(2) for c in range(0, UNIT, LANES)]
        arrive(n)
        results = [compute(unit, pl.ds(c, LANES), pl.ds(pl.multiple_of(unit * UNIT + c, LANES), LANES)) for unit, c in places]
        for (unit, c), result in zip(places, results):
            store(unit, pl.ds(c, LANES), result)
        leave(n)

    loop(units // 2, step)


def start_all(pairs, sems):
    copies = [pltpu.make_async_copy(src, dst, sems.at[n]) for n, (src, dst) in enumerate(pairs)]
    for copy in copies:
        copy.start()
    return copies


def field_copy(field_any, plane_ref, sems, first, unit):
    cols = pl.ds(pl.multiple_of((first + unit) * UNIT, UNIT), UNIT)
    return pltpu.make_async_copy(field_any.at[:, :, cols], plane_ref.at[unit], sems.at[unit])


def open_kernel(total, tile_cols, transfer_any, start_any, end_any, field_any, jitter_any, state_any, transfer_ref, start_ref,
                end_ref, plane_ref, jitter_ref, state_ref, gain_ref, few_sems, sems, out_sems):
    units, slab_len, rows, _ = plane_ref.shape
    arrival = functools.partial(field_copy, field_any, plane_ref, sems, 0)
    for unit in range(2):
        arrival(unit).start()
    pairs = [(transfer_any, transfer_ref), (start_any, start_ref), (end_any, end_ref)]
    pairs.append((jitter_any.at[:, pl.ds(0, units * UNIT)], jitter_ref))
    *early, jitter_copy = start_all(pairs, few_sems)
    base = lax.axis_index("depth") * slab_len
    for copy in early:
        copy.wait()
    levels = [jnp.full((rows, LANES), transfer_ref[i]) for i in range(3)]
    gain = jnp.full((SUBLANES, LANES), transfer_ref[3]) * (-LOG2E * 0.2 / total)
    for unit in range(2, units):
        arrival(unit).start()
    tile_gains(gain_ref, gain, base, 0, tile_cols, start_ref, end_ref)
    jitter_copy.wait()

    def arrive(n):
        for u in range(2):
            arrival(2 * n + u).wait()

    def compute(unit, cols, place):
        return march(gain_ref, plane_ref, unit, cols, place, jitter_ref[:, place], levels)

    def store(unit, cols, result):
        sums, before = result
        for i, value in enumerate([*sums, before]):
            state_ref[unit, i, :, cols] = value

    def leave(n):
        place = pl.ds(2 * n, 2)
        return pltpu.make_async_copy(state_ref.at[place], state_any.at[place], out_sems.at[n])

    each_pair(units, arrive, compute, store, lambda n: leave(n).start())
    loop(units // 2, lambda n: leave(n).wait())


def close_kernel(total, tile_cols, opened, transfer_any, start_any, end_any, field_any, halo_any, jitter_any, state_any,
                 out_any, transfer_ref, start_ref, end_ref, plane_ref, halo_ref, jitter_ref, out_ref, gain_ref, state_ref,
                 last_ref, last_gain_ref, few_sems, sems, out_sems):
    units, slab_len, rows, _ = plane_ref.shape
    opened_cols = opened * UNIT
    arrival = functools.partial(field_copy, field_any, plane_ref, sems, opened)
    for unit in range(2):
        arrival(unit).start()
    pairs = [(transfer_any, transfer_ref), (start_any, start_ref), (end_any, end_ref), (jitter_any, jitter_ref)]
    pairs += [(halo_any, halo_ref), (state_any, state_ref)]
    pairs.append((field_any.at[slab_len - 1, :, pl.ds(0, opened_cols)], last_ref))
    copies = start_all(pairs, few_sems)
    base = lax.axis_index("depth") * slab_len
    for copy in copies[:3]:
        copy.wait()
    shape = (rows, LANES)
    depth_gain = jnp.full(shape, transfer_ref[3]) * (0.2 / total)
    levels = [jnp.full(shape, transfer_ref[i]) for i in range(3)]
    depth_unit = 1.0 / (depth_gain * (slab_len * TOP))
    color_unit = [depth_unit * ((levels[i] + TOP) * (1.0 / TOP)) for i in range(3)]
    depth_span, color_span = spans(slab_len)
    gain = depth_gain[:SUBLANES] * -LOG2E
    for unit in range(2, units):
        arrival(unit).start()
    tile_gains(gain_ref, gain, base, opened_cols, tile_cols, start_ref, end_ref)
    tile_gains(last_gain_ref, gain, base + slab_len - 1, 0, tile_cols, start_ref, end_ref)
    for copy in copies[3:5]:
        copy.wait()

    def coded(sums, before):
        codes = [encode(color * color_unit[i], color_span) for i, color in enumerate(colors(sums, before, levels))]
        return codes + [encode(before * (depth_unit * (-1.0 / LOG2E)), depth_span)]

    def arrive(n):
        for u in range(2):
            arrival(2 * n + u).wait()

    def compute(unit, cols, place):
        whole = pl.ds(pl.multiple_of(opened_cols + place.start, LANES), LANES)
        return coded(*march(gain_ref, plane_ref, unit, cols, place, jitter_ref[:, whole], levels, halo_ref[:, whole]))

    def store(first, unit, cols, codes):
        for i, code in enumerate(codes):
            out_ref[first + unit, i, :, cols] = code

    def leave(n):
        place = pl.ds(2 * n, 2)
        return pltpu.make_async_copy(out_ref.at[place], out_any.at[place], out_sems.at[n])

    each_pair(units, arrive, compute, functools.partial(store, opened), lambda n: leave(opened // 2 + n).start())
    for copy in copies[5:]:
        copy.wait()

    def finish(unit, cols, place):
        jitter = jitter_ref[:, place]
        lower = last_ref[:, place].astype(jnp.float32)
        upper = halo_ref[:, place].astype(jnp.float32)
        value = (1.0 - jitter) * lower + jitter * upper
        before = state_ref[unit, 3, :, cols]
        beyond = before + last_gain_ref[0:1, place] * value
        weight = jnp.exp2(before) - jnp.exp2(beyond)
        sums = [state_ref[unit, i, :, cols] for i in range(3)]
        moment(sums, weight, value, levels)
        return coded(sums, beyond)

    each_pair(opened, lambda n: None, finish, functools.partial(store, 0), lambda n: leave(n).start())
    loop(out_ref.shape[0] // 2, lambda n: leave(n).wait())


def slab_codes(field, halo, jitter, transfer, ray_start, ray_end, total):
    slab_len, rows, cols = field.shape
    pieces = cols // UNIT
    opened = pieces * 3 // 16 * 2
    closed = pieces - opened
    ntiles = ray_start.shape[0]
    tile_cols = cols // ntiles
    own = pl.BlockSpec(memory_space=pl.ANY)
    scalars = [pltpu.SMEM(transfer.shape, transfer.dtype)] + [pltpu.SMEM((ntiles,), jnp.int32)] * 2

    def cost(units):
        work = slab_len * rows * units * UNIT
        return pl.CostEstimate(flops=work * 20, bytes_accessed=work * 2, transcendentals=work * 2)

    state = pl.pallas_call(
        functools.partial(open_kernel, total, tile_cols),
        in_specs=[own] * 5,
        out_specs=own,
        out_shape=jax.ShapeDtypeStruct((opened, 4, rows, UNIT), jnp.float32),
        scratch_shapes=scalars + [
            pltpu.VMEM((opened, slab_len, rows, UNIT), field.dtype),
            pltpu.VMEM((rows, opened * UNIT), jnp.float32),
            pltpu.VMEM((opened, 4, rows, UNIT), jnp.float32),
            pltpu.VMEM((slab_len, opened * UNIT), jnp.float32),
            pltpu.SemaphoreType.DMA((4,)),
            pltpu.SemaphoreType.DMA((opened,)),
            pltpu.SemaphoreType.DMA((opened // 2,)),
        ],
        compiler_params=pltpu.CompilerParams(vmem_limit_bytes=OPEN_BYTES),
        cost_estimate=cost(opened),
        name="open",
    )(transfer, ray_start, ray_end, field, jitter)

    return pl.pallas_call(
        functools.partial(close_kernel, total, tile_cols, opened),
        in_specs=[own] * 7,
        out_specs=own,
        out_shape=jax.ShapeDtypeStruct((pieces, 4, rows, UNIT), jnp.int16),
        scratch_shapes=scalars + [
            pltpu.VMEM((closed, slab_len, rows, UNIT), field.dtype),
            pltpu.VMEM((rows, cols), field.dtype),
            pltpu.VMEM((rows, cols), jnp.float32),
            pltpu.VMEM((pieces, 4, rows, UNIT), jnp.int16),
            pltpu.VMEM((slab_len, closed * UNIT), jnp.float32),
            pltpu.VMEM((opened, 4, rows, UNIT), jnp.float32),
            pltpu.VMEM((rows, opened * UNIT), field.dtype),
            pltpu.VMEM((SUBLANES, opened * UNIT), jnp.float32),
            pltpu.SemaphoreType.DMA((7,)),
            pltpu.SemaphoreType.DMA((closed,)),
            pltpu.SemaphoreType.DMA((pieces // 2,)),
        ],
        compiler_params=pltpu.CompilerParams(vmem_limit_bytes=CLOSE_BYTES),
        cost_estimate=cost(closed),
        name="close",
    )(transfer, ray_start, ray_end, field, halo, jitter, state)


def composite_kernel(total, slab_len, order_any, transfer_any, code_any, image_any, order_ref, transfer_ref, code_ref, out_ref,
                     sems, out_sems):
    copies = start_all([(order_any, order_ref), (transfer_any, transfer_ref)], sems)
    count, _, rows, width = code_ref.shape
    block = math.gcd(width, 2 * LANES)
    places = [pl.ds(col, block) for col in range(0, width, block)]
    codes = start_all([(code_any.at[:, :, :, cols], code_ref.at[:, :, :, cols]) for cols in places], sems.at[pl.ds(2, len(places))])
    shape = (rows, block)
    depth_span, color_span = spans(slab_len)
    for copy in copies:
        copy.wait()
    unit = jnp.full(shape, transfer_ref[3]) * (0.2 / total * slab_len * TOP)
    depth_unit = unit * LOG2E
    leaving = []
    for n, cols in enumerate(places):
        codes[n].wait()

        def number(slab, channel, span):
            return code_ref[slab, channel, :, cols].astype(jnp.int32).astype(jnp.float32) * (span / 65535.0)

        def step(j, carry):
            shift, *colors = carry
            slab = order_ref[j]
            code = number(slab, 3, depth_span)
            idle = code < depth_span * (-32767.5 / 65535.0)
            away = jnp.where(idle, FAR, shift)
            for i in range(3):
                colors[i] = colors[i] + jnp.exp2(number(slab, i, color_span) - away)
            own = jnp.where(idle, 0.0, jnp.exp2(code + lift(depth_span)))
            return shift + depth_unit * own, *colors

        zero = jnp.zeros(shape, jnp.float32)
        first = jnp.full(shape, -lift(color_span))
        shift, *colors = lax.fori_loop(0, count, step, (first, zero, zero, zero), unroll=math.gcd(count, 4))
        for i in range(3):
            out_ref[i, :, cols] = colors[i] * (unit * (TOP / (transfer_ref[i] + jnp.full(shape, TOP))))
        out_ref[3, :, cols] = 1.0 - jnp.exp2(first - shift)
        leaving.append(pltpu.make_async_copy(out_ref.at[:, :, cols], image_any.at[:, :, cols], out_sems.at[n]))
        leaving[-1].start()
    for copy in leaving:
        copy.wait()


def composite(codes, transfer, depth_order, total, slab_len):
    _, _, rows, width = codes.shape
    blocks = width // math.gcd(width, 2 * LANES)
    own = pl.BlockSpec(memory_space=pl.ANY)
    return pl.pallas_call(
        functools.partial(composite_kernel, total, slab_len),
        in_specs=[own] * 3,
        out_specs=own,
        out_shape=jax.ShapeDtypeStruct((4, rows, width), jnp.float32),
        scratch_shapes=[
            pltpu.SMEM(depth_order.shape, depth_order.dtype),
            pltpu.SMEM(transfer.shape, transfer.dtype),
            pltpu.VMEM(codes.shape, codes.dtype),
            pltpu.VMEM((4, rows, width), jnp.float32),
            pltpu.SemaphoreType.DMA((2 + blocks,)),
            pltpu.SemaphoreType.DMA((blocks,)),
        ],
        compiler_params=pltpu.CompilerParams(vmem_limit_bytes=SMALL_BYTES),
        name="composite",
    )(depth_order, transfer, codes)


def on_device(field, jitter, transfer, depth_order, ray_start, ray_end):
    count = lax.axis_size("depth")
    slab_len, rows, cols = field.shape
    total = slab_len * count
    width = cols // count
    halo = shifted(field[0], "depth", -1)
    codes = slab_codes(field, halo, jitter, transfer, ray_start, ray_end, total)
    if width != UNIT:
        codes = codes.transpose(1, 2, 0, 3).reshape(4, rows, count, width).transpose(2, 0, 1, 3)
    received = lax.all_to_all(codes, "depth", split_axis=0, concat_axis=0, tiled=True)
    return composite(received, transfer, depth_order, total, slab_len)


def solution(mesh):
    in_specs = (P("depth", "groups", None), P("groups", None), P(), P(), P(), P())
    out_specs = P(None, "groups", "depth")
    return jax.shard_map(
        on_device, mesh=mesh, in_specs=in_specs, out_specs=out_specs, check_vma=False
    )
```

```python
import functools
import math

import jax
import jax.numpy as jnp
from jax import lax
from jax.experimental import pallas as pl
from jax.experimental.pallas import tpu as pltpu
from jax.sharding import PartitionSpec as P

TOP = 5.2
LOG2E = math.log2(math.e)
SUBLANES = 8
LANES = 128
FAR = 1.0e4
UNIT = 512
NEAR = 8
OPEN_BYTES = 54 * 1024 * 1024
CLOSE_BYTES = 53 * 1024 * 1024
SMALL_BYTES = 16 * 1024 * 1024


def spans(slab_len):
    deep = math.log2(slab_len)
    return 6.8 + deep, 13.2 + deep


def lift(span):
    return span * (32768.0 / 65535.0) - span


def shifted(value, axis, steps):
    count = lax.axis_size(axis)
    initial, last = (max(0, -steps), min(count, count - steps))
    return lax.ppermute(value, axis, [(source, source + steps) for source in range(initial, last)])


def encode(value, span):
    code = jnp.log2(value) * (65535.0 / span) + 65535.5
    code = jnp.minimum(jnp.maximum(code, 0.0), 65535.0)
    return (code.astype(jnp.int32) - 32768).astype(jnp.int16)


def tile_gains(gain_ref, gain, base, tile_cols, start_ref, end_ref, piece_of):
    sample = lax.broadcasted_iota(jnp.int32, (SUBLANES, LANES), 0) + base
    lane = lax.broadcasted_iota(jnp.int32, (SUBLANES, LANES), 1)

    def block(n, carry):
        blocks = UNIT // LANES
        tile = (piece_of(n // blocks) * UNIT + n % blocks * LANES) // tile_cols
        start = jnp.full((SUBLANES, LANES), start_ref[tile])
        end = jnp.full((SUBLANES, LANES), end_ref[tile])
        for t in range(1, LANES // tile_cols):
            start = jnp.where(lane >= t * tile_cols, start_ref[tile + t], start)
            end = jnp.where(lane >= t * tile_cols, end_ref[tile + t], end)
        cols = pl.ds(pl.multiple_of(n * LANES, LANES), LANES)
        for k in range(0, gain_ref.shape[0], SUBLANES):
            active = (sample + k >= start) & (sample + k < end)
            gain_ref[k:k + SUBLANES, cols] = jnp.where(active, gain, 0.0)
        return carry

    blocks = gain_ref.shape[1] // LANES
    lax.fori_loop(0, blocks, block, 0, unroll=math.gcd(blocks, 8))


def moment(sums, weight, value, levels):
    whole = (levels[0] + value) * (levels[1] + value) * (levels[2] + value)
    share = weight * pl.reciprocal(whole, approx=True, full_range=False)
    for n in range(3):
        sums[n] = sums[n] + share
        share = share * value


def colors(sums, before, levels):
    emitted = 1.0 - jnp.exp2(before)
    others = [(levels[1], levels[2]), (levels[2], levels[0]), (levels[0], levels[1])]
    return [emitted - t * (sums[2] + (p + q) * sums[1] + (p * q) * sums[0]) for t, (p, q) in zip(levels, others)]


def march(gain_ref, plane_ref, unit, cols, place, jitter, levels, halo=None):
    slab_len = plane_ref.shape[1]
    shape = jitter.shape
    before = jnp.zeros(shape, jnp.float32)
    through = jnp.ones(shape, jnp.float32)
    sums = [jnp.zeros(shape, jnp.float32) for _ in range(3)]
    lower = plane_ref[unit, 0, :, cols].astype(jnp.float32)
    stay = lower - jitter * lower
    for k in range(slab_len - (halo is None)):
        following = plane_ref[unit, k + 1, :, cols] if k + 1 < slab_len else halo
        upper = following.astype(jnp.float32)
        moved = jitter * upper
        value = stay + moved
        before = before + gain_ref[k:k + 1, place] * value
        beyond = jnp.exp2(before)
        moment(sums, through - beyond, value, levels)
        through = beyond
        stay = upper - moved
    return sums, before


def loop(count, body):
    def step(n, carry):
        body(n)
        return carry

    lax.fori_loop(0, count, step, 0)


def each_pair(units, arrive, compute, store, leave):
    def step(n):
        places = [(2 * n + u, c) for u in range(2) for c in range(0, UNIT, LANES)]
        arrive(n)
        results = [compute(unit, pl.ds(c, LANES), pl.ds(pl.multiple_of(unit * UNIT + c, LANES), LANES)) for unit, c in places]
        for (unit, c), result in zip(places, results):
            store(unit, pl.ds(c, LANES), result)
        leave(n)

    loop(units // 2, step)


def start_all(pairs, sems):
    copies = [pltpu.make_async_copy(src, dst, sems.at[n]) for n, (src, dst) in enumerate(pairs)]
    for copy in copies:
        copy.start()
    return copies


class Pieces:
    def __init__(self, near):
        self.near = near
        self.here = lax.axis_index("depth")

    def far(self, n):
        if not self.near:
            return n
        return n + jnp.where(n >= self.here // self.near * self.near, self.near, 0)

    def close(self, n):
        return self.here ^ n


def columns(piece, col=0, size=UNIT):
    return pl.ds(pl.multiple_of(piece * UNIT + col, LANES), size)


def field_copy(field_any, plane_ref, sems, piece_of, unit):
    return pltpu.make_async_copy(field_any.at[:, :, columns(piece_of(unit))], plane_ref.at[unit], sems.at[unit])


def arrive_pair(arrival, n):
    for u in range(2):
        arrival(2 * n + u).wait()


def open_kernel(total, tile_cols, near, transfer_any, start_any, end_any, field_any, jitter_any, state_any, transfer_ref,
                start_ref, end_ref, plane_ref, jitter_ref, state_ref, gain_ref, few_sems, sems, out_sems):
    units, slab_len, rows, _ = plane_ref.shape
    piece_of = Pieces(near).far
    arrival = functools.partial(field_copy, field_any, plane_ref, sems, piece_of)
    for unit in range(2):
        arrival(unit).start()
    pairs = [(transfer_any, transfer_ref), (start_any, start_ref), (end_any, end_ref), (jitter_any, jitter_ref)]
    *early, jitter_copy = start_all(pairs, few_sems)
    base = lax.axis_index("depth") * slab_len
    for copy in early:
        copy.wait()
    levels = [jnp.full((rows, LANES), transfer_ref[i]) for i in range(3)]
    gain = jnp.full((SUBLANES, LANES), transfer_ref[3]) * (-LOG2E * 0.2 / total)
    for unit in range(2, units):
        arrival(unit).start()
    tile_gains(gain_ref, gain, base, tile_cols, start_ref, end_ref, piece_of)
    jitter_copy.wait()

    def compute(unit, cols, place):
        jitter = jitter_ref[:, columns(piece_of(unit), cols.start, LANES)]
        return march(gain_ref, plane_ref, unit, cols, place, jitter, levels)

    def store(unit, cols, result):
        sums, before = result
        for i, value in enumerate([*sums, before]):
            state_ref[unit, i, :, cols] = value

    def leave(n):
        place = pl.ds(2 * n, 2)
        return pltpu.make_async_copy(state_ref.at[place], state_any.at[place], out_sems.at[n])

    each_pair(units, functools.partial(arrive_pair, arrival), compute, store, lambda n: leave(n).start())
    loop(units // 2, lambda n: leave(n).wait())


class Coder:
    def __init__(self, total, slab_len, shape, transfer_ref):
        depth_gain = jnp.full(shape, transfer_ref[3]) * (0.2 / total)
        self.levels = [jnp.full(shape, transfer_ref[i]) for i in range(3)]
        self.depth_unit = 1.0 / (depth_gain * (slab_len * TOP))
        self.color_unit = [self.depth_unit * ((self.levels[i] + TOP) * (1.0 / TOP)) for i in range(3)]
        self.depth_span, self.color_span = spans(slab_len)
        self.gain = depth_gain[:SUBLANES] * -LOG2E

    def codes(self, sums, before):
        tints = colors(sums, before, self.levels)
        codes = [encode(color * unit, self.color_span) for color, unit in zip(tints, self.color_unit)]
        return codes + [encode(before * (self.depth_unit * (-1.0 / LOG2E)), self.depth_span)]


def close_kernel(total, tile_cols, near, opened, transfer_any, start_any, end_any, field_any, halo_any, jitter_any, state_any,
                 out_any, transfer_ref, start_ref, end_ref, plane_ref, halo_ref, jitter_ref, out_ref, gain_ref, state_ref,
                 last_ref, last_gain_ref, few_sems, sems, out_sems):
    units, slab_len, rows, _ = plane_ref.shape
    piece_of = Pieces(near).far
    later = lambda unit: piece_of(opened + unit)
    arrival = functools.partial(field_copy, field_any, plane_ref, sems, later)
    for unit in range(2):
        arrival(unit).start()
    pairs = [(transfer_any, transfer_ref), (start_any, start_ref), (end_any, end_ref), (jitter_any, jitter_ref)]
    pairs += [(halo_any, halo_ref), (state_any, state_ref), (field_any.at[slab_len - 1], last_ref)]
    copies = start_all(pairs, few_sems)
    base = lax.axis_index("depth") * slab_len
    for copy in copies[:3]:
        copy.wait()
    coder = Coder(total, slab_len, (rows, LANES), transfer_ref)
    for unit in range(2, units):
        arrival(unit).start()
    tile_gains(gain_ref, coder.gain, base, tile_cols, start_ref, end_ref, later)
    tile_gains(last_gain_ref, coder.gain, base + slab_len - 1, tile_cols, start_ref, end_ref, piece_of)
    for copy in copies[3:5]:
        copy.wait()

    def compute(unit, cols, place):
        whole = columns(later(unit), cols.start, LANES)
        jitter = jitter_ref[:, whole]
        return coder.codes(*march(gain_ref, plane_ref, unit, cols, place, jitter, coder.levels, halo_ref[:, whole]))

    def store(first, unit, cols, codes):
        for i, code in enumerate(codes):
            out_ref[first + unit, i, :, cols] = code

    def leave(unit):
        return pltpu.make_async_copy(out_ref.at[unit], out_any.at[piece_of(unit)], out_sems.at[unit])

    def leave_pair(first, n):
        for u in range(2):
            leave(first + 2 * n + u).start()

    each_pair(units, functools.partial(arrive_pair, arrival), compute, functools.partial(store, opened),
              functools.partial(leave_pair, opened))
    for copy in copies[5:]:
        copy.wait()

    def finish(unit, cols, place):
        whole = columns(piece_of(unit), cols.start, LANES)
        jitter = jitter_ref[:, whole]
        lower = last_ref[:, whole].astype(jnp.float32)
        upper = halo_ref[:, whole].astype(jnp.float32)
        value = (1.0 - jitter) * lower + jitter * upper
        before = state_ref[unit, 3, :, cols]
        beyond = before + last_gain_ref[0:1, place] * value
        weight = jnp.exp2(before) - jnp.exp2(beyond)
        sums = [state_ref[unit, i, :, cols] for i in range(3)]
        moment(sums, weight, value, coder.levels)
        return coder.codes(sums, beyond)

    each_pair(opened, lambda n: None, finish, functools.partial(store, 0), functools.partial(leave_pair, 0))
    loop(out_ref.shape[0], lambda unit: leave(unit).wait())


def near_kernel(total, tile_cols, near, transfer_any, start_any, end_any, field_any, halo_any, jitter_any, far_any, *refs):
    del far_any
    out_anys = refs[:near]
    transfer_ref, start_ref, end_ref, plane_ref, halo_ref, jitter_ref, out_ref, gain_ref, few_sems, sems, out_sems = refs[near:]
    units, slab_len, rows, _ = plane_ref.shape
    piece_of = Pieces(near).close
    arrival = functools.partial(field_copy, field_any, plane_ref, sems, piece_of)
    for unit in range(2):
        arrival(unit).start()
    pairs = [(transfer_any, transfer_ref), (start_any, start_ref), (end_any, end_ref), (jitter_any, jitter_ref)]
    copies = start_all(pairs + [(halo_any, halo_ref)], few_sems)
    base = lax.axis_index("depth") * slab_len
    for copy in copies[:3]:
        copy.wait()
    coder = Coder(total, slab_len, (rows, LANES), transfer_ref)
    for unit in range(2, units):
        arrival(unit).start()
    tile_gains(gain_ref, coder.gain, base, tile_cols, start_ref, end_ref, piece_of)
    for copy in copies[3:]:
        copy.wait()

    def compute(unit, cols, place):
        whole = columns(piece_of(unit), cols.start, LANES)
        jitter = jitter_ref[:, whole]
        return coder.codes(*march(gain_ref, plane_ref, unit, cols, place, jitter, coder.levels, halo_ref[:, whole]))

    def store(unit, cols, codes):
        for i, code in enumerate(codes):
            out_ref[unit, i, :, cols] = code

    each_pair(units, functools.partial(arrive_pair, arrival), compute, store, lambda n: None)
    pairs = [(out_ref.at[unit], out_anys[unit]) for unit in range(units)]
    for copy in start_all(pairs, out_sems):
        copy.wait()


def slab_codes(field, halo, jitter, transfer, ray_start, ray_end, total, near):
    slab_len, rows, cols = field.shape
    pieces = cols // UNIT
    opened = pieces * 3 // 16 * 2
    closed = pieces - near - opened
    ntiles = ray_start.shape[0]
    tile_cols = cols // ntiles
    own = pl.BlockSpec(memory_space=pl.ANY)
    scalars = [pltpu.SMEM(transfer.shape, transfer.dtype)] + [pltpu.SMEM((ntiles,), jnp.int32)] * 2
    plane = pltpu.VMEM((rows, cols), field.dtype)
    lean = pltpu.VMEM((rows, cols), jnp.float32)

    def cost(units):
        work = slab_len * rows * units * UNIT
        return pl.CostEstimate(flops=work * 20, bytes_accessed=work * 2, transcendentals=work * 2)

    def planes(units):
        return pltpu.VMEM((units, slab_len, rows, UNIT), field.dtype)

    def table(samples, units):
        return pltpu.VMEM((samples, units * UNIT), jnp.float32)

    state_shape = (opened, 4, rows, UNIT)
    state = pl.pallas_call(
        functools.partial(open_kernel, total, tile_cols, near),
        in_specs=[own] * 5,
        out_specs=own,
        out_shape=jax.ShapeDtypeStruct(state_shape, jnp.float32),
        scratch_shapes=scalars + [
            planes(opened), lean, pltpu.VMEM(state_shape, jnp.float32), table(slab_len, opened),
            pltpu.SemaphoreType.DMA((4,)),
            pltpu.SemaphoreType.DMA((opened,)),
            pltpu.SemaphoreType.DMA((opened // 2,)),
        ],
        compiler_params=pltpu.CompilerParams(vmem_limit_bytes=OPEN_BYTES),
        cost_estimate=cost(opened),
        name="open",
    )(transfer, ray_start, ray_end, field, jitter)
    far = pl.pallas_call(
        functools.partial(close_kernel, total, tile_cols, near, opened),
        in_specs=[own] * 7,
        out_specs=own,
        out_shape=jax.ShapeDtypeStruct((pieces, 4, rows, UNIT), jnp.int16),
        scratch_shapes=scalars + [
            planes(closed), plane, lean, pltpu.VMEM((opened + closed, 4, rows, UNIT), jnp.int16), table(slab_len, closed),
            pltpu.VMEM(state_shape, jnp.float32), plane, table(SUBLANES, opened),
            pltpu.SemaphoreType.DMA((7,)),
            pltpu.SemaphoreType.DMA((closed,)),
            pltpu.SemaphoreType.DMA((opened + closed,)),
        ],
        compiler_params=pltpu.CompilerParams(vmem_limit_bytes=CLOSE_BYTES),
        cost_estimate=cost(closed),
        name="close",
    )(transfer, ray_start, ray_end, field, halo, jitter, state)
    if not near:
        return far, []
    return far, pl.pallas_call(
        functools.partial(near_kernel, total, tile_cols, near),
        in_specs=[own] * 7,
        out_specs=[own] * near,
        out_shape=[jax.ShapeDtypeStruct((4, rows, UNIT), jnp.int16)] * near,
        scratch_shapes=scalars + [
            planes(near), plane, lean, pltpu.VMEM((near, 4, rows, UNIT), jnp.int16), table(slab_len, near),
            pltpu.SemaphoreType.DMA((5,)),
            pltpu.SemaphoreType.DMA((near,)),
            pltpu.SemaphoreType.DMA((near,)),
        ],
        compiler_params=pltpu.CompilerParams(vmem_limit_bytes=CLOSE_BYTES),
        cost_estimate=cost(near),
        name="near",
    )(transfer, ray_start, ray_end, field, halo, jitter, far)


def composite_kernel(total, slab_len, near, order_any, transfer_any, code_any, *refs):
    near_anys = refs[:near]
    image_any, order_ref, transfer_ref, code_ref, out_ref, sems, out_sems = refs[near:]
    count, _, rows, width = code_ref.shape
    here = lax.axis_index("depth")
    pairs = [(near_any, code_ref.at[here ^ n]) for n, near_any in enumerate(near_anys)]
    if near:
        for n in range(count // near - 1):
            group = n + jnp.where(n >= here // near, 1, 0)
            slabs = pl.ds(group * near, near)
            pairs.append((code_any.at[slabs], code_ref.at[slabs]))
    else:
        pairs.append((code_any, code_ref))
    copies = start_all([(order_any, order_ref), (transfer_any, transfer_ref)] + pairs, sems)
    block = math.gcd(width, 2 * LANES)
    places = [pl.ds(col, block) for col in range(0, width, block)]
    shape = (rows, block)
    depth_span, color_span = spans(slab_len)
    for copy in copies:
        copy.wait()
    unit = jnp.full(shape, transfer_ref[3]) * (0.2 / total * slab_len * TOP)
    depth_unit = unit * LOG2E
    leaving = []
    for n, cols in enumerate(places):

        def number(slab, channel, span):
            return code_ref[slab, channel, :, cols].astype(jnp.int32).astype(jnp.float32) * (span / 65535.0)

        def step(j, carry):
            shift, *colors = carry
            slab = order_ref[j]
            code = number(slab, 3, depth_span)
            idle = code < depth_span * (-32767.5 / 65535.0)
            away = jnp.where(idle, FAR, shift)
            for i in range(3):
                colors[i] = colors[i] + jnp.exp2(number(slab, i, color_span) - away)
            own = jnp.where(idle, 0.0, jnp.exp2(code + lift(depth_span)))
            return shift + depth_unit * own, *colors

        zero = jnp.zeros(shape, jnp.float32)
        first = jnp.full(shape, -lift(color_span))
        shift, *colors = lax.fori_loop(0, count, step, (first, zero, zero, zero), unroll=math.gcd(count, 4))
        for i in range(3):
            out_ref[i, :, cols] = colors[i] * (unit * (TOP / (transfer_ref[i] + jnp.full(shape, TOP))))
        out_ref[3, :, cols] = 1.0 - jnp.exp2(first - shift)
        leaving.append(pltpu.make_async_copy(out_ref.at[:, :, cols], image_any.at[:, :, cols], out_sems.at[n]))
        leaving[-1].start()
    for copy in leaving:
        copy.wait()


def composite(codes, near_codes, transfer, depth_order, total, slab_len):
    count, _, rows, width = codes.shape
    near = len(near_codes)
    blocks = width // math.gcd(width, 2 * LANES)
    own = pl.BlockSpec(memory_space=pl.ANY)
    return pl.pallas_call(
        functools.partial(composite_kernel, total, slab_len, near),
        in_specs=[own] * (3 + near),
        out_specs=own,
        out_shape=jax.ShapeDtypeStruct((4, rows, width), jnp.float32),
        scratch_shapes=[
            pltpu.SMEM(depth_order.shape, depth_order.dtype),
            pltpu.SMEM(transfer.shape, transfer.dtype),
            pltpu.VMEM(codes.shape, codes.dtype),
            pltpu.VMEM((4, rows, width), jnp.float32),
            pltpu.SemaphoreType.DMA((2 + near + (count // near - 1 if near else 1),)),
            pltpu.SemaphoreType.DMA((blocks,)),
        ],
        compiler_params=pltpu.CompilerParams(vmem_limit_bytes=SMALL_BYTES),
        name="composite",
    )(depth_order, transfer, codes, *near_codes)


def on_device(field, jitter, transfer, depth_order, ray_start, ray_end):
    count = lax.axis_size("depth")
    slab_len, rows, cols = field.shape
    total = slab_len * count
    width = cols // count
    near = NEAR if width == UNIT and count % (2 * NEAR) == 0 else 0
    halo = shifted(field[0], "depth", -1)
    codes, near_codes = slab_codes(field, halo, jitter, transfer, ray_start, ray_end, total, near)
    if width != UNIT:
        codes = codes.transpose(1, 2, 0, 3).reshape(4, rows, count, width).transpose(2, 0, 1, 3)
    received = lax.all_to_all(codes, "depth", split_axis=0, concat_axis=0, tiled=True)
    swapped = [lax.ppermute(near_codes[n], "depth", [(i, i ^ n) for i in range(count)]) for n in range(1, near)]
    return composite(received, [*near_codes[:1], *swapped], transfer, depth_order, total, slab_len)


def solution(mesh):
    in_specs = (P("depth", "groups", None), P("groups", None), P(), P(), P(), P())
    out_specs = P(None, "groups", "depth")
    return jax.shard_map(
        on_device, mesh=mesh, in_specs=in_specs, out_specs=out_specs, check_vma=False
    )
```

```python
import functools
import math

import jax
import jax.numpy as jnp
from jax import lax
from jax.experimental import pallas as pl
from jax.experimental.pallas import tpu as pltpu
from jax.sharding import PartitionSpec as P

TOP = 5.2
LOG2E = math.log2(math.e)
SUBLANES = 8
LANES = 128
FAR = 1.0e4
UNIT = 512
NEAR = 8
OPEN_BYTES = 54 * 1024 * 1024
CLOSE_BYTES = 53 * 1024 * 1024
SMALL_BYTES = 16 * 1024 * 1024


def spans(slab_len):
    deep = math.log2(slab_len)
    return 6.8 + deep, 13.2 + deep


def lift(span):
    return span * (32768.0 / 65535.0) - span


def shifted(value, axis, steps):
    count = lax.axis_size(axis)
    initial, last = (max(0, -steps), min(count, count - steps))
    return lax.ppermute(value, axis, [(source, source + steps) for source in range(initial, last)])


def encode(value, span):
    code = jnp.log2(value) * (65535.0 / span) + 65535.5
    code = jnp.minimum(jnp.maximum(code, 0.0), 65535.0)
    return (code.astype(jnp.int32) - 32768).astype(jnp.int16)


def tile_gains(gain_ref, gain, base, tile_cols, start_ref, end_ref, piece_of):
    sample = lax.broadcasted_iota(jnp.int32, (SUBLANES, LANES), 0) + base
    lane = lax.broadcasted_iota(jnp.int32, (SUBLANES, LANES), 1)

    def block(n, carry):
        blocks = UNIT // LANES
        tile = (piece_of(n // blocks) * UNIT + n % blocks * LANES) // tile_cols
        start = jnp.full((SUBLANES, LANES), start_ref[tile])
        end = jnp.full((SUBLANES, LANES), end_ref[tile])
        for t in range(1, LANES // tile_cols):
            start = jnp.where(lane >= t * tile_cols, start_ref[tile + t], start)
            end = jnp.where(lane >= t * tile_cols, end_ref[tile + t], end)
        cols = pl.ds(pl.multiple_of(n * LANES, LANES), LANES)
        for k in range(0, gain_ref.shape[0], SUBLANES):
            active = (sample + k >= start) & (sample + k < end)
            gain_ref[k:k + SUBLANES, cols] = jnp.where(active, gain, 0.0)
        return carry

    blocks = gain_ref.shape[1] // LANES
    lax.fori_loop(0, blocks, block, 0, unroll=math.gcd(blocks, 8))


def moment(sums, weight, value, levels):
    whole = (levels[0] + value) * (levels[1] + value) * (levels[2] + value)
    share = weight * pl.reciprocal(whole, approx=True, full_range=False)
    for n in range(3):
        sums[n] = sums[n] + share
        share = share * value


def colors(sums, before, levels):
    emitted = 1.0 - jnp.exp2(before)
    others = [(levels[1], levels[2]), (levels[2], levels[0]), (levels[0], levels[1])]
    return [emitted - t * (sums[2] + (p + q) * sums[1] + (p * q) * sums[0]) for t, (p, q) in zip(levels, others)]


def march(gain_ref, plane_ref, unit, cols, place, jitter, levels, halo=None):
    slab_len = plane_ref.shape[1]
    shape = jitter.shape
    before = jnp.zeros(shape, jnp.float32)
    through = jnp.ones(shape, jnp.float32)
    sums = [jnp.zeros(shape, jnp.float32) for _ in range(3)]
    lower = plane_ref[unit, 0, :, cols].astype(jnp.float32)
    stay = lower - jitter * lower
    for k in range(slab_len - (halo is None)):
        following = plane_ref[unit, k + 1, :, cols] if k + 1 < slab_len else halo
        upper = following.astype(jnp.float32)
        moved = jitter * upper
        value = stay + moved
        before = before + gain_ref[k:k + 1, place] * value
        beyond = jnp.exp2(before)
        moment(sums, through - beyond, value, levels)
        through = beyond
        stay = upper - moved
    return sums, before


def loop(count, body):
    def step(n, carry):
        body(n)
        return carry

    lax.fori_loop(0, count, step, 0)


def each_pair(units, arrive, compute, store, leave):
    def step(n):
        places = [(2 * n + u, c) for u in range(2) for c in range(0, UNIT, LANES)]
        arrive(n)
        results = [compute(unit, pl.ds(c, LANES), pl.ds(pl.multiple_of(unit * UNIT + c, LANES), LANES)) for unit, c in places]
        for (unit, c), result in zip(places, results):
            store(unit, pl.ds(c, LANES), result)
        leave(n)

    loop(units // 2, step)


def start_all(pairs, sems):
    copies = [pltpu.make_async_copy(src, dst, sems.at[n]) for n, (src, dst) in enumerate(pairs)]
    for copy in copies:
        copy.start()
    return copies


class Pieces:
    def __init__(self, near):
        self.near = near
        self.here = lax.axis_index("depth")

    def far(self, n):
        return self.here ^ (self.near + n) if self.near else n

    def close(self, n):
        return self.here ^ n


def columns(piece, col=0, size=UNIT):
    return pl.ds(pl.multiple_of(piece * UNIT + col, LANES), size)


def field_copy(field_any, plane_ref, sems, piece_of, unit):
    return pltpu.make_async_copy(field_any.at[:, :, columns(piece_of(unit))], plane_ref.at[unit], sems.at[unit])


def arrive_pair(arrival, n):
    for u in range(2):
        arrival(2 * n + u).wait()


def open_kernel(total, tile_cols, near, transfer_any, start_any, end_any, field_any, jitter_any, state_any, transfer_ref,
                start_ref, end_ref, plane_ref, jitter_ref, state_ref, gain_ref, few_sems, sems, out_sems):
    units, slab_len, rows, _ = plane_ref.shape
    piece_of = Pieces(near).far
    arrival = functools.partial(field_copy, field_any, plane_ref, sems, piece_of)
    for unit in range(2):
        arrival(unit).start()
    pairs = [(transfer_any, transfer_ref), (start_any, start_ref), (end_any, end_ref), (jitter_any, jitter_ref)]
    *early, jitter_copy = start_all(pairs, few_sems)
    base = lax.axis_index("depth") * slab_len
    for copy in early:
        copy.wait()
    levels = [jnp.full((rows, LANES), transfer_ref[i]) for i in range(3)]
    gain = jnp.full((SUBLANES, LANES), transfer_ref[3]) * (-LOG2E * 0.2 / total)
    for unit in range(2, units):
        arrival(unit).start()
    tile_gains(gain_ref, gain, base, tile_cols, start_ref, end_ref, piece_of)
    jitter_copy.wait()

    def compute(unit, cols, place):
        jitter = jitter_ref[:, columns(piece_of(unit), cols.start, LANES)]
        return march(gain_ref, plane_ref, unit, cols, place, jitter, levels)

    def store(unit, cols, result):
        sums, before = result
        for i, value in enumerate([*sums, before]):
            state_ref[unit, i, :, cols] = value

    def leave(n):
        place = pl.ds(2 * n, 2)
        return pltpu.make_async_copy(state_ref.at[place], state_any.at[place], out_sems.at[n])

    each_pair(units, functools.partial(arrive_pair, arrival), compute, store, lambda n: leave(n).start())
    loop(units // 2, lambda n: leave(n).wait())


class Coder:
    def __init__(self, total, slab_len, shape, transfer_ref):
        depth_gain = jnp.full(shape, transfer_ref[3]) * (0.2 / total)
        self.levels = [jnp.full(shape, transfer_ref[i]) for i in range(3)]
        self.depth_unit = 1.0 / (depth_gain * (slab_len * TOP))
        self.color_unit = [self.depth_unit * ((self.levels[i] + TOP) * (1.0 / TOP)) for i in range(3)]
        self.depth_span, self.color_span = spans(slab_len)
        self.gain = depth_gain[:SUBLANES] * -LOG2E

    def codes(self, sums, before):
        tints = colors(sums, before, self.levels)
        codes = [encode(color * unit, self.color_span) for color, unit in zip(tints, self.color_unit)]
        return codes + [encode(before * (self.depth_unit * (-1.0 / LOG2E)), self.depth_span)]


def close_kernel(total, tile_cols, near, opened, transfer_any, start_any, end_any, field_any, halo_any, jitter_any, state_any,
                 *refs):
    out_anys, refs = refs[:-14], refs[-14:]
    transfer_ref, start_ref, end_ref, plane_ref, halo_ref, jitter_ref, out_ref, gain_ref, state_ref, last_ref, last_gain_ref = (
        refs[:11])
    few_sems, sems, out_sems = refs[11:]
    units, slab_len, rows, _ = plane_ref.shape
    piece_of = Pieces(near).far
    later = lambda unit: piece_of(opened + unit)
    arrival = functools.partial(field_copy, field_any, plane_ref, sems, later)
    for unit in range(2):
        arrival(unit).start()
    pairs = [(transfer_any, transfer_ref), (start_any, start_ref), (end_any, end_ref), (jitter_any, jitter_ref)]
    pairs += [(halo_any, halo_ref), (state_any, state_ref), (field_any.at[slab_len - 1], last_ref)]
    copies = start_all(pairs, few_sems)
    base = lax.axis_index("depth") * slab_len
    for copy in copies[:3]:
        copy.wait()
    coder = Coder(total, slab_len, (rows, LANES), transfer_ref)
    for unit in range(2, units):
        arrival(unit).start()
    tile_gains(gain_ref, coder.gain, base, tile_cols, start_ref, end_ref, later)
    tile_gains(last_gain_ref, coder.gain, base + slab_len - 1, tile_cols, start_ref, end_ref, piece_of)
    for copy in copies[3:5]:
        copy.wait()

    def compute(unit, cols, place):
        whole = columns(later(unit), cols.start, LANES)
        jitter = jitter_ref[:, whole]
        return coder.codes(*march(gain_ref, plane_ref, unit, cols, place, jitter, coder.levels, halo_ref[:, whole]))

    def store(first, unit, cols, codes):
        for i, code in enumerate(codes):
            out_ref[first + unit, i, :, cols] = code

    def leave(first, count):
        pairs = [(out_ref.at[unit], out_anys[unit]) for unit in range(first, first + count)]
        return start_all(pairs, out_sems.at[pl.ds(first, count)])

    each_pair(units, functools.partial(arrive_pair, arrival), compute, functools.partial(store, opened), lambda n: None)
    leaving = leave(opened, units)
    for copy in copies[5:]:
        copy.wait()

    def finish(unit, cols, place):
        whole = columns(piece_of(unit), cols.start, LANES)
        jitter = jitter_ref[:, whole]
        lower = last_ref[:, whole].astype(jnp.float32)
        upper = halo_ref[:, whole].astype(jnp.float32)
        value = (1.0 - jitter) * lower + jitter * upper
        before = state_ref[unit, 3, :, cols]
        beyond = before + last_gain_ref[0:1, place] * value
        weight = jnp.exp2(before) - jnp.exp2(beyond)
        sums = [state_ref[unit, i, :, cols] for i in range(3)]
        moment(sums, weight, value, coder.levels)
        return coder.codes(sums, beyond)

    each_pair(opened, lambda n: None, finish, functools.partial(store, 0), lambda n: None)
    for copy in leaving + leave(0, opened):
        copy.wait()


def near_kernel(total, tile_cols, near, transfer_any, start_any, end_any, field_any, halo_any, jitter_any, far_any, *refs):
    del far_any
    out_anys = refs[:near]
    transfer_ref, start_ref, end_ref, plane_ref, halo_ref, jitter_ref, out_ref, gain_ref, few_sems, sems, out_sems = refs[near:]
    units, slab_len, rows, _ = plane_ref.shape
    piece_of = Pieces(near).close
    arrival = functools.partial(field_copy, field_any, plane_ref, sems, piece_of)
    for unit in range(2):
        arrival(unit).start()
    pairs = [(transfer_any, transfer_ref), (start_any, start_ref), (end_any, end_ref), (jitter_any, jitter_ref)]
    copies = start_all(pairs + [(halo_any, halo_ref)], few_sems)
    base = lax.axis_index("depth") * slab_len
    for copy in copies[:3]:
        copy.wait()
    coder = Coder(total, slab_len, (rows, LANES), transfer_ref)
    for unit in range(2, units):
        arrival(unit).start()
    tile_gains(gain_ref, coder.gain, base, tile_cols, start_ref, end_ref, piece_of)
    for copy in copies[3:]:
        copy.wait()

    def compute(unit, cols, place):
        whole = columns(piece_of(unit), cols.start, LANES)
        jitter = jitter_ref[:, whole]
        return coder.codes(*march(gain_ref, plane_ref, unit, cols, place, jitter, coder.levels, halo_ref[:, whole]))

    def store(unit, cols, codes):
        for i, code in enumerate(codes):
            out_ref[unit, i, :, cols] = code

    each_pair(units, functools.partial(arrive_pair, arrival), compute, store, lambda n: None)
    pairs = [(out_ref.at[unit], out_anys[unit]) for unit in range(units)]
    for copy in start_all(pairs, out_sems):
        copy.wait()


def slab_codes(field, halo, jitter, transfer, ray_start, ray_end, total, near):
    slab_len, rows, cols = field.shape
    pieces = cols // UNIT
    opened = pieces * 3 // 16 * 2
    closed = pieces - near - opened
    ntiles = ray_start.shape[0]
    tile_cols = cols // ntiles
    own = pl.BlockSpec(memory_space=pl.ANY)
    scalars = [pltpu.SMEM(transfer.shape, transfer.dtype)] + [pltpu.SMEM((ntiles,), jnp.int32)] * 2
    plane = pltpu.VMEM((rows, cols), field.dtype)
    lean = pltpu.VMEM((rows, cols), jnp.float32)

    def cost(units):
        work = slab_len * rows * units * UNIT
        return pl.CostEstimate(flops=work * 20, bytes_accessed=work * 2, transcendentals=work * 2)

    def planes(units):
        return pltpu.VMEM((units, slab_len, rows, UNIT), field.dtype)

    def table(samples, units):
        return pltpu.VMEM((samples, units * UNIT), jnp.float32)

    state_shape = (opened, 4, rows, UNIT)
    state = pl.pallas_call(
        functools.partial(open_kernel, total, tile_cols, near),
        in_specs=[own] * 5,
        out_specs=own,
        out_shape=jax.ShapeDtypeStruct(state_shape, jnp.float32),
        scratch_shapes=scalars + [
            planes(opened), lean, pltpu.VMEM(state_shape, jnp.float32), table(slab_len, opened),
            pltpu.SemaphoreType.DMA((4,)),
            pltpu.SemaphoreType.DMA((opened,)),
            pltpu.SemaphoreType.DMA((opened // 2,)),
        ],
        compiler_params=pltpu.CompilerParams(vmem_limit_bytes=OPEN_BYTES),
        cost_estimate=cost(opened),
        name="open",
    )(transfer, ray_start, ray_end, field, jitter)
    far = pl.pallas_call(
        functools.partial(close_kernel, total, tile_cols, near, opened),
        in_specs=[own] * 7,
        out_specs=[own] * (pieces - near),
        out_shape=[jax.ShapeDtypeStruct((4, rows, UNIT), jnp.int16)] * (pieces - near),
        scratch_shapes=scalars + [
            planes(closed), plane, lean, pltpu.VMEM((opened + closed, 4, rows, UNIT), jnp.int16), table(slab_len, closed),
            pltpu.VMEM(state_shape, jnp.float32), plane, table(SUBLANES, opened),
            pltpu.SemaphoreType.DMA((7,)),
            pltpu.SemaphoreType.DMA((closed,)),
            pltpu.SemaphoreType.DMA((opened + closed,)),
        ],
        compiler_params=pltpu.CompilerParams(vmem_limit_bytes=CLOSE_BYTES),
        cost_estimate=cost(closed),
        name="close",
    )(transfer, ray_start, ray_end, field, halo, jitter, state)
    if not near:
        return far, []
    return far, pl.pallas_call(
        functools.partial(near_kernel, total, tile_cols, near),
        in_specs=[own] * 7,
        out_specs=[own] * near,
        out_shape=[jax.ShapeDtypeStruct((4, rows, UNIT), jnp.int16)] * near,
        scratch_shapes=scalars + [
            planes(near), plane, lean, pltpu.VMEM((near, 4, rows, UNIT), jnp.int16), table(slab_len, near),
            pltpu.SemaphoreType.DMA((5,)),
            pltpu.SemaphoreType.DMA((near,)),
            pltpu.SemaphoreType.DMA((near,)),
        ],
        compiler_params=pltpu.CompilerParams(vmem_limit_bytes=CLOSE_BYTES),
        cost_estimate=cost(near),
        name="near",
    )(transfer, ray_start, ray_end, field, halo, jitter, far[0])


def composite_kernel(total, slab_len, order_any, transfer_any, *refs):
    code_anys, refs = refs[:-7], refs[-7:]
    image_any, order_ref, transfer_ref, code_ref, out_ref, sems, out_sems = refs
    count, _, rows, width = code_ref.shape
    here = lax.axis_index("depth")
    pairs = [(order_any, order_ref), (transfer_any, transfer_ref)]
    if len(code_anys) == 1:
        pairs.append((code_anys[0], code_ref))
    else:
        pairs += [(code_any, code_ref.at[here ^ n]) for n, code_any in enumerate(code_anys)]
    copies = start_all(pairs, sems)
    block = math.gcd(width, 2 * LANES)
    places = [pl.ds(col, block) for col in range(0, width, block)]
    shape = (rows, block)
    depth_span, color_span = spans(slab_len)
    for copy in copies:
        copy.wait()
    unit = jnp.full(shape, transfer_ref[3]) * (0.2 / total * slab_len * TOP)
    depth_unit = unit * LOG2E
    leaving = []
    for n, cols in enumerate(places):

        def number(slab, channel, span):
            return code_ref[slab, channel, :, cols].astype(jnp.int32).astype(jnp.float32) * (span / 65535.0)

        def step(j, carry):
            shift, *colors = carry
            slab = order_ref[j]
            code = number(slab, 3, depth_span)
            idle = code < depth_span * (-32767.5 / 65535.0)
            away = jnp.where(idle, FAR, shift)
            for i in range(3):
                colors[i] = colors[i] + jnp.exp2(number(slab, i, color_span) - away)
            own = jnp.where(idle, 0.0, jnp.exp2(code + lift(depth_span)))
            return shift + depth_unit * own, *colors

        zero = jnp.zeros(shape, jnp.float32)
        first = jnp.full(shape, -lift(color_span))
        shift, *colors = lax.fori_loop(0, count, step, (first, zero, zero, zero), unroll=math.gcd(count, 4))
        for i in range(3):
            out_ref[i, :, cols] = colors[i] * (unit * (TOP / (transfer_ref[i] + jnp.full(shape, TOP))))
        out_ref[3, :, cols] = 1.0 - jnp.exp2(first - shift)
        leaving.append(pltpu.make_async_copy(out_ref.at[:, :, cols], image_any.at[:, :, cols], out_sems.at[n]))
        leaving[-1].start()
    for copy in leaving:
        copy.wait()


def composite(codes, transfer, depth_order, total, slab_len):
    count = depth_order.shape[0]
    _, rows, width = codes[0].shape[-3:]
    blocks = width // math.gcd(width, 2 * LANES)
    own = pl.BlockSpec(memory_space=pl.ANY)
    return pl.pallas_call(
        functools.partial(composite_kernel, total, slab_len),
        in_specs=[own] * (2 + len(codes)),
        out_specs=own,
        out_shape=jax.ShapeDtypeStruct((4, rows, width), jnp.float32),
        scratch_shapes=[
            pltpu.SMEM(depth_order.shape, depth_order.dtype),
            pltpu.SMEM(transfer.shape, transfer.dtype),
            pltpu.VMEM((count, 4, rows, width), jnp.int16),
            pltpu.VMEM((4, rows, width), jnp.float32),
            pltpu.SemaphoreType.DMA((2 + len(codes),)),
            pltpu.SemaphoreType.DMA((blocks,)),
        ],
        compiler_params=pltpu.CompilerParams(vmem_limit_bytes=SMALL_BYTES),
        name="composite",
    )(depth_order, transfer, *codes)


def on_device(field, jitter, transfer, depth_order, ray_start, ray_end):
    count = lax.axis_size("depth")
    slab_len, rows, cols = field.shape
    total = slab_len * count
    width = cols // count
    near = NEAR if width == UNIT and count == 2 * NEAR else 0
    halo = shifted(field[0], "depth", -1)
    far_codes, near_codes = slab_codes(field, halo, jitter, transfer, ray_start, ray_end, total, near)
    if near:
        codes = [*near_codes, *far_codes]
        codes = codes[:1] + [lax.ppermute(codes[n], "depth", [(i, i ^ n) for i in range(count)]) for n in range(1, count)]
    else:
        codes = jnp.stack(far_codes).transpose(1, 2, 0, 3).reshape(4, rows, count, width).transpose(2, 0, 1, 3)
        codes = [lax.all_to_all(codes, "depth", split_axis=0, concat_axis=0, tiled=True)]
    return composite(codes, transfer, depth_order, total, slab_len)


def solution(mesh):
    in_specs = (P("depth", "groups", None), P("groups", None), P(), P(), P(), P())
    out_specs = P(None, "groups", "depth")
    return jax.shard_map(
        on_device, mesh=mesh, in_specs=in_specs, out_specs=out_specs, check_vma=False
    )
```

```python
import functools
import math

import jax
import jax.numpy as jnp
from jax import lax
from jax.experimental import pallas as pl
from jax.experimental.pallas import tpu as pltpu
from jax.sharding import PartitionSpec as P

TOP = 5.2
LOG2E = math.log2(math.e)
SUBLANES = 8
LANES = 128
FAR = 1.0e4
UNIT = 512
NEAR = 8
OPEN_BYTES = 54 * 1024 * 1024
CLOSE_BYTES = 53 * 1024 * 1024
SMALL_BYTES = 16 * 1024 * 1024


def spans(slab_len):
    deep = math.log2(slab_len)
    return 6.8 + deep, 13.2 + deep


def lift(span):
    return span * (32768.0 / 65535.0) - span


def shifted(value, axis, steps):
    count = lax.axis_size(axis)
    initial, last = (max(0, -steps), min(count, count - steps))
    return lax.ppermute(value, axis, [(source, source + steps) for source in range(initial, last)])


def encode(value, span):
    code = jnp.log2(value) * (65535.0 / span) + 65535.5
    code = jnp.minimum(jnp.maximum(code, 0.0), 65535.0)
    return (code.astype(jnp.int32) - 32768).astype(jnp.int16)


def tile_gains(gain_ref, gain, base, tile_cols, start_ref, end_ref, piece_of):
    sample = lax.broadcasted_iota(jnp.int32, (SUBLANES, LANES), 0) + base
    lane = lax.broadcasted_iota(jnp.int32, (SUBLANES, LANES), 1)

    def block(n, carry):
        blocks = UNIT // LANES
        tile = (piece_of(n // blocks) * UNIT + n % blocks * LANES) // tile_cols
        start = jnp.full((SUBLANES, LANES), start_ref[tile])
        end = jnp.full((SUBLANES, LANES), end_ref[tile])
        for t in range(1, LANES // tile_cols):
            start = jnp.where(lane >= t * tile_cols, start_ref[tile + t], start)
            end = jnp.where(lane >= t * tile_cols, end_ref[tile + t], end)
        cols = pl.ds(pl.multiple_of(n * LANES, LANES), LANES)
        for k in range(0, gain_ref.shape[0], SUBLANES):
            active = (sample + k >= start) & (sample + k < end)
            gain_ref[k:k + SUBLANES, cols] = jnp.where(active, gain, 0.0)
        return carry

    blocks = gain_ref.shape[1] // LANES
    lax.fori_loop(0, blocks, block, 0, unroll=math.gcd(blocks, 8))


def moment(sums, weight, value, levels):
    whole = (levels[0] + value) * (levels[1] + value) * (levels[2] + value)
    share = weight * pl.reciprocal(whole, approx=True, full_range=False)
    for n in range(3):
        sums[n] = sums[n] + share
        share = share * value


def colors(sums, before, levels):
    emitted = 1.0 - jnp.exp2(before)
    others = [(levels[1], levels[2]), (levels[2], levels[0]), (levels[0], levels[1])]
    return [emitted - t * (sums[2] + (p + q) * sums[1] + (p * q) * sums[0]) for t, (p, q) in zip(levels, others)]


def march(gain_ref, plane_ref, unit, cols, place, jitter, levels, halo=None):
    slab_len = plane_ref.shape[1]
    shape = jitter.shape
    before = jnp.zeros(shape, jnp.float32)
    through = jnp.ones(shape, jnp.float32)
    sums = [jnp.zeros(shape, jnp.float32) for _ in range(3)]
    lower = plane_ref[unit, 0, :, cols].astype(jnp.float32)
    stay = lower - jitter * lower
    for k in range(slab_len - (halo is None)):
        following = plane_ref[unit, k + 1, :, cols] if k + 1 < slab_len else halo
        upper = following.astype(jnp.float32)
        moved = jitter * upper
        value = stay + moved
        before = before + gain_ref[k:k + 1, place] * value
        beyond = jnp.exp2(before)
        moment(sums, through - beyond, value, levels)
        through = beyond
        stay = upper - moved
    return sums, before


def loop(count, body):
    def step(n, carry):
        body(n)
        return carry

    lax.fori_loop(0, count, step, 0)


def each_pair(units, arrive, compute, store, leave):
    def step(n):
        places = [(2 * n + u, c) for u in range(2) for c in range(0, UNIT, LANES)]
        arrive(n)
        results = [compute(unit, pl.ds(c, LANES), pl.ds(pl.multiple_of(unit * UNIT + c, LANES), LANES)) for unit, c in places]
        for (unit, c), result in zip(places, results):
            store(unit, pl.ds(c, LANES), result)
        leave(n)

    loop(units // 2, step)


def start_all(pairs, sems):
    copies = [pltpu.make_async_copy(src, dst, sems.at[n]) for n, (src, dst) in enumerate(pairs)]
    for copy in copies:
        copy.start()
    return copies


class Pieces:
    def __init__(self, near):
        self.near = near
        self.here = lax.axis_index("depth")

    def far(self, n):
        if not self.near:
            return n
        return n + jnp.where(n >= self.here // self.near * self.near, self.near, 0)

    def close(self, n):
        return self.here ^ n


def columns(piece, col=0, size=UNIT):
    return pl.ds(pl.multiple_of(piece * UNIT + col, LANES), size)


def field_copy(field_any, plane_ref, sems, piece_of, unit):
    return pltpu.make_async_copy(field_any.at[:, :, columns(piece_of(unit))], plane_ref.at[unit], sems.at[unit])


def arrive_pair(arrival, n):
    for u in range(2):
        arrival(2 * n + u).wait()


def open_kernel(total, tile_cols, near, transfer_any, start_any, end_any, field_any, jitter_any, state_any, transfer_ref,
                start_ref, end_ref, plane_ref, jitter_ref, state_ref, gain_ref, few_sems, sems, out_sems):
    units, slab_len, rows, _ = plane_ref.shape
    piece_of = Pieces(near).far
    arrival = functools.partial(field_copy, field_any, plane_ref, sems, piece_of)
    for unit in range(2):
        arrival(unit).start()
    pairs = [(transfer_any, transfer_ref), (start_any, start_ref), (end_any, end_ref), (jitter_any, jitter_ref)]
    *early, jitter_copy = start_all(pairs, few_sems)
    base = lax.axis_index("depth") * slab_len
    for copy in early:
        copy.wait()
    levels = [jnp.full((rows, LANES), transfer_ref[i]) for i in range(3)]
    gain = jnp.full((SUBLANES, LANES), transfer_ref[3]) * (-LOG2E * 0.2 / total)
    for unit in range(2, units):
        arrival(unit).start()
    tile_gains(gain_ref, gain, base, tile_cols, start_ref, end_ref, piece_of)
    jitter_copy.wait()

    def compute(unit, cols, place):
        jitter = jitter_ref[:, columns(piece_of(unit), cols.start, LANES)]
        return march(gain_ref, plane_ref, unit, cols, place, jitter, levels)

    def store(unit, cols, result):
        sums, before = result
        for i, value in enumerate([*sums, before]):
            state_ref[unit, i, :, cols] = value

    def leave(n):
        place = pl.ds(2 * n, 2)
        return pltpu.make_async_copy(state_ref.at[place], state_any.at[place], out_sems.at[n])

    each_pair(units, functools.partial(arrive_pair, arrival), compute, store, lambda n: leave(n).start())
    loop(units // 2, lambda n: leave(n).wait())


class Coder:
    def __init__(self, total, slab_len, shape, transfer_ref):
        depth_gain = jnp.full(shape, transfer_ref[3]) * (0.2 / total)
        self.levels = [jnp.full(shape, transfer_ref[i]) for i in range(3)]
        self.depth_unit = 1.0 / (depth_gain * (slab_len * TOP))
        self.color_unit = [self.depth_unit * ((self.levels[i] + TOP) * (1.0 / TOP)) for i in range(3)]
        self.depth_span, self.color_span = spans(slab_len)
        self.gain = depth_gain[:SUBLANES] * -LOG2E

    def codes(self, sums, before):
        tints = colors(sums, before, self.levels)
        codes = [encode(color * unit, self.color_span) for color, unit in zip(tints, self.color_unit)]
        return codes + [encode(before * (self.depth_unit * (-1.0 / LOG2E)), self.depth_span)]


def close_kernel(total, tile_cols, near, opened, transfer_any, start_any, end_any, field_any, halo_any, jitter_any, state_any,
                 out_any, transfer_ref, start_ref, end_ref, plane_ref, halo_ref, jitter_ref, out_ref, gain_ref, state_ref,
                 last_ref, last_gain_ref, few_sems, sems, out_sems):
    units, slab_len, rows, _ = plane_ref.shape
    piece_of = Pieces(near).far
    later = lambda unit: piece_of(opened + unit)
    arrival = functools.partial(field_copy, field_any, plane_ref, sems, later)
    for unit in range(2):
        arrival(unit).start()
    pairs = [(transfer_any, transfer_ref), (start_any, start_ref), (end_any, end_ref), (jitter_any, jitter_ref)]
    pairs += [(halo_any, halo_ref), (state_any, state_ref), (field_any.at[slab_len - 1], last_ref)]
    copies = start_all(pairs, few_sems)
    base = lax.axis_index("depth") * slab_len
    for copy in copies[:3]:
        copy.wait()
    coder = Coder(total, slab_len, (rows, LANES), transfer_ref)
    for unit in range(2, units):
        arrival(unit).start()
    tile_gains(gain_ref, coder.gain, base, tile_cols, start_ref, end_ref, later)
    tile_gains(last_gain_ref, coder.gain, base + slab_len - 1, tile_cols, start_ref, end_ref, piece_of)
    for copy in copies[3:5]:
        copy.wait()

    def compute(unit, cols, place):
        whole = columns(later(unit), cols.start, LANES)
        jitter = jitter_ref[:, whole]
        return coder.codes(*march(gain_ref, plane_ref, unit, cols, place, jitter, coder.levels, halo_ref[:, whole]))

    def store(first, unit, cols, codes):
        for i, code in enumerate(codes):
            out_ref[first + unit, i, :, cols] = code

    def leave(unit):
        return pltpu.make_async_copy(out_ref.at[unit], out_any.at[piece_of(unit)], out_sems.at[unit])

    def leave_pair(first, n):
        for u in range(2):
            leave(first + 2 * n + u).start()

    each_pair(units, functools.partial(arrive_pair, arrival), compute, functools.partial(store, opened),
              functools.partial(leave_pair, opened))
    for copy in copies[5:]:
        copy.wait()

    def finish(unit, cols, place):
        whole = columns(piece_of(unit), cols.start, LANES)
        jitter = jitter_ref[:, whole]
        lower = last_ref[:, whole].astype(jnp.float32)
        upper = halo_ref[:, whole].astype(jnp.float32)
        value = (1.0 - jitter) * lower + jitter * upper
        before = state_ref[unit, 3, :, cols]
        beyond = before + last_gain_ref[0:1, place] * value
        weight = jnp.exp2(before) - jnp.exp2(beyond)
        sums = [state_ref[unit, i, :, cols] for i in range(3)]
        moment(sums, weight, value, coder.levels)
        return coder.codes(sums, beyond)

    each_pair(opened, lambda n: None, finish, functools.partial(store, 0), functools.partial(leave_pair, 0))
    loop(out_ref.shape[0], lambda unit: leave(unit).wait())


def near_kernel(total, tile_cols, near, transfer_any, start_any, end_any, field_any, halo_any, jitter_any, far_any, *refs):
    del far_any
    out_anys = refs[:near]
    transfer_ref, start_ref, end_ref, plane_ref, halo_ref, jitter_ref, out_ref, gain_ref, few_sems, sems, out_sems = refs[near:]
    units, slab_len, rows, _ = plane_ref.shape
    piece_of = Pieces(near).close
    arrival = functools.partial(field_copy, field_any, plane_ref, sems, piece_of)
    for unit in range(2):
        arrival(unit).start()
    pairs = [(transfer_any, transfer_ref), (start_any, start_ref), (end_any, end_ref), (jitter_any, jitter_ref)]
    copies = start_all(pairs + [(halo_any, halo_ref)], few_sems)
    base = lax.axis_index("depth") * slab_len
    for copy in copies[:3]:
        copy.wait()
    coder = Coder(total, slab_len, (rows, LANES), transfer_ref)
    for unit in range(2, units):
        arrival(unit).start()
    tile_gains(gain_ref, coder.gain, base, tile_cols, start_ref, end_ref, piece_of)
    for copy in copies[3:]:
        copy.wait()

    def compute(unit, cols, place):
        whole = columns(piece_of(unit), cols.start, LANES)
        jitter = jitter_ref[:, whole]
        return coder.codes(*march(gain_ref, plane_ref, unit, cols, place, jitter, coder.levels, halo_ref[:, whole]))

    def store(unit, cols, codes):
        for i, code in enumerate(codes):
            out_ref[unit, i, :, cols] = code

    each_pair(units, functools.partial(arrive_pair, arrival), compute, store, lambda n: None)
    pairs = [(out_ref.at[unit], out_anys[unit]) for unit in range(units)]
    for copy in start_all(pairs, out_sems):
        copy.wait()


def slab_codes(field, halo, jitter, transfer, ray_start, ray_end, total, near):
    slab_len, rows, cols = field.shape
    pieces = cols // UNIT
    opened = pieces * 3 // 16 * 2
    closed = pieces - near - opened
    ntiles = ray_start.shape[0]
    tile_cols = cols // ntiles
    own = pl.BlockSpec(memory_space=pl.ANY)
    scalars = [pltpu.SMEM(transfer.shape, transfer.dtype)] + [pltpu.SMEM((ntiles,), jnp.int32)] * 2
    plane = pltpu.VMEM((rows, cols), field.dtype)
    lean = pltpu.VMEM((rows, cols), jnp.float32)

    def cost(units):
        work = slab_len * rows * units * UNIT
        return pl.CostEstimate(flops=work * 20, bytes_accessed=work * 2, transcendentals=work * 2)

    def planes(units):
        return pltpu.VMEM((units, slab_len, rows, UNIT), field.dtype)

    def table(samples, units):
        return pltpu.VMEM((samples, units * UNIT), jnp.float32)

    state_shape = (opened, 4, rows, UNIT)
    state = pl.pallas_call(
        functools.partial(open_kernel, total, tile_cols, near),
        in_specs=[own] * 5,
        out_specs=own,
        out_shape=jax.ShapeDtypeStruct(state_shape, jnp.float32),
        scratch_shapes=scalars + [
            planes(opened), lean, pltpu.VMEM(state_shape, jnp.float32), table(slab_len, opened),
            pltpu.SemaphoreType.DMA((4,)),
            pltpu.SemaphoreType.DMA((opened,)),
            pltpu.SemaphoreType.DMA((opened // 2,)),
        ],
        compiler_params=pltpu.CompilerParams(vmem_limit_bytes=OPEN_BYTES),
        cost_estimate=cost(opened),
        name="open",
    )(transfer, ray_start, ray_end, field, jitter)
    far = pl.pallas_call(
        functools.partial(close_kernel, total, tile_cols, near, opened),
        in_specs=[own] * 7,
        out_specs=own,
        out_shape=jax.ShapeDtypeStruct((pieces, 4, rows, UNIT), jnp.int16),
        scratch_shapes=scalars + [
            planes(closed), plane, lean, pltpu.VMEM((opened + closed, 4, rows, UNIT), jnp.int16), table(slab_len, closed),
            pltpu.VMEM(state_shape, jnp.float32), plane, table(SUBLANES, opened),
            pltpu.SemaphoreType.DMA((7,)),
            pltpu.SemaphoreType.DMA((closed,)),
            pltpu.SemaphoreType.DMA((opened + closed,)),
        ],
        compiler_params=pltpu.CompilerParams(vmem_limit_bytes=CLOSE_BYTES),
        cost_estimate=cost(closed),
        name="close",
    )(transfer, ray_start, ray_end, field, halo, jitter, state)
    if not near:
        return far, []
    return far, pl.pallas_call(
        functools.partial(near_kernel, total, tile_cols, near),
        in_specs=[own] * 7,
        out_specs=[own] * near,
        out_shape=[jax.ShapeDtypeStruct((4, rows, UNIT), jnp.int16)] * near,
        scratch_shapes=scalars + [
            planes(near), plane, lean, pltpu.VMEM((near, 4, rows, UNIT), jnp.int16), table(slab_len, near),
            pltpu.SemaphoreType.DMA((5,)),
            pltpu.SemaphoreType.DMA((near,)),
            pltpu.SemaphoreType.DMA((near,)),
        ],
        compiler_params=pltpu.CompilerParams(vmem_limit_bytes=CLOSE_BYTES),
        cost_estimate=cost(near),
        name="near",
    )(transfer, ray_start, ray_end, field, halo, jitter, far)


def composite_kernel(total, slab_len, near, order_any, transfer_any, code_any, *refs):
    near_anys = refs[:near]
    image_any, order_ref, transfer_ref, code_ref, out_ref, sems, out_sems = refs[near:]
    count, _, rows, width = code_ref.shape
    here = lax.axis_index("depth")
    pairs = [(near_any, code_ref.at[here ^ n]) for n, near_any in zip(reversed(range(near)), near_anys)]
    if near:
        for n in range(count // near - 1):
            group = n + jnp.where(n >= here // near, 1, 0)
            slabs = pl.ds(group * near, near)
            pairs.append((code_any.at[slabs], code_ref.at[slabs]))
    else:
        pairs.append((code_any, code_ref))
    copies = start_all([(order_any, order_ref), (transfer_any, transfer_ref)] + pairs, sems)
    block = math.gcd(width, 2 * LANES)
    places = [pl.ds(col, block) for col in range(0, width, block)]
    shape = (rows, block)
    depth_span, color_span = spans(slab_len)
    for copy in copies:
        copy.wait()
    unit = jnp.full(shape, transfer_ref[3]) * (0.2 / total * slab_len * TOP)
    depth_unit = unit * LOG2E
    leaving = []
    for n, cols in enumerate(places):

        def number(slab, channel, span):
            return code_ref[slab, channel, :, cols].astype(jnp.int32).astype(jnp.float32) * (span / 65535.0)

        def step(j, carry):
            shift, *colors = carry
            slab = order_ref[j]
            code = number(slab, 3, depth_span)
            idle = code < depth_span * (-32767.5 / 65535.0)
            away = jnp.where(idle, FAR, shift)
            for i in range(3):
                colors[i] = colors[i] + jnp.exp2(number(slab, i, color_span) - away)
            own = jnp.where(idle, 0.0, jnp.exp2(code + lift(depth_span)))
            return shift + depth_unit * own, *colors

        zero = jnp.zeros(shape, jnp.float32)
        first = jnp.full(shape, -lift(color_span))
        shift, *colors = lax.fori_loop(0, count, step, (first, zero, zero, zero), unroll=math.gcd(count, 4))
        for i in range(3):
            out_ref[i, :, cols] = colors[i] * (unit * (TOP / (transfer_ref[i] + jnp.full(shape, TOP))))
        out_ref[3, :, cols] = 1.0 - jnp.exp2(first - shift)
        leaving.append(pltpu.make_async_copy(out_ref.at[:, :, cols], image_any.at[:, :, cols], out_sems.at[n]))
        leaving[-1].start()
    for copy in leaving:
        copy.wait()


def composite(codes, near_codes, transfer, depth_order, total, slab_len):
    count, _, rows, width = codes.shape
    near = len(near_codes)
    blocks = width // math.gcd(width, 2 * LANES)
    own = pl.BlockSpec(memory_space=pl.ANY)
    return pl.pallas_call(
        functools.partial(composite_kernel, total, slab_len, near),
        in_specs=[own] * (3 + near),
        out_specs=own,
        out_shape=jax.ShapeDtypeStruct((4, rows, width), jnp.float32),
        scratch_shapes=[
            pltpu.SMEM(depth_order.shape, depth_order.dtype),
            pltpu.SMEM(transfer.shape, transfer.dtype),
            pltpu.VMEM(codes.shape, codes.dtype),
            pltpu.VMEM((4, rows, width), jnp.float32),
            pltpu.SemaphoreType.DMA((2 + near + (count // near - 1 if near else 1),)),
            pltpu.SemaphoreType.DMA((blocks,)),
        ],
        compiler_params=pltpu.CompilerParams(vmem_limit_bytes=SMALL_BYTES),
        name="composite",
    )(depth_order, transfer, codes, *near_codes)


def on_device(field, jitter, transfer, depth_order, ray_start, ray_end):
    count = lax.axis_size("depth")
    slab_len, rows, cols = field.shape
    total = slab_len * count
    width = cols // count
    near = NEAR if width == UNIT and count % (2 * NEAR) == 0 else 0
    halo = shifted(field[0], "depth", -1)
    codes, near_codes = slab_codes(field, halo, jitter, transfer, ray_start, ray_end, total, near)
    if width != UNIT:
        codes = codes.transpose(1, 2, 0, 3).reshape(4, rows, count, width).transpose(2, 0, 1, 3)
    received = lax.all_to_all(codes, "depth", split_axis=0, concat_axis=0, tiled=True)
    swapped = [lax.ppermute(near_codes[n], "depth", [(i, i ^ n) for i in range(count)]) for n in reversed(range(1, near))]
    return composite(received, [*swapped, *near_codes[:1]], transfer, depth_order, total, slab_len)


def solution(mesh):
    in_specs = (P("depth", "groups", None), P("groups", None), P(), P(), P(), P())
    out_specs = P(None, "groups", "depth")
    return jax.shard_map(
        on_device, mesh=mesh, in_specs=in_specs, out_specs=out_specs, check_vma=False
    )
```

```python
import functools
import math

import jax
import jax.numpy as jnp
from jax import lax
from jax.experimental import pallas as pl
from jax.experimental.pallas import tpu as pltpu
from jax.sharding import PartitionSpec as P

TOP = 5.2
LOG2E = math.log2(math.e)
SUBLANES = 8
LANES = 128
FAR = 1.0e4
UNIT = 512
NEAR = 8
OPEN_BYTES = 54 * 1024 * 1024
CLOSE_BYTES = 53 * 1024 * 1024
SMALL_BYTES = 16 * 1024 * 1024


def spans(slab_len):
    deep = math.log2(slab_len)
    return 6.8 + deep, 13.2 + deep


def lift(span):
    return span * (32768.0 / 65535.0) - span


def shifted(value, axis, steps):
    count = lax.axis_size(axis)
    initial, last = (max(0, -steps), min(count, count - steps))
    return lax.ppermute(value, axis, [(source, source + steps) for source in range(initial, last)])


def encode(value, span):
    code = jnp.log2(value) * (65535.0 / span) + 65535.5
    code = jnp.minimum(jnp.maximum(code, 0.0), 65535.0)
    return (code.astype(jnp.int32) - 32768).astype(jnp.int16)


def tile_gains(gain_ref, gain, base, tile_cols, start_ref, end_ref, piece_of):
    sample = lax.broadcasted_iota(jnp.int32, (SUBLANES, LANES), 0) + base
    lane = lax.broadcasted_iota(jnp.int32, (SUBLANES, LANES), 1)

    def block(n, carry):
        blocks = UNIT // LANES
        tile = (piece_of(n // blocks) * UNIT + n % blocks * LANES) // tile_cols
        start = jnp.full((SUBLANES, LANES), start_ref[tile])
        end = jnp.full((SUBLANES, LANES), end_ref[tile])
        for t in range(1, LANES // tile_cols):
            start = jnp.where(lane >= t * tile_cols, start_ref[tile + t], start)
            end = jnp.where(lane >= t * tile_cols, end_ref[tile + t], end)
        cols = pl.ds(pl.multiple_of(n * LANES, LANES), LANES)
        for k in range(0, gain_ref.shape[0], SUBLANES):
            active = (sample + k >= start) & (sample + k < end)
            gain_ref[k:k + SUBLANES, cols] = jnp.where(active, gain, 0.0)
        return carry

    blocks = gain_ref.shape[1] // LANES
    lax.fori_loop(0, blocks, block, 0, unroll=math.gcd(blocks, 8))


def moment(sums, weight, value, levels):
    whole = (levels[0] + value) * (levels[1] + value) * (levels[2] + value)
    share = weight * pl.reciprocal(whole, approx=True, full_range=False)
    for n in range(3):
        sums[n] = sums[n] + share
        share = share * value


def colors(sums, before, levels):
    emitted = 1.0 - jnp.exp2(before)
    others = [(levels[1], levels[2]), (levels[2], levels[0]), (levels[0], levels[1])]
    return [emitted - t * (sums[2] + (p + q) * sums[1] + (p * q) * sums[0]) for t, (p, q) in zip(levels, others)]


def march(gain_ref, plane_ref, unit, cols, place, jitter, levels, halo=None):
    slab_len = plane_ref.shape[1]
    shape = jitter.shape
    before = jnp.zeros(shape, jnp.float32)
    through = jnp.ones(shape, jnp.float32)
    sums = [jnp.zeros(shape, jnp.float32) for _ in range(3)]
    lower = plane_ref[unit, 0, :, cols].astype(jnp.float32)
    stay = lower - jitter * lower
    for k in range(slab_len - (halo is None)):
        following = plane_ref[unit, k + 1, :, cols] if k + 1 < slab_len else halo
        upper = following.astype(jnp.float32)
        moved = jitter * upper
        value = stay + moved
        before = before + gain_ref[k:k + 1, place] * value
        beyond = jnp.exp2(before)
        moment(sums, through - beyond, value, levels)
        through = beyond
        stay = upper - moved
    return sums, before


def loop(count, body):
    def step(n, carry):
        body(n)
        return carry

    lax.fori_loop(0, count, step, 0)


def each_pair(units, arrive, compute, store, leave):
    def step(n):
        places = [(2 * n + u, c) for u in range(2) for c in range(0, UNIT, LANES)]
        arrive(n)
        results = [compute(unit, pl.ds(c, LANES), pl.ds(pl.multiple_of(unit * UNIT + c, LANES), LANES)) for unit, c in places]
        for (unit, c), result in zip(places, results):
            store(unit, pl.ds(c, LANES), result)
        leave(n)

    loop(units // 2, step)


def start_all(pairs, sems):
    copies = [pltpu.make_async_copy(src, dst, sems.at[n]) for n, (src, dst) in enumerate(pairs)]
    for copy in copies:
        copy.start()
    return copies


class Pieces:
    def __init__(self, near):
        self.near = near
        self.here = lax.axis_index("depth")

    def far(self, n):
        if not self.near:
            return n
        return n + jnp.where(n >= self.here // self.near * self.near, self.near, 0)

    def close(self, n):
        return self.here ^ n

    def close_first(self):
        return self.here // self.near * self.near


def columns(piece, col=0, size=UNIT):
    return pl.ds(pl.multiple_of(piece * UNIT + col, LANES), size)


def field_copy(field_any, plane_ref, sems, piece_of, unit):
    return pltpu.make_async_copy(field_any.at[:, :, columns(piece_of(unit))], plane_ref.at[unit], sems.at[unit])


def arrive_pair(arrival, n):
    for u in range(2):
        arrival(2 * n + u).wait()


def open_kernel(total, tile_cols, near, transfer_any, start_any, end_any, field_any, jitter_any, state_any, transfer_ref,
                start_ref, end_ref, plane_ref, jitter_ref, state_ref, gain_ref, few_sems, sems, out_sems):
    units, slab_len, rows, _ = plane_ref.shape
    piece_of = Pieces(near).far
    arrival = functools.partial(field_copy, field_any, plane_ref, sems, piece_of)
    for unit in range(2):
        arrival(unit).start()
    pairs = [(transfer_any, transfer_ref), (start_any, start_ref), (end_any, end_ref)]
    pairs.append((jitter_any.at[:, columns(piece_of(0), 0, units * UNIT)], jitter_ref))
    *early, jitter_copy = start_all(pairs, few_sems)
    base = lax.axis_index("depth") * slab_len
    for copy in early:
        copy.wait()
    levels = [jnp.full((rows, LANES), transfer_ref[i]) for i in range(3)]
    gain = jnp.full((SUBLANES, LANES), transfer_ref[3]) * (-LOG2E * 0.2 / total)
    for unit in range(2, units):
        arrival(unit).start()
    tile_gains(gain_ref, gain, base, tile_cols, start_ref, end_ref, piece_of)
    jitter_copy.wait()

    def compute(unit, cols, place):
        return march(gain_ref, plane_ref, unit, cols, place, jitter_ref[:, place], levels)

    def store(unit, cols, result):
        sums, before = result
        for i, value in enumerate([*sums, before]):
            state_ref[unit, i, :, cols] = value

    def leave(n):
        place = pl.ds(2 * n, 2)
        return pltpu.make_async_copy(state_ref.at[place], state_any.at[place], out_sems.at[n])

    each_pair(units, functools.partial(arrive_pair, arrival), compute, store, lambda n: leave(n).start())
    loop(units // 2, lambda n: leave(n).wait())


class Coder:
    def __init__(self, total, slab_len, shape, transfer_ref):
        depth_gain = jnp.full(shape, transfer_ref[3]) * (0.2 / total)
        self.levels = [jnp.full(shape, transfer_ref[i]) for i in range(3)]
        self.depth_unit = 1.0 / (depth_gain * (slab_len * TOP))
        self.color_unit = [self.depth_unit * ((self.levels[i] + TOP) * (1.0 / TOP)) for i in range(3)]
        self.depth_span, self.color_span = spans(slab_len)
        self.gain = depth_gain[:SUBLANES] * -LOG2E

    def codes(self, sums, before):
        tints = colors(sums, before, self.levels)
        codes = [encode(color * unit, self.color_span) for color, unit in zip(tints, self.color_unit)]
        return codes + [encode(before * (self.depth_unit * (-1.0 / LOG2E)), self.depth_span)]


def close_kernel(total, tile_cols, near, opened, transfer_any, start_any, end_any, field_any, halo_any, jitter_any, state_any,
                 out_any, transfer_ref, start_ref, end_ref, plane_ref, halo_ref, jitter_ref, out_ref, gain_ref, state_ref,
                 last_ref, last_gain_ref, few_sems, sems, out_sems):
    units, slab_len, rows, _ = plane_ref.shape
    piece_of = Pieces(near).far
    later = lambda unit: piece_of(opened + unit)
    arrival = functools.partial(field_copy, field_any, plane_ref, sems, later)
    for unit in range(2):
        arrival(unit).start()
    mine = columns(piece_of(0), 0, (opened + units) * UNIT)
    pairs = [(transfer_any, transfer_ref), (start_any, start_ref), (end_any, end_ref)]
    pairs += [(jitter_any.at[:, mine], jitter_ref), (halo_any.at[:, mine], halo_ref), (state_any, state_ref)]
    pairs.append((field_any.at[slab_len - 1, :, columns(piece_of(0), 0, opened * UNIT)], last_ref))
    copies = start_all(pairs, few_sems)
    base = lax.axis_index("depth") * slab_len
    for copy in copies[:3]:
        copy.wait()
    coder = Coder(total, slab_len, (rows, LANES), transfer_ref)
    for unit in range(2, units):
        arrival(unit).start()
    tile_gains(gain_ref, coder.gain, base, tile_cols, start_ref, end_ref, later)
    tile_gains(last_gain_ref, coder.gain, base + slab_len - 1, tile_cols, start_ref, end_ref, piece_of)
    for copy in copies[3:5]:
        copy.wait()

    def compute(unit, cols, place):
        whole = columns(opened + unit, cols.start, LANES)
        jitter = jitter_ref[:, whole]
        return coder.codes(*march(gain_ref, plane_ref, unit, cols, place, jitter, coder.levels, halo_ref[:, whole]))

    def store(first, unit, cols, codes):
        for i, code in enumerate(codes):
            out_ref[first + unit, i, :, cols] = code

    def leave(unit):
        return pltpu.make_async_copy(out_ref.at[unit], out_any.at[piece_of(unit)], out_sems.at[unit])

    def leave_pair(first, n):
        for u in range(2):
            leave(first + 2 * n + u).start()

    each_pair(units, functools.partial(arrive_pair, arrival), compute, functools.partial(store, opened),
              functools.partial(leave_pair, opened))
    for copy in copies[5:]:
        copy.wait()

    def finish(unit, cols, place):
        jitter = jitter_ref[:, place]
        lower = last_ref[:, place].astype(jnp.float32)
        upper = halo_ref[:, place].astype(jnp.float32)
        value = (1.0 - jitter) * lower + jitter * upper
        before = state_ref[unit, 3, :, cols]
        beyond = before + last_gain_ref[0:1, place] * value
        weight = jnp.exp2(before) - jnp.exp2(beyond)
        sums = [state_ref[unit, i, :, cols] for i in range(3)]
        moment(sums, weight, value, coder.levels)
        return coder.codes(sums, beyond)

    each_pair(opened, lambda n: None, finish, functools.partial(store, 0), functools.partial(leave_pair, 0))
    loop(out_ref.shape[0], lambda unit: leave(unit).wait())


def near_kernel(total, tile_cols, near, transfer_any, start_any, end_any, field_any, halo_any, jitter_any, far_any, *refs):
    del far_any
    out_anys = refs[:near]
    transfer_ref, start_ref, end_ref, plane_ref, halo_ref, jitter_ref, out_ref, gain_ref, few_sems, sems, out_sems = refs[near:]
    units, slab_len, rows, _ = plane_ref.shape
    piece_of = Pieces(near).close
    arrival = functools.partial(field_copy, field_any, plane_ref, sems, piece_of)
    for unit in range(2):
        arrival(unit).start()
    first = Pieces(near).close_first()
    mine = columns(first, 0, near * UNIT)
    pairs = [(transfer_any, transfer_ref), (start_any, start_ref), (end_any, end_ref)]
    copies = start_all(pairs + [(jitter_any.at[:, mine], jitter_ref), (halo_any.at[:, mine], halo_ref)], few_sems)
    base = lax.axis_index("depth") * slab_len
    for copy in copies[:3]:
        copy.wait()
    coder = Coder(total, slab_len, (rows, LANES), transfer_ref)
    for unit in range(2, units):
        arrival(unit).start()
    tile_gains(gain_ref, coder.gain, base, tile_cols, start_ref, end_ref, piece_of)
    for copy in copies[3:]:
        copy.wait()

    def compute(unit, cols, place):
        whole = columns(piece_of(unit) - first, cols.start, LANES)
        jitter = jitter_ref[:, whole]
        return coder.codes(*march(gain_ref, plane_ref, unit, cols, place, jitter, coder.levels, halo_ref[:, whole]))

    def store(unit, cols, codes):
        for i, code in enumerate(codes):
            out_ref[unit, i, :, cols] = code

    each_pair(units, functools.partial(arrive_pair, arrival), compute, store, lambda n: None)
    pairs = [(out_ref.at[unit], out_anys[unit]) for unit in range(units)]
    for copy in start_all(pairs, out_sems):
        copy.wait()


def slab_codes(field, halo, jitter, transfer, ray_start, ray_end, total, near):
    slab_len, rows, cols = field.shape
    pieces = cols // UNIT
    opened = pieces * 3 // 16 * 2
    closed = pieces - near - opened
    ntiles = ray_start.shape[0]
    tile_cols = cols // ntiles
    own = pl.BlockSpec(memory_space=pl.ANY)
    scalars = [pltpu.SMEM(transfer.shape, transfer.dtype)] + [pltpu.SMEM((ntiles,), jnp.int32)] * 2

    def cost(units):
        work = slab_len * rows * units * UNIT
        return pl.CostEstimate(flops=work * 20, bytes_accessed=work * 2, transcendentals=work * 2)

    def planes(units):
        return pltpu.VMEM((units, slab_len, rows, UNIT), field.dtype)

    def flat(units, dtype):
        return pltpu.VMEM((rows, units * UNIT), dtype)

    def table(samples, units):
        return pltpu.VMEM((samples, units * UNIT), jnp.float32)

    state_shape = (opened, 4, rows, UNIT)
    state = pl.pallas_call(
        functools.partial(open_kernel, total, tile_cols, near),
        in_specs=[own] * 5,
        out_specs=own,
        out_shape=jax.ShapeDtypeStruct(state_shape, jnp.float32),
        scratch_shapes=scalars + [
            planes(opened), flat(opened, jnp.float32), pltpu.VMEM(state_shape, jnp.float32), table(slab_len, opened),
            pltpu.SemaphoreType.DMA((4,)),
            pltpu.SemaphoreType.DMA((opened,)),
            pltpu.SemaphoreType.DMA((opened // 2,)),
        ],
        compiler_params=pltpu.CompilerParams(vmem_limit_bytes=OPEN_BYTES),
        cost_estimate=cost(opened),
        name="open",
    )(transfer, ray_start, ray_end, field, jitter)
    far = pl.pallas_call(
        functools.partial(close_kernel, total, tile_cols, near, opened),
        in_specs=[own] * 7,
        out_specs=own,
        out_shape=jax.ShapeDtypeStruct((pieces, 4, rows, UNIT), jnp.int16),
        scratch_shapes=scalars + [
            planes(closed), flat(opened + closed, field.dtype), flat(opened + closed, jnp.float32),
            pltpu.VMEM((opened + closed, 4, rows, UNIT), jnp.int16), table(slab_len, closed),
            pltpu.VMEM(state_shape, jnp.float32), flat(opened, field.dtype), table(SUBLANES, opened),
            pltpu.SemaphoreType.DMA((7,)),
            pltpu.SemaphoreType.DMA((closed,)),
            pltpu.SemaphoreType.DMA((opened + closed,)),
        ],
        compiler_params=pltpu.CompilerParams(vmem_limit_bytes=CLOSE_BYTES),
        cost_estimate=cost(closed),
        name="close",
    )(transfer, ray_start, ray_end, field, halo, jitter, state)
    if not near:
        return far, []
    return far, pl.pallas_call(
        functools.partial(near_kernel, total, tile_cols, near),
        in_specs=[own] * 7,
        out_specs=[own] * near,
        out_shape=[jax.ShapeDtypeStruct((4, rows, UNIT), jnp.int16)] * near,
        scratch_shapes=scalars + [
            planes(near), flat(near, field.dtype), flat(near, jnp.float32), pltpu.VMEM((near, 4, rows, UNIT), jnp.int16), table(slab_len, near),
            pltpu.SemaphoreType.DMA((5,)),
            pltpu.SemaphoreType.DMA((near,)),
            pltpu.SemaphoreType.DMA((near,)),
        ],
        compiler_params=pltpu.CompilerParams(vmem_limit_bytes=CLOSE_BYTES),
        cost_estimate=cost(near),
        name="near",
    )(transfer, ray_start, ray_end, field, halo, jitter, far)


def composite_kernel(total, slab_len, near, order_any, transfer_any, code_any, *refs):
    near_anys = refs[:near]
    image_any, order_ref, transfer_ref, code_ref, out_ref, sems, out_sems = refs[near:]
    count, _, rows, width = code_ref.shape
    here = lax.axis_index("depth")
    pairs = [(near_any, code_ref.at[here ^ n]) for n, near_any in zip(reversed(range(near)), near_anys)]
    if near:
        for n in range(count // near - 1):
            group = n + jnp.where(n >= here // near, 1, 0)
            slabs = pl.ds(group * near, near)
            pairs.append((code_any.at[slabs], code_ref.at[slabs]))
    else:
        pairs.append((code_any, code_ref))
    copies = start_all([(order_any, order_ref), (transfer_any, transfer_ref)] + pairs, sems)
    block = math.gcd(width, 2 * LANES)
    places = [pl.ds(col, block) for col in range(0, width, block)]
    shape = (rows, block)
    depth_span, color_span = spans(slab_len)
    for copy in copies:
        copy.wait()
    unit = jnp.full(shape, transfer_ref[3]) * (0.2 / total * slab_len * TOP)
    depth_unit = unit * LOG2E
    leaving = []
    for n, cols in enumerate(places):

        def number(slab, channel, span):
            return code_ref[slab, channel, :, cols].astype(jnp.int32).astype(jnp.float32) * (span / 65535.0)

        def step(j, carry):
            shift, *colors = carry
            slab = order_ref[j]
            code = number(slab, 3, depth_span)
            idle = code < depth_span * (-32767.5 / 65535.0)
            away = jnp.where(idle, FAR, shift)
            for i in range(3):
                colors[i] = colors[i] + jnp.exp2(number(slab, i, color_span) - away)
            own = jnp.where(idle, 0.0, jnp.exp2(code + lift(depth_span)))
            return shift + depth_unit * own, *colors

        zero = jnp.zeros(shape, jnp.float32)
        first = jnp.full(shape, -lift(color_span))
        shift, *colors = lax.fori_loop(0, count, step, (first, zero, zero, zero), unroll=math.gcd(count, 4))
        for i in range(3):
            out_ref[i, :, cols] = colors[i] * (unit * (TOP / (transfer_ref[i] + jnp.full(shape, TOP))))
        out_ref[3, :, cols] = 1.0 - jnp.exp2(first - shift)
        leaving.append(pltpu.make_async_copy(out_ref.at[:, :, cols], image_any.at[:, :, cols], out_sems.at[n]))
        leaving[-1].start()
    for copy in leaving:
        copy.wait()


def composite(codes, near_codes, transfer, depth_order, total, slab_len):
    count, _, rows, width = codes.shape
    near = len(near_codes)
    blocks = width // math.gcd(width, 2 * LANES)
    own = pl.BlockSpec(memory_space=pl.ANY)
    return pl.pallas_call(
        functools.partial(composite_kernel, total, slab_len, near),
        in_specs=[own] * (3 + near),
        out_specs=own,
        out_shape=jax.ShapeDtypeStruct((4, rows, width), jnp.float32),
        scratch_shapes=[
            pltpu.SMEM(depth_order.shape, depth_order.dtype),
            pltpu.SMEM(transfer.shape, transfer.dtype),
            pltpu.VMEM(codes.shape, codes.dtype),
            pltpu.VMEM((4, rows, width), jnp.float32),
            pltpu.SemaphoreType.DMA((2 + near + (count // near - 1 if near else 1),)),
            pltpu.SemaphoreType.DMA((blocks,)),
        ],
        compiler_params=pltpu.CompilerParams(vmem_limit_bytes=SMALL_BYTES),
        name="composite",
    )(depth_order, transfer, codes, *near_codes)


def on_device(field, jitter, transfer, depth_order, ray_start, ray_end):
    count = lax.axis_size("depth")
    slab_len, rows, cols = field.shape
    total = slab_len * count
    width = cols // count
    near = NEAR if width == UNIT and count == 2 * NEAR else 0
    halo = shifted(field[0], "depth", -1)
    codes, near_codes = slab_codes(field, halo, jitter, transfer, ray_start, ray_end, total, near)
    if width != UNIT:
        codes = codes.transpose(1, 2, 0, 3).reshape(4, rows, count, width).transpose(2, 0, 1, 3)
    received = lax.all_to_all(codes, "depth", split_axis=0, concat_axis=0, tiled=True)
    swapped = [lax.ppermute(near_codes[n], "depth", [(i, i ^ n) for i in range(count)]) for n in reversed(range(1, near))]
    return composite(received, [*swapped, *near_codes[:1]], transfer, depth_order, total, slab_len)


def solution(mesh):
    in_specs = (P("depth", "groups", None), P("groups", None), P(), P(), P(), P())
    out_specs = P(None, "groups", "depth")
    return jax.shard_map(
        on_device, mesh=mesh, in_specs=in_specs, out_specs=out_specs, check_vma=False
    )
```

```python
import functools
import math

import jax
import jax.numpy as jnp
from jax import lax
from jax.experimental import pallas as pl
from jax.experimental.pallas import tpu as pltpu
from jax.sharding import PartitionSpec as P

TOP = 5.2
LOG2E = math.log2(math.e)
SUBLANES = 8
LANES = 128
FAR = 1.0e4
UNIT = 512
NEAR = 8
OPEN_BYTES = 54 * 1024 * 1024
CLOSE_BYTES = 53 * 1024 * 1024
SMALL_BYTES = 16 * 1024 * 1024


def spans(slab_len):
    deep = math.log2(slab_len)
    return 6.8 + deep, 13.2 + deep


def lift(span):
    return span * (32768.0 / 65535.0) - span


def shifted(value, axis, steps):
    count = lax.axis_size(axis)
    initial, last = (max(0, -steps), min(count, count - steps))
    return lax.ppermute(value, axis, [(source, source + steps) for source in range(initial, last)])


def encode(value, span):
    code = jnp.log2(value) * (65535.0 / span) + 65535.5
    code = jnp.minimum(jnp.maximum(code, 0.0), 65535.0)
    return (code.astype(jnp.int32) - 32768).astype(jnp.int16)


def tile_gains(gain_ref, gain, base, tile_cols, start_ref, end_ref, piece_of):
    sample = lax.broadcasted_iota(jnp.int32, (SUBLANES, LANES), 0) + base
    lane = lax.broadcasted_iota(jnp.int32, (SUBLANES, LANES), 1)

    def block(n, carry):
        blocks = UNIT // LANES
        tile = (piece_of(n // blocks) * UNIT + n % blocks * LANES) // tile_cols
        start = jnp.full((SUBLANES, LANES), start_ref[tile])
        end = jnp.full((SUBLANES, LANES), end_ref[tile])
        for t in range(1, LANES // tile_cols):
            start = jnp.where(lane >= t * tile_cols, start_ref[tile + t], start)
            end = jnp.where(lane >= t * tile_cols, end_ref[tile + t], end)
        cols = pl.ds(pl.multiple_of(n * LANES, LANES), LANES)
        for k in range(0, gain_ref.shape[0], SUBLANES):
            active = (sample + k >= start) & (sample + k < end)
            gain_ref[k:k + SUBLANES, cols] = jnp.where(active, gain, 0.0)
        return carry

    blocks = gain_ref.shape[1] // LANES
    lax.fori_loop(0, blocks, block, 0, unroll=math.gcd(blocks, 8))


def moment(sums, weight, value, levels):
    whole = (levels[0] + value) * (levels[1] + value) * (levels[2] + value)
    share = weight * pl.reciprocal(whole, approx=True, full_range=False)
    for n in range(3):
        sums[n] = sums[n] + share
        share = share * value


def colors(sums, before, levels):
    emitted = 1.0 - jnp.exp2(before)
    others = [(levels[1], levels[2]), (levels[2], levels[0]), (levels[0], levels[1])]
    return [emitted - t * (sums[2] + (p + q) * sums[1] + (p * q) * sums[0]) for t, (p, q) in zip(levels, others)]


def march(gain_ref, plane_ref, unit, cols, place, jitter, levels, halo=None):
    slab_len = plane_ref.shape[1]
    shape = jitter.shape
    before = jnp.zeros(shape, jnp.float32)
    through = jnp.ones(shape, jnp.float32)
    sums = [jnp.zeros(shape, jnp.float32) for _ in range(3)]
    lower = plane_ref[unit, 0, :, cols].astype(jnp.float32)
    stay = lower - jitter * lower
    for k in range(slab_len - (halo is None)):
        following = plane_ref[unit, k + 1, :, cols] if k + 1 < slab_len else halo
        upper = following.astype(jnp.float32)
        moved = jitter * upper
        value = stay + moved
        before = before + gain_ref[k:k + 1, place] * value
        beyond = jnp.exp2(before)
        moment(sums, through - beyond, value, levels)
        through = beyond
        stay = upper - moved
    return sums, before


def loop(count, body):
    def step(n, carry):
        body(n)
        return carry

    lax.fori_loop(0, count, step, 0)


def each_group(units, group, arrive, compute, store, leave):
    def step(n):
        places = [(group * n + u, c) for u in range(group) for c in range(0, UNIT, LANES)]
        arrive(n)
        results = [compute(unit, pl.ds(c, LANES), pl.ds(pl.multiple_of(unit * UNIT + c, LANES), LANES)) for unit, c in places]
        for (unit, c), result in zip(places, results):
            store(unit, pl.ds(c, LANES), result)
        leave(n)

    loop(units // group, step)


def start_all(pairs, sems):
    copies = [pltpu.make_async_copy(src, dst, sems.at[n]) for n, (src, dst) in enumerate(pairs)]
    for copy in copies:
        copy.start()
    return copies


class Pieces:
    def __init__(self, near):
        self.near = near
        self.here = lax.axis_index("depth")

    def far(self, n):
        if not self.near:
            return n
        return n + jnp.where(n >= self.here // self.near * self.near, self.near, 0)

    def close(self, n):
        return self.here ^ n

    def close_first(self):
        return self.here // self.near * self.near


def columns(piece, col=0, size=UNIT):
    return pl.ds(pl.multiple_of(piece * UNIT + col, LANES), size)


def field_copy(field_any, plane_ref, sems, piece_of, unit):
    return pltpu.make_async_copy(field_any.at[:, :, columns(piece_of(unit))], plane_ref.at[unit], sems.at[unit])


def arrive_pair(arrival, n):
    for u in range(2):
        arrival(2 * n + u).wait()


def open_kernel(total, tile_cols, near, transfer_any, start_any, end_any, field_any, jitter_any, state_any, transfer_ref,
                start_ref, end_ref, plane_ref, jitter_ref, state_ref, gain_ref, few_sems, sems, out_sems):
    units, slab_len, rows, _ = plane_ref.shape
    piece_of = Pieces(near).far
    arrival = functools.partial(field_copy, field_any, plane_ref, sems, piece_of)
    for unit in range(2):
        arrival(unit).start()
    pairs = [(transfer_any, transfer_ref), (start_any, start_ref), (end_any, end_ref)]
    pairs.append((jitter_any.at[:, columns(piece_of(0), 0, units * UNIT)], jitter_ref))
    *early, jitter_copy = start_all(pairs, few_sems)
    base = lax.axis_index("depth") * slab_len
    for copy in early:
        copy.wait()
    levels = [jnp.full((rows, LANES), transfer_ref[i]) for i in range(3)]
    gain = jnp.full((SUBLANES, LANES), transfer_ref[3]) * (-LOG2E * 0.2 / total)
    for unit in range(2, units):
        arrival(unit).start()
    tile_gains(gain_ref, gain, base, tile_cols, start_ref, end_ref, piece_of)
    jitter_copy.wait()

    def compute(unit, cols, place):
        return march(gain_ref, plane_ref, unit, cols, place, jitter_ref[:, place], levels)

    def store(unit, cols, result):
        sums, before = result
        for i, value in enumerate([*sums, before]):
            state_ref[unit, i, :, cols] = value

    def leave(n):
        place = pl.ds(2 * n, 2)
        return pltpu.make_async_copy(state_ref.at[place], state_any.at[place], out_sems.at[n])

    each_group(units, 2, functools.partial(arrive_pair, arrival), compute, store, lambda n: leave(n).start())
    loop(units // 2, lambda n: leave(n).wait())


class Coder:
    def __init__(self, total, slab_len, shape, transfer_ref):
        depth_gain = jnp.full(shape, transfer_ref[3]) * (0.2 / total)
        self.levels = [jnp.full(shape, transfer_ref[i]) for i in range(3)]
        self.depth_unit = 1.0 / (depth_gain * (slab_len * TOP))
        self.color_unit = [self.depth_unit * ((self.levels[i] + TOP) * (1.0 / TOP)) for i in range(3)]
        self.depth_span, self.color_span = spans(slab_len)
        self.gain = depth_gain[:SUBLANES] * -LOG2E

    def codes(self, sums, before):
        tints = colors(sums, before, self.levels)
        codes = [encode(color * unit, self.color_span) for color, unit in zip(tints, self.color_unit)]
        return codes + [encode(before * (self.depth_unit * (-1.0 / LOG2E)), self.depth_span)]


def close_kernel(total, tile_cols, near, opened, transfer_any, start_any, end_any, field_any, halo_any, jitter_any, state_any,
                 out_any, transfer_ref, start_ref, end_ref, plane_ref, halo_ref, jitter_ref, out_ref, gain_ref, state_ref,
                 last_ref, last_gain_ref, few_sems, sems, out_sems):
    units, slab_len, rows, _ = plane_ref.shape
    piece_of = Pieces(near).far
    later = lambda unit: piece_of(opened + unit)
    arrival = functools.partial(field_copy, field_any, plane_ref, sems, later)
    for unit in range(2):
        arrival(unit).start()
    mine = columns(piece_of(0), 0, (opened + units) * UNIT)
    pairs = [(transfer_any, transfer_ref), (start_any, start_ref), (end_any, end_ref)]
    pairs += [(jitter_any.at[:, mine], jitter_ref), (halo_any.at[:, mine], halo_ref), (state_any, state_ref)]
    pairs.append((field_any.at[slab_len - 1, :, columns(piece_of(0), 0, opened * UNIT)], last_ref))
    copies = start_all(pairs, few_sems)
    base = lax.axis_index("depth") * slab_len
    for copy in copies[:3]:
        copy.wait()
    coder = Coder(total, slab_len, (rows, LANES), transfer_ref)
    for unit in range(2, units):
        arrival(unit).start()
    tile_gains(gain_ref, coder.gain, base, tile_cols, start_ref, end_ref, later)
    tile_gains(last_gain_ref, coder.gain, base + slab_len - 1, tile_cols, start_ref, end_ref, piece_of)
    for copy in copies[3:5]:
        copy.wait()

    def compute(unit, cols, place):
        whole = columns(opened + unit, cols.start, LANES)
        jitter = jitter_ref[:, whole]
        return coder.codes(*march(gain_ref, plane_ref, unit, cols, place, jitter, coder.levels, halo_ref[:, whole]))

    def store(first, unit, cols, codes):
        for i, code in enumerate(codes):
            out_ref[first + unit, i, :, cols] = code

    def leave(unit):
        return pltpu.make_async_copy(out_ref.at[unit], out_any.at[piece_of(unit)], out_sems.at[unit])

    def leave_pair(first, n):
        for u in range(2):
            leave(first + 2 * n + u).start()

    each_group(units, 2, functools.partial(arrive_pair, arrival), compute, functools.partial(store, opened),
              functools.partial(leave_pair, opened))
    for copy in copies[5:]:
        copy.wait()

    def finish(unit, cols, place):
        jitter = jitter_ref[:, place]
        lower = last_ref[:, place].astype(jnp.float32)
        upper = halo_ref[:, place].astype(jnp.float32)
        value = (1.0 - jitter) * lower + jitter * upper
        before = state_ref[unit, 3, :, cols]
        beyond = before + last_gain_ref[0:1, place] * value
        weight = jnp.exp2(before) - jnp.exp2(beyond)
        sums = [state_ref[unit, i, :, cols] for i in range(3)]
        moment(sums, weight, value, coder.levels)
        return coder.codes(sums, beyond)

    group = math.gcd(opened, 3)

    def leave_finished(n):
        for u in range(group):
            leave(group * n + u).start()

    each_group(opened, group, lambda n: None, finish, functools.partial(store, 0), leave_finished)
    loop(out_ref.shape[0], lambda unit: leave(unit).wait())


def near_kernel(total, tile_cols, near, transfer_any, start_any, end_any, field_any, halo_any, jitter_any, far_any, *refs):
    del far_any
    out_anys = refs[:near]
    transfer_ref, start_ref, end_ref, plane_ref, halo_ref, jitter_ref, out_ref, gain_ref, few_sems, sems, out_sems = refs[near:]
    units, slab_len, rows, _ = plane_ref.shape
    piece_of = Pieces(near).close
    arrival = functools.partial(field_copy, field_any, plane_ref, sems, piece_of)
    for unit in range(2):
        arrival(unit).start()
    first = Pieces(near).close_first()
    mine = columns(first, 0, near * UNIT)
    pairs = [(transfer_any, transfer_ref), (start_any, start_ref), (end_any, end_ref)]
    copies = start_all(pairs + [(jitter_any.at[:, mine], jitter_ref), (halo_any.at[:, mine], halo_ref)], few_sems)
    base = lax.axis_index("depth") * slab_len
    for copy in copies[:3]:
        copy.wait()
    coder = Coder(total, slab_len, (rows, LANES), transfer_ref)
    for unit in range(2, units):
        arrival(unit).start()
    tile_gains(gain_ref, coder.gain, base, tile_cols, start_ref, end_ref, piece_of)
    for copy in copies[3:]:
        copy.wait()

    def compute(unit, cols, place):
        whole = columns(piece_of(unit) - first, cols.start, LANES)
        jitter = jitter_ref[:, whole]
        return coder.codes(*march(gain_ref, plane_ref, unit, cols, place, jitter, coder.levels, halo_ref[:, whole]))

    def store(unit, cols, codes):
        for i, code in enumerate(codes):
            out_ref[unit, i, :, cols] = code

    each_group(units, 2, functools.partial(arrive_pair, arrival), compute, store, lambda n: None)
    pairs = [(out_ref.at[unit], out_anys[unit]) for unit in range(units)]
    for copy in start_all(pairs, out_sems):
        copy.wait()


def slab_codes(field, halo, jitter, transfer, ray_start, ray_end, total, near):
    slab_len, rows, cols = field.shape
    pieces = cols // UNIT
    opened = pieces * 3 // 16 * 2
    closed = pieces - near - opened
    ntiles = ray_start.shape[0]
    tile_cols = cols // ntiles
    own = pl.BlockSpec(memory_space=pl.ANY)
    scalars = [pltpu.SMEM(transfer.shape, transfer.dtype)] + [pltpu.SMEM((ntiles,), jnp.int32)] * 2

    def cost(units):
        work = slab_len * rows * units * UNIT
        return pl.CostEstimate(flops=work * 20, bytes_accessed=work * 2, transcendentals=work * 2)

    def planes(units):
        return pltpu.VMEM((units, slab_len, rows, UNIT), field.dtype)

    def flat(units, dtype):
        return pltpu.VMEM((rows, units * UNIT), dtype)

    def table(samples, units):
        return pltpu.VMEM((samples, units * UNIT), jnp.float32)

    state_shape = (opened, 4, rows, UNIT)
    state = pl.pallas_call(
        functools.partial(open_kernel, total, tile_cols, near),
        in_specs=[own] * 5,
        out_specs=own,
        out_shape=jax.ShapeDtypeStruct(state_shape, jnp.float32),
        scratch_shapes=scalars + [
            planes(opened), flat(opened, jnp.float32), pltpu.VMEM(state_shape, jnp.float32), table(slab_len, opened),
            pltpu.SemaphoreType.DMA((4,)),
            pltpu.SemaphoreType.DMA((opened,)),
            pltpu.SemaphoreType.DMA((opened // 2,)),
        ],
        compiler_params=pltpu.CompilerParams(vmem_limit_bytes=OPEN_BYTES),
        cost_estimate=cost(opened),
        name="open",
    )(transfer, ray_start, ray_end, field, jitter)
    far = pl.pallas_call(
        functools.partial(close_kernel, total, tile_cols, near, opened),
        in_specs=[own] * 7,
        out_specs=own,
        out_shape=jax.ShapeDtypeStruct((pieces, 4, rows, UNIT), jnp.int16),
        scratch_shapes=scalars + [
            planes(closed), flat(opened + closed, field.dtype), flat(opened + closed, jnp.float32),
            pltpu.VMEM((opened + closed, 4, rows, UNIT), jnp.int16), table(slab_len, closed),
            pltpu.VMEM(state_shape, jnp.float32), flat(opened, field.dtype), table(SUBLANES, opened),
            pltpu.SemaphoreType.DMA((7,)),
            pltpu.SemaphoreType.DMA((closed,)),
            pltpu.SemaphoreType.DMA((opened + closed,)),
        ],
        compiler_params=pltpu.CompilerParams(vmem_limit_bytes=CLOSE_BYTES),
        cost_estimate=cost(closed),
        name="close",
    )(transfer, ray_start, ray_end, field, halo, jitter, state)
    if not near:
        return far, []
    return far, pl.pallas_call(
        functools.partial(near_kernel, total, tile_cols, near),
        in_specs=[own] * 7,
        out_specs=[own] * near,
        out_shape=[jax.ShapeDtypeStruct((4, rows, UNIT), jnp.int16)] * near,
        scratch_shapes=scalars + [
            planes(near), flat(near, field.dtype), flat(near, jnp.float32), pltpu.VMEM((near, 4, rows, UNIT), jnp.int16), table(slab_len, near),
            pltpu.SemaphoreType.DMA((5,)),
            pltpu.SemaphoreType.DMA((near,)),
            pltpu.SemaphoreType.DMA((near,)),
        ],
        compiler_params=pltpu.CompilerParams(vmem_limit_bytes=CLOSE_BYTES),
        cost_estimate=cost(near),
        name="near",
    )(transfer, ray_start, ray_end, field, halo, jitter, far)


def composite_kernel(total, slab_len, near, order_any, transfer_any, code_any, *refs):
    near_anys = refs[:near]
    image_any, order_ref, transfer_ref, code_ref, out_ref, sems, out_sems = refs[near:]
    count, _, rows, width = code_ref.shape
    here = lax.axis_index("depth")
    pairs = [(near_any, code_ref.at[here ^ n]) for n, near_any in zip(reversed(range(near)), near_anys)]
    if near:
        for n in range(count // near - 1):
            group = n + jnp.where(n >= here // near, 1, 0)
            slabs = pl.ds(group * near, near)
            pairs.append((code_any.at[slabs], code_ref.at[slabs]))
    else:
        pairs.append((code_any, code_ref))
    copies = start_all([(order_any, order_ref), (transfer_any, transfer_ref)] + pairs, sems)
    block = math.gcd(width, 2 * LANES)
    places = [pl.ds(col, block) for col in range(0, width, block)]
    shape = (rows, block)
    depth_span, color_span = spans(slab_len)
    for copy in copies:
        copy.wait()
    unit = jnp.full(shape, transfer_ref[3]) * (0.2 / total * slab_len * TOP)
    depth_unit = unit * LOG2E
    leaving = []
    for n, cols in enumerate(places):

        def number(slab, channel, span):
            return code_ref[slab, channel, :, cols].astype(jnp.int32).astype(jnp.float32) * (span / 65535.0)

        def step(j, carry):
            shift, *colors = carry
            slab = order_ref[j]
            code = number(slab, 3, depth_span)
            idle = code < depth_span * (-32767.5 / 65535.0)
            away = jnp.where(idle, FAR, shift)
            for i in range(3):
                colors[i] = colors[i] + jnp.exp2(number(slab, i, color_span) - away)
            own = jnp.where(idle, 0.0, jnp.exp2(code + lift(depth_span)))
            return shift + depth_unit * own, *colors

        zero = jnp.zeros(shape, jnp.float32)
        first = jnp.full(shape, -lift(color_span))
        shift, *colors = lax.fori_loop(0, count, step, (first, zero, zero, zero), unroll=math.gcd(count, 16))
        for i in range(3):
            out_ref[i, :, cols] = colors[i] * (unit * (TOP / (transfer_ref[i] + jnp.full(shape, TOP))))
        out_ref[3, :, cols] = 1.0 - jnp.exp2(first - shift)
        leaving.append(pltpu.make_async_copy(out_ref.at[:, :, cols], image_any.at[:, :, cols], out_sems.at[n]))
        leaving[-1].start()
    for copy in leaving:
        copy.wait()


def composite(codes, near_codes, transfer, depth_order, total, slab_len):
    count, _, rows, width = codes.shape
    near = len(near_codes)
    blocks = width // math.gcd(width, 2 * LANES)
    own = pl.BlockSpec(memory_space=pl.ANY)
    return pl.pallas_call(
        functools.partial(composite_kernel, total, slab_len, near),
        in_specs=[own] * (3 + near),
        out_specs=own,
        out_shape=jax.ShapeDtypeStruct((4, rows, width), jnp.float32),
        scratch_shapes=[
            pltpu.SMEM(depth_order.shape, depth_order.dtype),
            pltpu.SMEM(transfer.shape, transfer.dtype),
            pltpu.VMEM(codes.shape, codes.dtype),
            pltpu.VMEM((4, rows, width), jnp.float32),
            pltpu.SemaphoreType.DMA((2 + near + (count // near - 1 if near else 1),)),
            pltpu.SemaphoreType.DMA((blocks,)),
        ],
        compiler_params=pltpu.CompilerParams(vmem_limit_bytes=SMALL_BYTES),
        name="composite",
    )(depth_order, transfer, codes, *near_codes)


def on_device(field, jitter, transfer, depth_order, ray_start, ray_end):
    count = lax.axis_size("depth")
    slab_len, rows, cols = field.shape
    total = slab_len * count
    width = cols // count
    near = NEAR if width == UNIT and count == 2 * NEAR else 0
    halo = shifted(field[0], "depth", -1)
    codes, near_codes = slab_codes(field, halo, jitter, transfer, ray_start, ray_end, total, near)
    if width != UNIT:
        codes = codes.transpose(1, 2, 0, 3).reshape(4, rows, count, width).transpose(2, 0, 1, 3)
    received = lax.all_to_all(codes, "depth", split_axis=0, concat_axis=0, tiled=True)
    swapped = [lax.ppermute(near_codes[n], "depth", [(i, i ^ n) for i in range(count)]) for n in reversed(range(1, near))]
    return composite(received, [*swapped, *near_codes[:1]], transfer, depth_order, total, slab_len)


def solution(mesh):
    in_specs = (P("depth", "groups", None), P("groups", None), P(), P(), P(), P())
    out_specs = P(None, "groups", "depth")
    return jax.shard_map(
        on_device, mesh=mesh, in_specs=in_specs, out_specs=out_specs, check_vma=False
    )
```

```python
import functools
import math

import jax
import jax.numpy as jnp
from jax import lax
from jax.experimental import pallas as pl
from jax.experimental.pallas import tpu as pltpu
from jax.sharding import PartitionSpec as P

TOP = 5.2
LOG2E = math.log2(math.e)
SUBLANES = 8
LANES = 128
FAR = 1.0e4
UNIT = 512
NEAR = 8
OPEN_BYTES = 54 * 1024 * 1024
CLOSE_BYTES = 53 * 1024 * 1024
SMALL_BYTES = 16 * 1024 * 1024


def spans(slab_len):
    deep = math.log2(slab_len)
    return 6.8 + deep, 13.2 + deep


def lift(span):
    return span * (32768.0 / 65535.0) - span


def shifted(value, axis, steps):
    count = lax.axis_size(axis)
    initial, last = (max(0, -steps), min(count, count - steps))
    return lax.ppermute(value, axis, [(source, source + steps) for source in range(initial, last)])


def encode(value, span):
    code = jnp.log2(value) * (65535.0 / span) + 65535.5
    code = jnp.minimum(jnp.maximum(code, 0.0), 65535.0)
    return (code.astype(jnp.int32) - 32768).astype(jnp.int16)


def tile_gains(gain_ref, gain, base, tile_cols, start_ref, end_ref, piece_of):
    sample = lax.broadcasted_iota(jnp.int32, (SUBLANES, LANES), 0) + base
    lane = lax.broadcasted_iota(jnp.int32, (SUBLANES, LANES), 1)

    def block(n, carry):
        blocks = UNIT // LANES
        tile = (piece_of(n // blocks) * UNIT + n % blocks * LANES) // tile_cols
        start = jnp.full((SUBLANES, LANES), start_ref[tile])
        end = jnp.full((SUBLANES, LANES), end_ref[tile])
        for t in range(1, LANES // tile_cols):
            start = jnp.where(lane >= t * tile_cols, start_ref[tile + t], start)
            end = jnp.where(lane >= t * tile_cols, end_ref[tile + t], end)
        cols = pl.ds(pl.multiple_of(n * LANES, LANES), LANES)
        for k in range(0, gain_ref.shape[0], SUBLANES):
            active = (sample + k >= start) & (sample + k < end)
            gain_ref[k:k + SUBLANES, cols] = jnp.where(active, gain, 0.0)
        return carry

    blocks = gain_ref.shape[1] // LANES
    lax.fori_loop(0, blocks, block, 0, unroll=math.gcd(blocks, 8))


def moment(sums, weight, value, levels):
    whole = (levels[0] + value) * (levels[1] + value) * (levels[2] + value)
    share = weight * pl.reciprocal(whole, approx=True, full_range=False)
    for n in range(3):
        sums[n] = sums[n] + share
        share = share * value


def colors(sums, before, levels):
    emitted = 1.0 - jnp.exp2(before)
    others = [(levels[1], levels[2]), (levels[2], levels[0]), (levels[0], levels[1])]
    return [emitted - t * (sums[2] + (p + q) * sums[1] + (p * q) * sums[0]) for t, (p, q) in zip(levels, others)]


def march(gain_ref, plane_ref, unit, cols, place, jitter, levels, halo=None):
    slab_len = plane_ref.shape[1]
    shape = jitter.shape
    before = jnp.zeros(shape, jnp.float32)
    through = jnp.ones(shape, jnp.float32)
    sums = [jnp.zeros(shape, jnp.float32) for _ in range(3)]
    lower = plane_ref[unit, 0, :, cols].astype(jnp.float32)
    stay = lower - jitter * lower
    for k in range(slab_len - (halo is None)):
        following = plane_ref[unit, k + 1, :, cols] if k + 1 < slab_len else halo
        upper = following.astype(jnp.float32)
        moved = jitter * upper
        value = stay + moved
        before = before + gain_ref[k:k + 1, place] * value
        beyond = jnp.exp2(before)
        moment(sums, through - beyond, value, levels)
        through = beyond
        stay = upper - moved
    return sums, before


def loop(count, body):
    def step(n, carry):
        body(n)
        return carry

    lax.fori_loop(0, count, step, 0)


def each_group(units, group, arrive, compute, store, leave):
    def step(n):
        places = [(group * n + u, c) for u in range(group) for c in range(0, UNIT, LANES)]
        arrive(n)
        results = [compute(unit, pl.ds(c, LANES), pl.ds(pl.multiple_of(unit * UNIT + c, LANES), LANES)) for unit, c in places]
        for (unit, c), result in zip(places, results):
            store(unit, pl.ds(c, LANES), result)
        leave(n)

    loop(units // group, step)


def start_all(pairs, sems):
    copies = [pltpu.make_async_copy(src, dst, sems.at[n]) for n, (src, dst) in enumerate(pairs)]
    for copy in copies:
        copy.start()
    return copies


class Pieces:
    def __init__(self, near):
        self.near = near
        self.here = lax.axis_index("depth")

    def far(self, n):
        if not self.near:
            return n
        return n + jnp.where(n >= self.here // self.near * self.near, self.near, 0)

    def close(self, n):
        return self.here ^ n

    def close_first(self):
        return self.here // self.near * self.near


def columns(piece, col=0, size=UNIT):
    return pl.ds(pl.multiple_of(piece * UNIT + col, LANES), size)


def field_copy(field_any, plane_ref, sems, piece_of, unit):
    return pltpu.make_async_copy(field_any.at[:, :, columns(piece_of(unit))], plane_ref.at[unit], sems.at[unit])


def arrive_pair(arrival, n):
    for u in range(2):
        arrival(2 * n + u).wait()


def open_kernel(total, tile_cols, near, transfer_any, start_any, end_any, field_any, jitter_any, state_any, transfer_ref,
                start_ref, end_ref, plane_ref, jitter_ref, state_ref, gain_ref, few_sems, sems, out_sems):
    units, slab_len, rows, _ = plane_ref.shape
    piece_of = Pieces(near).far
    arrival = functools.partial(field_copy, field_any, plane_ref, sems, piece_of)
    early = start_all([(transfer_any, transfer_ref), (start_any, start_ref), (end_any, end_ref)], few_sems)
    for unit in range(2):
        arrival(unit).start()
    jitter_copy = pltpu.make_async_copy(jitter_any.at[:, columns(piece_of(0), 0, units * UNIT)], jitter_ref, few_sems.at[3])
    jitter_copy.start()
    base = lax.axis_index("depth") * slab_len
    for copy in early:
        copy.wait()
    levels = [jnp.full((rows, LANES), transfer_ref[i]) for i in range(3)]
    gain = jnp.full((SUBLANES, LANES), transfer_ref[3]) * (-LOG2E * 0.2 / total)
    for unit in range(2, units):
        arrival(unit).start()
    tile_gains(gain_ref, gain, base, tile_cols, start_ref, end_ref, piece_of)
    jitter_copy.wait()

    def compute(unit, cols, place):
        return march(gain_ref, plane_ref, unit, cols, place, jitter_ref[:, place], levels)

    def store(unit, cols, result):
        sums, before = result
        for i, value in enumerate([*sums, before]):
            state_ref[unit, i, :, cols] = value

    def leave(n):
        place = pl.ds(2 * n, 2)
        return pltpu.make_async_copy(state_ref.at[place], state_any.at[place], out_sems.at[n])

    each_group(units, 2, functools.partial(arrive_pair, arrival), compute, store, lambda n: leave(n).start())
    loop(units // 2, lambda n: leave(n).wait())


class Coder:
    def __init__(self, total, slab_len, shape, transfer_ref):
        depth_gain = jnp.full(shape, transfer_ref[3]) * (0.2 / total)
        self.levels = [jnp.full(shape, transfer_ref[i]) for i in range(3)]
        self.depth_unit = 1.0 / (depth_gain * (slab_len * TOP))
        self.color_unit = [self.depth_unit * ((self.levels[i] + TOP) * (1.0 / TOP)) for i in range(3)]
        self.depth_span, self.color_span = spans(slab_len)
        self.gain = depth_gain[:SUBLANES] * -LOG2E

    def codes(self, sums, before):
        tints = colors(sums, before, self.levels)
        codes = [encode(color * unit, self.color_span) for color, unit in zip(tints, self.color_unit)]
        return codes + [encode(before * (self.depth_unit * (-1.0 / LOG2E)), self.depth_span)]


def close_kernel(total, tile_cols, near, opened, transfer_any, start_any, end_any, field_any, halo_any, jitter_any, state_any,
                 out_any, transfer_ref, start_ref, end_ref, plane_ref, halo_ref, jitter_ref, out_ref, gain_ref, state_ref,
                 last_ref, last_gain_ref, few_sems, sems, out_sems):
    units, slab_len, rows, _ = plane_ref.shape
    piece_of = Pieces(near).far
    later = lambda unit: piece_of(opened + unit)
    arrival = functools.partial(field_copy, field_any, plane_ref, sems, later)
    copies = start_all([(transfer_any, transfer_ref), (start_any, start_ref), (end_any, end_ref)], few_sems)
    for unit in range(2):
        arrival(unit).start()
    mine = columns(piece_of(0), 0, (opened + units) * UNIT)
    pairs = [(jitter_any.at[:, mine], jitter_ref), (halo_any.at[:, mine], halo_ref), (state_any, state_ref)]
    pairs.append((field_any.at[slab_len - 1, :, columns(piece_of(0), 0, opened * UNIT)], last_ref))
    copies += start_all(pairs, few_sems.at[pl.ds(3, len(pairs))])
    base = lax.axis_index("depth") * slab_len
    for copy in copies[:3]:
        copy.wait()
    coder = Coder(total, slab_len, (rows, LANES), transfer_ref)
    for unit in range(2, units):
        arrival(unit).start()
    tile_gains(gain_ref, coder.gain, base, tile_cols, start_ref, end_ref, later)
    tile_gains(last_gain_ref, coder.gain, base + slab_len - 1, tile_cols, start_ref, end_ref, piece_of)
    for copy in copies[3:5]:
        copy.wait()

    def compute(unit, cols, place):
        whole = columns(opened + unit, cols.start, LANES)
        jitter = jitter_ref[:, whole]
        return coder.codes(*march(gain_ref, plane_ref, unit, cols, place, jitter, coder.levels, halo_ref[:, whole]))

    def store(first, unit, cols, codes):
        for i, code in enumerate(codes):
            out_ref[first + unit, i, :, cols] = code

    def leave(unit):
        return pltpu.make_async_copy(out_ref.at[unit], out_any.at[piece_of(unit)], out_sems.at[unit])

    def leave_pair(first, n):
        for u in range(2):
            leave(first + 2 * n + u).start()

    each_group(units, 2, functools.partial(arrive_pair, arrival), compute, functools.partial(store, opened),
              functools.partial(leave_pair, opened))
    for copy in copies[5:]:
        copy.wait()

    def finish(unit, cols, place):
        jitter = jitter_ref[:, place]
        lower = last_ref[:, place].astype(jnp.float32)
        upper = halo_ref[:, place].astype(jnp.float32)
        value = (1.0 - jitter) * lower + jitter * upper
        before = state_ref[unit, 3, :, cols]
        beyond = before + last_gain_ref[0:1, place] * value
        weight = jnp.exp2(before) - jnp.exp2(beyond)
        sums = [state_ref[unit, i, :, cols] for i in range(3)]
        moment(sums, weight, value, coder.levels)
        return coder.codes(sums, beyond)

    group = math.gcd(opened, 3)

    def leave_finished(n):
        for u in range(group):
            leave(group * n + u).start()

    each_group(opened, group, lambda n: None, finish, functools.partial(store, 0), leave_finished)
    loop(out_ref.shape[0], lambda unit: leave(unit).wait())


def near_kernel(total, tile_cols, near, transfer_any, start_any, end_any, field_any, halo_any, jitter_any, far_any, *refs):
    del far_any
    out_anys = refs[:near]
    transfer_ref, start_ref, end_ref, plane_ref, halo_ref, jitter_ref, out_ref, gain_ref, few_sems, sems, out_sems = refs[near:]
    units, slab_len, rows, _ = plane_ref.shape
    piece_of = Pieces(near).close
    arrival = functools.partial(field_copy, field_any, plane_ref, sems, piece_of)
    copies = start_all([(transfer_any, transfer_ref), (start_any, start_ref), (end_any, end_ref)], few_sems)
    for unit in range(2):
        arrival(unit).start()
    first = Pieces(near).close_first()
    mine = columns(first, 0, near * UNIT)
    copies += start_all([(jitter_any.at[:, mine], jitter_ref), (halo_any.at[:, mine], halo_ref)], few_sems.at[pl.ds(3, 2)])
    base = lax.axis_index("depth") * slab_len
    for copy in copies[:3]:
        copy.wait()
    coder = Coder(total, slab_len, (rows, LANES), transfer_ref)
    for unit in range(2, units):
        arrival(unit).start()
    tile_gains(gain_ref, coder.gain, base, tile_cols, start_ref, end_ref, piece_of)
    for copy in copies[3:]:
        copy.wait()

    def compute(unit, cols, place):
        whole = columns(piece_of(unit) - first, cols.start, LANES)
        jitter = jitter_ref[:, whole]
        return coder.codes(*march(gain_ref, plane_ref, unit, cols, place, jitter, coder.levels, halo_ref[:, whole]))

    def store(unit, cols, codes):
        for i, code in enumerate(codes):
            out_ref[unit, i, :, cols] = code

    each_group(units, 2, functools.partial(arrive_pair, arrival), compute, store, lambda n: None)
    pairs = [(out_ref.at[unit], out_anys[unit]) for unit in range(units)]
    for copy in start_all(pairs, out_sems):
        copy.wait()


def slab_codes(field, halo, jitter, transfer, ray_start, ray_end, total, near):
    slab_len, rows, cols = field.shape
    pieces = cols // UNIT
    opened = pieces * 3 // 16 * 2
    closed = pieces - near - opened
    ntiles = ray_start.shape[0]
    tile_cols = cols // ntiles
    own = pl.BlockSpec(memory_space=pl.ANY)
    scalars = [pltpu.SMEM(transfer.shape, transfer.dtype)] + [pltpu.SMEM((ntiles,), jnp.int32)] * 2

    def cost(units):
        work = slab_len * rows * units * UNIT
        return pl.CostEstimate(flops=work * 20, bytes_accessed=work * 2, transcendentals=work * 2)

    def planes(units):
        return pltpu.VMEM((units, slab_len, rows, UNIT), field.dtype)

    def flat(units, dtype):
        return pltpu.VMEM((rows, units * UNIT), dtype)

    def table(samples, units):
        return pltpu.VMEM((samples, units * UNIT), jnp.float32)

    state_shape = (opened, 4, rows, UNIT)
    state = pl.pallas_call(
        functools.partial(open_kernel, total, tile_cols, near),
        in_specs=[own] * 5,
        out_specs=own,
        out_shape=jax.ShapeDtypeStruct(state_shape, jnp.float32),
        scratch_shapes=scalars + [
            planes(opened), flat(opened, jnp.float32), pltpu.VMEM(state_shape, jnp.float32), table(slab_len, opened),
            pltpu.SemaphoreType.DMA((4,)),
            pltpu.SemaphoreType.DMA((opened,)),
            pltpu.SemaphoreType.DMA((opened // 2,)),
        ],
        compiler_params=pltpu.CompilerParams(vmem_limit_bytes=OPEN_BYTES),
        cost_estimate=cost(opened),
        name="open",
    )(transfer, ray_start, ray_end, field, jitter)
    far = pl.pallas_call(
        functools.partial(close_kernel, total, tile_cols, near, opened),
        in_specs=[own] * 7,
        out_specs=own,
        out_shape=jax.ShapeDtypeStruct((pieces, 4, rows, UNIT), jnp.int16),
        scratch_shapes=scalars + [
            planes(closed), flat(opened + closed, field.dtype), flat(opened + closed, jnp.float32),
            pltpu.VMEM((opened + closed, 4, rows, UNIT), jnp.int16), table(slab_len, closed),
            pltpu.VMEM(state_shape, jnp.float32), flat(opened, field.dtype), table(SUBLANES, opened),
            pltpu.SemaphoreType.DMA((7,)),
            pltpu.SemaphoreType.DMA((closed,)),
            pltpu.SemaphoreType.DMA((opened + closed,)),
        ],
        compiler_params=pltpu.CompilerParams(vmem_limit_bytes=CLOSE_BYTES),
        cost_estimate=cost(closed),
        name="close",
    )(transfer, ray_start, ray_end, field, halo, jitter, state)
    if not near:
        return far, []
    return far, pl.pallas_call(
        functools.partial(near_kernel, total, tile_cols, near),
        in_specs=[own] * 7,
        out_specs=[own] * near,
        out_shape=[jax.ShapeDtypeStruct((4, rows, UNIT), jnp.int16)] * near,
        scratch_shapes=scalars + [
            planes(near), flat(near, field.dtype), flat(near, jnp.float32), pltpu.VMEM((near, 4, rows, UNIT), jnp.int16), table(slab_len, near),
            pltpu.SemaphoreType.DMA((5,)),
            pltpu.SemaphoreType.DMA((near,)),
            pltpu.SemaphoreType.DMA((near,)),
        ],
        compiler_params=pltpu.CompilerParams(vmem_limit_bytes=CLOSE_BYTES),
        cost_estimate=cost(near),
        name="near",
    )(transfer, ray_start, ray_end, field, halo, jitter, far)


def composite_kernel(total, slab_len, near, order_any, transfer_any, code_any, *refs):
    near_anys = refs[:near]
    image_any, order_ref, transfer_ref, code_ref, out_ref, sems, out_sems = refs[near:]
    count, _, rows, width = code_ref.shape
    here = lax.axis_index("depth")
    pairs = [(near_any, code_ref.at[here ^ n]) for n, near_any in zip(reversed(range(near)), near_anys)]
    if near:
        for n in range(count // near - 1):
            group = n + jnp.where(n >= here // near, 1, 0)
            slabs = pl.ds(group * near, near)
            pairs.append((code_any.at[slabs], code_ref.at[slabs]))
    else:
        pairs.append((code_any, code_ref))
    copies = start_all([(order_any, order_ref), (transfer_any, transfer_ref)] + pairs, sems)
    block = math.gcd(width, 2 * LANES)
    places = [pl.ds(col, block) for col in range(0, width, block)]
    shape = (rows, block)
    depth_span, color_span = spans(slab_len)
    for copy in copies:
        copy.wait()
    unit = jnp.full(shape, transfer_ref[3]) * (0.2 / total * slab_len * TOP)
    depth_unit = unit * LOG2E
    leaving = []
    for n, cols in enumerate(places):

        def number(slab, channel, span):
            return code_ref[slab, channel, :, cols].astype(jnp.int32).astype(jnp.float32) * (span / 65535.0)

        def step(j, carry):
            shift, *colors = carry
            slab = order_ref[j]
            code = number(slab, 3, depth_span)
            idle = code < depth_span * (-32767.5 / 65535.0)
            away = jnp.where(idle, FAR, shift)
            for i in range(3):
                colors[i] = colors[i] + jnp.exp2(number(slab, i, color_span) - away)
            own = jnp.where(idle, 0.0, jnp.exp2(code + lift(depth_span)))
            return shift + depth_unit * own, *colors

        zero = jnp.zeros(shape, jnp.float32)
        first = jnp.full(shape, -lift(color_span))
        shift, *colors = lax.fori_loop(0, count, step, (first, zero, zero, zero), unroll=math.gcd(count, 16))
        for i in range(3):
            out_ref[i, :, cols] = colors[i] * (unit * (TOP / (transfer_ref[i] + jnp.full(shape, TOP))))
        out_ref[3, :, cols] = 1.0 - jnp.exp2(first - shift)
        leaving.append(pltpu.make_async_copy(out_ref.at[:, :, cols], image_any.at[:, :, cols], out_sems.at[n]))
        leaving[-1].start()
    for copy in leaving:
        copy.wait()


def composite(codes, near_codes, transfer, depth_order, total, slab_len):
    count, _, rows, width = codes.shape
    near = len(near_codes)
    blocks = width // math.gcd(width, 2 * LANES)
    own = pl.BlockSpec(memory_space=pl.ANY)
    return pl.pallas_call(
        functools.partial(composite_kernel, total, slab_len, near),
        in_specs=[own] * (3 + near),
        out_specs=own,
        out_shape=jax.ShapeDtypeStruct((4, rows, width), jnp.float32),
        scratch_shapes=[
            pltpu.SMEM(depth_order.shape, depth_order.dtype),
            pltpu.SMEM(transfer.shape, transfer.dtype),
            pltpu.VMEM(codes.shape, codes.dtype),
            pltpu.VMEM((4, rows, width), jnp.float32),
            pltpu.SemaphoreType.DMA((2 + near + (count // near - 1 if near else 1),)),
            pltpu.SemaphoreType.DMA((blocks,)),
        ],
        compiler_params=pltpu.CompilerParams(vmem_limit_bytes=SMALL_BYTES),
        name="composite",
    )(depth_order, transfer, codes, *near_codes)


def on_device(field, jitter, transfer, depth_order, ray_start, ray_end):
    count = lax.axis_size("depth")
    slab_len, rows, cols = field.shape
    total = slab_len * count
    width = cols // count
    near = NEAR if width == UNIT and count == 2 * NEAR else 0
    halo = shifted(field[0], "depth", -1)
    codes, near_codes = slab_codes(field, halo, jitter, transfer, ray_start, ray_end, total, near)
    if width != UNIT:
        codes = codes.transpose(1, 2, 0, 3).reshape(4, rows, count, width).transpose(2, 0, 1, 3)
    received = lax.all_to_all(codes, "depth", split_axis=0, concat_axis=0, tiled=True)
    swapped = [lax.ppermute(near_codes[n], "depth", [(i, i ^ n) for i in range(count)]) for n in reversed(range(1, near))]
    return composite(received, [*swapped, *near_codes[:1]], transfer, depth_order, total, slab_len)


def solution(mesh):
    in_specs = (P("depth", "groups", None), P("groups", None), P(), P(), P(), P())
    out_specs = P(None, "groups", "depth")
    return jax.shard_map(
        on_device, mesh=mesh, in_specs=in_specs, out_specs=out_specs, check_vma=False
    )
```

```python
import functools
import math

import jax
import jax.numpy as jnp
from jax import lax
from jax.experimental import pallas as pl
from jax.experimental.pallas import tpu as pltpu
from jax.sharding import PartitionSpec as P

TOP = 5.2
LOG2E = math.log2(math.e)
SUBLANES = 8
LANES = 128
FAR = 1.0e4
UNIT = 512
NEAR = 8
OPEN_BYTES = 54 * 1024 * 1024
CLOSE_BYTES = 53 * 1024 * 1024
SMALL_BYTES = 16 * 1024 * 1024


def spans(slab_len):
    deep = math.log2(slab_len)
    return 6.8 + deep, 13.2 + deep


def lift(span):
    return span * (32768.0 / 65535.0) - span


def shifted(value, axis, steps):
    count = lax.axis_size(axis)
    initial, last = (max(0, -steps), min(count, count - steps))
    return lax.ppermute(value, axis, [(source, source + steps) for source in range(initial, last)])


def encode(value, span):
    code = jnp.log2(value) * (65535.0 / span) + 65535.5
    code = jnp.minimum(jnp.maximum(code, 0.0), 65535.0)
    return (code.astype(jnp.int32) - 32768).astype(jnp.int16)


def tile_gains(gain_ref, gain, base, tile_cols, start_ref, end_ref, piece_of):
    sample = lax.broadcasted_iota(jnp.int32, (SUBLANES, LANES), 0) + base
    lane = lax.broadcasted_iota(jnp.int32, (SUBLANES, LANES), 1)

    def block(n, carry):
        blocks = UNIT // LANES
        tile = (piece_of(n // blocks) * UNIT + n % blocks * LANES) // tile_cols
        start = jnp.full((SUBLANES, LANES), start_ref[tile])
        end = jnp.full((SUBLANES, LANES), end_ref[tile])
        for t in range(1, LANES // tile_cols):
            start = jnp.where(lane >= t * tile_cols, start_ref[tile + t], start)
            end = jnp.where(lane >= t * tile_cols, end_ref[tile + t], end)
        cols = pl.ds(pl.multiple_of(n * LANES, LANES), LANES)
        for k in range(0, gain_ref.shape[0], SUBLANES):
            active = (sample + k >= start) & (sample + k < end)
            gain_ref[k:k + SUBLANES, cols] = jnp.where(active, gain, 0.0)
        return carry

    blocks = gain_ref.shape[1] // LANES
    lax.fori_loop(0, blocks, block, 0, unroll=math.gcd(blocks, 8))


def moment(sums, weight, value, levels):
    whole = (levels[0] + value) * (levels[1] + value) * (levels[2] + value)
    share = weight * pl.reciprocal(whole, approx=True, full_range=False)
    for n in range(3):
        sums[n] = sums[n] + share
        share = share * value


def colors(sums, before, levels):
    emitted = 1.0 - jnp.exp2(before)
    others = [(levels[1], levels[2]), (levels[2], levels[0]), (levels[0], levels[1])]
    return [emitted - t * (sums[2] + (p + q) * sums[1] + (p * q) * sums[0]) for t, (p, q) in zip(levels, others)]


def march(gain_ref, plane_ref, unit, cols, place, jitter, levels, halo=None):
    slab_len = plane_ref.shape[1]
    shape = jitter.shape
    before = jnp.zeros(shape, jnp.float32)
    through = jnp.ones(shape, jnp.float32)
    sums = [jnp.zeros(shape, jnp.float32) for _ in range(3)]
    lower = plane_ref[unit, 0, :, cols].astype(jnp.float32)
    stay = lower - jitter * lower
    for k in range(slab_len - (halo is None)):
        following = plane_ref[unit, k + 1, :, cols] if k + 1 < slab_len else halo
        upper = following.astype(jnp.float32)
        moved = jitter * upper
        value = stay + moved
        before = before + gain_ref[k:k + 1, place] * value
        beyond = jnp.exp2(before)
        moment(sums, through - beyond, value, levels)
        through = beyond
        stay = upper - moved
    return sums, before


def loop(count, body):
    def step(n, carry):
        body(n)
        return carry

    lax.fori_loop(0, count, step, 0)


def each_group(units, group, arrive, compute, store, leave):
    def step(n):
        places = [(group * n + u, c) for u in range(group) for c in range(0, UNIT, LANES)]
        arrive(n)
        results = [compute(unit, pl.ds(c, LANES), pl.ds(pl.multiple_of(unit * UNIT + c, LANES), LANES)) for unit, c in places]
        for (unit, c), result in zip(places, results):
            store(unit, pl.ds(c, LANES), result)
        leave(n)

    loop(units // group, step)


def start_all(pairs, sems):
    copies = [pltpu.make_async_copy(src, dst, sems.at[n]) for n, (src, dst) in enumerate(pairs)]
    for copy in copies:
        copy.start()
    return copies


class Pieces:
    def __init__(self, near):
        self.near = near
        self.here = lax.axis_index("depth")

    def far(self, n):
        if not self.near:
            return n
        return n + jnp.where(n >= self.here // self.near * self.near, self.near, 0)

    def close(self, top, jump, unit):
        return self.here ^ (top - unit - jnp.where(unit >= jump, 2, 0))

    def close_first(self):
        return self.here // self.near * self.near


def columns(piece, col=0, size=UNIT):
    return pl.ds(pl.multiple_of(piece * UNIT + col, LANES), size)


def field_copy(field_any, plane_ref, sems, piece_of, unit):
    return pltpu.make_async_copy(field_any.at[:, :, columns(piece_of(unit))], plane_ref.at[unit], sems.at[unit])


def arrive_pair(arrival, n):
    for u in range(2):
        arrival(2 * n + u).wait()


def open_kernel(total, tile_cols, near, transfer_any, start_any, end_any, field_any, jitter_any, state_any, transfer_ref,
                start_ref, end_ref, plane_ref, jitter_ref, state_ref, gain_ref, few_sems, sems, out_sems):
    units, slab_len, rows, _ = plane_ref.shape
    piece_of = Pieces(near).far
    arrival = functools.partial(field_copy, field_any, plane_ref, sems, piece_of)
    for unit in range(2):
        arrival(unit).start()
    pairs = [(transfer_any, transfer_ref), (start_any, start_ref), (end_any, end_ref)]
    pairs.append((jitter_any.at[:, columns(piece_of(0), 0, units * UNIT)], jitter_ref))
    *early, jitter_copy = start_all(pairs, few_sems)
    base = lax.axis_index("depth") * slab_len
    for copy in early:
        copy.wait()
    levels = [jnp.full((rows, LANES), transfer_ref[i]) for i in range(3)]
    gain = jnp.full((SUBLANES, LANES), transfer_ref[3]) * (-LOG2E * 0.2 / total)
    for unit in range(2, units):
        arrival(unit).start()
    tile_gains(gain_ref, gain, base, tile_cols, start_ref, end_ref, piece_of)
    jitter_copy.wait()

    def compute(unit, cols, place):
        return march(gain_ref, plane_ref, unit, cols, place, jitter_ref[:, place], levels)

    def store(unit, cols, result):
        sums, before = result
        for i, value in enumerate([*sums, before]):
            state_ref[unit, i, :, cols] = value

    def leave(n):
        place = pl.ds(2 * n, 2)
        return pltpu.make_async_copy(state_ref.at[place], state_any.at[place], out_sems.at[n])

    each_group(units, 2, functools.partial(arrive_pair, arrival), compute, store, lambda n: leave(n).start())
    loop(units // 2, lambda n: leave(n).wait())


class Coder:
    def __init__(self, total, slab_len, shape, transfer_ref):
        depth_gain = jnp.full(shape, transfer_ref[3]) * (0.2 / total)
        self.levels = [jnp.full(shape, transfer_ref[i]) for i in range(3)]
        self.depth_unit = 1.0 / (depth_gain * (slab_len * TOP))
        self.color_unit = [self.depth_unit * ((self.levels[i] + TOP) * (1.0 / TOP)) for i in range(3)]
        self.depth_span, self.color_span = spans(slab_len)
        self.gain = depth_gain[:SUBLANES] * -LOG2E

    def codes(self, sums, before):
        tints = colors(sums, before, self.levels)
        codes = [encode(color * unit, self.color_span) for color, unit in zip(tints, self.color_unit)]
        return codes + [encode(before * (self.depth_unit * (-1.0 / LOG2E)), self.depth_span)]


def close_kernel(total, tile_cols, near, opened, transfer_any, start_any, end_any, field_any, halo_any, jitter_any, state_any,
                 out_any, transfer_ref, start_ref, end_ref, plane_ref, halo_ref, jitter_ref, out_ref, gain_ref, state_ref,
                 last_ref, last_gain_ref, few_sems, sems, out_sems):
    units, slab_len, rows, _ = plane_ref.shape
    piece_of = Pieces(near).far
    later = lambda unit: piece_of(opened + unit)
    arrival = functools.partial(field_copy, field_any, plane_ref, sems, later)
    for unit in range(2):
        arrival(unit).start()
    mine = columns(piece_of(0), 0, (opened + units) * UNIT)
    pairs = [(transfer_any, transfer_ref), (start_any, start_ref), (end_any, end_ref)]
    pairs += [(jitter_any.at[:, mine], jitter_ref), (halo_any.at[:, mine], halo_ref), (state_any, state_ref)]
    pairs.append((field_any.at[slab_len - 1, :, columns(piece_of(0), 0, opened * UNIT)], last_ref))
    copies = start_all(pairs, few_sems)
    base = lax.axis_index("depth") * slab_len
    for copy in copies[:3]:
        copy.wait()
    coder = Coder(total, slab_len, (rows, LANES), transfer_ref)
    for unit in range(2, units):
        arrival(unit).start()
    tile_gains(gain_ref, coder.gain, base, tile_cols, start_ref, end_ref, later)
    tile_gains(last_gain_ref, coder.gain, base + slab_len - 1, tile_cols, start_ref, end_ref, piece_of)
    for copy in copies[3:5]:
        copy.wait()

    def compute(unit, cols, place):
        whole = columns(opened + unit, cols.start, LANES)
        jitter = jitter_ref[:, whole]
        return coder.codes(*march(gain_ref, plane_ref, unit, cols, place, jitter, coder.levels, halo_ref[:, whole]))

    def store(first, unit, cols, codes):
        for i, code in enumerate(codes):
            out_ref[first + unit, i, :, cols] = code

    def leave(unit):
        return pltpu.make_async_copy(out_ref.at[unit], out_any.at[piece_of(unit)], out_sems.at[unit])

    def leave_pair(first, n):
        for u in range(2):
            leave(first + 2 * n + u).start()

    each_group(units, 2, functools.partial(arrive_pair, arrival), compute, functools.partial(store, opened),
              functools.partial(leave_pair, opened))
    for copy in copies[5:]:
        copy.wait()

    def finish(unit, cols, place):
        jitter = jitter_ref[:, place]
        lower = last_ref[:, place].astype(jnp.float32)
        upper = halo_ref[:, place].astype(jnp.float32)
        value = (1.0 - jitter) * lower + jitter * upper
        before = state_ref[unit, 3, :, cols]
        beyond = before + last_gain_ref[0:1, place] * value
        weight = jnp.exp2(before) - jnp.exp2(beyond)
        sums = [state_ref[unit, i, :, cols] for i in range(3)]
        moment(sums, weight, value, coder.levels)
        return coder.codes(sums, beyond)

    group = math.gcd(opened, 3)

    def leave_finished(n):
        for u in range(group):
            leave(group * n + u).start()

    each_group(opened, group, lambda n: None, finish, functools.partial(store, 0), leave_finished)
    loop(out_ref.shape[0], lambda unit: leave(unit).wait())


def near_kernel(total, tile_cols, near, top, jump, transfer_any, start_any, end_any, field_any, halo_any, jitter_any, prior_any,
                *refs):
    del prior_any
    out_anys, refs = refs[:-11], refs[-11:]
    transfer_ref, start_ref, end_ref, plane_ref, halo_ref, jitter_ref, out_ref, gain_ref, few_sems, sems, out_sems = refs
    units, slab_len, rows, _ = plane_ref.shape
    piece_of = functools.partial(Pieces(near).close, top, jump)
    arrival = functools.partial(field_copy, field_any, plane_ref, sems, piece_of)
    for unit in range(2):
        arrival(unit).start()
    first = Pieces(near).close_first()
    mine = columns(first, 0, near * UNIT)
    pairs = [(transfer_any, transfer_ref), (start_any, start_ref), (end_any, end_ref)]
    copies = start_all(pairs + [(jitter_any.at[:, mine], jitter_ref), (halo_any.at[:, mine], halo_ref)], few_sems)
    base = lax.axis_index("depth") * slab_len
    for copy in copies[:3]:
        copy.wait()
    coder = Coder(total, slab_len, (rows, LANES), transfer_ref)
    for unit in range(2, units):
        arrival(unit).start()
    tile_gains(gain_ref, coder.gain, base, tile_cols, start_ref, end_ref, piece_of)
    for copy in copies[3:]:
        copy.wait()

    def compute(unit, cols, place):
        whole = columns(piece_of(unit) - first, cols.start, LANES)
        jitter = jitter_ref[:, whole]
        return coder.codes(*march(gain_ref, plane_ref, unit, cols, place, jitter, coder.levels, halo_ref[:, whole]))

    def store(unit, cols, codes):
        for i, code in enumerate(codes):
            out_ref[unit, i, :, cols] = code

    each_group(units, 2, functools.partial(arrive_pair, arrival), compute, store, lambda n: None)
    pairs = [(out_ref.at[unit], out_anys[unit]) for unit in range(units)]
    for copy in start_all(pairs, out_sems):
        copy.wait()


def slab_codes(field, halo, jitter, transfer, ray_start, ray_end, total, near):
    slab_len, rows, cols = field.shape
    pieces = cols // UNIT
    opened = pieces * 3 // 16 * 2
    closed = pieces - near - opened
    ntiles = ray_start.shape[0]
    tile_cols = cols // ntiles
    own = pl.BlockSpec(memory_space=pl.ANY)
    scalars = [pltpu.SMEM(transfer.shape, transfer.dtype)] + [pltpu.SMEM((ntiles,), jnp.int32)] * 2

    def cost(units):
        work = slab_len * rows * units * UNIT
        return pl.CostEstimate(flops=work * 20, bytes_accessed=work * 2, transcendentals=work * 2)

    def planes(units):
        return pltpu.VMEM((units, slab_len, rows, UNIT), field.dtype)

    def flat(units, dtype):
        return pltpu.VMEM((rows, units * UNIT), dtype)

    def table(samples, units):
        return pltpu.VMEM((samples, units * UNIT), jnp.float32)

    state_shape = (opened, 4, rows, UNIT)
    state = pl.pallas_call(
        functools.partial(open_kernel, total, tile_cols, near),
        in_specs=[own] * 5,
        out_specs=own,
        out_shape=jax.ShapeDtypeStruct(state_shape, jnp.float32),
        scratch_shapes=scalars + [
            planes(opened), flat(opened, jnp.float32), pltpu.VMEM(state_shape, jnp.float32), table(slab_len, opened),
            pltpu.SemaphoreType.DMA((4,)),
            pltpu.SemaphoreType.DMA((opened,)),
            pltpu.SemaphoreType.DMA((opened // 2,)),
        ],
        compiler_params=pltpu.CompilerParams(vmem_limit_bytes=OPEN_BYTES),
        cost_estimate=cost(opened),
        name="open",
    )(transfer, ray_start, ray_end, field, jitter)
    far = pl.pallas_call(
        functools.partial(close_kernel, total, tile_cols, near, opened),
        in_specs=[own] * 7,
        out_specs=own,
        out_shape=jax.ShapeDtypeStruct((pieces, 4, rows, UNIT), jnp.int16),
        scratch_shapes=scalars + [
            planes(closed), flat(opened + closed, field.dtype), flat(opened + closed, jnp.float32),
            pltpu.VMEM((opened + closed, 4, rows, UNIT), jnp.int16), table(slab_len, closed),
            pltpu.VMEM(state_shape, jnp.float32), flat(opened, field.dtype), table(SUBLANES, opened),
            pltpu.SemaphoreType.DMA((7,)),
            pltpu.SemaphoreType.DMA((closed,)),
            pltpu.SemaphoreType.DMA((opened + closed,)),
        ],
        compiler_params=pltpu.CompilerParams(vmem_limit_bytes=CLOSE_BYTES),
        cost_estimate=cost(closed),
        name="close",
    )(transfer, ray_start, ray_end, field, halo, jitter, state)

    def near_codes(top, jump, units, prior):
        return pl.pallas_call(
            functools.partial(near_kernel, total, tile_cols, near, top, jump),
            in_specs=[own] * 7,
            out_specs=[own] * units,
            out_shape=[jax.ShapeDtypeStruct((4, rows, UNIT), jnp.int16)] * units,
            scratch_shapes=scalars + [
                planes(units), flat(near, field.dtype), flat(near, jnp.float32),
                pltpu.VMEM((units, 4, rows, UNIT), jnp.int16), table(slab_len, units),
                pltpu.SemaphoreType.DMA((5,)),
                pltpu.SemaphoreType.DMA((units,)),
                pltpu.SemaphoreType.DMA((units,)),
            ],
            compiler_params=pltpu.CompilerParams(vmem_limit_bytes=CLOSE_BYTES),
            cost_estimate=cost(units),
            name="near",
        )(transfer, ray_start, ray_end, field, halo, jitter, prior)

    return far, near_codes


def composite_kernel(total, slab_len, nears, order_any, transfer_any, code_any, *refs):
    near = len(nears)
    near_anys = refs[:near]
    image_any, order_ref, transfer_ref, code_ref, out_ref, sems, out_sems = refs[near:]
    count, _, rows, width = code_ref.shape
    here = lax.axis_index("depth")
    pairs = [(near_any, code_ref.at[here ^ n]) for n, near_any in zip(nears, near_anys)]
    if near:
        for n in range(count // near - 1):
            group = n + jnp.where(n >= here // near, 1, 0)
            slabs = pl.ds(group * near, near)
            pairs.append((code_any.at[slabs], code_ref.at[slabs]))
    else:
        pairs.append((code_any, code_ref))
    copies = start_all([(order_any, order_ref), (transfer_any, transfer_ref)] + pairs, sems)
    block = math.gcd(width, 2 * LANES)
    places = [pl.ds(col, block) for col in range(0, width, block)]
    shape = (rows, block)
    depth_span, color_span = spans(slab_len)
    for copy in copies:
        copy.wait()
    unit = jnp.full(shape, transfer_ref[3]) * (0.2 / total * slab_len * TOP)
    depth_unit = unit * LOG2E
    leaving = []
    for n, cols in enumerate(places):

        def number(slab, channel, span):
            return code_ref[slab, channel, :, cols].astype(jnp.int32).astype(jnp.float32) * (span / 65535.0)

        def step(j, carry):
            shift, *colors = carry
            slab = order_ref[j]
            code = number(slab, 3, depth_span)
            idle = code < depth_span * (-32767.5 / 65535.0)
            away = jnp.where(idle, FAR, shift)
            for i in range(3):
                colors[i] = colors[i] + jnp.exp2(number(slab, i, color_span) - away)
            own = jnp.where(idle, 0.0, jnp.exp2(code + lift(depth_span)))
            return shift + depth_unit * own, *colors

        zero = jnp.zeros(shape, jnp.float32)
        first = jnp.full(shape, -lift(color_span))
        shift, *colors = lax.fori_loop(0, count, step, (first, zero, zero, zero), unroll=math.gcd(count, 16))
        for i in range(3):
            out_ref[i, :, cols] = colors[i] * (unit * (TOP / (transfer_ref[i] + jnp.full(shape, TOP))))
        out_ref[3, :, cols] = 1.0 - jnp.exp2(first - shift)
        leaving.append(pltpu.make_async_copy(out_ref.at[:, :, cols], image_any.at[:, :, cols], out_sems.at[n]))
        leaving[-1].start()
    for copy in leaving:
        copy.wait()


def composite(codes, near_codes, transfer, depth_order, total, slab_len):
    count, _, rows, width = codes.shape
    near = len(near_codes)
    blocks = width // math.gcd(width, 2 * LANES)
    own = pl.BlockSpec(memory_space=pl.ANY)
    return pl.pallas_call(
        functools.partial(composite_kernel, total, slab_len, tuple(near_codes)),
        in_specs=[own] * (3 + near),
        out_specs=own,
        out_shape=jax.ShapeDtypeStruct((4, rows, width), jnp.float32),
        scratch_shapes=[
            pltpu.SMEM(depth_order.shape, depth_order.dtype),
            pltpu.SMEM(transfer.shape, transfer.dtype),
            pltpu.VMEM(codes.shape, codes.dtype),
            pltpu.VMEM((4, rows, width), jnp.float32),
            pltpu.SemaphoreType.DMA((2 + near + (count // near - 1 if near else 1),)),
            pltpu.SemaphoreType.DMA((blocks,)),
        ],
        compiler_params=pltpu.CompilerParams(vmem_limit_bytes=SMALL_BYTES),
        name="composite",
    )(depth_order, transfer, codes, *near_codes.values())


def on_device(field, jitter, transfer, depth_order, ray_start, ray_end):
    count = lax.axis_size("depth")
    slab_len, rows, cols = field.shape
    total = slab_len * count
    width = cols // count
    near = NEAR if width == UNIT and count == 2 * NEAR else 0
    halo = shifted(field[0], "depth", -1)
    codes, codes_near = slab_codes(field, halo, jitter, transfer, ray_start, ray_end, total, near)
    if width != UNIT:
        codes = codes.transpose(1, 2, 0, 3).reshape(4, rows, count, width).transpose(2, 0, 1, 3)
    received = lax.all_to_all(codes, "depth", split_axis=0, concat_axis=0, tiled=True)
    if not near:
        return composite(received, {}, transfer, depth_order, total, slab_len)

    def swapped(codes, n):
        return lax.ppermute(codes, "depth", [(i, i ^ n) for i in range(count)])

    top = near - 1
    first = codes_near(top, near - 4, near - 2, codes)
    near_codes = {top - n: swapped(first[n], top - n) for n in range(near - 4)}
    near_codes[1] = swapped(first[near - 4], 1)
    second = codes_near(3, 2, 2, near_codes[1])
    near_codes.update({3: swapped(second[0], 3), 2: swapped(second[1], 2), 0: first[near - 3]})
    return composite(received, near_codes, transfer, depth_order, total, slab_len)


def solution(mesh):
    in_specs = (P("depth", "groups", None), P("groups", None), P(), P(), P(), P())
    out_specs = P(None, "groups", "depth")
    return jax.shard_map(
        on_device, mesh=mesh, in_specs=in_specs, out_specs=out_specs, check_vma=False
    )
```

```python
import functools
import math

import jax
import jax.numpy as jnp
from jax import lax
from jax.experimental import pallas as pl
from jax.experimental.pallas import tpu as pltpu
from jax.sharding import PartitionSpec as P

TOP = 5.2
LOG2E = math.log2(math.e)
SUBLANES = 8
LANES = 128
FAR = 1.0e4
UNIT = 512
NEAR = 8
OPEN_BYTES = 54 * 1024 * 1024
CLOSE_BYTES = 53 * 1024 * 1024
SMALL_BYTES = 16 * 1024 * 1024


def spans(slab_len):
    deep = math.log2(slab_len)
    return 6.8 + deep, 13.2 + deep


def lift(span):
    return span * (32768.0 / 65535.0) - span


def shifted(value, axis, steps):
    count = lax.axis_size(axis)
    initial, last = (max(0, -steps), min(count, count - steps))
    return lax.ppermute(value, axis, [(source, source + steps) for source in range(initial, last)])


def encode(value, span):
    code = jnp.log2(value) * (65535.0 / span) + 65535.5
    code = jnp.minimum(jnp.maximum(code, 0.0), 65535.0)
    return (code.astype(jnp.int32) - 32768).astype(jnp.int16)


def tile_gains(gain_ref, gain, base, tile_cols, start_ref, end_ref, piece_of):
    sample = lax.broadcasted_iota(jnp.int32, (SUBLANES, LANES), 0) + base
    lane = lax.broadcasted_iota(jnp.int32, (SUBLANES, LANES), 1)

    def block(n, carry):
        blocks = UNIT // LANES
        tile = (piece_of(n // blocks) * UNIT + n % blocks * LANES) // tile_cols
        start = jnp.full((SUBLANES, LANES), start_ref[tile])
        end = jnp.full((SUBLANES, LANES), end_ref[tile])
        for t in range(1, LANES // tile_cols):
            start = jnp.where(lane >= t * tile_cols, start_ref[tile + t], start)
            end = jnp.where(lane >= t * tile_cols, end_ref[tile + t], end)
        cols = pl.ds(pl.multiple_of(n * LANES, LANES), LANES)
        for k in range(0, gain_ref.shape[0], SUBLANES):
            active = (sample + k >= start) & (sample + k < end)
            gain_ref[k:k + SUBLANES, cols] = jnp.where(active, gain, 0.0)
        return carry

    blocks = gain_ref.shape[1] // LANES
    lax.fori_loop(0, blocks, block, 0, unroll=math.gcd(blocks, 8))


def moment(sums, weight, value, levels):
    whole = (levels[0] + value) * (levels[1] + value) * (levels[2] + value)
    share = weight * pl.reciprocal(whole, approx=True, full_range=False)
    for n in range(3):
        sums[n] = sums[n] + share
        share = share * value


def colors(sums, before, levels):
    emitted = 1.0 - jnp.exp2(before)
    others = [(levels[1], levels[2]), (levels[2], levels[0]), (levels[0], levels[1])]
    return [emitted - t * (sums[2] + (p + q) * sums[1] + (p * q) * sums[0]) for t, (p, q) in zip(levels, others)]


def march(gain_ref, plane_ref, unit, cols, place, jitter, levels, halo=None):
    slab_len = plane_ref.shape[1]
    shape = jitter.shape
    before = jnp.zeros(shape, jnp.float32)
    through = jnp.ones(shape, jnp.float32)
    sums = [jnp.zeros(shape, jnp.float32) for _ in range(3)]
    lower = plane_ref[unit, 0, :, cols].astype(jnp.float32)
    stay = lower - jitter * lower
    for k in range(slab_len - (halo is None)):
        following = plane_ref[unit, k + 1, :, cols] if k + 1 < slab_len else halo
        upper = following.astype(jnp.float32)
        moved = jitter * upper
        value = stay + moved
        before = before + gain_ref[k:k + 1, place] * value
        beyond = jnp.exp2(before)
        moment(sums, through - beyond, value, levels)
        through = beyond
        stay = upper - moved
    return sums, before


def loop(count, body):
    def step(n, carry):
        body(n)
        return carry

    lax.fori_loop(0, count, step, 0)


def each_group(units, group, arrive, compute, store, leave):
    def step(n):
        places = [(group * n + u, c) for u in range(group) for c in range(0, UNIT, LANES)]
        arrive(n)
        results = [compute(unit, pl.ds(c, LANES), pl.ds(pl.multiple_of(unit * UNIT + c, LANES), LANES)) for unit, c in places]
        for (unit, c), result in zip(places, results):
            store(unit, pl.ds(c, LANES), result)
        leave(n)

    loop(units // group, step)


def start_all(pairs, sems):
    copies = [pltpu.make_async_copy(src, dst, sems.at[n]) for n, (src, dst) in enumerate(pairs)]
    for copy in copies:
        copy.start()
    return copies


class Pieces:
    def __init__(self, near):
        self.near = near
        self.here = lax.axis_index("depth")

    def far(self, n):
        if not self.near:
            return n
        return n + jnp.where(n >= self.here // self.near * self.near, self.near, 0)

    def close(self, n):
        return self.here ^ n

    def close_first(self):
        return self.here // self.near * self.near


def columns(piece, col=0, size=UNIT):
    return pl.ds(pl.multiple_of(piece * UNIT + col, LANES), size)


def field_copy(field_any, plane_ref, sems, piece_of, unit):
    return pltpu.make_async_copy(field_any.at[:, :, columns(piece_of(unit))], plane_ref.at[unit], sems.at[unit])


def arrive_pair(arrival, n):
    for u in range(2):
        arrival(2 * n + u).wait()


def open_kernel(total, tile_cols, near, transfer_any, start_any, end_any, field_any, jitter_any, state_any, transfer_ref,
                start_ref, end_ref, plane_ref, jitter_ref, state_ref, gain_ref, few_sems, sems, out_sems):
    units, slab_len, rows, _ = plane_ref.shape
    piece_of = Pieces(near).far
    arrival = functools.partial(field_copy, field_any, plane_ref, sems, piece_of)
    for unit in range(2):
        arrival(unit).start()
    pairs = [(transfer_any, transfer_ref), (start_any, start_ref), (end_any, end_ref)]
    pairs.append((jitter_any.at[:, columns(piece_of(0), 0, units * UNIT)], jitter_ref))
    *early, jitter_copy = start_all(pairs, few_sems)
    base = lax.axis_index("depth") * slab_len
    for copy in early:
        copy.wait()
    levels = [jnp.full((rows, LANES), transfer_ref[i]) for i in range(3)]
    gain = jnp.full((SUBLANES, LANES), transfer_ref[3]) * (-LOG2E * 0.2 / total)
    for unit in range(2, units):
        arrival(unit).start()
    tile_gains(gain_ref, gain, base, tile_cols, start_ref, end_ref, piece_of)
    jitter_copy.wait()

    def compute(unit, cols, place):
        return march(gain_ref, plane_ref, unit, cols, place, jitter_ref[:, place], levels)

    def store(unit, cols, result):
        sums, before = result
        for i, value in enumerate([*sums, before]):
            state_ref[unit, i, :, cols] = value

    def leave(n):
        place = pl.ds(2 * n, 2)
        return pltpu.make_async_copy(state_ref.at[place], state_any.at[place], out_sems.at[n])

    each_group(units, 2, functools.partial(arrive_pair, arrival), compute, store, lambda n: leave(n).start())
    loop(units // 2, lambda n: leave(n).wait())


class Coder:
    def __init__(self, total, slab_len, shape, transfer_ref):
        depth_gain = jnp.full(shape, transfer_ref[3]) * (0.2 / total)
        self.levels = [jnp.full(shape, transfer_ref[i]) for i in range(3)]
        self.depth_unit = 1.0 / (depth_gain * (slab_len * TOP))
        self.color_unit = [self.depth_unit * ((self.levels[i] + TOP) * (1.0 / TOP)) for i in range(3)]
        self.depth_span, self.color_span = spans(slab_len)
        self.gain = depth_gain[:SUBLANES] * -LOG2E

    def codes(self, sums, before):
        tints = colors(sums, before, self.levels)
        codes = [encode(color * unit, self.color_span) for color, unit in zip(tints, self.color_unit)]
        return codes + [encode(before * (self.depth_unit * (-1.0 / LOG2E)), self.depth_span)]


def close_kernel(total, tile_cols, near, opened, transfer_any, start_any, end_any, field_any, halo_any, jitter_any, state_any,
                 out_any, transfer_ref, start_ref, end_ref, plane_ref, halo_ref, jitter_ref, out_ref, gain_ref, state_ref,
                 last_ref, last_gain_ref, few_sems, sems, out_sems):
    units, slab_len, rows, _ = plane_ref.shape
    piece_of = Pieces(near).far
    later = lambda unit: piece_of(opened + unit)
    arrival = functools.partial(field_copy, field_any, plane_ref, sems, later)
    for unit in range(2):
        arrival(unit).start()
    mine = columns(piece_of(0), 0, (opened + units) * UNIT)
    pairs = [(transfer_any, transfer_ref), (start_any, start_ref), (end_any, end_ref)]
    pairs += [(jitter_any.at[:, mine], jitter_ref), (halo_any.at[:, mine], halo_ref), (state_any, state_ref)]
    pairs.append((field_any.at[slab_len - 1, :, columns(piece_of(0), 0, opened * UNIT)], last_ref))
    copies = start_all(pairs, few_sems)
    base = lax.axis_index("depth") * slab_len
    for copy in copies[:3]:
        copy.wait()
    coder = Coder(total, slab_len, (rows, LANES), transfer_ref)
    for unit in range(2, units):
        arrival(unit).start()
    tile_gains(gain_ref, coder.gain, base, tile_cols, start_ref, end_ref, later)
    tile_gains(last_gain_ref, coder.gain, base + slab_len - 1, tile_cols, start_ref, end_ref, piece_of)
    for copy in copies[3:5]:
        copy.wait()

    def compute(unit, cols, place):
        whole = columns(opened + unit, cols.start, LANES)
        jitter = jitter_ref[:, whole]
        return coder.codes(*march(gain_ref, plane_ref, unit, cols, place, jitter, coder.levels, halo_ref[:, whole]))

    def store(first, unit, cols, codes):
        for i, code in enumerate(codes):
            out_ref[first + unit, i, :, cols] = code

    def leave(unit):
        return pltpu.make_async_copy(out_ref.at[unit], out_any.at[piece_of(unit)], out_sems.at[unit])

    def leave_pair(first, n):
        for u in range(2):
            leave(first + 2 * n + u).start()

    each_group(units, 2, functools.partial(arrive_pair, arrival), compute, functools.partial(store, opened),
              functools.partial(leave_pair, opened))
    for copy in copies[5:]:
        copy.wait()

    def finish(unit, cols, place):
        jitter = jitter_ref[:, place]
        lower = last_ref[:, place].astype(jnp.float32)
        upper = halo_ref[:, place].astype(jnp.float32)
        value = (1.0 - jitter) * lower + jitter * upper
        before = state_ref[unit, 3, :, cols]
        beyond = before + last_gain_ref[0:1, place] * value
        weight = jnp.exp2(before) - jnp.exp2(beyond)
        sums = [state_ref[unit, i, :, cols] for i in range(3)]
        moment(sums, weight, value, coder.levels)
        return coder.codes(sums, beyond)

    group = math.gcd(opened, 3)

    def leave_finished(n):
        for u in range(group):
            leave(group * n + u).start()

    each_group(opened, group, lambda n: None, finish, functools.partial(store, 0), leave_finished)
    loop(out_ref.shape[0], lambda unit: leave(unit).wait())


def near_kernel(total, tile_cols, near, transfer_any, start_any, end_any, field_any, halo_any, jitter_any, far_any, *refs):
    del far_any
    out_anys = refs[:near]
    transfer_ref, start_ref, end_ref, plane_ref, halo_ref, jitter_ref, out_ref, gain_ref, few_sems, sems, out_sems = refs[near:]
    units, slab_len, rows, _ = plane_ref.shape
    piece_of = Pieces(near).close
    arrival = functools.partial(field_copy, field_any, plane_ref, sems, piece_of)
    for unit in range(2):
        arrival(unit).start()
    first = Pieces(near).close_first()
    mine = columns(first, 0, near * UNIT)
    pairs = [(transfer_any, transfer_ref), (start_any, start_ref), (end_any, end_ref)]
    copies = start_all(pairs + [(jitter_any.at[:, mine], jitter_ref), (halo_any.at[:, mine], halo_ref)], few_sems)
    base = lax.axis_index("depth") * slab_len
    for copy in copies[:3]:
        copy.wait()
    coder = Coder(total, slab_len, (rows, LANES), transfer_ref)
    for unit in range(2, units):
        arrival(unit).start()
    tile_gains(gain_ref, coder.gain, base, tile_cols, start_ref, end_ref, piece_of)
    for copy in copies[3:]:
        copy.wait()

    def compute(unit, cols, place):
        whole = columns(piece_of(unit) - first, cols.start, LANES)
        jitter = jitter_ref[:, whole]
        return coder.codes(*march(gain_ref, plane_ref, unit, cols, place, jitter, coder.levels, halo_ref[:, whole]))

    def store(unit, cols, codes):
        for i, code in enumerate(codes):
            out_ref[unit, i, :, cols] = code

    each_group(units, 2, functools.partial(arrive_pair, arrival), compute, store, lambda n: None)
    pairs = [(out_ref.at[unit], out_anys[unit]) for unit in range(units)]
    for copy in start_all(pairs, out_sems):
        copy.wait()


def slab_codes(field, halo, jitter, transfer, ray_start, ray_end, total, near):
    slab_len, rows, cols = field.shape
    pieces = cols // UNIT
    opened = pieces * 3 // 16 * 2
    closed = pieces - near - opened
    ntiles = ray_start.shape[0]
    tile_cols = cols // ntiles
    own = pl.BlockSpec(memory_space=pl.ANY)
    scalars = [pltpu.SMEM(transfer.shape, transfer.dtype)] + [pltpu.SMEM((ntiles,), jnp.int32)] * 2

    def cost(units):
        work = slab_len * rows * units * UNIT
        return pl.CostEstimate(flops=work * 20, bytes_accessed=work * 2, transcendentals=work * 2)

    def planes(units):
        return pltpu.VMEM((units, slab_len, rows, UNIT), field.dtype)

    def flat(units, dtype):
        return pltpu.VMEM((rows, units * UNIT), dtype)

    def table(samples, units):
        return pltpu.VMEM((samples, units * UNIT), jnp.float32)

    state_shape = (opened, 4, rows, UNIT)
    state = pl.pallas_call(
        functools.partial(open_kernel, total, tile_cols, near),
        in_specs=[own] * 5,
        out_specs=own,
        out_shape=jax.ShapeDtypeStruct(state_shape, jnp.float32),
        scratch_shapes=scalars + [
            planes(opened), flat(opened, jnp.float32), pltpu.VMEM(state_shape, jnp.float32), table(slab_len, opened),
            pltpu.SemaphoreType.DMA((4,)),
            pltpu.SemaphoreType.DMA((opened,)),
            pltpu.SemaphoreType.DMA((opened // 2,)),
        ],
        compiler_params=pltpu.CompilerParams(vmem_limit_bytes=OPEN_BYTES),
        cost_estimate=cost(opened),
        name="open",
    )(transfer, ray_start, ray_end, field, jitter)
    far = pl.pallas_call(
        functools.partial(close_kernel, total, tile_cols, near, opened),
        in_specs=[own] * 7,
        out_specs=own,
        out_shape=jax.ShapeDtypeStruct((pieces, 4, rows, UNIT), jnp.int16),
        scratch_shapes=scalars + [
            planes(closed), flat(opened + closed, field.dtype), flat(opened + closed, jnp.float32),
            pltpu.VMEM((opened + closed, 4, rows, UNIT), jnp.int16), table(slab_len, closed),
            pltpu.VMEM(state_shape, jnp.float32), flat(opened, field.dtype), table(SUBLANES, opened),
            pltpu.SemaphoreType.DMA((7,)),
            pltpu.SemaphoreType.DMA((closed,)),
            pltpu.SemaphoreType.DMA((opened + closed,)),
        ],
        compiler_params=pltpu.CompilerParams(vmem_limit_bytes=CLOSE_BYTES),
        cost_estimate=cost(closed),
        name="close",
    )(transfer, ray_start, ray_end, field, halo, jitter, state)
    if not near:
        return far, []
    return far, pl.pallas_call(
        functools.partial(near_kernel, total, tile_cols, near),
        in_specs=[own] * 7,
        out_specs=[own] * near,
        out_shape=[jax.ShapeDtypeStruct((4, rows, UNIT), jnp.int16)] * near,
        scratch_shapes=scalars + [
            planes(near), flat(near, field.dtype), flat(near, jnp.float32), pltpu.VMEM((near, 4, rows, UNIT), jnp.int16), table(slab_len, near),
            pltpu.SemaphoreType.DMA((5,)),
            pltpu.SemaphoreType.DMA((near,)),
            pltpu.SemaphoreType.DMA((near,)),
        ],
        compiler_params=pltpu.CompilerParams(vmem_limit_bytes=CLOSE_BYTES),
        cost_estimate=cost(near),
        name="near",
    )(transfer, ray_start, ray_end, field, halo, jitter, far)


def composite_kernel(total, slab_len, near, order_any, transfer_any, code_any, *refs):
    near_anys = refs[:near]
    image_any, order_ref, transfer_ref, code_ref, out_ref, sems, out_sems = refs[near:]
    count, _, rows, width = code_ref.shape
    here = lax.axis_index("depth")
    pairs = [(near_any, code_ref.at[here ^ n]) for n, near_any in zip(reversed(range(near)), near_anys)]
    if near:
        for n in range(count // near - 1):
            group = n + jnp.where(n >= here // near, 1, 0)
            slabs = pl.ds(group * near, near)
            pairs.append((code_any.at[slabs], code_ref.at[slabs]))
    else:
        pairs.append((code_any, code_ref))
    copies = start_all([(order_any, order_ref), (transfer_any, transfer_ref)] + pairs, sems)
    block = math.gcd(width, 2 * LANES)
    places = [pl.ds(col, block) for col in range(0, width, block)]
    shape = (rows, block)
    depth_span, color_span = spans(slab_len)
    for copy in copies:
        copy.wait()
    unit = jnp.full(shape, transfer_ref[3]) * (0.2 / total * slab_len * TOP)
    depth_unit = unit * LOG2E
    leaving = []
    for n, cols in enumerate(places):

        def number(slab, channel, span):
            return code_ref[slab, channel, :, cols].astype(jnp.int32).astype(jnp.float32) * (span / 65535.0)

        def step(j, carry):
            shift, *colors = carry
            slab = order_ref[j]
            code = number(slab, 3, depth_span)
            idle = code < depth_span * (-32767.5 / 65535.0)
            away = jnp.where(idle, FAR, shift)
            for i in range(3):
                colors[i] = colors[i] + jnp.exp2(number(slab, i, color_span) - away)
            own = jnp.where(idle, 0.0, jnp.exp2(code + lift(depth_span)))
            return shift + depth_unit * own, *colors

        zero = jnp.zeros(shape, jnp.float32)
        first = jnp.full(shape, -lift(color_span))
        shift, *colors = lax.fori_loop(0, count, step, (first, zero, zero, zero), unroll=math.gcd(count, 16))
        for i in range(3):
            out_ref[i, :, cols] = colors[i] * (unit * (TOP / (transfer_ref[i] + jnp.full(shape, TOP))))
        out_ref[3, :, cols] = 1.0 - jnp.exp2(first - shift)
        leaving.append(pltpu.make_async_copy(out_ref.at[:, :, cols], image_any.at[:, :, cols], out_sems.at[n]))
        leaving[-1].start()
    for copy in leaving:
        copy.wait()


def composite(codes, near_codes, transfer, depth_order, total, slab_len):
    count, _, rows, width = codes.shape
    near = len(near_codes)
    blocks = width // math.gcd(width, 2 * LANES)
    own = pl.BlockSpec(memory_space=pl.ANY)
    return pl.pallas_call(
        functools.partial(composite_kernel, total, slab_len, near),
        in_specs=[own] * (3 + near),
        out_specs=own,
        out_shape=jax.ShapeDtypeStruct((4, rows, width), jnp.float32),
        scratch_shapes=[
            pltpu.SMEM(depth_order.shape, depth_order.dtype),
            pltpu.SMEM(transfer.shape, transfer.dtype),
            pltpu.VMEM(codes.shape, codes.dtype),
            pltpu.VMEM((4, rows, width), jnp.float32),
            pltpu.SemaphoreType.DMA((2 + near + (count // near - 1 if near else 1),)),
            pltpu.SemaphoreType.DMA((blocks,)),
        ],
        compiler_params=pltpu.CompilerParams(vmem_limit_bytes=SMALL_BYTES),
        name="composite",
    )(depth_order, transfer, codes, *near_codes)


def first_plane(field):
    own = pl.BlockSpec(memory_space=pl.ANY)

    def kernel(field_any, plane_any, sem):
        copy = pltpu.make_async_copy(field_any.at[0], plane_any, sem)
        copy.start()
        copy.wait()

    return pl.pallas_call(
        kernel,
        in_specs=[own],
        out_specs=own,
        out_shape=jax.ShapeDtypeStruct(field.shape[1:], field.dtype),
        scratch_shapes=[pltpu.SemaphoreType.DMA],
        compiler_params=pltpu.CompilerParams(vmem_limit_bytes=OPEN_BYTES),
        name="first_plane",
    )(field)


def on_device(field, jitter, transfer, depth_order, ray_start, ray_end):
    count = lax.axis_size("depth")
    slab_len, rows, cols = field.shape
    total = slab_len * count
    width = cols // count
    near = NEAR if width == UNIT and count == 2 * NEAR else 0
    halo = shifted(first_plane(field), "depth", -1)
    codes, near_codes = slab_codes(field, halo, jitter, transfer, ray_start, ray_end, total, near)
    if width != UNIT:
        codes = codes.transpose(1, 2, 0, 3).reshape(4, rows, count, width).transpose(2, 0, 1, 3)
    received = lax.all_to_all(codes, "depth", split_axis=0, concat_axis=0, tiled=True)
    swapped = [lax.ppermute(near_codes[n], "depth", [(i, i ^ n) for i in range(count)]) for n in reversed(range(1, near))]
    return composite(received, [*swapped, *near_codes[:1]], transfer, depth_order, total, slab_len)


def solution(mesh):
    in_specs = (P("depth", "groups", None), P("groups", None), P(), P(), P(), P())
    out_specs = P(None, "groups", "depth")
    return jax.shard_map(
        on_device, mesh=mesh, in_specs=in_specs, out_specs=out_specs, check_vma=False
    )
```

```python
import functools
import math

import jax
import jax.numpy as jnp
from jax import lax
from jax.experimental import pallas as pl
from jax.experimental.pallas import tpu as pltpu
from jax.sharding import PartitionSpec as P

TOP = 5.2
LOG2E = math.log2(math.e)
SUBLANES = 8
LANES = 128
FAR = 1.0e4
UNIT = 512
NEAR = 8
OPEN_BYTES = 54 * 1024 * 1024
CLOSE_BYTES = 53 * 1024 * 1024
SMALL_BYTES = 16 * 1024 * 1024


def spans(slab_len):
    deep = math.log2(slab_len)
    return 6.8 + deep, 13.2 + deep


def lift(span):
    return span * (32768.0 / 65535.0) - span


def shifted(value, axis, steps):
    count = lax.axis_size(axis)
    initial, last = (max(0, -steps), min(count, count - steps))
    return lax.ppermute(value, axis, [(source, source + steps) for source in range(initial, last)])


def encode(value, span):
    code = jnp.log2(value) * (65535.0 / span) + 65535.5
    code = jnp.minimum(jnp.maximum(code, 0.0), 65535.0)
    return (code.astype(jnp.int32) - 32768).astype(jnp.int16)


def tile_gains(gain_ref, gain, base, tile_cols, start_ref, end_ref, piece_of):
    sample = lax.broadcasted_iota(jnp.int32, (SUBLANES, LANES), 0) + base
    lane = lax.broadcasted_iota(jnp.int32, (SUBLANES, LANES), 1)

    def block(n, carry):
        blocks = UNIT // LANES
        tile = (piece_of(n // blocks) * UNIT + n % blocks * LANES) // tile_cols
        start = jnp.full((SUBLANES, LANES), start_ref[tile])
        end = jnp.full((SUBLANES, LANES), end_ref[tile])
        for t in range(1, LANES // tile_cols):
            start = jnp.where(lane >= t * tile_cols, start_ref[tile + t], start)
            end = jnp.where(lane >= t * tile_cols, end_ref[tile + t], end)
        cols = pl.ds(pl.multiple_of(n * LANES, LANES), LANES)
        for k in range(0, gain_ref.shape[0], SUBLANES):
            active = (sample + k >= start) & (sample + k < end)
            gain_ref[k:k + SUBLANES, cols] = jnp.where(active, gain, 0.0)
        return carry

    blocks = gain_ref.shape[1] // LANES
    lax.fori_loop(0, blocks, block, 0, unroll=math.gcd(blocks, 8))


def moment(sums, weight, value, levels):
    whole = (levels[0] + value) * (levels[1] + value) * (levels[2] + value)
    share = weight * pl.reciprocal(whole, approx=True, full_range=False)
    for n in range(3):
        sums[n] = sums[n] + share
        share = share * value


def colors(sums, before, levels):
    emitted = 1.0 - jnp.exp2(before)
    others = [(levels[1], levels[2]), (levels[2], levels[0]), (levels[0], levels[1])]
    return [emitted - t * (sums[2] + (p + q) * sums[1] + (p * q) * sums[0]) for t, (p, q) in zip(levels, others)]


def march(gain_ref, plane_ref, unit, cols, place, jitter, levels, halo=None):
    slab_len = plane_ref.shape[1]
    shape = jitter.shape
    before = jnp.zeros(shape, jnp.float32)
    through = jnp.ones(shape, jnp.float32)
    sums = [jnp.zeros(shape, jnp.float32) for _ in range(3)]
    lower = plane_ref[unit, 0, :, cols].astype(jnp.float32)
    stay = lower - jitter * lower
    for k in range(slab_len - (halo is None)):
        following = plane_ref[unit, k + 1, :, cols] if k + 1 < slab_len else halo
        upper = following.astype(jnp.float32)
        moved = jitter * upper
        value = stay + moved
        before = before + gain_ref[k:k + 1, place] * value
        beyond = jnp.exp2(before)
        moment(sums, through - beyond, value, levels)
        through = beyond
        stay = upper - moved
    return sums, before


def loop(count, body):
    def step(n, carry):
        body(n)
        return carry

    lax.fori_loop(0, count, step, 0)


def each_group(units, group, arrive, compute, store, leave):
    def step(n):
        places = [(group * n + u, c) for u in range(group) for c in range(0, UNIT, LANES)]
        arrive(n)
        results = [compute(unit, pl.ds(c, LANES), pl.ds(pl.multiple_of(unit * UNIT + c, LANES), LANES)) for unit, c in places]
        for (unit, c), result in zip(places, results):
            store(unit, pl.ds(c, LANES), result)
        leave(n)

    loop(units // group, step)


def start_all(pairs, sems):
    copies = [pltpu.make_async_copy(src, dst, sems.at[n]) for n, (src, dst) in enumerate(pairs)]
    for copy in copies:
        copy.start()
    return copies


class Pieces:
    def __init__(self, near):
        self.near = near
        self.here = lax.axis_index("depth")

    def far(self, n):
        if not self.near:
            return n
        return n + jnp.where(n >= self.here // self.near * self.near, self.near, 0)

    def close(self, n):
        return self.here ^ n

    def close_first(self):
        return self.here // self.near * self.near


def columns(piece, col=0, size=UNIT):
    return pl.ds(pl.multiple_of(piece * UNIT + col, LANES), size)


def field_copy(field_any, plane_ref, sems, piece_of, unit):
    return pltpu.make_async_copy(field_any.at[:, :, columns(piece_of(unit))], plane_ref.at[unit], sems.at[unit])


def arrive_pair(arrival, n):
    for u in range(2):
        arrival(2 * n + u).wait()


def open_kernel(total, tile_cols, near, transfer_any, start_any, end_any, field_any, jitter_any, state_any, transfer_ref,
                start_ref, end_ref, plane_ref, jitter_ref, state_ref, gain_ref, few_sems, sems, out_sems):
    units, slab_len, rows, _ = plane_ref.shape
    piece_of = Pieces(near).far
    arrival = functools.partial(field_copy, field_any, plane_ref, sems, piece_of)
    for unit in range(2):
        arrival(unit).start()
    pairs = [(transfer_any, transfer_ref), (start_any, start_ref), (end_any, end_ref)]
    pairs.append((jitter_any.at[:, columns(piece_of(0), 0, units * UNIT)], jitter_ref))
    *early, jitter_copy = start_all(pairs, few_sems)
    base = lax.axis_index("depth") * slab_len
    for copy in early:
        copy.wait()
    levels = [jnp.full((rows, LANES), transfer_ref[i]) for i in range(3)]
    gain = jnp.full((SUBLANES, LANES), transfer_ref[3]) * (-LOG2E * 0.2 / total)
    for unit in range(2, units):
        arrival(unit).start()
    tile_gains(gain_ref, gain, base, tile_cols, start_ref, end_ref, piece_of)
    jitter_copy.wait()

    def compute(unit, cols, place):
        return march(gain_ref, plane_ref, unit, cols, place, jitter_ref[:, place], levels)

    def store(unit, cols, result):
        sums, before = result
        for i, value in enumerate([*sums, before]):
            state_ref[unit, i, :, cols] = value

    def leave(n):
        return pltpu.make_async_copy(state_ref.at[n], state_any.at[n], out_sems.at[n])

    each_group(units, 1, lambda n: arrival(n).wait(), compute, store, lambda n: leave(n).start())
    loop(units, lambda n: leave(n).wait())


class Coder:
    def __init__(self, total, slab_len, shape, transfer_ref):
        depth_gain = jnp.full(shape, transfer_ref[3]) * (0.2 / total)
        self.levels = [jnp.full(shape, transfer_ref[i]) for i in range(3)]
        self.depth_unit = 1.0 / (depth_gain * (slab_len * TOP))
        self.color_unit = [self.depth_unit * ((self.levels[i] + TOP) * (1.0 / TOP)) for i in range(3)]
        self.depth_span, self.color_span = spans(slab_len)
        self.gain = depth_gain[:SUBLANES] * -LOG2E

    def codes(self, sums, before):
        tints = colors(sums, before, self.levels)
        codes = [encode(color * unit, self.color_span) for color, unit in zip(tints, self.color_unit)]
        return codes + [encode(before * (self.depth_unit * (-1.0 / LOG2E)), self.depth_span)]


def close_kernel(total, tile_cols, near, opened, transfer_any, start_any, end_any, field_any, halo_any, jitter_any, state_any,
                 out_any, transfer_ref, start_ref, end_ref, plane_ref, halo_ref, jitter_ref, out_ref, gain_ref, state_ref,
                 last_ref, last_gain_ref, few_sems, sems, out_sems):
    units, slab_len, rows, _ = plane_ref.shape
    piece_of = Pieces(near).far
    later = lambda unit: piece_of(opened + unit)
    arrival = functools.partial(field_copy, field_any, plane_ref, sems, later)
    for unit in range(2):
        arrival(unit).start()
    mine = columns(piece_of(0), 0, (opened + units) * UNIT)
    pairs = [(transfer_any, transfer_ref), (start_any, start_ref), (end_any, end_ref)]
    pairs += [(jitter_any.at[:, mine], jitter_ref), (halo_any.at[:, mine], halo_ref), (state_any, state_ref)]
    pairs.append((field_any.at[slab_len - 1, :, columns(piece_of(0), 0, opened * UNIT)], last_ref))
    copies = start_all(pairs, few_sems)
    base = lax.axis_index("depth") * slab_len
    for copy in copies[:3]:
        copy.wait()
    coder = Coder(total, slab_len, (rows, LANES), transfer_ref)
    for unit in range(2, units):
        arrival(unit).start()
    tile_gains(gain_ref, coder.gain, base, tile_cols, start_ref, end_ref, later)
    tile_gains(last_gain_ref, coder.gain, base + slab_len - 1, tile_cols, start_ref, end_ref, piece_of)
    for copy in copies[3:5]:
        copy.wait()

    def compute(unit, cols, place):
        whole = columns(opened + unit, cols.start, LANES)
        jitter = jitter_ref[:, whole]
        return coder.codes(*march(gain_ref, plane_ref, unit, cols, place, jitter, coder.levels, halo_ref[:, whole]))

    def store(first, unit, cols, codes):
        for i, code in enumerate(codes):
            out_ref[first + unit, i, :, cols] = code

    def leave(unit):
        return pltpu.make_async_copy(out_ref.at[unit], out_any.at[piece_of(unit)], out_sems.at[unit])

    def leave_pair(first, n):
        for u in range(2):
            leave(first + 2 * n + u).start()

    each_group(units, 2, functools.partial(arrive_pair, arrival), compute, functools.partial(store, opened),
              functools.partial(leave_pair, opened))
    for copy in copies[5:]:
        copy.wait()

    def finish(unit, cols, place):
        jitter = jitter_ref[:, place]
        lower = last_ref[:, place].astype(jnp.float32)
        upper = halo_ref[:, place].astype(jnp.float32)
        value = (1.0 - jitter) * lower + jitter * upper
        before = state_ref[unit, 3, :, cols]
        beyond = before + last_gain_ref[0:1, place] * value
        weight = jnp.exp2(before) - jnp.exp2(beyond)
        sums = [state_ref[unit, i, :, cols] for i in range(3)]
        moment(sums, weight, value, coder.levels)
        return coder.codes(sums, beyond)

    group = math.gcd(opened, 3)

    def leave_finished(n):
        for u in range(group):
            leave(group * n + u).start()

    each_group(opened, group, lambda n: None, finish, functools.partial(store, 0), leave_finished)
    loop(out_ref.shape[0], lambda unit: leave(unit).wait())


def near_kernel(total, tile_cols, near, transfer_any, start_any, end_any, field_any, halo_any, jitter_any, far_any, *refs):
    del far_any
    out_anys = refs[:near]
    transfer_ref, start_ref, end_ref, plane_ref, halo_ref, jitter_ref, out_ref, gain_ref, few_sems, sems, out_sems = refs[near:]
    units, slab_len, rows, _ = plane_ref.shape
    piece_of = Pieces(near).close
    arrival = functools.partial(field_copy, field_any, plane_ref, sems, piece_of)
    for unit in range(2):
        arrival(unit).start()
    first = Pieces(near).close_first()
    mine = columns(first, 0, near * UNIT)
    pairs = [(transfer_any, transfer_ref), (start_any, start_ref), (end_any, end_ref)]
    copies = start_all(pairs + [(jitter_any.at[:, mine], jitter_ref), (halo_any.at[:, mine], halo_ref)], few_sems)
    base = lax.axis_index("depth") * slab_len
    for copy in copies[:3]:
        copy.wait()
    coder = Coder(total, slab_len, (rows, LANES), transfer_ref)
    for unit in range(2, units):
        arrival(unit).start()
    tile_gains(gain_ref, coder.gain, base, tile_cols, start_ref, end_ref, piece_of)
    for copy in copies[3:]:
        copy.wait()

    def compute(unit, cols, place):
        whole = columns(piece_of(unit) - first, cols.start, LANES)
        jitter = jitter_ref[:, whole]
        return coder.codes(*march(gain_ref, plane_ref, unit, cols, place, jitter, coder.levels, halo_ref[:, whole]))

    def store(unit, cols, codes):
        for i, code in enumerate(codes):
            out_ref[unit, i, :, cols] = code

    each_group(units, 2, functools.partial(arrive_pair, arrival), compute, store, lambda n: None)
    pairs = [(out_ref.at[unit], out_anys[unit]) for unit in range(units)]
    for copy in start_all(pairs, out_sems):
        copy.wait()


def slab_codes(field, halo, jitter, transfer, ray_start, ray_end, total, near):
    slab_len, rows, cols = field.shape
    pieces = cols // UNIT
    opened = pieces * 3 // 16 * 2
    closed = pieces - near - opened
    ntiles = ray_start.shape[0]
    tile_cols = cols // ntiles
    own = pl.BlockSpec(memory_space=pl.ANY)
    scalars = [pltpu.SMEM(transfer.shape, transfer.dtype)] + [pltpu.SMEM((ntiles,), jnp.int32)] * 2

    def cost(units):
        work = slab_len * rows * units * UNIT
        return pl.CostEstimate(flops=work * 20, bytes_accessed=work * 2, transcendentals=work * 2)

    def planes(units):
        return pltpu.VMEM((units, slab_len, rows, UNIT), field.dtype)

    def flat(units, dtype):
        return pltpu.VMEM((rows, units * UNIT), dtype)

    def table(samples, units):
        return pltpu.VMEM((samples, units * UNIT), jnp.float32)

    state_shape = (opened, 4, rows, UNIT)
    state = pl.pallas_call(
        functools.partial(open_kernel, total, tile_cols, near),
        in_specs=[own] * 5,
        out_specs=own,
        out_shape=jax.ShapeDtypeStruct(state_shape, jnp.float32),
        scratch_shapes=scalars + [
            planes(opened), flat(opened, jnp.float32), pltpu.VMEM(state_shape, jnp.float32), table(slab_len, opened),
            pltpu.SemaphoreType.DMA((4,)),
            pltpu.SemaphoreType.DMA((opened,)),
            pltpu.SemaphoreType.DMA((opened,)),
        ],
        compiler_params=pltpu.CompilerParams(vmem_limit_bytes=OPEN_BYTES),
        cost_estimate=cost(opened),
        name="open",
    )(transfer, ray_start, ray_end, field, jitter)
    far = pl.pallas_call(
        functools.partial(close_kernel, total, tile_cols, near, opened),
        in_specs=[own] * 7,
        out_specs=own,
        out_shape=jax.ShapeDtypeStruct((pieces, 4, rows, UNIT), jnp.int16),
        scratch_shapes=scalars + [
            planes(closed), flat(opened + closed, field.dtype), flat(opened + closed, jnp.float32),
            pltpu.VMEM((opened + closed, 4, rows, UNIT), jnp.int16), table(slab_len, closed),
            pltpu.VMEM(state_shape, jnp.float32), flat(opened, field.dtype), table(SUBLANES, opened),
            pltpu.SemaphoreType.DMA((7,)),
            pltpu.SemaphoreType.DMA((closed,)),
            pltpu.SemaphoreType.DMA((opened + closed,)),
        ],
        compiler_params=pltpu.CompilerParams(vmem_limit_bytes=CLOSE_BYTES),
        cost_estimate=cost(closed),
        name="close",
    )(transfer, ray_start, ray_end, field, halo, jitter, state)
    if not near:
        return far, []
    return far, pl.pallas_call(
        functools.partial(near_kernel, total, tile_cols, near),
        in_specs=[own] * 7,
        out_specs=[own] * near,
        out_shape=[jax.ShapeDtypeStruct((4, rows, UNIT), jnp.int16)] * near,
        scratch_shapes=scalars + [
            planes(near), flat(near, field.dtype), flat(near, jnp.float32), pltpu.VMEM((near, 4, rows, UNIT), jnp.int16), table(slab_len, near),
            pltpu.SemaphoreType.DMA((5,)),
            pltpu.SemaphoreType.DMA((near,)),
            pltpu.SemaphoreType.DMA((near,)),
        ],
        compiler_params=pltpu.CompilerParams(vmem_limit_bytes=CLOSE_BYTES),
        cost_estimate=cost(near),
        name="near",
    )(transfer, ray_start, ray_end, field, halo, jitter, far)


def composite_kernel(total, slab_len, near, order_any, transfer_any, code_any, *refs):
    near_anys = refs[:near]
    image_any, order_ref, transfer_ref, code_ref, out_ref, sems, out_sems = refs[near:]
    count, _, rows, width = code_ref.shape
    here = lax.axis_index("depth")
    pairs = [(near_any, code_ref.at[here ^ n]) for n, near_any in zip(reversed(range(near)), near_anys)]
    if near:
        for n in range(count // near - 1):
            group = n + jnp.where(n >= here // near, 1, 0)
            slabs = pl.ds(group * near, near)
            pairs.append((code_any.at[slabs], code_ref.at[slabs]))
    else:
        pairs.append((code_any, code_ref))
    copies = start_all([(order_any, order_ref), (transfer_any, transfer_ref)] + pairs, sems)
    block = math.gcd(width, 2 * LANES)
    places = [pl.ds(col, block) for col in range(0, width, block)]
    shape = (rows, block)
    depth_span, color_span = spans(slab_len)
    for copy in copies:
        copy.wait()
    unit = jnp.full(shape, transfer_ref[3]) * (0.2 / total * slab_len * TOP)
    depth_unit = unit * LOG2E
    leaving = []
    for n, cols in enumerate(places):

        def number(slab, channel, span):
            return code_ref[slab, channel, :, cols].astype(jnp.int32).astype(jnp.float32) * (span / 65535.0)

        def step(j, carry):
            shift, *colors = carry
            slab = order_ref[j]
            code = number(slab, 3, depth_span)
            idle = code < depth_span * (-32767.5 / 65535.0)
            away = jnp.where(idle, FAR, shift)
            for i in range(3):
                colors[i] = colors[i] + jnp.exp2(number(slab, i, color_span) - away)
            own = jnp.where(idle, 0.0, jnp.exp2(code + lift(depth_span)))
            return shift + depth_unit * own, *colors

        zero = jnp.zeros(shape, jnp.float32)
        first = jnp.full(shape, -lift(color_span))
        shift, *colors = lax.fori_loop(0, count, step, (first, zero, zero, zero), unroll=math.gcd(count, 16))
        for i in range(3):
            out_ref[i, :, cols] = colors[i] * (unit * (TOP / (transfer_ref[i] + jnp.full(shape, TOP))))
        out_ref[3, :, cols] = 1.0 - jnp.exp2(first - shift)
        leaving.append(pltpu.make_async_copy(out_ref.at[:, :, cols], image_any.at[:, :, cols], out_sems.at[n]))
        leaving[-1].start()
    for copy in leaving:
        copy.wait()


def composite(codes, near_codes, transfer, depth_order, total, slab_len):
    count, _, rows, width = codes.shape
    near = len(near_codes)
    blocks = width // math.gcd(width, 2 * LANES)
    own = pl.BlockSpec(memory_space=pl.ANY)
    return pl.pallas_call(
        functools.partial(composite_kernel, total, slab_len, near),
        in_specs=[own] * (3 + near),
        out_specs=own,
        out_shape=jax.ShapeDtypeStruct((4, rows, width), jnp.float32),
        scratch_shapes=[
            pltpu.SMEM(depth_order.shape, depth_order.dtype),
            pltpu.SMEM(transfer.shape, transfer.dtype),
            pltpu.VMEM(codes.shape, codes.dtype),
            pltpu.VMEM((4, rows, width), jnp.float32),
            pltpu.SemaphoreType.DMA((2 + near + (count // near - 1 if near else 1),)),
            pltpu.SemaphoreType.DMA((blocks,)),
        ],
        compiler_params=pltpu.CompilerParams(vmem_limit_bytes=SMALL_BYTES),
        name="composite",
    )(depth_order, transfer, codes, *near_codes)


def on_device(field, jitter, transfer, depth_order, ray_start, ray_end):
    count = lax.axis_size("depth")
    slab_len, rows, cols = field.shape
    total = slab_len * count
    width = cols // count
    near = NEAR if width == UNIT and count == 2 * NEAR else 0
    halo = shifted(field[0], "depth", -1)
    codes, near_codes = slab_codes(field, halo, jitter, transfer, ray_start, ray_end, total, near)
    if width != UNIT:
        codes = codes.transpose(1, 2, 0, 3).reshape(4, rows, count, width).transpose(2, 0, 1, 3)
    received = lax.all_to_all(codes, "depth", split_axis=0, concat_axis=0, tiled=True)
    swapped = [lax.ppermute(near_codes[n], "depth", [(i, i ^ n) for i in range(count)]) for n in reversed(range(1, near))]
    return composite(received, [*swapped, *near_codes[:1]], transfer, depth_order, total, slab_len)


def solution(mesh):
    in_specs = (P("depth", "groups", None), P("groups", None), P(), P(), P(), P())
    out_specs = P(None, "groups", "depth")
    return jax.shard_map(
        on_device, mesh=mesh, in_specs=in_specs, out_specs=out_specs, check_vma=False
    )
```
